32 devices in a mesh: dp: 8 (over z, y), fsdp: 4 (over x, core).
Axes of the slice: x: 2, y: 2, z: 4, core: 2. Of those that a mesh axis runs over, the one named last changes fastest.
Arguments:
- tokens: bfloat16 [16384, 768], P(('dp', 'fsdp')), may hold values from -6 to 6
- lengths: int32 [32], P(('dp', 'fsdp')), may hold values from 80 to 512, as said below
- cotangent: bfloat16 [16384, 768], P(('dp', 'fsdp')), may hold values from -6 to 6
- qkv_weight: float32 [768, 2304], P('dp', 'fsdp'), may hold values from -0.109375 to 0.109375
- out_weight: float32 [768, 768], P('dp', 'fsdp'), may hold values from -1.75 to 1.75
- fc_weight: float32 [768, 3072], P('dp', 'fsdp'), may hold values from -0.21875 to 0.21875
- proj_weight: float32 [3072, 768], P('dp', 'fsdp'), may hold values from -0.109375 to 0.109375
- vectors: float32 [768, 12], P('dp', 'fsdp'), as said below
- qkv_first: float32 [768, 2304], P('dp', 'fsdp'), may hold values from -0.00024414062 to 0.00024414062
- out_first: float32 [768, 768], P('dp', 'fsdp'), may hold values from -4.5776367e-05 to 4.5776367e-05
- fc_first: float32 [768, 3072], P('dp', 'fsdp'), may hold values from -0.00024414062 to 0.00024414062
- proj_first: float32 [3072, 768], P('dp', 'fsdp'), may hold values from -0.00024414062 to 0.00024414062
- vectors_first: float32 [768, 12], P('dp', 'fsdp'), may hold values from -0.00024414062 to 0.00024414062
- qkv_second: float32 [768, 2304], P('dp', 'fsdp'), may hold values from 4.2330406e-09 to 3.5275338e-08
- out_second: float32 [768, 768], P('dp', 'fsdp'), may hold values from 1.4110135e-10 to 1.1288108e-09
- fc_second: float32 [768, 3072], P('dp', 'fsdp'), may hold values from 4.2330406e-09 to 2.8220272e-08
- proj_second: float32 [3072, 768], P('dp', 'fsdp'), may hold values from 4.2330406e-09 to 2.8220272e-08
- vectors_second: float32 [768, 12], P('dp', 'fsdp'), may hold values from 7.055068e-09 to 4.2330406e-08
Outputs:
- output: bfloat16 [16384, 768], P(('dp', 'fsdp'))
- input_grad: bfloat16 [16384, 768], P(('dp', 'fsdp'))
- grad_norm: float32 [], replicated
- qkv_weight_new: float32 [768, 2304], P('dp', 'fsdp')
- out_weight_new: float32 [768, 768], P('dp', 'fsdp')
- fc_weight_new: float32 [768, 3072], P('dp', 'fsdp')
- proj_weight_new: float32 [3072, 768], P('dp', 'fsdp')
- vectors_new: float32 [768, 12], P('dp', 'fsdp')
- qkv_first_new: float32 [768, 2304], P('dp', 'fsdp')
- out_first_new: float32 [768, 768], P('dp', 'fsdp')
- fc_first_new: float32 [768, 3072], P('dp', 'fsdp')
- proj_first_new: float32 [3072, 768], P('dp', 'fsdp')
- vectors_first_new: float32 [768, 12], P('dp', 'fsdp')
- qkv_second_new: float32 [768, 2304], P('dp', 'fsdp')
- out_second_new: float32 [768, 768], P('dp', 'fsdp')
- fc_second_new: float32 [768, 3072], P('dp', 'fsdp')
- proj_second_new: float32 [3072, 768], P('dp', 'fsdp')
- vectors_second_new: float32 [768, 12], P('dp', 'fsdp')
The draws below stay inside these ranges and needn't reach their ends.
Inputs may be any that keep to these rules, and one draw needn't show every extreme that they name: lengths[s] counts the leading slots of sequence s that hold real tokens; one sequence has exactly 512 and another exactly 80. `vectors`: columns 0 and 2 are positive.
All inputs are finite; a program needn't handle non-finite values.
Results may differ from the reference program's by a relative error of at most 0.013.
The reference program's roundings to bfloat16 on the way count: a program that leaves them out, or rounds other values in their place, can miss the bound.
Values may be sent and summed in bfloat16 or wider, within the bound.
No kernel may reach another device: no remote copies, remote signals or barrier semaphores. Data moves between devices by JAX's collectives and lax.ppermute only.
A program may use at most 192 MiB of HBM per device.

```python
import math
import jax
import jax.numpy as jnp
from jax import lax

D = 768
HEADS = 12
HEAD_DIM = 64
FF = 3072
SEQ = 512
MIN_LEN = 80
STEP = 10
SEQS = 32
TOKENS = 16384
VCOLS = 12
PARAMS = 7087104


def draw_lengths(key, part):
    key = jax.random.fold_in(key, 11)
    key_draw, key_long, key_short = jax.random.split(key, 3)
    drawn = jax.random.randint(key_draw, (SEQS,), MIN_LEN, SEQ + 1, dtype=jnp.int32)
    long_slot = jax.random.randint(key_long, (), 0, SEQS, dtype=jnp.int32)
    offset = jax.random.randint(key_short, (), 1, SEQS, dtype=jnp.int32)
    short_slot = (long_slot + offset) % SEQS
    slots = jnp.arange(SEQS, dtype=jnp.int32)
    drawn = jnp.where(slots == long_slot, SEQ, drawn)
    drawn = jnp.where(slots == short_slot, MIN_LEN, drawn)
    return drawn.astype(jnp.int32)


def draw_vectors(key, part):
    key = jax.random.fold_in(key, 23)
    factor_key, bias_key = jax.random.split(key)
    ceiling = 3.0
    biases = 0.2 * jax.random.normal(bias_key, (D, VCOLS), jnp.float32)
    ramp = 1.0 + (ceiling - 1.0) * jnp.arange(D, dtype=jnp.float32) / (D - 1)
    factors = jax.random.uniform(factor_key, (D, VCOLS), jnp.float32, 0.75, 1.25)
    gains = ramp[:, None] * factors
    columns = jnp.arange(VCOLS, dtype=jnp.int32)
    gain_column = (columns == 0) | (columns == 2)
    return jnp.where(gain_column[None, :], gains, biases).astype(jnp.float32)


def draw_cotangent(key, part):
    key = jax.random.fold_in(key, 37)
    noise_key, common_key = jax.random.split(key)
    level = (PARAMS / (TOKENS * FF * D)) ** 0.5
    noise = jnp.clip(jax.random.normal(noise_key, (TOKENS, D), jnp.float32), -5.5, 5.5)
    strength = 3.0
    common = strength * level * jax.random.uniform(common_key, (D,), jnp.float32, 0.5, 1.5)
    return (noise + common[None, :]).astype(jnp.bfloat16)


def shard_levels(own_key, shape, shards, low, top_value):
    def one(dim, shards_of):
        steps = jax.random.uniform(jax.random.fold_in(jax.random.fold_in(own_key, 6), dim), (shards_of,), jnp.float32, low / len(shards), top_value / len(shards))
        return jnp.repeat(jnp.exp(steps), shape[dim] // shards_of).reshape((-1,) + (1,) * (len(shape) - dim - 1))

    loudness = one(*shards[0])
    for cut in shards[1:]:
        loudness = loudness * one(*cut)
    return loudness


def bell_draw(own_key, extent, scale, bound, cuts=(), kind=jnp.bfloat16):
    values = jax.random.normal(own_key, extent, jnp.float32) * scale
    if len(cuts) > 0:
        values = shard_levels(own_key, extent, cuts, -0.22, 0.18) * values
    return jnp.clip(values, min=-bound, max=bound).astype(kind)


def setup_inputs(seed: int = 0) -> dict:
    splits = jax.random.split(jax.random.key(seed), 19)
    return {
        "tokens": bell_draw(splits[0], (TOKENS, D), 1.0, 6.0, ((0, 32),)),
        "lengths": draw_lengths(jax.random.fold_in(splits[18], 71), 0),
        "cotangent": draw_cotangent(jax.random.fold_in(splits[18], 71), 0),
        "qkv_weight": bell_draw(splits[3], (D, 3 * D), (4 * D) ** -0.5, 0.109375, ((0, 8), (1, 4)), jnp.float32),
        "out_weight": bell_draw(splits[4], (D, D), (max(D // 64, 2)) ** -0.5, 1.75, ((0, 8), (1, 4)), jnp.float32),
        "fc_weight": bell_draw(splits[5], (D, FF), D ** -0.5, 0.21875, ((0, 8), (1, 4)), jnp.float32),
        "proj_weight": bell_draw(splits[6], (FF, D), FF ** -0.5, 0.109375, ((0, 8), (1, 4)), jnp.float32),
        "vectors": draw_vectors(jax.random.fold_in(splits[18], 71), 0),
        "qkv_first": bell_draw(splits[8], (D, 3 * D), (0.11 / PARAMS ** 0.5), 0.00024414062, ((0, 8), (1, 4)), jnp.float32),
        "out_first": bell_draw(splits[9], (D, D), (0.02 / PARAMS ** 0.5), 4.57763671875e-05, ((0, 8), (1, 4)), jnp.float32),
        "fc_first": bell_draw(splits[10], (D, FF), (0.1 / PARAMS ** 0.5), 0.00024414062, ((0, 8), (1, 4)), jnp.float32),
        "proj_first": bell_draw(splits[11], (FF, D), (0.1 / PARAMS ** 0.5), 0.00024414062, ((0, 8), (1, 4)), jnp.float32),
        "vectors_first": bell_draw(splits[12], (D, VCOLS), (0.11 / PARAMS ** 0.5), 0.00024414062, ((0, 8), (1, 4)), jnp.float32),
        "qkv_second": jnp.clip(jnp.exp(math.log(3.5275338206020024e-08) - 2.1202635 * jax.random.uniform(splits[13], (D, 3 * D), jnp.float32) ** shard_levels(splits[13], (D, 3 * D), ((0, 8), (1, 4)), -0.2, 0.2)), 4.233040584722403e-09, 3.5275338206020024e-08),
        "out_second": jnp.clip(jnp.exp(math.log(1.1288108225926408e-09) - 2.0794415 * jax.random.uniform(splits[14], (D, D), jnp.float32) ** shard_levels(splits[14], (D, D), ((0, 8), (1, 4)), -0.2, 0.2)), 1.411013528240801e-10, 1.1288108225926408e-09),
        "fc_second": jnp.clip(jnp.exp(math.log(2.822027234117286e-08) - 1.89712 * jax.random.uniform(splits[15], (D, FF), jnp.float32) ** shard_levels(splits[15], (D, FF), ((0, 8), (1, 4)), -0.2, 0.2)), 4.233040584722403e-09, 2.822027234117286e-08),
        "proj_second": jnp.clip(jnp.exp(math.log(2.822027234117286e-08) - 1.89712 * jax.random.uniform(splits[16], (FF, D), jnp.float32) ** shard_levels(splits[16], (FF, D), ((0, 8), (1, 4)), -0.2, 0.2)), 4.233040584722403e-09, 2.822027234117286e-08),
        "vectors_second": jnp.clip(jnp.exp(math.log(4.233040584722403e-08) - 1.7917594 * jax.random.uniform(splits[17], (D, VCOLS), jnp.float32) ** shard_levels(splits[17], (D, VCOLS), ((0, 8), (1, 4)), -0.2, 0.2)), 7.055068085293215e-09, 4.233040584722403e-08),
    }


@jax.custom_vjp
def low(v):
    return lax.optimization_barrier(v.astype(jnp.bfloat16)).astype(jnp.float32)

@jax.custom_vjp
def low_back(v):
    return v

def low_keep(v):
    return (low(v), None)

def low_pass(kept, grad):
    return (grad,)

def back_keep(v):
    return (v, None)

def back_low(kept, grad):
    return (low(grad),)
low.defvjp(low_keep, low_pass)
low_back.defvjp(back_keep, back_low)
beta_one = 0.9
beta_two = 0.95
clip_limit = 1.0
rate_matrix = 0.1
rate_vector = 1.0
decay_matrix = 0.1
gelu_coeff = 0.7978845608028654
cubic_coeff = 0.044715
neg_large = -1e+30

def product(left, right):
    return jnp.dot(left, right, precision=lax.Precision.HIGHEST)

def layer_norm(values, gain, shift):
    average = lax.optimization_barrier(jnp.mean(values, axis=-1, keepdims=True))
    centred = values - average
    spread = lax.optimization_barrier(jnp.mean(centred * centred, axis=-1, keepdims=True))
    return centred * lax.rsqrt(spread + 1e-05) * gain + shift

def gelu_tanh(values):
    inner_arg = gelu_coeff * (values + cubic_coeff * values * values * values)
    return 0.5 * values * (1.0 + jnp.tanh(inner_arg))

def sequence_forward(rounded, tokens, length):
    qkv_weight, out_weight, fc_weight, proj_weight, vectors = rounded
    gain_one = vectors[:, 0]
    shift_one = vectors[:, 1]
    gain_two = vectors[:, 2]
    shift_two = vectors[:, 3]
    bias_q = vectors[:, 4]
    bias_v = vectors[:, 5]
    bias_out = vectors[:, 6]
    bias_proj = vectors[:, 7]
    bias_fc = jnp.transpose(vectors[:, 8:]).reshape(FF)
    seq_len = tokens.shape[0]
    positions = jnp.arange(seq_len, dtype=jnp.int32)
    key_mask = (positions[None, :] <= positions[:, None]) & (positions[None, :] < length)
    act_one = low(layer_norm(tokens, gain_one, shift_one))
    bias_qkv = jnp.concatenate([bias_q, jnp.zeros_like(bias_q), bias_v])
    qkv = low(low_back(product(act_one, qkv_weight) + bias_qkv))
    head_parts = qkv.reshape(seq_len, 3, HEADS, HEAD_DIM).transpose(1, 2, 0, 3)
    scores = jnp.einsum('hqd,hkd->hqk', head_parts[0], head_parts[1], precision=lax.Precision.HIGHEST)
    scores = low_back(scores * HEAD_DIM ** (-0.5))
    scores = jnp.where(key_mask[None, :, :], scores, neg_large)
    prob_rows = low(jax.nn.softmax(scores, axis=-1))
    head_out = jnp.einsum('hqk,hkd->hqd', prob_rows, head_parts[2], precision=lax.Precision.HIGHEST)
    mixed_low = low(low_back(head_out))
    attention = mixed_low.transpose(1, 0, 2).reshape(seq_len, D)
    resid_two = tokens + low_back(product(attention, out_weight) + bias_out)
    act_two = low(layer_norm(resid_two, gain_two, shift_two))
    pre_act = low_back(product(act_two, fc_weight) + bias_fc)
    gelu_low = low(gelu_tanh(pre_act))
    return resid_two + low_back(product(gelu_low, proj_weight) + bias_proj)

def forward_all(weights, inputs, lengths):
    rounded = tuple((low(piece) for piece in weights))
    checked = jax.checkpoint(sequence_forward)

    def scan_step(carry, operands):
        return (carry, checked(rounded, operands[0], operands[1]))
    carry_out, stacked = lax.scan(scan_step, jnp.zeros((), jnp.float32), (inputs.reshape(SEQS, SEQ, D), lengths))
    return stacked.reshape(SEQS * SEQ, D)

def adam_update(weight, gradient, moment_one, moment_two, factor, step_rate, decay_rate):
    clipped = gradient * factor
    moment_one_new = beta_one * moment_one + (1.0 - beta_one) * clipped
    moment_two_new = beta_two * moment_two + (1.0 - beta_two) * clipped * clipped
    first_hat = moment_one_new / (1.0 - beta_one ** STEP)
    second_hat = moment_two_new / (1.0 - beta_two ** STEP)
    weight_new = weight - step_rate * (first_hat / (jnp.sqrt(second_hat) + 1e-08) + decay_rate * weight)
    return (weight_new, moment_one_new, moment_two_new)

def reference(tokens, lengths, cotangent, qkv_weight, out_weight, fc_weight, proj_weight, vectors, qkv_first, out_first, fc_first, proj_first, vectors_first, qkv_second, out_second, fc_second, proj_second, vectors_second):
    weights = (qkv_weight, out_weight, fc_weight, proj_weight, vectors)
    inputs = tokens.astype(jnp.float32)

    def forward_fixed(params, values):
        return forward_all(params, values, lengths)
    result, pullback = jax.vjp(forward_fixed, weights, inputs)
    grads, grad_inputs = pullback(cotangent.astype(jnp.float32))
    squares = jnp.sum(grads[0] * grads[0]) + jnp.sum(grads[1] * grads[1]) + jnp.sum(grads[2] * grads[2])
    squares = squares + jnp.sum(grads[3] * grads[3]) + jnp.sum(grads[4] * grads[4])
    grad_norm = jnp.sqrt(squares)
    factor = jnp.minimum(1.0, clip_limit / (grad_norm + 1e-06))
    firsts = (qkv_first, out_first, fc_first, proj_first, vectors_first)
    seconds = (qkv_second, out_second, fc_second, proj_second, vectors_second)
    upd_qkv = adam_update(weights[0], grads[0], firsts[0], seconds[0], factor, rate_matrix, decay_matrix)
    upd_out = adam_update(weights[1], grads[1], firsts[1], seconds[1], factor, rate_matrix, decay_matrix)
    upd_fc = adam_update(weights[2], grads[2], firsts[2], seconds[2], factor, rate_matrix, decay_matrix)
    upd_proj = adam_update(weights[3], grads[3], firsts[3], seconds[3], factor, rate_matrix, decay_matrix)
    upd_vectors = adam_update(weights[4], grads[4], firsts[4], seconds[4], factor, rate_vector, 0.0)
    return (result.astype(jnp.bfloat16), grad_inputs.astype(jnp.bfloat16), grad_norm, upd_qkv[0], upd_out[0], upd_fc[0], upd_proj[0], upd_vectors[0], upd_qkv[1], upd_out[1], upd_fc[1], upd_proj[1], upd_vectors[1], upd_qkv[2], upd_out[2], upd_fc[2], upd_proj[2], upd_vectors[2])
```

```python
import functools

import jax
import jax.numpy as jnp
from jax import lax
from jax.experimental import pallas as pl
from jax.experimental.pallas import tpu as pltpu
from jax.sharding import PartitionSpec as P

HEAD_DIM = 64
STEP = 10

beta_one = 0.9
beta_two = 0.95
clip_limit = 1.0
rate_matrix = 0.1
rate_vector = 1.0
decay_matrix = 0.1
gelu_coeff = 0.7978845608028654
cubic_coeff = 0.044715
neg_large = -1e30
VEC_ROWS = 16

F32 = jnp.float32
BF16 = jnp.bfloat16
VMEM = pl.BlockSpec(memory_space=pltpu.VMEM)
ANY = pl.BlockSpec(memory_space=pl.ANY)
SMEM = pl.BlockSpec(memory_space=pltpu.SMEM)


def dot_nn(a, b):
    return lax.dot_general(a, b, (((1,), (0,)), ((), ())), preferred_element_type=F32)


def dot_nt(a, b):
    return lax.dot_general(a, b, (((1,), (1,)), ((), ())), preferred_element_type=F32)


def dot_tn(a, b):
    return lax.dot_general(a, b, (((0,), (0,)), ((), ())), preferred_element_type=F32)


def sds(shape, dtype):
    return jax.ShapeDtypeStruct(shape, dtype)


def call(body, ins, in_specs, outs, out_specs, scratch, flops, moved, limit):
    return pl.pallas_call(
        body,
        out_shape=outs,
        in_specs=in_specs,
        out_specs=out_specs,
        scratch_shapes=scratch,
        compiler_params=pltpu.CompilerParams(vmem_limit_bytes=limit << 20),
        cost_estimate=pl.CostEstimate(flops=flops, bytes_accessed=moved, transcendentals=0),
    )(*ins)


class Plan:
    def __init__(self, dp, fsdp, model, hidden):
        self.dp, self.fsdp = dp, fsdp
        self.sizes = {"x": fsdp // 2, "y": 2, "z": dp // 2}
        self.rows = model // dp
        self.cols = model // fsdp
        self.deep = hidden // dp
        self.direct = (
            dp % 2 == 0
            and fsdp % 2 == 0
            and self.rows % 32 == 0
            and self.cols % 32 == 0
            and self.deep % 128 == 0
        )

    def partner(self, value, stage, k):
        axis, step = {"x": ("fsdp", 2), "y": ("dp", 1), "z": ("dp", 2), "core": ("fsdp", 1)}[stage]
        n = self.dp if axis == "dp" else self.fsdp
        return lax.ppermute(value, axis, [(i, i ^ (step * k)) for i in range(n)])

    def blocks(self, order):
        out = []
        for x in range(self.sizes["x"]):
            for y in range(self.sizes["y"]):
                for z in range(self.sizes["z"]):
                    at, place, scale = {"x": x, "y": y, "z": z}, 0, 1
                    for s in order:
                        place += at[s] * scale
                        scale *= self.sizes[s]
                    out.append((place, 2 * z + y, 2 * x))
        return out

    def gather(self, value, order):
        held = value[None]
        for s in order:
            parts = [held] + [self.partner(held, s, k) for k in range(1, self.sizes[s])]
            held = jnp.concatenate(parts, axis=0)
        return held, self.partner(held, "core", 1)

    def scatter(self, own, away, order):
        arrived = self.partner(away, "core", 1)
        held, other = own, arrived
        for i, s in enumerate(reversed(order)):
            n = self.sizes[s]
            last = i == len(order) - 1
            shape = (n, held.shape[0] // n) + held.shape[1:]
            a, b = held.reshape(shape), other.reshape(shape)
            sums = [
                (a[k].astype(F32) + b[k].astype(F32)).astype(BF16) for k in list(range(1, n)) + [0]
            ]
            came = [self.partner(sums[k - 1], s, k) for k in range(1, n)]
            if last:
                return [sums[-1][0]] + [c[0] for c in came]
            held = sums[-1]
            if len(came) == 1:
                other = came[0]
            else:
                total = held.astype(F32)
                for c in came[:-1]:
                    total = total + c.astype(F32)
                held, other = total.astype(BF16), came[-1]


def block_copies(plan, order, half, place_of, me, piece, make):
    for core in range(2):
        for place, off_d, off_f in plan.blocks(order):
            make(piece[core], place, me[0] ^ off_d, me[1] ^ (off_f + core))


def pack_body(rows, deep, qkv, out, fc, proj, vec, a1, a2, b1, b2, c1, c2):
    half = rows // 2
    wide = qkv.shape[1]
    for ref, lo in ((a1, 0), (a2, half)):
        ref[0:half, 0:wide] = qkv[lo : lo + half, :].astype(BF16)
        ref[0:half, wide:] = out[lo : lo + half, :].astype(BF16)
    a1[half:, :] = jnp.zeros((VEC_ROWS, a1.shape[1]), BF16)
    eye = (
        lax.broadcasted_iota(jnp.int32, (rows, 128), 0)
        == lax.broadcasted_iota(jnp.int32, (rows, 128), 1)
    ).astype(BF16)
    turned = dot_tn(vec[...].astype(BF16), eye)
    a1[half : half + turned.shape[0], 0:128] = turned.astype(BF16)
    b1[...] = fc[0:half, :].astype(BF16)
    b2[...] = fc[half:, :].astype(BF16)
    flipped = jnp.transpose(proj[...]).astype(BF16)
    mid = flipped.shape[0] // 2
    c1[...] = flipped[:mid]
    c2[...] = flipped[mid:]


def normed(values):
    mean = jnp.mean(values, axis=-1, keepdims=True)
    centred = values - mean
    spread = jnp.mean(centred * centred, axis=-1, keepdims=True)
    inverse = lax.rsqrt(spread + 1e-05)
    return centred * inverse, inverse


def norm_back(grad_hidden, n, inverse, gain):
    g = grad_hidden * gain
    mean_plain = jnp.mean(g, axis=-1, keepdims=True)
    mean_cross = jnp.mean(g * n, axis=-1, keepdims=True)
    return inverse * (g - mean_plain - n * mean_cross)


class Table:
    def __init__(self, fsdp):
        self.per = 12 // fsdp

    def row(self, k):
        return (k // self.per) * VEC_ROWS + k % self.per

    def get(self, ref, k):
        r = self.row(k)
        return ref[r : r + 1, :]


def spread_matrix(rows, model, d):
    r = lax.broadcasted_iota(jnp.int32, (128, model), 0)
    c = lax.broadcasted_iota(jnp.int32, (128, model), 1)
    return ((c == r + d * rows) & (r < rows)).astype(BF16)


def front_body(plan, orders, n_in, me_ref, tokens, *refs):
    ins = refs[:n_in]
    qkv, act, a_out, t_out = refs[n_in : n_in + 4]
    a_v, vec_v, bias_v, sem, vec_sem, out_sem = refs[n_in + 4 :]
    fsdp, rows, half = plan.fsdp, plan.rows, plan.rows // 2
    model = a_v.shape[1]
    wide = qkv.shape[2]
    table = Table(fsdp)
    if plan.direct:
        me = (me_ref[0], me_ref[1])
        for h in range(2):

            def start(ref, place, d, f):
                at = pl.multiple_of(d * rows + h * half, 16)
                pltpu.make_async_copy(
                    ref.at[place, pl.ds(0, half), :], a_v.at[f, pl.ds(at, half), :], sem.at[f]
                ).start()
                if h == 0:
                    pltpu.make_async_copy(
                        ref.at[place, pl.ds(half, VEC_ROWS), pl.ds(0, 128)],
                        vec_v.at[d, pl.ds(pl.multiple_of(f * VEC_ROWS, 16), VEC_ROWS), :],
                        vec_sem,
                    ).start()

            block_copies(plan, orders[h], h, None, me, ins[2 * h : 2 * h + 2], start)
    else:
        for f in range(fsdp):
            pltpu.make_async_copy(ins[0].at[f], a_v.at[f], sem.at[f]).start()
    n, _ = normed(tokens[...].astype(F32))
    if plan.direct:
        pltpu.make_async_copy(vec_v, vec_v, vec_sem).wait()
        total = jnp.zeros(t_out.shape, F32)
        for d in range(plan.dp):
            total = total + dot_nn(vec_v[d], spread_matrix(rows, model, d))
        t_out[...] = total
    else:
        t_out[...] = ins[1][...]
    bias_v[:, 0:model] = jnp.broadcast_to(table.get(t_out, 4), (8, model))
    bias_v[:, model : 2 * model] = jnp.zeros((8, model), F32)
    bias_v[:, 2 * model :] = jnp.broadcast_to(table.get(t_out, 5), (8, model))
    act[...] = (n * table.get(t_out, 0) + table.get(t_out, 1)).astype(BF16)
    for f in range(fsdp):
        pltpu.make_async_copy(a_v.at[f], a_v.at[f], sem.at[f]).wait()
        pltpu.make_async_copy(a_v.at[f], a_out.at[f], out_sem.at[f]).start()
        r = dot_nn(act[...], a_v[f])[:, :wide] + bias_v[0:1, f * wide : (f + 1) * wide]
        qkv[f] = r.astype(BF16)
    for f in range(fsdp):
        pltpu.make_async_copy(a_v.at[f], a_out.at[f], out_sem.at[f]).wait()


def front(plan, orders, me, tokens, pieces, model, wide, cut):
    t = tokens.shape[0]
    fsdp = plan.fsdp
    full = wide + cut
    scratch = [
        pltpu.VMEM((fsdp, model, full), BF16),
        pltpu.VMEM((plan.dp if plan.direct else 1, fsdp * VEC_ROWS, 128), BF16),
        pltpu.VMEM((8, 3 * model), F32),
        pltpu.SemaphoreType.DMA((fsdp,)),
        pltpu.SemaphoreType.DMA,
        pltpu.SemaphoreType.DMA((fsdp,)),
    ]
    specs = [ANY] * len(pieces) if plan.direct else [ANY, VMEM]
    return call(
        functools.partial(front_body, plan, orders, len(pieces)),
        (me, tokens, *pieces),
        [SMEM, VMEM] + specs,
        (
            sds((fsdp, t, wide), BF16),
            sds((t, model), BF16),
            sds((fsdp, model, full), BF16),
            sds((fsdp * VEC_ROWS, model), F32),
        ),
        (VMEM, VMEM, ANY, VMEM),
        scratch,
        2 * t * model * 3 * model,
        12 << 20,
        48,
    )


def head_place(g, wide):
    return g // wide, g % wide


def masks(length, lo, size, keys):
    q = lax.broadcasted_iota(jnp.int32, (size, 1), 0) + lo
    limit = jnp.minimum(q, length - 1)
    k = lax.broadcasted_iota(jnp.int32, (size, keys), 1)
    return k <= limit


QBLOCK = 256


def attend_body(heads, wide, model, length_ref, qkv, mixed, logs):
    t = mixed.shape[0]
    length = length_ref[0]
    scale = HEAD_DIM**-0.5

    def part(h, which):
        f, o = head_place(which * model + h * HEAD_DIM, wide)
        return qkv[f, :, o : o + HEAD_DIM]

    for h in heads:
        q = part(h, 0) * jnp.asarray(scale, BF16)
        k, v = part(h, 1), part(h, 2)
        for lo in range(0, t, QBLOCK):
            n = lo + QBLOCK
            s = dot_nt(q[lo:n], k[:n])
            s = jnp.where(masks(length, lo, QBLOCK, n), s, neg_large)
            top = jnp.max(s, axis=-1, keepdims=True)
            e = jnp.exp(s - top)
            total = jnp.sum(e, axis=-1, keepdims=True)
            p = (e * (1.0 / total)).astype(BF16)
            o = dot_nn(p, v[:n])
            mixed[lo:n, h * HEAD_DIM : (h + 1) * HEAD_DIM] = o.astype(BF16)
            logs[lo:n, h : h + 1] = top + jnp.log(total)


def attend(qkv, length, model):
    fsdp, t, wide = qkv.shape
    heads = model // HEAD_DIM
    return call(
        functools.partial(attend_body, range(heads), wide, model),
        (length, qkv),
        [SMEM, VMEM],
        (sds((t, model), BF16), sds((t, 128), F32)),
        (VMEM, VMEM),
        [],
        4 * t * t * model,
        4 << 20,
        48,
    )


def join_body(table, wide, tokens, mixed, a_in, t_in, resid, act, wout):
    fsdp = a_in.shape[0]
    cut = a_in.shape[2] - wide
    for f in range(fsdp):
        wout[:, f * cut : (f + 1) * cut] = a_in[f, :, wide:]
    r = tokens[...].astype(F32) + dot_nn(mixed[...], wout[...]) + table.get(t_in, 6)
    resid[...] = r
    n, _ = normed(r)
    act[...] = (n * table.get(t_in, 2) + table.get(t_in, 3)).astype(BF16)


def join(plan, wide, tokens, mixed, a_can, t_can):
    t, model = tokens.shape
    return call(
        functools.partial(join_body, Table(plan.fsdp), wide),
        (tokens, mixed, a_can, t_can),
        [VMEM] * 4,
        (sds((t, model), F32), sds((t, model), BF16), sds((model, model), BF16)),
        (VMEM, VMEM, VMEM),
        [],
        2 * t * model * model,
        9 << 20,
        48,
    )


def grad_out_copies(plan, order, me, outs, slot_src, d, f, h, sem):
    off_d, off_f = d ^ me[0], f ^ me[1]
    at = {"x": off_f // 2, "y": off_d % 2, "z": off_d // 2}
    place, scale = 0, 1
    for s in order:
        place = place + at[s] * scale
        scale *= plan.sizes[s]
    core = off_f % 2
    for c in range(2):

        @pl.when(core == c)
        def _():
            pltpu.make_async_copy(slot_src, outs[2 * h + c].at[place], sem).start()


def mlp_body(plan, orders_b, orders_c, n_in, n_out, me_ref, act, cot, resid, t_in, *refs):
    ins, refs = refs[:n_in], refs[n_in:]
    output, gpre, b_out, g_b_fc, g_b_proj = refs[:5]
    gouts, refs = refs[5 : 5 + n_out], refs[5 + n_out :]
    b_v, c_v, acc, gp_v, sem, csem, osem, gsem = refs
    fsdp, rows, half = plan.fsdp, plan.rows, plan.rows // 2
    cols, chalf, deep = plan.cols, plan.cols // 2, plan.deep
    t, model = act.shape
    table = Table(fsdp)
    per = plan.dp // fsdp
    me = (me_ref[0], me_ref[1])
    if plan.direct:
        for h in range(2):

            def start_c(ref, place, d, f):
                pltpu.make_async_copy(
                    ref.at[place],
                    c_v.at[
                        pl.ds(pl.multiple_of(f * cols + h * chalf, 16), chalf),
                        pl.ds(pl.multiple_of(d * deep, 128), deep),
                    ],
                    csem.at[d // per],
                ).start()

            def start_b(ref, place, d, f):
                at = pl.multiple_of(d * rows + h * half, 16)
                pltpu.make_async_copy(
                    ref.at[place], b_v.at[f, pl.ds(at, half), :], sem.at[f]
                ).start()

            block_copies(plan, orders_b[h], h, None, me, ins[2 * h : 2 * h + 2], start_b)
            block_copies(plan, orders_c[h], h, None, me, ins[4 + 2 * h : 6 + 2 * h], start_c)
    else:
        for f in range(fsdp):
            pltpu.make_async_copy(ins[0].at[f], b_v.at[f], sem.at[f]).start()
            lanes = pl.ds(f * model, model)
            pltpu.make_async_copy(ins[1].at[:, lanes], c_v.at[:, lanes], csem.at[f]).start()
    acc[...] = resid[...] + table.get(t_in, 7)
    g_b_proj[...] = jnp.sum(cot[...].astype(F32), axis=0, keepdims=True)

    def drain(slot):
        pltpu.make_async_copy(gp_v.at[slot], gp_v.at[slot], gsem.at[slot]).wait()

    for j in range(fsdp):
        slot = j % 2
        lanes = pl.ds(j * model, model)
        pltpu.make_async_copy(b_v.at[j], b_v.at[j], sem.at[j]).wait()
        pltpu.make_async_copy(c_v.at[:, lanes], c_v.at[:, lanes], csem.at[j]).wait()
        pltpu.make_async_copy(b_v.at[j], b_out.at[j], osem.at[j]).start()
        pre = dot_nn(act[...], b_v[j]) + table.get(t_in, 8 + j)
        sq = pre * pre
        th = jnp.tanh(gelu_coeff * (pre + cubic_coeff * sq * pre))
        plus = 0.5 * (1.0 + th)
        gel = (pre * plus).astype(BF16)
        slope = plus + 0.5 * pre * (1.0 - th * th) * gelu_coeff * (1.0 + 3.0 * cubic_coeff * sq)
        acc[...] += dot_nt(gel, c_v[:, j * model : (j + 1) * model])
        gg = dot_nn(cot[...], c_v[:, j * model : (j + 1) * model]) * slope
        low = gg.astype(BF16)
        gpre[:, j * model : (j + 1) * model] = low
        g_b_fc[j : j + 1, :] = jnp.sum(low.astype(F32), axis=0, keepdims=True)
        if j >= 2:
            drain(slot)
        gp_v[slot] = dot_tn(cot[...], gel).astype(BF16)
        if plan.direct:
            for d in range(j * per, (j + 1) * per):
                for f in range(fsdp):
                    for h in range(2):
                        src = gp_v.at[
                            slot,
                            pl.ds(f * cols + h * chalf, chalf),
                            pl.ds((d - j * per) * deep, deep),
                        ]
                        grad_out_copies(plan, orders_c[h], me, gouts, src, d, f, h, gsem.at[slot])
        else:
            pltpu.make_async_copy(gp_v.at[slot], gouts[0].at[:, lanes], gsem.at[slot]).start()
    output[...] = acc[...].astype(BF16)
    drain(0)
    drain(1)
    for f in range(fsdp):
        pltpu.make_async_copy(b_v.at[f], b_out.at[f], osem.at[f]).wait()


def chunk_shapes(plan, rows, cols):
    n = plan.dp * plan.fsdp // 2
    return [sds((n, r, cols), BF16) for r in rows for _ in range(2)]


def mlp(plan, orders_b, orders_c, me, act, cot, resid, t_can, pieces, hidden):
    t, model = act.shape
    fsdp = plan.fsdp
    if plan.direct:
        grads = chunk_shapes(plan, [plan.cols // 2] * 2, plan.deep)
    else:
        grads = [sds((model, hidden), BF16)]
    return call(
        functools.partial(mlp_body, plan, orders_b, orders_c, len(pieces), len(grads)),
        (me, act, cot, resid, t_can, *pieces),
        [SMEM] + [VMEM] * 4 + [ANY] * len(pieces),
        (
            sds((t, model), BF16),
            sds((t, hidden), BF16),
            sds((fsdp, model, model), BF16),
            sds((fsdp, model), F32),
            sds((1, model), F32),
            *grads,
        ),
        (VMEM, VMEM, ANY, VMEM, VMEM) + (ANY,) * len(grads),
        [
            pltpu.VMEM((fsdp, model, model), BF16),
            pltpu.VMEM((model, hidden), BF16),
            pltpu.VMEM((t, model), F32),
            pltpu.VMEM((2, model, model), BF16),
            pltpu.SemaphoreType.DMA((fsdp,)),
            pltpu.SemaphoreType.DMA((fsdp,)),
            pltpu.SemaphoreType.DMA((fsdp,)),
            pltpu.SemaphoreType.DMA((2,)),
        ],
        8 * t * model * hidden,
        32 << 20,
        56,
    )


def mlp_back_body(plan, orders, n_out, me_ref, act, gpre, b_in, *refs):
    gact = refs[0]
    gouts = refs[1 : 1 + n_out]
    g_v, gsem = refs[1 + n_out :]
    fsdp, rows, half = plan.fsdp, plan.rows, plan.rows // 2
    model = act.shape[1]
    me = (me_ref[0], me_ref[1])

    def drain(slot):
        pltpu.make_async_copy(g_v.at[slot], g_v.at[slot], gsem.at[slot]).wait()

    for j in range(fsdp):
        slot = j % 2
        part = gpre[:, j * model : (j + 1) * model]
        if j >= 2:
            drain(slot)
        g_v[slot] = dot_tn(act[...], part).astype(BF16)
        if plan.direct:
            for d in range(plan.dp):
                for h in range(2):
                    src = g_v.at[slot, pl.ds(d * rows + h * half, half), :]
                    grad_out_copies(plan, orders[h], me, gouts, src, d, j, h, gsem.at[slot])
        else:
            pltpu.make_async_copy(g_v.at[slot], gouts[0].at[j], gsem.at[slot]).start()
        back = dot_nt(part, b_in[j])
        if j == 0:
            gact[...] = back
        else:
            gact[...] += back
    drain(0)
    drain(1)


def mlp_back(plan, orders, me, act, gpre, b_can):
    t, model = act.shape
    fsdp = plan.fsdp
    if plan.direct:
        grads = chunk_shapes(plan, [plan.rows // 2] * 2, model)
    else:
        grads = [sds((fsdp, model, model), BF16)]
    return call(
        functools.partial(mlp_back_body, plan, orders, len(grads)),
        (me, act, gpre, b_can),
        [SMEM] + [VMEM] * 3,
        (sds((t, model), F32), *grads),
        (VMEM,) + (ANY,) * len(grads),
        [pltpu.VMEM((2, model, model), BF16), pltpu.SemaphoreType.DMA((2,))],
        4 * t * model * gpre.shape[1],
        16 << 20,
        48,
    )


def join_back_body(table, gact, cot, resid, mixed, wout, t_in, gresid, gmixed, g_out, g_vec):
    n, inverse = normed(resid[...])
    e = gact[...]
    g_vec[...] = jnp.zeros(g_vec.shape, F32)
    g_vec[0:1, :] = jnp.sum(e * n, axis=0, keepdims=True)
    g_vec[1:2, :] = jnp.sum(e, axis=0, keepdims=True)
    r = cot[...].astype(F32) + norm_back(e, n, inverse, table.get(t_in, 2))
    gresid[...] = r
    branch = r.astype(BF16)
    g_vec[2:3, :] = jnp.sum(branch.astype(F32), axis=0, keepdims=True)
    gmixed[...] = dot_nt(branch, wout[...]).astype(BF16)
    g_out[...] = dot_tn(mixed[...], branch).astype(BF16)


def join_back(plan, gact, cot, resid, mixed, wout, t_can):
    t, model = cot.shape
    return call(
        functools.partial(join_back_body, Table(plan.fsdp)),
        (gact, cot, resid, mixed, wout, t_can),
        [VMEM] * 6,
        (
            sds((t, model), F32),
            sds((t, model), BF16),
            sds((model, model), BF16),
            sds((8, model), F32),
        ),
        (VMEM,) * 4,
        [],
        4 * t * model * model,
        10 << 20,
        48,
    )


def attend_back_body(heads, wide, model, length_ref, qkv, gmixed, logs, gqkv):
    t = gmixed.shape[0]
    length = length_ref[0]
    scale = HEAD_DIM**-0.5

    def put(h, which, lo, hi, value):
        f, o = head_place(which * model + h * HEAD_DIM, wide)
        gqkv[f, lo:hi, o : o + HEAD_DIM] = value.astype(BF16)

    def part(h, which):
        f, o = head_place(which * model + h * HEAD_DIM, wide)
        return qkv[f, :, o : o + HEAD_DIM]

    for h in heads:
        q = part(h, 0)
        small = q * jnp.asarray(scale, BF16)
        k, v = part(h, 1), part(h, 2)
        go = gmixed[:, h * HEAD_DIM : (h + 1) * HEAD_DIM]
        gk, gv = [], []
        for lo in range(0, t, QBLOCK):
            n = lo + QBLOCK
            s = dot_nt(small[lo:n], k[:n])
            s = jnp.where(masks(length, lo, QBLOCK, n), s, neg_large)
            p = jnp.exp(s - logs[lo:n, h : h + 1])
            gp = dot_nt(go[lo:n], v[:n])
            inner = jnp.sum(p * gp, axis=-1, keepdims=True)
            ds = (p * (gp - inner)).astype(BF16)
            put(h, 0, lo, n, dot_nn(ds, k[:n]) * scale)
            gv.append(dot_tn(p.astype(BF16), go[lo:n]))
            gk.append(dot_tn(ds, small[lo:n]))
        for b in range(t // QBLOCK):
            rows = slice(b * QBLOCK, (b + 1) * QBLOCK)
            put(h, 1, rows.start, rows.stop, sum(x[rows] for x in gk[b:]))
            put(h, 2, rows.start, rows.stop, sum(x[rows] for x in gv[b:]))


def attend_back(qkv, gmixed, logs, length):
    fsdp, t, wide = qkv.shape
    model = gmixed.shape[1]
    heads = model // HEAD_DIM
    return call(
        functools.partial(attend_back_body, range(heads), wide, model),
        (length, qkv, gmixed, logs),
        [SMEM] + [VMEM] * 3,
        sds(qkv.shape, BF16),
        VMEM,
        [],
        10 * t * t * model,
        6 << 20,
        48,
    )


def back_body(plan, orders, n_out, me_ref, tokens, act, gqkv, a_in, g_out, gresid, t_in, g_two, g_b_fc, g_b_proj, *refs):
    input_grad = refs[0]
    gouts = refs[1 : 1 + n_out]
    g_v, tab, vec_v, sum_v, gsem, vsem = refs[1 + n_out :]
    fsdp, rows, half = plan.fsdp, plan.rows, plan.rows // 2
    t, model = tokens.shape
    wide = gqkv.shape[2]
    cut = a_in.shape[2] - wide
    table = Table(fsdp)
    me = (me_ref[0], me_ref[1])
    back = jnp.zeros((t, model), F32)
    for f in range(fsdp):
        part = gqkv[f]
        g_v[f, :, 0:wide] = dot_tn(act[...], part).astype(BF16)
        g_v[f, :, wide:] = g_out[:, f * cut : (f + 1) * cut]
        if plan.direct:
            for d in range(plan.dp):
                for h in range(2):
                    src = g_v.at[f, pl.ds(d * rows + h * half, half), :]
                    if h == 0:
                        pieces = [r.at[:, pl.ds(0, half), :] for r in gouts[:2]]
                    else:
                        pieces = gouts[2:]
                    grad_out_copies(plan, orders[h], me, pieces, src, d, f, 0, gsem)
        else:
            pltpu.make_async_copy(g_v.at[f], gouts[0].at[f], gsem).start()
        sum_v[0:1, f * wide : (f + 1) * wide] = jnp.sum(part.astype(F32), axis=0, keepdims=True)
        back = back + dot_nt(part, a_in[f, :, :wide])
    n, inverse = normed(tokens[...].astype(F32))
    tab[...] = jnp.zeros(tab.shape, F32)

    def put(k, value):
        r = table.row(k)
        tab[r : r + 1, :] = value

    put(0, jnp.sum(back * n, axis=0, keepdims=True))
    put(1, jnp.sum(back, axis=0, keepdims=True))
    put(2, g_two[0:1, :])
    put(3, g_two[1:2, :])
    put(4, sum_v[0:1, 0:model])
    put(5, sum_v[0:1, 2 * model :])
    put(6, g_two[2:3, :])
    put(7, g_b_proj[...])
    for j in range(fsdp):
        put(8 + j, g_b_fc[j : j + 1, :])
    low = tab[...].astype(BF16)
    if plan.direct:
        vec_v[...] = jnp.zeros(vec_v.shape, BF16)
        for d in range(plan.dp):
            vec_v[d, :, 0:128] = dot_nt(low, spread_matrix(rows, model, d)).astype(BF16)
            for f in range(fsdp):
                src = vec_v.at[d, pl.ds(f * VEC_ROWS, VEC_ROWS), :]
                pieces = [r.at[:, pl.ds(half, VEC_ROWS), :] for r in gouts[:2]]
                grad_out_copies(plan, orders[0], me, pieces, src, d, f, 0, vsem)
    else:
        vec_v[0] = low
        pltpu.make_async_copy(vec_v.at[0], gouts[1], vsem).start()
    r = gresid[...] + norm_back(back, n, inverse, table.get(t_in, 0))
    input_grad[...] = r.astype(BF16)
    pltpu.make_async_copy(g_v, g_v, gsem).wait()
    pltpu.make_async_copy(vec_v, vec_v, vsem).wait()


def back_end(plan, orders, me, tokens, act, gqkv, a_can, g_out, gresid, t_can, g_two, g_b_fc, g_b_proj):
    t, model = tokens.shape
    fsdp, _, wide = gqkv.shape
    full = a_can.shape[2]
    half = plan.rows // 2
    if plan.direct:
        grads = chunk_shapes(plan, [half + VEC_ROWS, half], full)
    else:
        grads = [sds((fsdp, model, full), BF16), sds((fsdp * VEC_ROWS, model), BF16)]
    return call(
        functools.partial(back_body, plan, orders, len(grads)),
        (me, tokens, act, gqkv, a_can, g_out, gresid, t_can, g_two, g_b_fc, g_b_proj),
        [SMEM] + [VMEM] * 10,
        (sds((t, model), BF16), *grads),
        (VMEM,) + (ANY,) * len(grads),
        [
            pltpu.VMEM((fsdp, model, full), BF16),
            pltpu.VMEM((fsdp * VEC_ROWS, model), F32),
            pltpu.VMEM((plan.dp if plan.direct else 1, fsdp * VEC_ROWS, model), BF16),
            pltpu.VMEM((8, 3 * model), F32),
            pltpu.SemaphoreType.DMA,
            pltpu.SemaphoreType.DMA,
        ],
        4 * t * model * 3 * model,
        20 << 20,
        56,
    )


def total_of(refs):
    s = refs[0][...].astype(F32)
    for r in refs[1:]:
        s = s + r[...].astype(F32)
    return s


def finish_body(kind, wide, rows, per, counts, *refs):
    n = sum(counts)
    ins, outs = refs[:n], refs[n:]
    one, two = total_of(ins[: counts[0]]), total_of(ins[counts[0] :])
    square = outs[-1]
    if kind == "fc":
        half = rows // 2
        outs[0][0:half, :] = one
        outs[0][half:, :] = two
        total = jnp.sum(one * one) + jnp.sum(two * two)
    elif kind == "proj":
        both = jnp.concatenate([one, two], axis=0)
        outs[0][...] = jnp.transpose(both)
        total = jnp.sum(both * both)
    else:
        half = rows // 2
        turned = one[half : half + VEC_ROWS, 0:128]
        one = one[0:half]
        outs[0][0:half, :] = one[:, :wide]
        outs[0][half:, :] = two[:, :wide]
        outs[1][0:half, :] = one[:, wide:]
        outs[1][half:, :] = two[:, wide:]
        flat = jnp.transpose(turned)
        vec = flat[0:rows, 0:per]
        outs[2][...] = vec
        total = jnp.sum(one * one) + jnp.sum(two * two) + jnp.sum(vec * vec)
    square[...] = jnp.broadcast_to(total, square.shape)


def finish(kind, first, second, outs, wide, rows, per):
    outs = [sds(s, F32) for s in outs] + [sds((1, 128), F32)]
    ins = (*first, *second)
    return call(
        functools.partial(finish_body, kind, wide, rows, per, (len(first), len(second))),
        ins,
        [VMEM] * len(ins),
        tuple(outs),
        (VMEM,) * len(outs),
        [],
        1 << 20,
        2 << 20,
        16,
    )


def update_body(count, *refs):
    norms = refs[0]
    ins, outs = refs[1 : 1 + 4 * count], refs[1 + 4 * count :]
    norm = jnp.sqrt(jnp.sum(norms[...], axis=0, keepdims=True))
    outs[0][...] = norm
    factor = jnp.minimum(1.0, clip_limit / (norm[:, 0:1] + 1e-06))
    for i in range(count):
        w, g, one, two = (r[...] for r in ins[4 * i : 4 * i + 4])
        last = i == count - 1
        rate, decay = (rate_vector, 0.0) if last else (rate_matrix, decay_matrix)
        clipped = g * factor
        one_new = beta_one * one + (1.0 - beta_one) * clipped
        two_new = beta_two * two + (1.0 - beta_two) * clipped * clipped
        first_hat = one_new / (1.0 - beta_one**STEP)
        second_hat = two_new / (1.0 - beta_two**STEP)
        outs[1 + i][...] = w - rate * (first_hat / (jnp.sqrt(second_hat) + 1e-08) + decay * w)
        outs[1 + count + i][...] = one_new
        outs[1 + 2 * count + i][...] = two_new


def update(norms, weights, grads, firsts, seconds):
    count = len(weights)
    ins = [norms]
    for group in zip(weights, grads, firsts, seconds):
        ins += group
    outs = [sds((1, 128), F32)] + [sds(w.shape, F32) for w in weights] * 3
    return call(
        functools.partial(update_body, count),
        ins,
        [VMEM] * len(ins),
        tuple(outs),
        (VMEM,) * len(outs),
        [],
        4 << 20,
        6 << 20,
        32,
    )


def body(
    tokens,
    lengths,
    cotangent,
    qkv_weight,
    out_weight,
    fc_weight,
    proj_weight,
    vectors,
    qkv_first,
    out_first,
    fc_first,
    proj_first,
    vectors_first,
    qkv_second,
    out_second,
    fc_second,
    proj_second,
    vectors_second,
):
    dp, fsdp = lax.axis_size("dp"), lax.axis_size("fsdp")
    model = tokens.shape[1]
    wide, cut = qkv_weight.shape[1], out_weight.shape[1]
    hidden = fc_weight.shape[1] * fsdp
    per = vectors.shape[1]
    plan = Plan(dp, fsdp, model, hidden)
    rows, half = plan.rows, plan.rows // 2
    me = jnp.stack([lax.axis_index("dp"), lax.axis_index("fsdp")]).astype(jnp.int32)
    orders_a = (("z", "y", "x"), ("z", "x", "y"))
    orders_b = (("z", "y", "x"), ("z", "x", "y"))
    orders_c = (("y", "z", "x"), ("x", "z", "y"))

    if plan.direct:
        packed = call(
            functools.partial(pack_body, rows, plan.deep),
            (qkv_weight, out_weight, fc_weight, proj_weight, vectors),
            [VMEM] * 5,
            (
                sds((half + VEC_ROWS, wide + cut), BF16),
                sds((half, wide + cut), BF16),
                sds((half, model), BF16),
                sds((half, model), BF16),
                sds((plan.cols // 2, plan.deep), BF16),
                sds((plan.cols // 2, plan.deep), BF16),
            ),
            (VMEM,) * 6,
            [],
            1 << 20,
            2 << 20,
            16,
        )
        a_in = [r for h in range(2) for r in plan.gather(packed[h], orders_a[h])]
        b_in = [r for h in range(2) for r in plan.gather(packed[2 + h], orders_b[h])]
        c_in = [r for h in range(2) for r in plan.gather(packed[4 + h], orders_c[h])]
        bc_in = b_in + c_in
    else:

        def whole(shard):
            down = lax.all_gather(shard.astype(BF16), "dp", axis=0, tiled=True)
            return lax.all_gather(down, "fsdp", axis=0, tiled=False)

        a_all = whole(jnp.concatenate([qkv_weight, out_weight], axis=1))
        b_all = whole(fc_weight)
        c_all = jnp.transpose(whole(proj_weight), (0, 2, 1)).reshape(model, hidden)
        v_all = jnp.transpose(whole(vectors).astype(F32), (0, 2, 1))
        v_all = jnp.pad(v_all, ((0, 0), (0, VEC_ROWS - per), (0, 0)))
        a_in = [a_all, v_all.reshape(fsdp * VEC_ROWS, model)]
        bc_in = [b_all, c_all]

    qkv, act_one, a_can, t_can = front(plan, orders_a, me, tokens, a_in, model, wide, cut)
    mixed, logs = attend(qkv, lengths, model)
    resid_two, act_two, wout = join(plan, wide, tokens, mixed, a_can, t_can)
    output, gpre, b_can, g_b_fc, g_b_proj, *g_proj = mlp(
        plan, orders_b, orders_c, me, act_two, cotangent, resid_two, t_can, bc_in, hidden
    )
    gact, *g_fc = mlp_back(plan, orders_b, me, act_two, gpre, b_can)
    gresid, gmixed, g_out, g_two = join_back(
        plan, gact, cotangent, resid_two, mixed, wout, t_can
    )
    gqkv = attend_back(qkv, gmixed, logs, lengths)
    input_grad, *g_a = back_end(
        plan, orders_a, me, tokens, act_one, gqkv, a_can, g_out, gresid, t_can, g_two, g_b_fc, g_b_proj
    )

    if plan.direct:
        c_sum = [plan.scatter(g_proj[2 * h], g_proj[2 * h + 1], orders_c[h]) for h in range(2)]
        b_sum = [plan.scatter(g_fc[2 * h], g_fc[2 * h + 1], orders_b[h]) for h in range(2)]
        a_sum = [plan.scatter(g_a[2 * h], g_a[2 * h + 1], orders_a[h]) for h in range(2)]
        d_proj, s_c = finish("proj", c_sum[0], c_sum[1], [proj_weight.shape], wide, rows, per)
        d_fc, s_b = finish("fc", b_sum[0], b_sum[1], [fc_weight.shape], wide, rows, per)
        shapes = [qkv_weight.shape, out_weight.shape, vectors.shape]
        d_qkv, d_out, d_vec, s_a = finish("attention", a_sum[0], a_sum[1], shapes, wide, rows, per)
        squares = s_a + s_b + s_c
    else:

        def shared(value):
            mine = lax.psum_scatter(value, "fsdp", scatter_dimension=0, tiled=False)
            return lax.psum_scatter(mine, "dp", scatter_dimension=0, tiled=True).astype(F32)

        d_a = shared(g_a[0])
        d_qkv, d_out = d_a[:, :wide], d_a[:, wide:]
        d_fc = shared(g_fc[0])
        d_proj = shared(jnp.transpose(g_proj[0].reshape(fsdp, plan.cols, hidden), (0, 2, 1)))
        d_vec = shared(jnp.transpose(g_a[1].reshape(fsdp, VEC_ROWS, model)[:, :per], (0, 2, 1)))
        total = sum(jnp.sum(d * d) for d in (d_qkv, d_out, d_fc, d_proj, d_vec))
        squares = jnp.full((1, 128), total)

    sent = jnp.broadcast_to(squares[None], (dp * fsdp, 1, 128))
    norms = lax.all_to_all(sent, ("dp", "fsdp"), 0, 0, tiled=True).reshape(dp * fsdp, 128)
    result = update(
        norms,
        (qkv_weight, out_weight, fc_weight, proj_weight, vectors),
        (d_qkv, d_out, d_fc, d_proj, d_vec),
        (qkv_first, out_first, fc_first, proj_first, vectors_first),
        (qkv_second, out_second, fc_second, proj_second, vectors_second),
    )
    return (output, input_grad, result[0][0, 0], *result[1:])


def solution(mesh):
    tokens = P(("dp", "fsdp"), None)
    table = P("dp", "fsdp")
    return jax.shard_map(
        body,
        mesh=mesh,
        in_specs=(tokens, P(("dp", "fsdp")), tokens) + (table,) * 15,
        out_specs=(tokens, tokens, P()) + (table,) * 15,
        check_vma=False,
    )
```

```python
import functools

import jax
import jax.numpy as jnp
from jax import lax
from jax.experimental import pallas as pl
from jax.experimental.pallas import tpu as pltpu
from jax.sharding import PartitionSpec as P

HEAD_DIM = 64
STEP = 10

beta_one = 0.9
beta_two = 0.95
clip_limit = 1.0
rate_matrix = 0.1
rate_vector = 1.0
decay_matrix = 0.1
gelu_coeff = 0.7978845608028654
cubic_coeff = 0.044715
neg_large = -1e30
VEC_ROWS = 16

F32 = jnp.float32
BF16 = jnp.bfloat16
VMEM = pl.BlockSpec(memory_space=pltpu.VMEM)
HELD = pl.BlockSpec(memory_space=pltpu.VMEM)
ANY = pl.BlockSpec(memory_space=pl.ANY)
HBM = pl.BlockSpec(memory_space=pltpu.HBM)
SMEM = pl.BlockSpec(memory_space=pltpu.SMEM)
ALL = slice(None)


def dot_nn(a, b):
    return lax.dot_general(a, b, (((1,), (0,)), ((), ())), preferred_element_type=F32)


def dot_nt(a, b):
    return lax.dot_general(a, b, (((1,), (1,)), ((), ())), preferred_element_type=F32)


def dot_tn(a, b):
    return lax.dot_general(a, b, (((0,), (0,)), ((), ())), preferred_element_type=F32)


def sds(shape, dtype):
    return jax.ShapeDtypeStruct(shape, dtype)


class Chain:
    def __init__(self):
        self.waits = []

    def wait_for(self, *arrays):
        self.waits += arrays

    def call(self, name, body, ins, in_specs, outs, out_specs, scratch, limit, aliases=None):
        several = isinstance(outs, (tuple, list))
        if not several:
            outs, out_specs = (outs,), (out_specs,)
        n_in, extra = len(ins), len(self.waits)
        pins = ((HELD, pltpu.VMEM), (HBM, pltpu.HBM))

        def run(*refs):
            body(*refs[:n_in], *refs[n_in + extra :])

        placed, made = [], []
        for v, spec in zip(ins, in_specs):
            for pin, space in pins:
                if spec is pin:
                    v = pltpu.with_memory_space_constraint(v, space)
            placed.append(v)
        for o, spec in zip(outs, out_specs):
            for pin, space in pins:
                if spec is pin:
                    o = space(o.shape, o.dtype)
            made.append(o)
        results = pl.pallas_call(
            run,
            name=name,
            input_output_aliases=aliases or {},
            out_shape=tuple(made),
            in_specs=[*in_specs, *[ANY] * extra],
            out_specs=tuple(out_specs),
            scratch_shapes=scratch,
            compiler_params=pltpu.CompilerParams(vmem_limit_bytes=limit << 20),
        )(*placed, *self.waits)
        self.waits = [min(results, key=lambda r: r.size)]
        return results if several else results[0]


class Plan:
    def __init__(self, dp, fsdp, model, hidden):
        self.dp, self.fsdp = dp, fsdp
        self.nz, self.nx = dp // 2, fsdp // 2
        self.rows = model // dp
        self.cols = model // fsdp
        self.deep = hidden // dp
        self.direct = (
            dp == 2 * fsdp
            and fsdp % 2 == 0
            and self.rows % 32 == 0
            and self.cols % 32 == 0
            and self.deep % 128 == 0
            and hidden == fsdp * model
            and fsdp == 4
        )

    def partner(self, name, value, stage, k=1):
        axis, step = {"x": ("fsdp", 2), "y": ("dp", 1), "z": ("dp", 2), "core": ("fsdp", 1)}[stage]
        n = self.dp if axis == "dp" else self.fsdp
        with jax.named_scope(f"{name}_{stage}"):
            return lax.ppermute(value, axis, [(i, i ^ (step * k)) for i in range(n)])

    def along_z(self, name, value):
        groups = [[2 * z + y for z in range(self.nz)] for y in range(2)]
        with jax.named_scope(f"{name}_z"):
            return lax.all_to_all(value, "dp", 0, 0, tiled=True, axis_index_groups=groups)

    def split(self):
        return (self.nz, 2, 2, self.rows // 2) if self.direct else (1, 1, 1, self.rows * self.dp)


class Me:
    def __init__(self, ref):
        self.z, self.y, self.x, self.core = ref[0], ref[1], ref[2], ref[3]
        self.other_y, self.other_x = 1 - self.y, 1 - self.x

    def fsdp(self, x, away):
        return 2 * x + (self.core ^ away)


def move(chain, name, me, arrays, outs, copies):
    n, m = len(arrays), len(outs)
    still = copies(Me([0, 0, 0, 0]))
    count = sum(len(targets) for _, _, _, targets in still)

    def body(me_ref, *refs):
        ins, outs_, refs = refs[:n], refs[n : n + m], refs[n + m :]
        held, sem, out_sem = refs[:-2], refs[-2], refs[-1]
        todo = copies(Me(me_ref))
        loads = [
            pltpu.make_async_copy(ins[s].at[si], held[i], sem.at[i])
            for i, (s, si, _, _) in enumerate(todo)
        ]
        for c in loads:
            c.start()
        stores = []
        for i, (_, _, _, targets) in enumerate(todo):
            loads[i].wait()
            for t, ti in targets:
                c = pltpu.make_async_copy(held[i], outs_[t].at[ti], out_sem.at[len(stores)])
                c.start()
                stores.append(c)
        for c in stores:
            c.wait()

    return chain.call(
        name,
        body,
        (me, *arrays),
        [SMEM] + [ANY] * n,
        tuple(sds(s, BF16) for s in outs),
        (ANY,) * m,
        [pltpu.VMEM(shape, BF16) for _, _, shape, _ in still]
        + [pltpu.SemaphoreType.DMA((len(still),)), pltpu.SemaphoreType.DMA((count,))],
        12,
    )


def gate(chain, name, *arrays):
    return chain.call(
        name,
        lambda *refs: None,
        arrays,
        [ANY] * len(arrays),
        tuple(sds(v.shape, v.dtype) for v in arrays),
        (ANY,) * len(arrays),
        [],
        1,
        {i: i for i in range(len(arrays))},
    )


def add_up(chain, name, me, arrays, outs, sums, after=None, big=False):
    n, m = len(arrays), len(outs)
    still = sums(Me([0, 0, 0, 0]))
    terms = [shape for _, _, shape, parts in still for _ in parts]

    def body(me_ref, *refs):
        ins, outs_, refs = refs[:n], refs[n : n + m], refs[n + m :]
        held, sem = refs[:-1], refs[-1]
        todo, i = [], 0
        for t, ti, shape, parts in sums(Me(me_ref)):
            group = []
            for s, si in parts:
                src = ins[s].at[si] if si is not None else ins[s]
                c = pltpu.make_async_copy(src, held[i], sem.at[i])
                c.start()
                group.append((c, held[i]))
                i += 1
            todo.append((t, ti, group))
        done = []
        for t, ti, group in todo:
            total = None
            for c, ref in group:
                c.wait()
                v = ref[...].astype(F32)
                total = v if total is None else total + v
            if after is None:
                outs_[t][ti] = total.astype(BF16)
            else:
                done.append(total)
        if after is not None:
            after(done, outs_)

    return chain.call(
        name,
        body,
        (me, *arrays),
        [SMEM] + [HBM if i == 0 and big else ANY for i in range(n)],
        tuple(outs),
        (VMEM,) * m,
        [pltpu.VMEM(s, BF16) for s in terms] + [pltpu.SemaphoreType.DMA((len(terms),))],
        16,
    )


def pack_body(ins, outs, held, sem):
    todo = [pltpu.make_async_copy(i, h, sem.at[k]) for k, (i, h) in enumerate(zip(ins, held))]
    for c in todo:
        c.start()
    for c in todo:
        c.wait()
    qkv, out, fc, proj, vec = (h[...] for h in held)
    a, b, c = outs
    wide, model = qkv.shape[1], fc.shape[1]
    columns = jnp.transpose(vec)
    start = wide // 128 * 128
    for i in range(a.shape[0]):
        a[i, :, start:] = jnp.zeros((a.shape[1], a.shape[2] - start), BF16)
        a[i, :, 0:wide] = qkv.astype(BF16)
        a[i, :, wide : wide + columns.shape[1]] = columns.astype(BF16)
    b[:, model:] = jnp.zeros((b.shape[0], b.shape[1] - model), BF16)
    b[:, 0:model] = fc.astype(BF16)
    b[:, model : model + out.shape[1]] = out.astype(BF16)
    c[...] = proj.astype(BF16).reshape(c.shape)


def pack(chain, plan, weights, a_full, b_full):
    count = len(weights)

    def run(*refs):
        pack_body(refs[:count], refs[count : count + 3], refs[count + 3 : -1], refs[-1])

    return chain.call(
        "pack",
        run,
        weights,
        [HBM] * count,
        (
            sds((plan.nz, plan.rows, a_full), BF16),
            sds((plan.rows, b_full), BF16),
            sds((2, plan.cols // 2, plan.deep), BF16),
        ),
        (VMEM,) * 3,
        [pltpu.VMEM(w.shape, F32) for w in weights] + [pltpu.SemaphoreType.DMA((count,))],
        6,
    )


def normed(values):
    mean = jnp.mean(values, axis=-1, keepdims=True)
    centred = values - mean
    spread = jnp.mean(centred * centred, axis=-1, keepdims=True)
    inverse = lax.rsqrt(spread + 1e-05)
    return centred * inverse, inverse


def norm_back(grad_hidden, n, inverse, gain):
    g = grad_hidden * gain
    mean_plain = jnp.mean(g, axis=-1, keepdims=True)
    mean_cross = jnp.mean(g * n, axis=-1, keepdims=True)
    return inverse * (g - mean_plain - n * mean_cross)


class Table:
    def __init__(self, fsdp):
        self.per = 12 // fsdp

    def row(self, k):
        return (k // self.per) * VEC_ROWS + k % self.per

    def get(self, ref, k):
        r = self.row(k)
        return ref[r : r + 1, :]


def spread_matrix(rows, model, d):
    r = lax.broadcasted_iota(jnp.int32, (128, model), 0)
    c = lax.broadcasted_iota(jnp.int32, (128, model), 1)
    return ((c == r + d * rows) & (r < rows)).astype(BF16)


def table_loads(plan, me, ins):
    for away in range(2):
        p, r0, r1 = ins[3 * away : 3 * away + 3]
        for y in range(2):
            for x, ref in ((me.x, p.at[0]), (me.other_x, r0)):
                yield ref, (y,), me.fsdp(x, away), (ALL, y), 0
        for y, ref in ((me.y, p.at[1]), (me.other_y, r1)):
            for x in range(plan.nx):
                yield ref, (x,), me.fsdp(x, away), (ALL, y), 1


def front_body(plan, n_in, me_ref, tokens, *refs):
    ins = refs[:n_in]
    qkv, act, a_out, t_out = refs[n_in : n_in + 4]
    a_v, bias_v, sem, out_sem = refs[n_in + 4 :]
    fsdp = plan.fsdp
    full = a_v.shape[-1]
    model = tokens.shape[1]
    wide = qkv.shape[2]
    table = Table(fsdp)
    if plan.direct:
        for ref, si, f, ti, h in table_loads(plan, Me(me_ref), ins):
            pltpu.make_async_copy(ref.at[si], a_v.at[(f, *ti, h)], sem.at[f]).start()
    else:
        for f in range(fsdp):
            pltpu.make_async_copy(ins[0].at[f], a_v.at[f], sem.at[f]).start()
    n, _ = normed(tokens[...].astype(F32))
    start = wide // 128 * 128
    for f in range(fsdp):
        pltpu.make_async_copy(a_v.at[f], a_v.at[f], sem.at[f]).wait()
        pltpu.make_async_copy(a_v.at[f], a_out.at[f], out_sem.at[f]).start()
        turned = jnp.transpose(a_v[f].reshape(model, full)[:, start:].astype(F32))
        t_out[f * VEC_ROWS : f * VEC_ROWS + table.per, :] = turned[
            wide - start : wide - start + table.per
        ]
    bias_v[:, 0:model] = jnp.broadcast_to(table.get(t_out, 4), (8, model))
    bias_v[:, model : 2 * model] = jnp.zeros((8, model), F32)
    bias_v[:, 2 * model :] = jnp.broadcast_to(table.get(t_out, 5), (8, model))
    act[...] = (n * table.get(t_out, 0) + table.get(t_out, 1)).astype(BF16)
    for f in range(fsdp):
        r = dot_nn(act[...], a_v[f].reshape(model, full))[:, :wide]
        qkv[f] = (r + bias_v[0:1, f * wide : (f + 1) * wide]).astype(BF16)
    for f in range(fsdp):
        pltpu.make_async_copy(a_v.at[f], a_out.at[f], out_sem.at[f]).wait()


def front(chain, plan, me, tokens, pieces, wide):
    t, model = tokens.shape
    fsdp = plan.fsdp
    full = pieces[0].shape[-1]
    lead = (fsdp, *plan.split(), full)
    return chain.call(
        "front",
        functools.partial(front_body, plan, len(pieces)),
        (me, tokens, *pieces),
        [SMEM, VMEM] + [ANY] * len(pieces),
        (
            sds((fsdp, t, wide), BF16),
            sds((t, model), BF16),
            sds(lead, BF16),
            sds((fsdp * VEC_ROWS, model), F32),
        ),
        (HELD, HELD, HBM, HELD),
        [
            pltpu.VMEM(lead, BF16),
            pltpu.VMEM((8, 3 * model), F32),
            pltpu.SemaphoreType.DMA((fsdp,)),
            pltpu.SemaphoreType.DMA((fsdp,)),
        ],
        14,
    )


def head_place(g, wide):
    return g // wide, g % wide


def masks(length, lo, size, keys):
    q = lax.broadcasted_iota(jnp.int32, (size, 1), 0) + lo
    limit = jnp.minimum(q, length - 1)
    k = lax.broadcasted_iota(jnp.int32, (size, keys), 1)
    return k <= limit


QBLOCK = 256


def attend_body(heads, wide, model, length_ref, qkv, mixed, logs):
    t = mixed.shape[0]
    length = length_ref[0]
    scale = HEAD_DIM**-0.5

    def part(h, which):
        f, o = head_place(which * model + h * HEAD_DIM, wide)
        return qkv[f, :, o : o + HEAD_DIM]

    for i, h in enumerate(heads):
        q = part(h, 0) * jnp.asarray(scale, BF16)
        k, v = part(h, 1), part(h, 2)
        for lo in range(0, t, QBLOCK):
            n = lo + QBLOCK
            s = dot_nt(q[lo:n], k[:n])
            s = jnp.where(masks(length, lo, QBLOCK, n), s, neg_large)
            top = jnp.max(s, axis=-1, keepdims=True)
            e = jnp.exp(s - top)
            total = jnp.sum(e, axis=-1, keepdims=True)
            p = (e * (1.0 / total)).astype(BF16)
            o = dot_nn(p, v[:n])
            mixed[lo:n, i * HEAD_DIM : (i + 1) * HEAD_DIM] = o.astype(BF16)
            logs[lo:n, i : i + 1] = top + jnp.log(total)


def attend(chain, qkv, length, model, heads):
    fsdp, t, wide = qkv.shape
    return chain.call(
        "attend",
        functools.partial(attend_body, heads, wide, model),
        (length, qkv),
        [SMEM, HELD],
        (sds((t, len(heads) * HEAD_DIM), BF16), sds((t, 128), F32)),
        (HELD, HELD),
        [],
        8,
    )


def join_body(plan, cut, n_in, n_mixed, me_ref, tokens, t_in, *refs):
    ins, refs = refs[:n_in], refs[n_in:]
    parts, (resid, act, wout, mixed, o_v, sem) = refs[:n_mixed], refs[n_mixed:]
    model = tokens.shape[1]
    fsdp = plan.fsdp
    table = Table(fsdp)
    lanes = pl.ds(model, o_v.shape[-1])
    if plan.direct:
        for ref, si, f, ti, h in table_loads(plan, Me(me_ref), ins):
            src = ref.at[(*si, ALL, ALL, lanes)]
            pltpu.make_async_copy(src, o_v.at[(f, *ti, h)], sem).start()
    else:
        for f in range(fsdp):
            src = ins[0].at[(f, ALL, ALL, ALL, ALL, lanes)]
            pltpu.make_async_copy(src, o_v.at[f], sem).start()
    at = 0
    for p in parts:
        mixed[:, at : at + p.shape[1]] = p[...]
        at += p.shape[1]
    pltpu.make_async_copy(o_v, o_v, sem).wait()
    for f in range(fsdp):
        wout[:, f * cut : (f + 1) * cut] = o_v[f].reshape(model, o_v.shape[-1])[:, :cut]
    r = tokens[...].astype(F32) + dot_nn(mixed[...], wout[...]) + table.get(t_in, 6)
    resid[...] = r
    n, _ = normed(r)
    act[...] = (n * table.get(t_in, 2) + table.get(t_in, 3)).astype(BF16)


def join(chain, plan, me, cut, tokens, parts, pieces, t_can):
    t, model = tokens.shape
    spare = pieces[0].shape[-1] - model
    return chain.call(
        "join",
        functools.partial(join_body, plan, cut, len(pieces), len(parts)),
        (me, tokens, t_can, *pieces, *parts),
        [SMEM, VMEM, HELD] + [ANY] * len(pieces) + [HELD] * len(parts),
        (
            sds((t, model), F32),
            sds((t, model), BF16),
            sds((model, model), BF16),
            sds((t, model), BF16),
        ),
        (HELD,) * 4,
        [pltpu.VMEM((plan.fsdp, *plan.split(), spare), BF16), pltpu.SemaphoreType.DMA],
        12,
    )


def mlp_up_body(plan, n_in, n_out, me_ref, act, cot, t_in, *refs):
    ins, refs = refs[:n_in], refs[n_in:]
    gel_out, slope_out, b_v, g_b_proj = refs[:4]
    gouts, refs = refs[4 : 4 + n_out], refs[4 + n_out :]
    gp_v, sem, gsem = refs
    fsdp, half = plan.fsdp, plan.cols // 2
    model = act.shape[1]
    deep = gp_v.shape[-1]
    table = Table(fsdp)
    me = Me(me_ref)
    if plan.direct:
        for ref, si, f, ti, h in table_loads(plan, me, ins):
            src = ref.at[(*si, ALL, ALL, pl.ds(0, model))]
            pltpu.make_async_copy(src, b_v.at[(f, *ti, h)], sem.at[f]).start()
    else:
        for f in range(fsdp):
            src = ins[0].at[(f, ALL, ALL, ALL, ALL, pl.ds(0, model))]
            pltpu.make_async_copy(src, b_v.at[f], sem.at[f]).start()
    g_b_proj[...] = jnp.sum(cot[...].astype(F32), axis=0, keepdims=True)
    for j in range(fsdp):
        lanes = slice(j * model, (j + 1) * model)
        pltpu.make_async_copy(b_v.at[j], b_v.at[j], sem.at[j]).wait()
        pre = dot_nn(act[...], b_v[j].reshape(model, model)) + table.get(t_in, 8 + j)
        sq = pre * pre
        th = jnp.tanh(gelu_coeff * (pre + cubic_coeff * sq * pre))
        plus = 0.5 * (1.0 + th)
        gel = (pre * plus).astype(BF16)
        gel_out[:, lanes] = gel
        slope_out[:, lanes] = plus + 0.5 * pre * (1.0 - th * th) * gelu_coeff * (
            1.0 + 3.0 * cubic_coeff * sq
        )
        grad = dot_tn(cot[...], gel).astype(BF16)
        gp_v[j, 0] = grad[:, :deep]
        gp_v[j, 1] = grad[:, deep:]
        if plan.direct and j % 2 == 1:
            span = pl.ds(j - 1, 2)
            for away in range(2):
                for x in range(plan.nx):
                    f = me.fsdp(x, away)
                    for h in range(2):
                        rows = pl.ds(pl.multiple_of(f * plan.cols + h * half, 16), half)
                        src = gp_v.at[span, :, rows]
                        pltpu.make_async_copy(src, gouts[away].at[h, x, span], gsem).start()
    if not plan.direct:
        pltpu.make_async_copy(gp_v, gouts[0], gsem).start()
    pltpu.make_async_copy(gp_v, gp_v, gsem).wait()


def mlp_up(chain, plan, me, act, cot, t_can, pieces, hidden):
    t, model = act.shape
    fsdp = plan.fsdp
    per = hidden // fsdp // 2
    if plan.direct:
        grads = [sds((2, plan.nx, plan.nz, 2, plan.cols // 2, plan.deep), BF16)] * 2
    else:
        grads = [sds((fsdp, 2, model, per), BF16)]
    lead = (fsdp, *plan.split(), model)
    return chain.call(
        "mlp_up",
        functools.partial(mlp_up_body, plan, len(pieces), len(grads)),
        (me, act, cot, t_can, *pieces),
        [SMEM, HELD, VMEM, HELD] + [ANY] * len(pieces),
        (
            sds((t, hidden), BF16),
            sds((t, hidden), F32),
            sds(lead, BF16),
            sds((1, model), F32),
            *grads,
        ),
        (HELD,) * 4 + (HBM,) * len(grads),
        [
            pltpu.VMEM((fsdp, 2, model, per), BF16),
            pltpu.SemaphoreType.DMA((fsdp,)),
            pltpu.SemaphoreType.DMA,
        ],
        22,
    )


def mlp_down_body(plan, n_in, me_ref, cot, resid, gel, slope, t_in, *refs):
    ins, refs = refs[:n_in], refs[n_in:]
    output, gpre, g_b_fc, c_v, acc, csem = refs
    fsdp, half = plan.fsdp, plan.cols // 2
    model = cot.shape[1]
    table = Table(fsdp)
    if plan.direct:
        for ref, si, f, ti, h in table_loads(plan, Me(me_ref), ins):
            rows = pl.ds(pl.multiple_of(f * plan.cols + h * half, 16), half)
            pltpu.make_async_copy(ref.at[si], c_v.at[(*ti, rows)], csem).start()
    else:
        pltpu.make_async_copy(ins[0], c_v, csem).start()
    acc[...] = resid[...] + table.get(t_in, 7)
    pltpu.make_async_copy(c_v, c_v, csem).wait()
    for j in range(fsdp):
        lanes = slice(j * model, (j + 1) * model)
        down = jnp.concatenate([c_v[j, 0], c_v[j, 1]], axis=1)
        low = (dot_nn(cot[...], down) * slope[:, lanes]).astype(BF16)
        gpre[:, lanes] = low
        g_b_fc[j : j + 1, :] = jnp.sum(low.astype(F32), axis=0, keepdims=True)
        acc[...] += dot_nt(gel[:, lanes], down)
    output[...] = acc[...].astype(BF16)


def mlp_down(chain, plan, me, cot, resid, gel, slope, t_can, pieces):
    t, model = cot.shape
    fsdp, hidden = plan.fsdp, gel.shape[1]
    return chain.call(
        "mlp_down",
        functools.partial(mlp_down_body, plan, len(pieces)),
        (me, cot, resid, gel, slope, t_can, *pieces),
        [SMEM, VMEM, HELD, HELD, HELD, HELD] + [ANY] * len(pieces),
        (sds((t, model), BF16), sds((t, hidden), BF16), sds((fsdp, model), F32)),
        (VMEM, HELD, HELD),
        [
            pltpu.VMEM((fsdp, 2, model, hidden // fsdp // 2), BF16),
            pltpu.VMEM((t, model), F32),
            pltpu.SemaphoreType.DMA,
        ],
        18,
    )


def mlp_back_body(plan, n_out, me_ref, act, gpre, b_in, *refs):
    gact = refs[0]
    gouts = refs[1 : 1 + n_out]
    g_v, gsem = refs[1 + n_out :]
    model = act.shape[1]
    me = Me(me_ref)
    first = True
    order = [
        (x, away, me.fsdp(x, away) if plan.direct else 2 * x + away)
        for away in range(2)
        for x in range(plan.nx)
    ]
    for x, away, f in order:
        part = gpre[:, pl.ds(pl.multiple_of(f * model, model), model)]
        slot = 2 * x + away
        g_v[slot] = dot_tn(act[...], part).astype(BF16).reshape(g_v.shape[1:])
        if plan.direct:
            for h in range(2):
                src = g_v.at[slot, :, :, h]
                dst = gouts[away].at[h, x, :, :, :, pl.ds(0, model)]
                pltpu.make_async_copy(src, dst, gsem).start()
        else:
            pltpu.make_async_copy(g_v.at[slot], gouts[0].at[f], gsem).start()
        back = dot_nt(part, b_in[f].reshape(model, model))
        if first:
            gact[...] = back
        else:
            gact[...] += back
        first = False
    pltpu.make_async_copy(g_v, g_v, gsem).wait()


def mlp_back(chain, plan, me, act, gpre, b_can, b_full):
    t, model = act.shape
    fsdp = plan.fsdp
    lead = (fsdp, *plan.split(), model)
    if plan.direct:
        grads = [sds((2, plan.nx, plan.nz, 2, plan.rows // 2, b_full), BF16)] * 2
    else:
        grads = [sds(lead, BF16)]
    return chain.call(
        "mlp_back",
        functools.partial(mlp_back_body, plan, len(grads)),
        (me, act, gpre, b_can),
        [SMEM, HELD, HELD, HELD],
        (sds((t, model), F32), *grads),
        (HELD,) + (HBM,) * len(grads),
        [
            pltpu.VMEM(lead, BF16),
            pltpu.SemaphoreType.DMA,
        ],
        14,
    )


def join_back_body(plan, n_in, me_ref, gact, cot, resid, mixed, wout, t_in, *refs):
    gresid, gmixed, g_vec, *gouts = refs[n_in:-2]
    o_v, sem = refs[-2:]
    model = cot.shape[1]
    table = Table(plan.fsdp)
    n, inverse = normed(resid[...])
    e = gact[...]
    g_vec[...] = jnp.zeros(g_vec.shape, F32)
    g_vec[0:1, :] = jnp.sum(e * n, axis=0, keepdims=True)
    g_vec[1:2, :] = jnp.sum(e, axis=0, keepdims=True)
    r = cot[...].astype(F32) + norm_back(e, n, inverse, table.get(t_in, 2))
    gresid[...] = r
    branch = r.astype(BF16)
    g_vec[2:3, :] = jnp.sum(branch.astype(F32), axis=0, keepdims=True)
    grad = dot_tn(mixed[...], branch).astype(BF16)
    if plan.direct:
        me = Me(me_ref)
        cut = plan.cols
        for f in range(plan.fsdp):
            part = grad[:, f * cut : (f + 1) * cut]
            o_v[f, :, :, :, :, 0:cut] = part.reshape(*o_v.shape[1:-1], cut)
            o_v[f, :, :, :, :, cut:] = jnp.zeros((*o_v.shape[1:-1], o_v.shape[-1] - cut), BF16)
        for away in range(2):
            for x in range(plan.nx):
                f = me.fsdp(x, away)
                for h in range(2):
                    dst = gouts[away].at[h, x, :, :, :, pl.ds(model, o_v.shape[-1])]
                    pltpu.make_async_copy(o_v.at[f, :, :, h], dst, sem).start()
    else:
        gouts[0][...] = grad
    gmixed[...] = dot_nt(branch, wout[...]).astype(BF16)
    if plan.direct:
        pltpu.make_async_copy(o_v, o_v, sem).wait()


def join_back(chain, plan, me, gact, cot, resid, mixed, wout, t_can, g_b):
    t, model = cot.shape
    ins = [me, gact, cot, resid, mixed, wout, t_can]
    if plan.direct:
        spare = g_b[0].shape[-1] - model
        grads, grad_specs = [sds(g.shape, BF16) for g in g_b], [HBM] * len(g_b)
        aliases = {len(ins) + i: 3 + i for i in range(len(g_b))}
    else:
        spare = 128
        grads, grad_specs, aliases, g_b = [sds((model, model), BF16)], [VMEM], {}, []
    return chain.call(
        "join_back",
        functools.partial(join_back_body, plan, len(g_b)),
        (*ins, *g_b),
        [SMEM, HELD, VMEM, HELD, HELD, HELD, HELD] + [HBM] * len(g_b),
        (sds((t, model), F32), sds((t, model), BF16), sds((8, model), F32), *grads),
        (HELD, HELD, HELD, *grad_specs),
        [pltpu.VMEM((plan.fsdp, *plan.split(), spare), BF16), pltpu.SemaphoreType.DMA],
        18,
        aliases,
    )


def attend_back_body(heads, wide, model, length_ref, qkv, gmixed, logs, out):
    t = gmixed.shape[0]
    length = length_ref[0]
    scale = HEAD_DIM**-0.5

    def part(h, which):
        f, o = head_place(which * model + h * HEAD_DIM, wide)
        return qkv[f, :, o : o + HEAD_DIM]

    for i, h in enumerate(heads):
        lanes = slice(i * HEAD_DIM, (i + 1) * HEAD_DIM)
        q = part(h, 0)
        small = q * jnp.asarray(scale, BF16)
        k, v = part(h, 1), part(h, 2)
        go = gmixed[:, h * HEAD_DIM : (h + 1) * HEAD_DIM]
        gk, gv = [], []
        for lo in range(0, t, QBLOCK):
            n = lo + QBLOCK
            s = dot_nt(small[lo:n], k[:n])
            s = jnp.where(masks(length, lo, QBLOCK, n), s, neg_large)
            p = jnp.exp(s - logs[lo:n, i : i + 1])
            gp = dot_nt(go[lo:n], v[:n])
            inner = jnp.sum(p * gp, axis=-1, keepdims=True)
            ds = (p * (gp - inner)).astype(BF16)
            out[0, lo:n, lanes] = (dot_nn(ds, k[:n]) * scale).astype(BF16)
            gv.append(dot_tn(p.astype(BF16), go[lo:n]))
            gk.append(dot_tn(ds, small[lo:n]))
        for b in range(t // QBLOCK):
            rows = slice(b * QBLOCK, (b + 1) * QBLOCK)
            out[1, rows, lanes] = sum(x[rows] for x in gk[b:]).astype(BF16)
            out[2, rows, lanes] = sum(x[rows] for x in gv[b:]).astype(BF16)


def attend_back(chain, qkv, gmixed, logs, length, heads):
    fsdp, t, wide = qkv.shape
    model = gmixed.shape[1]
    return chain.call(
        "attend_back",
        functools.partial(attend_back_body, heads, wide, model),
        (length, qkv, gmixed, logs),
        [SMEM, HELD, HELD, HELD],
        sds((3, t, len(heads) * HEAD_DIM), BF16),
        HELD,
        [],
        10,
    )


def whole_qkv(parts, gq_v):
    model = gq_v.shape[1] // 3
    at = 0
    for p in parts:
        size = p.shape[2]
        for which in range(3):
            gq_v[:, which * model + at : which * model + at + size] = p[which]
        at += size


def back_body(plan, wide, n_parts, n_out, me_ref, tokens, act, a_in, gresid, t_in, g_two, g_b_fc, g_b_proj, *refs):
    parts, refs = refs[:n_parts], refs[n_parts:]
    input_grad, gouts, refs = refs[0], refs[1 : 1 + n_out], refs[1 + n_out :]
    gq_v, g_v, tab, a_v, sem, in_sem = refs
    late = pltpu.make_async_copy(a_in, a_v, in_sem)
    late.start()
    fsdp = plan.fsdp
    t, model = tokens.shape
    full = a_in.shape[-1]
    table = Table(fsdp)
    spare = full - wide
    whole_qkv(parts, gq_v)
    for f in range(fsdp):
        grad = dot_tn(act[...], gq_v[:, f * wide : (f + 1) * wide]).astype(BF16)
        g_v[f, :, :, :, :, 0:wide] = grad.reshape(*g_v.shape[1:-1], wide)
    back = jnp.zeros((t, model), F32)
    late.wait()
    for f in range(fsdp):
        part = gq_v[:, f * wide : (f + 1) * wide]
        back = back + dot_nt(part, a_v[f].reshape(model, full)[:, :wide])
    sums = jnp.sum(gq_v[...].astype(F32), axis=0, keepdims=True)
    n, inverse = normed(tokens[...].astype(F32))
    tab[...] = jnp.zeros(tab.shape, F32)

    def put(k, value):
        r = (k // table.per) * spare + k % table.per
        tab[r : r + 1, :] = value

    put(0, jnp.sum(back * n, axis=0, keepdims=True))
    put(1, jnp.sum(back, axis=0, keepdims=True))
    put(2, g_two[0:1, :])
    put(3, g_two[1:2, :])
    put(4, sums[:, 0:model])
    put(5, sums[:, 2 * model :])
    put(6, g_two[2:3, :])
    put(7, g_b_proj[...])
    for j in range(fsdp):
        put(8 + j, g_b_fc[j : j + 1, :])
    for f in range(fsdp):
        columns = jnp.transpose(tab[f * spare : (f + 1) * spare, :]).astype(BF16)
        g_v[f, :, :, :, :, wide:] = columns.reshape(*g_v.shape[1:-1], spare)
    if plan.direct:
        me = Me(me_ref)
        for away in range(2):
            for x in range(plan.nx):
                f = me.fsdp(x, away)
                for h in range(2):
                    dst = gouts[1 + h].at[x] if away else gouts[0].at[h, x]
                    pltpu.make_async_copy(g_v.at[f, :, :, h], dst, sem).start()
    else:
        pltpu.make_async_copy(g_v, gouts[0], sem).start()
    r = gresid[...] + norm_back(back, n, inverse, table.get(t_in, 0))
    input_grad[...] = r.astype(BF16)
    pltpu.make_async_copy(g_v, g_v, sem).wait()


def back(chain, plan, wide, me, tokens, act, parts, a_can, gresid, t_can, g_two, g_b_fc, g_b_proj):
    t, model = tokens.shape
    fsdp, full = plan.fsdp, a_can.shape[-1]
    lead = (fsdp, *plan.split(), full)
    if plan.direct:
        one = (plan.nx, plan.nz, 2, plan.rows // 2, full)
        grads = [sds((2, *one), BF16), sds(one, BF16), sds(one, BF16)]
    else:
        grads = [sds(lead, BF16)]
    return chain.call(
        "back",
        functools.partial(back_body, plan, wide, len(parts), len(grads)),
        (me, tokens, act, a_can, gresid, t_can, g_two, g_b_fc, g_b_proj, *parts),
        [SMEM, VMEM, HELD, HBM] + [HELD] * (5 + len(parts)),
        (sds((t, model), BF16), *grads),
        (VMEM,) + (HBM,) * len(grads),
        [
            pltpu.VMEM((t, 3 * model), BF16),
            pltpu.VMEM(lead, BF16),
            pltpu.VMEM((fsdp * (full - wide), model), F32),
            pltpu.VMEM(lead, BF16),
            pltpu.SemaphoreType.DMA,
            pltpu.SemaphoreType.DMA,
        ],
        26,
    )


def update_body(count, *refs):
    norms = refs[0]
    n = 4 * count
    ins, outs = refs[1 : 1 + n], refs[1 + n : 2 + n + 3 * count]
    held, sem = refs[2 + n + 3 * count : -1], refs[-1]
    todo = [pltpu.make_async_copy(i, h, sem.at[k]) for k, (i, h) in enumerate(zip(ins, held))]
    for c in todo:
        c.start()
    norm = jnp.sqrt(jnp.sum(norms[...], axis=0, keepdims=True))
    outs[0][...] = norm
    factor = jnp.minimum(1.0, clip_limit / (norm[:, 0:1] + 1e-06))
    for i in range(count):
        for c in todo[4 * i : 4 * i + 4]:
            c.wait()
        w, g, one, two = (r[...] for r in held[4 * i : 4 * i + 4])
        last = i == count - 1
        rate, decay = (rate_vector, 0.0) if last else (rate_matrix, decay_matrix)
        clipped = g * factor
        one_new = beta_one * one + (1.0 - beta_one) * clipped
        two_new = beta_two * two + (1.0 - beta_two) * clipped * clipped
        first_hat = one_new / (1.0 - beta_one**STEP)
        second_hat = two_new / (1.0 - beta_two**STEP)
        outs[1 + i][...] = w - rate * (first_hat / (jnp.sqrt(second_hat) + 1e-08) + decay * w)
        outs[1 + count + i][...] = one_new
        outs[1 + 2 * count + i][...] = two_new


def update(chain, norms, weights, grads, firsts, seconds):
    count = len(weights)
    ins = []
    for group in zip(weights, grads, firsts, seconds):
        ins += group
    outs = [sds((1, 128), F32)] + [sds(w.shape, F32) for w in weights] * 3
    return chain.call(
        "update",
        functools.partial(update_body, count),
        [norms, *ins],
        [VMEM] + [HBM if i % 4 != 1 else ANY for i in range(len(ins))],
        tuple(outs),
        (VMEM,) * len(outs),
        [pltpu.VMEM(i.shape, F32) for i in ins] + [pltpu.SemaphoreType.DMA((len(ins),))],
        16,
    )


def place_first(chain, name, plan, me, came, cut, spare, spare_shape, copies_of):
    n, rows, cols = came.shape

    def copies(m):
        return [
            (0, (ALL, pl.ds(0, cut)), (n, cut, cols), [(0, (ALL,))]),
            (0, (ALL, pl.ds(cut, rows - cut)), (n, rows - cut, cols), [(1, (ALL,))]),
        ] + copies_of(m)

    outs = [(n, cut, cols), (n, rows - cut, cols), spare_shape]
    return move(chain, name, me, [came, *spare], outs, copies)


def place_second(chain, name, plan, me, z0, r0, z1, r1):
    def copies(m):
        return [
            (0, (ALL,), z0.shape, [(0, (m.y,)), (2, (0, m.y))]),
            (1, (ALL,), z0.shape, [(0, (m.other_y,)), (2, (0, m.other_y))]),
            (2, (ALL,), z1.shape, [(1, (m.x,)), (2, (1, m.x))]),
            (3, (ALL,), z1.shape, [(1, (m.other_x,)), (2, (1, m.other_x))]),
        ]

    outs = [(2, *z0.shape), (2, *z1.shape), (2, 2, *z0.shape)]
    return move(chain, name, me, [z0, r0, z1, r1], outs, copies)


def both(came, h, at):
    if len(came) == 1:
        return [(0, (h, *at)), (1, (h, *at))]
    return [(0, (h, *at)), (1 + h, at)]


def first_sums(chain, plan, name, me, own, came):
    nx, nz, _, rows, cols = own.shape[1:]

    def sums(m):
        return [
            (0, ALL, (nz, 2, rows, cols), both(came, 0, (m.other_x,))),
            (1, ALL, (nx, nz, rows, cols), both(came, 1, (ALL, ALL, m.other_y))),
        ]

    outs = [sds((nz, 2, rows, cols), BF16), sds((nx, nz, rows, cols), BF16)]
    s0, s1 = add_up(chain, name + "1", me, [own, *came], outs, sums, big=True)
    return plan.partner(name, s0, "x"), plan.partner(name, s1, "y")


def second_sums(chain, plan, name, me, own, came, f0, f1):
    nx, nz, _, rows, cols = own.shape[1:]
    n = 1 + len(came)

    def sums(m):
        at0, at1 = (m.x, ALL, m.other_y), (m.other_x, ALL, m.y)
        return [
            (0, ALL, (nz, rows, cols), both(came, 0, at0) + [(n, (ALL, m.other_y))]),
            (1, ALL, (nz, rows, cols), both(came, 1, at1) + [(n + 1, (m.other_x,))]),
        ]

    outs = [sds((nz, rows, cols), BF16)] * 2
    s0, s1 = add_up(chain, name + "2", me, [own, *came, f0, f1], outs, sums, big=True)
    return plan.partner(name, s0, "y"), plan.partner(name, s1, "x")


def third_sums(chain, plan, name, me, own, came, f0, f1, s0, s1):
    nx, nz, _, rows, cols = own.shape[1:]
    n = 1 + len(came)

    def sums(m):
        at = (m.x, ALL, m.y)
        one = both(came, 0, at) + [(n, (ALL, m.y)), (n + 2, (ALL,))]
        two = both(came, 1, at) + [(n + 1, (m.x,)), (n + 3, (ALL,))]
        return [
            (0, (ALL, slice(0, rows)), (nz, rows, cols), one),
            (0, (ALL, slice(rows, 2 * rows)), (nz, rows, cols), two),
        ]

    outs = [sds((nz, 2 * rows, cols), BF16)]
    arrays = [own, *came, f0, f1, s0, s1]
    (sent,) = add_up(chain, name + "3", me, arrays, outs, sums, big=True)
    return plan.along_z(name, sent)


def squared(*values):
    return jnp.broadcast_to(sum(jnp.sum(v * v) for v in values), (1, 128))


def body(
    tokens,
    lengths,
    cotangent,
    qkv_weight,
    out_weight,
    fc_weight,
    proj_weight,
    vectors,
    qkv_first,
    out_first,
    fc_first,
    proj_first,
    vectors_first,
    qkv_second,
    out_second,
    fc_second,
    proj_second,
    vectors_second,
):
    dp, fsdp = lax.axis_size("dp"), lax.axis_size("fsdp")
    model = tokens.shape[1]
    wide, cut = qkv_weight.shape[1], out_weight.shape[1]
    hidden = fc_weight.shape[1] * fsdp
    per = vectors.shape[1]
    plan = Plan(dp, fsdp, model, hidden)
    rows, half, chalf, nz = plan.rows, plan.rows // 2, plan.cols // 2, plan.nz
    a_full = -(-(wide + per) // 128) * 128
    b_full = model + -(-cut // 128) * 128
    chain = Chain()
    at_dp, at_fsdp = lax.axis_index("dp"), lax.axis_index("fsdp")
    me = jnp.stack([at_dp // 2, at_dp % 2, at_fsdp // 2, at_fsdp % 2]).astype(jnp.int32)
    heads = model // HEAD_DIM
    third = [range(i, i + heads // 3) for i in range(0, heads, heads // 3)]

    def turned(value):
        return jnp.transpose(value)

    if plan.direct:
        weights = (qkv_weight, out_weight, fc_weight, turned(proj_weight), turned(vectors))
        a_own, b_own, c_own = pack(chain, plan, weights, a_full, b_full)
        a_came = plan.along_z("gather_a", a_own)
        c_y, c_x = plan.partner("gather_c", c_own[0], "y"), plan.partner("gather_c", c_own[1], "x")
        chain.wait_for(c_y, c_x)
        a_z0, a_z1, b_own = place_first(
            chain,
            "place_a1",
            plan,
            me,
            a_came,
            half,
            [b_own],
            (nz, *b_own.shape),
            lambda m: [(1, (ALL,), b_own.shape, [(2, (z,)) for z in range(nz)])],
        )
        a_r0, a_r1 = plan.partner("gather_a", a_z0, "y"), plan.partner("gather_a", a_z1, "x")
        b_came = plan.along_z("gather_b", b_own)
        a_p0, a_p1, a_p = place_second(chain, "place_a2", plan, me, a_z0, a_r0, a_z1, a_r1)
        a_in = [a_p, plan.partner("gather_a", a_p0, "x"), plan.partner("gather_a", a_p1, "y")]
        a_in = a_in + [plan.partner("gather_a", v, "core") for v in a_in]

        def pairs(m):
            block = (chalf, plan.deep)
            zs = range(nz)
            return [
                (1, (0,), block, [(2, (z, m.y)) for z in zs]),
                (2, (ALL,), block, [(2, (z, m.other_y)) for z in zs]),
                (1, (1,), block, [(2, (z, 2 + m.x)) for z in zs]),
                (3, (ALL,), block, [(2, (z, 2 + m.other_x)) for z in zs]),
            ]

        spare = [c_own, c_y, c_x]
        b_z0, b_z1, c_pair = place_first(
            chain, "place_b1", plan, me, b_came, half, spare, (nz, 4, chalf, plan.deep), pairs
        )
        b_r0, b_r1 = plan.partner("gather_b", b_z0, "y"), plan.partner("gather_b", b_z1, "x")
        c_came = plan.along_z("gather_c", c_pair)
    else:

        def whole(shard):
            down = lax.all_gather(shard.astype(BF16), "dp", axis=0, tiled=True)
            return lax.all_gather(down, "fsdp", axis=0, tiled=False)

        def padded(parts, full):
            both = jnp.concatenate(parts, axis=1)
            both = whole(jnp.pad(both, ((0, 0), (0, full - both.shape[1]))))
            return both.reshape(fsdp, *plan.split(), full)

        a_in = [padded([qkv_weight, vectors], a_full)]
        b_in = [padded([fc_weight, out_weight], b_full)]
        c_all = jnp.transpose(whole(proj_weight), (0, 2, 1))
        c_all = c_all.reshape(model, fsdp, 2, hidden // fsdp // 2)
        c_in = [jnp.transpose(c_all, (1, 2, 0, 3))]

    qkv, act_one, a_can, t_can = front(chain, plan, me, tokens, a_in, wide)
    parts = []
    if plan.direct:
        b_p0, b_p1, b_p = place_second(chain, "place_b2", plan, me, b_z0, b_r0, b_z1, b_r1)
        b_q0, b_q1 = plan.partner("gather_b", b_p0, "x"), plan.partner("gather_b", b_p1, "y")
        b_pc = plan.partner("gather_b", b_p, "core")
    for group in third:
        parts.append(attend(chain, qkv, lengths, model, group))
    if plan.direct:
        b_q0, b_q1 = gate(chain, "gate_b", b_q0, b_q1)
        b_in = [b_p, b_q0, b_q1, b_pc] + [plan.partner("gather_b", v, "core") for v in (b_q0, b_q1)]
        def place_c(m):
            block = (nz, chalf, plan.deep)
            out = [(0, (ALL, i), block, [(0, (i,)), (2, (0, i))]) for i in range(2)]
            return out + [(0, (ALL, 2 + i), block, [(1, (i,)), (2, (1, i))]) for i in range(2)]

        block = (2, nz, chalf, plan.deep)
        outs = [block, block, (2, *block)]
        chain.wait_for(b_pc)
        c_p0, c_p1, c_p = move(chain, "place_c2", me, [c_came], outs, place_c)
        c_in = [c_p, plan.partner("gather_c", c_p0, "x"), plan.partner("gather_c", c_p1, "y")]
        c_in = c_in + [plan.partner("gather_c", v, "core") for v in c_in]
    logs = [p[1] for p in parts]
    resid_two, act_two, wout, mixed = join(
        chain, plan, me, cut, tokens, [p[0] for p in parts], b_in, t_can
    )
    gel, slope, b_can, g_b_proj, *g_c = mlp_up(
        chain, plan, me, act_two, cotangent, t_can, b_in, hidden
    )
    output, gpre, g_b_fc = mlp_down(
        chain, plan, me, cotangent, resid_two, gel, slope, t_can, c_in
    )

    if plan.direct:
        g_c[1:] = gate(chain, "gate_c", g_c[1])
        c_away = plan.partner("sum_c", g_c[1], "core")
    gact, *g_b = mlp_back(chain, plan, me, act_two, gpre, b_can, b_full)
    if plan.direct:
        chain.wait_for(c_away)
    gresid, gmixed, g_two, *g_o = join_back(
        chain, plan, me, gact, cotangent, resid_two, mixed, wout, t_can, g_b
    )
    if plan.direct:
        g_b = g_o
        b_away = plan.partner("sum_b", g_b[1], "core")
        c_f0, c_f1 = first_sums(chain, plan, "sum_c", me, g_c[0], [c_away])
    gparts = [
        attend_back(chain, qkv, gmixed, log, lengths, group) for log, group in zip(logs, third)
    ]
    input_grad, *g_a = back(
        chain, plan, wide, me, tokens, act_one, gparts, a_can, gresid, t_can, g_two, g_b_fc, g_b_proj
    )

    if plan.direct:
        a_away = [plan.partner("sum_a", v, "core") for v in g_a[1:]]

        def sums_cz(m):
            block = (nz, 2, chalf, plan.deep)
            at = (0, m.x)
            out = [(0, (ALL, slice(0, 2)), block, [(0, at), (1, at), (2, (ALL,))])]
            for x in range(plan.nx):
                at = (1, x, ALL, m.y)
                terms = [(0, at), (1, at), (3, (x,))]
                out.append((0, (ALL, 2 + x), (nz, chalf, plan.deep), terms))
            return out

        outs = [sds((nz, 4, chalf, plan.deep), BF16)]
        arrays = [g_c[0], c_away, c_f0, c_f1]
        (c_sent,) = add_up(chain, "sum_c2", me, arrays, outs, sums_cz, big=True)
        c_z = plan.along_z("sum_c", c_sent)
        b_f0, b_f1 = first_sums(chain, plan, "sum_b", me, g_b[0], [b_away])
        b_s0, b_s1 = second_sums(chain, plan, "sum_b", me, g_b[0], [b_away], b_f0, b_f1)
        a_f0, a_f1 = first_sums(chain, plan, "sum_a", me, g_a[0], a_away)

        def sums_c3(m):
            block = (chalf, plan.deep)
            one = [(0, (z, m.other_y)) for z in range(nz)]
            two = [(0, (z, 2 + m.other_x)) for z in range(nz)]
            return [(0, ALL, block, one), (1, ALL, block, two)]

        outs = [sds((chalf, plan.deep), BF16)] * 2
        s0, s1 = add_up(chain, "sum_c3", me, [c_z], outs, sums_c3)
        c_l0, c_l1 = plan.partner("sum_c", s0, "y"), plan.partner("sum_c", s1, "x")
        b_z = third_sums(chain, plan, "sum_b", me, g_b[0], [b_away], b_f0, b_f1, b_s0, b_s1)
        a_s0, a_s1 = second_sums(chain, plan, "sum_a", me, g_a[0], a_away, a_f0, a_f1)

        def sums_c(m):
            block = (chalf, plan.deep)
            one = [(0, (z, m.y)) for z in range(nz)] + [(1, (ALL,))]
            two = [(0, (z, 2 + m.x)) for z in range(nz)] + [(2, (ALL,))]
            return [(0, ALL, block, one), (1, ALL, block, two)]

        def end_c(done, outs):
            outs[0][0:chalf, :] = done[0]
            outs[0][chalf:, :] = done[1]
            outs[1][...] = squared(*done)

        d_proj, s_c = add_up(
            chain,
            "end_c",
            me,
            [c_z, c_l0, c_l1],
            [sds((plan.cols, plan.deep), F32), sds((1, 128), F32)],
            sums_c,
            end_c,
        )
        a_z = third_sums(chain, plan, "sum_a", me, g_a[0], a_away, a_f0, a_f1, a_s0, a_s1)

        def last(cols):
            return lambda m: [(0, ALL, (nz, 2 * half, cols), [(0, (ALL,))])]

        def end_b(done, outs):
            total = jnp.sum(done[0], axis=0)
            fc, out = total[:, :model], total[:, model : model + cut]
            outs[0][...] = fc
            outs[1][...] = out
            outs[2][...] = squared(fc, out)

        shapes = [fc_weight.shape, out_weight.shape, (1, 128)]
        d_fc, d_out, s_b = add_up(
            chain, "end_b", me, [b_z], [sds(s, F32) for s in shapes], last(b_full), end_b
        )

        def end_a(done, outs):
            total = jnp.sum(done[0], axis=0)
            start = wide // 128 * 128
            vec = jnp.transpose(total[:, start:])[wide - start : wide - start + per]
            qkv = total[:, :wide]
            outs[0][...] = qkv
            outs[1][...] = vec
            outs[2][...] = squared(qkv, vec)

        shapes = [qkv_weight.shape, (per, rows), (1, 128)]
        d_qkv, d_vec, s_a = add_up(
            chain, "end_a", me, [a_z], [sds(s, F32) for s in shapes], last(a_full), end_a
        )
        squares = s_a + s_b + s_c
    else:

        def shared(value):
            mine = lax.psum_scatter(value, "fsdp", scatter_dimension=0, tiled=False)
            return lax.psum_scatter(mine, "dp", scatter_dimension=0, tiled=True).astype(F32)

        d_a = shared(g_a[0].reshape(fsdp, model, a_full))
        d_qkv, d_vec = d_a[:, :wide], turned(d_a[:, wide : wide + per])
        d_out = shared(jnp.transpose(g_o[0].reshape(model, fsdp, cut), (1, 0, 2)))
        d_fc = shared(g_b[0].reshape(fsdp, model, model))
        d_c = jnp.transpose(g_c[0], (2, 0, 1, 3)).reshape(fsdp, plan.cols, hidden)
        d_proj = turned(shared(jnp.transpose(d_c, (0, 2, 1))))
        total = sum(jnp.sum(d * d) for d in (d_qkv, d_out, d_fc, d_proj, d_vec))
        squares = jnp.full((1, 128), total)

    sent = jnp.broadcast_to(squares[None], (dp * fsdp, 1, 128))
    with jax.named_scope("norm"):
        norms = lax.all_to_all(sent, ("dp", "fsdp"), 0, 0, tiled=True).reshape(dp * fsdp, 128)
    norm, *new = update(
        chain,
        norms,
        (qkv_weight, out_weight, fc_weight, turned(proj_weight), turned(vectors)),
        (d_qkv, d_out, d_fc, d_proj, d_vec),
        (qkv_first, out_first, fc_first, turned(proj_first), turned(vectors_first)),
        (qkv_second, out_second, fc_second, turned(proj_second), turned(vectors_second)),
    )
    new = [turned(v) if i % 5 in (3, 4) else v for i, v in enumerate(new)]
    return (output, input_grad, norm[0, 0], *new)


def solution(mesh):
    tokens = P(("dp", "fsdp"), None)
    table = P("dp", "fsdp")
    return jax.shard_map(
        body,
        mesh=mesh,
        in_specs=(tokens, P(("dp", "fsdp")), tokens) + (table,) * 15,
        out_specs=(tokens, tokens, P()) + (table,) * 15,
        check_vma=False,
    )
```

```python
import functools

import jax
import jax.numpy as jnp
from jax import lax
from jax.experimental import pallas as pl
from jax.experimental.pallas import tpu as pltpu
from jax.sharding import PartitionSpec as P

HEAD_DIM = 64
STEP = 10

beta_one = 0.9
beta_two = 0.95
clip_limit = 1.0
rate_matrix = 0.1
rate_vector = 1.0
decay_matrix = 0.1
gelu_coeff = 0.7978845608028654
cubic_coeff = 0.044715
neg_large = -1e30
VEC_ROWS = 16

F32 = jnp.float32
BF16 = jnp.bfloat16
VMEM = pl.BlockSpec(memory_space=pltpu.VMEM)
HELD = pl.BlockSpec(memory_space=pltpu.VMEM)
ANY = pl.BlockSpec(memory_space=pl.ANY)
HBM = pl.BlockSpec(memory_space=pltpu.HBM)
SMEM = pl.BlockSpec(memory_space=pltpu.SMEM)
ALL = slice(None)


def dot_nn(a, b):
    return lax.dot_general(a, b, (((1,), (0,)), ((), ())), preferred_element_type=F32)


def dot_nt(a, b):
    return lax.dot_general(a, b, (((1,), (1,)), ((), ())), preferred_element_type=F32)


def dot_tn(a, b):
    return lax.dot_general(a, b, (((0,), (0,)), ((), ())), preferred_element_type=F32)


def sds(shape, dtype):
    return jax.ShapeDtypeStruct(shape, dtype)


class Chain:
    def __init__(self):
        self.waits = []

    def wait_for(self, *arrays):
        self.waits += arrays

    def call(self, name, body, ins, in_specs, outs, out_specs, scratch, limit, aliases=None):
        several = isinstance(outs, (tuple, list))
        if not several:
            outs, out_specs = (outs,), (out_specs,)
        n_in, extra, n_out = len(ins), len(self.waits), len(outs)
        pins = ((HELD, pltpu.VMEM), (HBM, pltpu.HBM))

        def run(*refs):
            given, refs = refs[:n_in], refs[n_in + extra :]
            refs[n_out][...] = jnp.zeros(refs[n_out].shape, F32)
            body(*given, *refs[:n_out], *refs[n_out + 1 :])

        placed, made = [], []
        for v, spec in zip(ins, in_specs):
            for pin, space in pins:
                if spec is pin:
                    v = pltpu.with_memory_space_constraint(v, space)
            placed.append(v)
        for o, spec in zip(outs, out_specs):
            for pin, space in pins:
                if spec is pin:
                    o = space(o.shape, o.dtype)
            made.append(o)
        results = pl.pallas_call(
            run,
            name=name,
            input_output_aliases=aliases or {},
            out_shape=(*made, pltpu.VMEM((8, 128), F32)),
            in_specs=[*in_specs, *[ANY] * extra],
            out_specs=(*out_specs, HELD),
            scratch_shapes=scratch,
            compiler_params=pltpu.CompilerParams(vmem_limit_bytes=limit << 20),
        )(*placed, *self.waits)
        *results, token = results
        self.waits = [pltpu.with_memory_space_constraint(token, pltpu.VMEM)]
        return results if several else results[0]


class Plan:
    def __init__(self, dp, fsdp, model, hidden):
        self.dp, self.fsdp = dp, fsdp
        self.nz, self.nx = dp // 2, fsdp // 2
        self.rows = model // dp
        self.cols = model // fsdp
        self.deep = hidden // dp
        self.direct = (
            dp == 2 * fsdp
            and fsdp % 2 == 0
            and self.rows % 32 == 0
            and self.cols % 32 == 0
            and self.deep % 128 == 0
            and hidden == fsdp * model
            and dp == 8
        )

    def partner(self, name, value, stage, k=1):
        axis, step = {"x": ("fsdp", 2), "y": ("dp", 1), "z": ("dp", 2), "core": ("fsdp", 1)}[stage]
        n = self.dp if axis == "dp" else self.fsdp
        with jax.named_scope(f"{name}_{stage}"):
            return lax.ppermute(value, axis, [(i, i ^ (step * k)) for i in range(n)])

    def gather_z(self, name, value):
        near, far = self.partner(name, value, "z", 1), self.partner(name, value, "z", 2)
        return [near, far, self.partner(name, far, "z", 1)]

    def split(self):
        return (self.nz, 2, 2, self.rows // 2) if self.direct else (1, 1, 1, self.rows * self.dp)


class Me:
    def __init__(self, ref):
        self.z, self.y, self.x, self.core = ref[0], ref[1], ref[2], ref[3]
        self.other_y, self.other_x = 1 - self.y, 1 - self.x

    def fsdp(self, x, away):
        return 2 * x + (self.core ^ away)


def move(chain, name, me, arrays, outs, copies):
    n = len(arrays)

    def body(me_ref, *refs):
        for s, si, targets in copies(Me(me_ref)):
            value = refs[s][si]
            for t, ti in targets:
                refs[n + t][ti] = value

    return chain.call(
        name,
        body,
        (me, *arrays),
        [SMEM] + [VMEM] * n,
        tuple(sds(s, BF16) for s in outs),
        (HELD,) * len(outs),
        [],
        12,
    )


def gate(chain, name, *arrays, far=0):
    specs = [ANY] * (len(arrays) - far) + [HBM] * far
    return chain.call(
        name,
        lambda *refs: None,
        arrays,
        specs,
        tuple(sds(v.shape, v.dtype) for v in arrays),
        tuple(specs),
        [],
        1,
        {i: i for i in range(len(arrays))},
    )


def add_up(chain, name, me, arrays, outs, sums, after=None, big=False):
    n, m = len(arrays), len(outs)
    loaded = [shape for _, _, shape, parts in sums(Me([0, 0, 0, 0])) for s, _ in parts if s == 0] if big else []

    def body(me_ref, *refs):
        ins, outs_, refs = refs[:n], refs[n : n + m], refs[n + m :]
        held, sem = refs[: len(loaded)], refs[len(loaded) :]
        todo, i = [], 0
        for t, ti, shape, parts in sums(Me(me_ref)):
            group = []
            for s, si in parts:
                copy = None
                if big and s == 0:
                    copy = pltpu.make_async_copy(ins[0].at[si], held[i], sem[0].at[i])
                    copy.start()
                    i += 1
                group.append((copy, s, si, i - 1))
            todo.append((t, ti, group))
        done = []
        for t, ti, group in todo:
            total = None
            for copy, s, si, k in reversed(group):
                if copy is not None:
                    copy.wait()
                v = (ins[s][si] if copy is None else held[k][...]).astype(F32)
                total = v if total is None else total + v
            if after is None:
                outs_[t][ti] = total.astype(outs_[t].dtype)
            else:
                done.append(total)
        if after is not None:
            after(done, outs_)

    return chain.call(
        name,
        body,
        (me, *arrays),
        [SMEM] + [HBM if i == 0 and big else VMEM for i in range(n)],
        tuple(outs),
        (HELD if after is None else VMEM,) * m,
        [pltpu.VMEM(shape, BF16) for shape in loaded]
        + ([pltpu.SemaphoreType.DMA((len(loaded),))] if loaded else []),
        16,
    )


def pack_body(ins, outs, held, sem):
    todo = [pltpu.make_async_copy(i, h, sem.at[k]) for k, (i, h) in enumerate(zip(ins, held))]
    for c in todo:
        c.start()
    for c in todo:
        c.wait()
    qkv, out, fc, proj, vec = (h[...] for h in held)
    a, b, c = outs
    wide, model = qkv.shape[1], fc.shape[1]
    columns = jnp.transpose(vec)
    start = wide // 128 * 128
    a[:, start:] = jnp.zeros((a.shape[0], a.shape[1] - start), BF16)
    a[:, 0:wide] = qkv.astype(BF16)
    a[:, wide : wide + columns.shape[1]] = columns.astype(BF16)
    b[:, model:] = jnp.zeros((b.shape[0], b.shape[1] - model), BF16)
    b[:, 0:model] = fc.astype(BF16)
    b[:, model : model + out.shape[1]] = out.astype(BF16)
    c[...] = proj.astype(BF16).reshape(c.shape)


def pack(chain, plan, weights, a_full, b_full):
    count = len(weights)

    def run(*refs):
        pack_body(refs[:count], refs[count : count + 3], refs[count + 3 : -1], refs[-1])

    return chain.call(
        "pack",
        run,
        weights,
        [HBM] * count,
        (
            sds((plan.rows, a_full), BF16),
            sds((plan.rows, b_full), BF16),
            sds((2, plan.cols // 2, plan.deep), BF16),
        ),
        (VMEM,) * 3,
        [pltpu.VMEM(w.shape, F32) for w in weights] + [pltpu.SemaphoreType.DMA((count,))],
        6,
    )


def normed(values):
    mean = jnp.mean(values, axis=-1, keepdims=True)
    centred = values - mean
    spread = jnp.mean(centred * centred, axis=-1, keepdims=True)
    inverse = lax.rsqrt(spread + 1e-05)
    return centred * inverse, inverse


def norm_back(grad_hidden, n, inverse, gain):
    g = grad_hidden * gain
    mean_plain = jnp.mean(g, axis=-1, keepdims=True)
    mean_cross = jnp.mean(g * n, axis=-1, keepdims=True)
    return inverse * (g - mean_plain - n * mean_cross)


class Table:
    def __init__(self, fsdp):
        self.per = 12 // fsdp

    def row(self, k):
        return (k // self.per) * VEC_ROWS + k % self.per

    def get(self, ref, k):
        r = self.row(k)
        return ref[r : r + 1, :]


def spread_matrix(rows, model, d):
    r = lax.broadcasted_iota(jnp.int32, (128, model), 0)
    c = lax.broadcasted_iota(jnp.int32, (128, model), 1)
    return ((c == r + d * rows) & (r < rows)).astype(BF16)


def table_loads(plan, me, ins):
    for away in range(2):
        p, r0, r1 = ins[3 * away : 3 * away + 3]
        for y in range(2):
            for x, ref in ((me.x, p.at[0]), (me.other_x, r0)):
                yield ref, (y,), me.fsdp(x, away), (ALL, y), 0
        for y, ref in ((me.y, p.at[1]), (me.other_y, r1)):
            for x in range(plan.nx):
                yield ref, (x,), me.fsdp(x, away), (ALL, y), 1


def front_body(plan, n_in, me_ref, tokens, *refs):
    ins = refs[:n_in]
    qkv, act, a_out, t_out = refs[n_in : n_in + 4]
    a_v, bias_v, sem, out_sem = refs[n_in + 4 :]
    fsdp = plan.fsdp
    full = a_v.shape[-1]
    model = tokens.shape[1]
    wide = qkv.shape[2]
    table = Table(fsdp)
    if plan.direct:
        for ref, si, f, ti, h in table_loads(plan, Me(me_ref), ins):
            pltpu.make_async_copy(ref.at[si], a_v.at[(f, *ti, h)], sem.at[f]).start()
    else:
        for f in range(fsdp):
            pltpu.make_async_copy(ins[0].at[f], a_v.at[f], sem.at[f]).start()
    n, _ = normed(tokens[...].astype(F32))
    start = wide // 128 * 128
    for f in range(fsdp):
        pltpu.make_async_copy(a_v.at[f], a_v.at[f], sem.at[f]).wait()
        pltpu.make_async_copy(a_v.at[f], a_out.at[f], out_sem.at[f]).start()
        turned = jnp.transpose(a_v[f].reshape(model, full)[:, start:].astype(F32))
        t_out[f * VEC_ROWS : f * VEC_ROWS + table.per, :] = turned[
            wide - start : wide - start + table.per
        ]
    bias_v[:, 0:model] = jnp.broadcast_to(table.get(t_out, 4), (8, model))
    bias_v[:, model : 2 * model] = jnp.zeros((8, model), F32)
    bias_v[:, 2 * model :] = jnp.broadcast_to(table.get(t_out, 5), (8, model))
    act[...] = (n * table.get(t_out, 0) + table.get(t_out, 1)).astype(BF16)
    for f in range(fsdp):
        r = dot_nn(act[...], a_v[f].reshape(model, full))[:, :wide]
        qkv[f] = (r + bias_v[0:1, f * wide : (f + 1) * wide]).astype(BF16)
    for f in range(fsdp):
        pltpu.make_async_copy(a_v.at[f], a_out.at[f], out_sem.at[f]).wait()


def front(chain, plan, me, tokens, pieces, wide):
    t, model = tokens.shape
    fsdp = plan.fsdp
    full = pieces[0].shape[-1]
    lead = (fsdp, *plan.split(), full)
    return chain.call(
        "front",
        functools.partial(front_body, plan, len(pieces)),
        (me, tokens, *pieces),
        [SMEM, VMEM] + [ANY] * len(pieces),
        (
            sds((fsdp, t, wide), BF16),
            sds((t, model), BF16),
            sds(lead, BF16),
            sds((fsdp * VEC_ROWS, model), F32),
        ),
        (HELD, HELD, HBM, HELD),
        [
            pltpu.VMEM(lead, BF16),
            pltpu.VMEM((8, 3 * model), F32),
            pltpu.SemaphoreType.DMA((fsdp,)),
            pltpu.SemaphoreType.DMA((fsdp,)),
        ],
        14,
    )


def head_place(g, wide):
    return g // wide, g % wide


def masks(length, lo, size, keys):
    q = lax.broadcasted_iota(jnp.int32, (size, 1), 0) + lo
    limit = jnp.minimum(q, length - 1)
    k = lax.broadcasted_iota(jnp.int32, (size, keys), 1)
    return k <= limit


QBLOCK = 256


def attend_body(heads, wide, model, length_ref, qkv, mixed, logs):
    t = mixed.shape[0]
    length = length_ref[0]
    scale = HEAD_DIM**-0.5

    def part(h, which):
        f, o = head_place(which * model + h * HEAD_DIM, wide)
        return qkv[f, :, o : o + HEAD_DIM]

    for i, h in enumerate(heads):
        q = part(h, 0) * jnp.asarray(scale, BF16)
        k, v = part(h, 1), part(h, 2)
        for lo in range(0, t, QBLOCK):
            n = lo + QBLOCK
            s = dot_nt(q[lo:n], k[:n])
            s = jnp.where(masks(length, lo, QBLOCK, n), s, neg_large)
            top = jnp.max(s, axis=-1, keepdims=True)
            e = jnp.exp(s - top)
            total = jnp.sum(e, axis=-1, keepdims=True)
            p = (e * (1.0 / total)).astype(BF16)
            o = dot_nn(p, v[:n])
            mixed[lo:n, i * HEAD_DIM : (i + 1) * HEAD_DIM] = o.astype(BF16)
            logs[lo:n, i : i + 1] = top + jnp.log(total)


def attend(chain, qkv, length, model, heads):
    fsdp, t, wide = qkv.shape
    return chain.call(
        "attend",
        functools.partial(attend_body, heads, wide, model),
        (length, qkv),
        [SMEM, HELD],
        (sds((t, len(heads) * HEAD_DIM), BF16), sds((t, 128), F32)),
        (HELD, HELD),
        [],
        8,
    )


def join_body(plan, cut, n_in, n_mixed, me_ref, tokens, t_in, *refs):
    ins, refs = refs[:n_in], refs[n_in:]
    parts, (resid, act, wout, mixed, o_v, sem) = refs[:n_mixed], refs[n_mixed:]
    model = tokens.shape[1]
    fsdp = plan.fsdp
    table = Table(fsdp)
    lanes = pl.ds(model, o_v.shape[-1])
    if plan.direct:
        for ref, si, f, ti, h in table_loads(plan, Me(me_ref), ins):
            src = ref.at[(*si, ALL, ALL, lanes)]
            pltpu.make_async_copy(src, o_v.at[(f, *ti, h)], sem).start()
    else:
        for f in range(fsdp):
            src = ins[0].at[(f, ALL, ALL, ALL, ALL, lanes)]
            pltpu.make_async_copy(src, o_v.at[f], sem).start()
    at = 0
    for p in parts:
        mixed[:, at : at + p.shape[1]] = p[...]
        at += p.shape[1]
    pltpu.make_async_copy(o_v, o_v, sem).wait()
    for f in range(fsdp):
        wout[:, f * cut : (f + 1) * cut] = o_v[f].reshape(model, o_v.shape[-1])[:, :cut]
    r = tokens[...].astype(F32) + dot_nn(mixed[...], wout[...]) + table.get(t_in, 6)
    resid[...] = r
    n, _ = normed(r)
    act[...] = (n * table.get(t_in, 2) + table.get(t_in, 3)).astype(BF16)


def join(chain, plan, me, cut, tokens, parts, pieces, t_can):
    t, model = tokens.shape
    spare = pieces[0].shape[-1] - model
    return chain.call(
        "join",
        functools.partial(join_body, plan, cut, len(pieces), len(parts)),
        (me, tokens, t_can, *pieces, *parts),
        [SMEM, VMEM, HELD] + [ANY] * len(pieces) + [HELD] * len(parts),
        (
            sds((t, model), F32),
            sds((t, model), BF16),
            sds((model, model), BF16),
            sds((t, model), BF16),
        ),
        (HELD,) * 4,
        [pltpu.VMEM((plan.fsdp, *plan.split(), spare), BF16), pltpu.SemaphoreType.DMA],
        12,
    )


def mlp_up_body(plan, n_in, n_out, me_ref, act, cot, t_in, *refs):
    ins, refs = refs[:n_in], refs[n_in:]
    gel_out, slope_out, b_v, g_b_proj = refs[:4]
    gouts, refs = refs[4 : 4 + n_out], refs[4 + n_out :]
    gp_v, sem, gsem = refs
    fsdp, half = plan.fsdp, plan.cols // 2
    model = act.shape[1]
    deep = gp_v.shape[-1]
    table = Table(fsdp)
    me = Me(me_ref)
    if plan.direct:
        for ref, si, f, ti, h in table_loads(plan, me, ins):
            src = ref.at[(*si, ALL, ALL, pl.ds(0, model))]
            pltpu.make_async_copy(src, b_v.at[(f, *ti, h)], sem.at[f]).start()
    else:
        for f in range(fsdp):
            src = ins[0].at[(f, ALL, ALL, ALL, ALL, pl.ds(0, model))]
            pltpu.make_async_copy(src, b_v.at[f], sem.at[f]).start()
    g_b_proj[...] = jnp.sum(cot[...].astype(F32), axis=0, keepdims=True)
    for j in range(fsdp):
        lanes = slice(j * model, (j + 1) * model)
        pltpu.make_async_copy(b_v.at[j], b_v.at[j], sem.at[j]).wait()
        pre = dot_nn(act[...], b_v[j].reshape(model, model)) + table.get(t_in, 8 + j)
        sq = pre * pre
        th = jnp.tanh(gelu_coeff * (pre + cubic_coeff * sq * pre))
        plus = 0.5 * (1.0 + th)
        gel = (pre * plus).astype(BF16)
        gel_out[:, lanes] = gel
        slope_out[:, lanes] = plus + 0.5 * pre * (1.0 - th * th) * gelu_coeff * (
            1.0 + 3.0 * cubic_coeff * sq
        )
        grad = dot_tn(cot[...], gel).astype(BF16)
        gp_v[j, 0] = grad[:, :deep]
        gp_v[j, 1] = grad[:, deep:]
        if plan.direct and j % 2 == 1:
            span = pl.ds(j - 1, 2)
            for away in range(2):
                for x in range(plan.nx):
                    f = me.fsdp(x, away)
                    for h in range(2):
                        rows = pl.ds(pl.multiple_of(f * plan.cols + h * half, 16), half)
                        src = gp_v.at[span, :, rows]
                        pltpu.make_async_copy(src, gouts[away].at[h, x, span], gsem).start()
    if not plan.direct:
        pltpu.make_async_copy(gp_v, gouts[0], gsem).start()
    pltpu.make_async_copy(gp_v, gp_v, gsem).wait()


def mlp_up(chain, plan, me, act, cot, t_can, pieces, hidden):
    t, model = act.shape
    fsdp = plan.fsdp
    per = hidden // fsdp // 2
    if plan.direct:
        grads = [sds((2, plan.nx, plan.nz, 2, plan.cols // 2, plan.deep), BF16)] * 2
    else:
        grads = [sds((fsdp, 2, model, per), BF16)]
    lead = (fsdp, *plan.split(), model)
    return chain.call(
        "mlp_up",
        functools.partial(mlp_up_body, plan, len(pieces), len(grads)),
        (me, act, cot, t_can, *pieces),
        [SMEM, HELD, VMEM, HELD] + [ANY] * len(pieces),
        (
            sds((t, hidden), BF16),
            sds((t, hidden), F32),
            sds(lead, BF16),
            sds((1, model), F32),
            *grads,
        ),
        (HELD,) * 4 + (HBM,) * len(grads),
        [
            pltpu.VMEM((fsdp, 2, model, per), BF16),
            pltpu.SemaphoreType.DMA((fsdp,)),
            pltpu.SemaphoreType.DMA,
        ],
        22,
    )


def mlp_down_body(plan, n_in, me_ref, cot, resid, gel, slope, t_in, *refs):
    ins, refs = refs[:n_in], refs[n_in:]
    output, gpre, g_b_fc, c_v, acc, csem = refs
    fsdp, half = plan.fsdp, plan.cols // 2
    model = cot.shape[1]
    table = Table(fsdp)
    if plan.direct:
        for ref, si, f, ti, h in table_loads(plan, Me(me_ref), ins):
            rows = pl.ds(pl.multiple_of(f * plan.cols + h * half, 16), half)
            pltpu.make_async_copy(ref.at[si], c_v.at[(*ti, rows)], csem).start()
    else:
        pltpu.make_async_copy(ins[0], c_v, csem).start()
    acc[...] = resid[...] + table.get(t_in, 7)
    pltpu.make_async_copy(c_v, c_v, csem).wait()
    for j in range(fsdp):
        lanes = slice(j * model, (j + 1) * model)
        down = jnp.concatenate([c_v[j, 0], c_v[j, 1]], axis=1)
        low = (dot_nn(cot[...], down) * slope[:, lanes]).astype(BF16)
        gpre[:, lanes] = low
        g_b_fc[j : j + 1, :] = jnp.sum(low.astype(F32), axis=0, keepdims=True)
        acc[...] += dot_nt(gel[:, lanes], down)
    output[...] = acc[...].astype(BF16)


def mlp_down(chain, plan, me, cot, resid, gel, slope, t_can, pieces):
    t, model = cot.shape
    fsdp, hidden = plan.fsdp, gel.shape[1]
    return chain.call(
        "mlp_down",
        functools.partial(mlp_down_body, plan, len(pieces)),
        (me, cot, resid, gel, slope, t_can, *pieces),
        [SMEM, VMEM, HELD, HELD, HELD, HELD] + [ANY] * len(pieces),
        (sds((t, model), BF16), sds((t, hidden), BF16), sds((fsdp, model), F32)),
        (VMEM, HELD, HELD),
        [
            pltpu.VMEM((fsdp, 2, model, hidden // fsdp // 2), BF16),
            pltpu.VMEM((t, model), F32),
            pltpu.SemaphoreType.DMA,
        ],
        18,
    )


def mlp_back_body(plan, n_out, me_ref, act, gpre, b_in, *refs):
    gact = refs[0]
    gouts = refs[1 : 1 + n_out]
    g_v, gsem = refs[1 + n_out :]
    model = act.shape[1]
    me = Me(me_ref)
    first = True
    order = [
        (x, away, me.fsdp(x, away) if plan.direct else 2 * x + away)
        for away in range(2)
        for x in range(plan.nx)
    ]
    for x, away, f in order:
        part = gpre[:, pl.ds(pl.multiple_of(f * model, model), model)]
        slot = 2 * x + away
        g_v[slot] = dot_tn(act[...], part).astype(BF16).reshape(g_v.shape[1:])
        if plan.direct:
            for h in range(2):
                src = g_v.at[slot, :, :, h]
                dst = gouts[away].at[h, x, :, :, :, pl.ds(0, model)]
                pltpu.make_async_copy(src, dst, gsem).start()
        else:
            pltpu.make_async_copy(g_v.at[slot], gouts[0].at[f], gsem).start()
        back = dot_nt(part, b_in[f].reshape(model, model))
        if first:
            gact[...] = back
        else:
            gact[...] += back
        first = False
    pltpu.make_async_copy(g_v, g_v, gsem).wait()


def mlp_back(chain, plan, me, act, gpre, b_can, b_full):
    t, model = act.shape
    fsdp = plan.fsdp
    lead = (fsdp, *plan.split(), model)
    if plan.direct:
        grads = [sds((2, plan.nx, plan.nz, 2, plan.rows // 2, b_full), BF16)] * 2
    else:
        grads = [sds(lead, BF16)]
    return chain.call(
        "mlp_back",
        functools.partial(mlp_back_body, plan, len(grads)),
        (me, act, gpre, b_can),
        [SMEM, HELD, HELD, HELD],
        (sds((t, model), F32), *grads),
        (HELD,) + (HBM,) * len(grads),
        [
            pltpu.VMEM(lead, BF16),
            pltpu.SemaphoreType.DMA,
        ],
        14,
    )


def join_back_body(plan, n_in, me_ref, gact, cot, resid, mixed, wout, t_in, *refs):
    gresid, gmixed, g_vec, *gouts = refs[n_in:-2]
    o_v, sem = refs[-2:]
    model = cot.shape[1]
    table = Table(plan.fsdp)
    n, inverse = normed(resid[...])
    e = gact[...]
    g_vec[...] = jnp.zeros(g_vec.shape, F32)
    g_vec[0:1, :] = jnp.sum(e * n, axis=0, keepdims=True)
    g_vec[1:2, :] = jnp.sum(e, axis=0, keepdims=True)
    r = cot[...].astype(F32) + norm_back(e, n, inverse, table.get(t_in, 2))
    gresid[...] = r
    branch = r.astype(BF16)
    g_vec[2:3, :] = jnp.sum(branch.astype(F32), axis=0, keepdims=True)
    grad = dot_tn(mixed[...], branch).astype(BF16)
    if plan.direct:
        me = Me(me_ref)
        cut = plan.cols
        for f in range(plan.fsdp):
            part = grad[:, f * cut : (f + 1) * cut]
            o_v[f, :, :, :, :, 0:cut] = part.reshape(*o_v.shape[1:-1], cut)
            o_v[f, :, :, :, :, cut:] = jnp.zeros((*o_v.shape[1:-1], o_v.shape[-1] - cut), BF16)
        for away in range(2):
            for x in range(plan.nx):
                f = me.fsdp(x, away)
                for h in range(2):
                    dst = gouts[away].at[h, x, :, :, :, pl.ds(model, o_v.shape[-1])]
                    pltpu.make_async_copy(o_v.at[f, :, :, h], dst, sem).start()
    else:
        gouts[0][...] = grad
    gmixed[...] = dot_nt(branch, wout[...]).astype(BF16)
    if plan.direct:
        pltpu.make_async_copy(o_v, o_v, sem).wait()


def join_back(chain, plan, me, gact, cot, resid, mixed, wout, t_can, g_b):
    t, model = cot.shape
    ins = [me, gact, cot, resid, mixed, wout, t_can]
    if plan.direct:
        spare = g_b[0].shape[-1] - model
        grads, grad_specs = [sds(g.shape, BF16) for g in g_b], [HBM] * len(g_b)
        aliases = {len(ins) + i: 3 + i for i in range(len(g_b))}
    else:
        spare = 128
        grads, grad_specs, aliases, g_b = [sds((model, model), BF16)], [VMEM], {}, []
    return chain.call(
        "join_back",
        functools.partial(join_back_body, plan, len(g_b)),
        (*ins, *g_b),
        [SMEM, HELD, VMEM, HELD, HELD, HELD, HELD] + [HBM] * len(g_b),
        (sds((t, model), F32), sds((t, model), BF16), sds((8, model), F32), *grads),
        (HELD, HELD, HELD, *grad_specs),
        [pltpu.VMEM((plan.fsdp, *plan.split(), spare), BF16), pltpu.SemaphoreType.DMA],
        18,
        aliases,
    )


def attend_back_body(heads, wide, model, length_ref, qkv, gmixed, logs, out):
    t = gmixed.shape[0]
    length = length_ref[0]
    scale = HEAD_DIM**-0.5

    def part(h, which):
        f, o = head_place(which * model + h * HEAD_DIM, wide)
        return qkv[f, :, o : o + HEAD_DIM]

    for i, h in enumerate(heads):
        lanes = slice(i * HEAD_DIM, (i + 1) * HEAD_DIM)
        q = part(h, 0)
        small = q * jnp.asarray(scale, BF16)
        k, v = part(h, 1), part(h, 2)
        go = gmixed[:, h * HEAD_DIM : (h + 1) * HEAD_DIM]
        gk, gv = [], []
        for lo in range(0, t, QBLOCK):
            n = lo + QBLOCK
            s = dot_nt(small[lo:n], k[:n])
            s = jnp.where(masks(length, lo, QBLOCK, n), s, neg_large)
            p = jnp.exp(s - logs[lo:n, i : i + 1])
            gp = dot_nt(go[lo:n], v[:n])
            inner = jnp.sum(p * gp, axis=-1, keepdims=True)
            ds = (p * (gp - inner)).astype(BF16)
            out[0, lo:n, lanes] = (dot_nn(ds, k[:n]) * scale).astype(BF16)
            gv.append(dot_tn(p.astype(BF16), go[lo:n]))
            gk.append(dot_tn(ds, small[lo:n]))
        for b in range(t // QBLOCK):
            rows = slice(b * QBLOCK, (b + 1) * QBLOCK)
            out[1, rows, lanes] = sum(x[rows] for x in gk[b:]).astype(BF16)
            out[2, rows, lanes] = sum(x[rows] for x in gv[b:]).astype(BF16)


def attend_back(chain, qkv, gmixed, logs, length, heads):
    fsdp, t, wide = qkv.shape
    model = gmixed.shape[1]
    return chain.call(
        "attend_back",
        functools.partial(attend_back_body, heads, wide, model),
        (length, qkv, gmixed, logs),
        [SMEM, HELD, HELD, HELD],
        sds((3, t, len(heads) * HEAD_DIM), BF16),
        HELD,
        [],
        10,
    )


def whole_qkv(parts, gq_v):
    model = gq_v.shape[1] // 3
    at = 0
    for p in parts:
        size = p.shape[2]
        for which in range(3):
            gq_v[:, which * model + at : which * model + at + size] = p[which]
        at += size


def back_body(plan, wide, n_parts, n_out, me_ref, tokens, act, a_in, gresid, t_in, g_two, g_b_fc, g_b_proj, *refs):
    parts, refs = refs[:n_parts], refs[n_parts:]
    input_grad, gouts, refs = refs[0], refs[1 : 1 + n_out], refs[1 + n_out :]
    gq_v, g_v, tab, a_v, sem, in_sem = refs
    late = pltpu.make_async_copy(a_in, a_v, in_sem)
    late.start()
    fsdp = plan.fsdp
    t, model = tokens.shape
    full = a_in.shape[-1]
    table = Table(fsdp)
    spare = full - wide
    whole_qkv(parts, gq_v)
    for f in range(fsdp):
        grad = dot_tn(act[...], gq_v[:, f * wide : (f + 1) * wide]).astype(BF16)
        g_v[f, :, :, :, :, 0:wide] = grad.reshape(*g_v.shape[1:-1], wide)
    back = jnp.zeros((t, model), F32)
    late.wait()
    for f in range(fsdp):
        part = gq_v[:, f * wide : (f + 1) * wide]
        back = back + dot_nt(part, a_v[f].reshape(model, full)[:, :wide])
    sums = jnp.sum(gq_v[...].astype(F32), axis=0, keepdims=True)
    n, inverse = normed(tokens[...].astype(F32))
    tab[...] = jnp.zeros(tab.shape, F32)

    def put(k, value):
        r = (k // table.per) * spare + k % table.per
        tab[r : r + 1, :] = value

    put(0, jnp.sum(back * n, axis=0, keepdims=True))
    put(1, jnp.sum(back, axis=0, keepdims=True))
    put(2, g_two[0:1, :])
    put(3, g_two[1:2, :])
    put(4, sums[:, 0:model])
    put(5, sums[:, 2 * model :])
    put(6, g_two[2:3, :])
    put(7, g_b_proj[...])
    for j in range(fsdp):
        put(8 + j, g_b_fc[j : j + 1, :])
    for f in range(fsdp):
        columns = jnp.transpose(tab[f * spare : (f + 1) * spare, :]).astype(BF16)
        g_v[f, :, :, :, :, wide:] = columns.reshape(*g_v.shape[1:-1], spare)
    if plan.direct:
        me = Me(me_ref)
        for away in range(2):
            for x in range(plan.nx):
                f = me.fsdp(x, away)
                for h in range(2):
                    dst = gouts[1 + h].at[x] if away else gouts[0].at[h, x]
                    pltpu.make_async_copy(g_v.at[f, :, :, h], dst, sem).start()
    else:
        pltpu.make_async_copy(g_v, gouts[0], sem).start()
    r = gresid[...] + norm_back(back, n, inverse, table.get(t_in, 0))
    input_grad[...] = r.astype(BF16)
    pltpu.make_async_copy(g_v, g_v, sem).wait()


def back(chain, plan, wide, me, tokens, act, parts, a_can, gresid, t_can, g_two, g_b_fc, g_b_proj):
    t, model = tokens.shape
    fsdp, full = plan.fsdp, a_can.shape[-1]
    lead = (fsdp, *plan.split(), full)
    if plan.direct:
        one = (plan.nx, plan.nz, 2, plan.rows // 2, full)
        grads = [sds((2, *one), BF16), sds(one, BF16), sds(one, BF16)]
    else:
        grads = [sds(lead, BF16)]
    return chain.call(
        "back",
        functools.partial(back_body, plan, wide, len(parts), len(grads)),
        (me, tokens, act, a_can, gresid, t_can, g_two, g_b_fc, g_b_proj, *parts),
        [SMEM, VMEM, HELD, HBM] + [HELD] * (5 + len(parts)),
        (sds((t, model), BF16), *grads),
        (VMEM,) + (HBM,) * len(grads),
        [
            pltpu.VMEM((t, 3 * model), BF16),
            pltpu.VMEM(lead, BF16),
            pltpu.VMEM((fsdp * (full - wide), model), F32),
            pltpu.VMEM(lead, BF16),
            pltpu.SemaphoreType.DMA,
            pltpu.SemaphoreType.DMA,
        ],
        26,
    )


def update_body(count, *refs):
    norms = refs[0]
    n = 4 * count
    ins, outs = refs[1 : 1 + n], refs[1 + n : 2 + n + 3 * count]
    held, sem = refs[2 + n + 3 * count : -1], refs[-1]
    todo = [pltpu.make_async_copy(i, h, sem.at[k]) for k, (i, h) in enumerate(zip(ins, held))]
    for c in todo:
        c.start()
    norm = jnp.sqrt(jnp.sum(norms[...], axis=0, keepdims=True))
    outs[0][...] = norm
    factor = jnp.minimum(1.0, clip_limit / (norm[:, 0:1] + 1e-06))
    for i in range(count):
        for c in todo[4 * i : 4 * i + 4]:
            c.wait()
        w, g, one, two = (r[...] for r in held[4 * i : 4 * i + 4])
        last = i == count - 1
        rate, decay = (rate_vector, 0.0) if last else (rate_matrix, decay_matrix)
        clipped = g * factor
        one_new = beta_one * one + (1.0 - beta_one) * clipped
        two_new = beta_two * two + (1.0 - beta_two) * clipped * clipped
        first_hat = one_new / (1.0 - beta_one**STEP)
        second_hat = two_new / (1.0 - beta_two**STEP)
        outs[1 + i][...] = w - rate * (first_hat / (jnp.sqrt(second_hat) + 1e-08) + decay * w)
        outs[1 + count + i][...] = one_new
        outs[1 + 2 * count + i][...] = two_new


def update(chain, norms, weights, grads, firsts, seconds):
    count = len(weights)
    ins = []
    for group in zip(weights, grads, firsts, seconds):
        ins += group
    outs = [sds((1, 128), F32)] + [sds(w.shape, F32) for w in weights] * 3
    return chain.call(
        "update",
        functools.partial(update_body, count),
        [norms, *ins],
        [VMEM] + [HBM if i % 4 != 1 else ANY for i in range(len(ins))],
        tuple(outs),
        (VMEM,) * len(outs),
        [pltpu.VMEM(i.shape, F32) for i in ins] + [pltpu.SemaphoreType.DMA((len(ins),))],
        16,
    )


def place_second(chain, name, plan, me, z0, r0, z1, r1):
    def copies(m):
        return [
            (0, ALL, [(0, (m.y,)), (2, (0, m.y))]),
            (1, ALL, [(0, (m.other_y,)), (2, (0, m.other_y))]),
            (2, ALL, [(1, (m.x,)), (2, (1, m.x))]),
            (3, ALL, [(1, (m.other_x,)), (2, (1, m.other_x))]),
        ]

    outs = [(2, *z0.shape), (2, *z1.shape), (2, 2, *z0.shape)]
    return move(chain, name, me, [z0, r0, z1, r1], outs, copies)


def both(came, h, at):
    if len(came) == 1:
        return [(0, (h, *at)), (1, (h, *at))]
    return [(0, (h, *at)), (1 + h, at)]


def first_sums(chain, plan, name, me, own, came):
    nx, nz, _, rows, cols = own.shape[1:]

    def sums(m):
        return [
            (0, ALL, (nz, 2, rows, cols), both(came, 0, (m.other_x,))),
            (1, ALL, (nx, nz, rows, cols), both(came, 1, (ALL, ALL, m.other_y))),
        ]

    outs = [sds((nz, 2, rows, cols), BF16), sds((nx, nz, rows, cols), BF16)]
    s0, s1 = add_up(chain, name + "1", me, [own, *came], outs, sums, big=True)
    return plan.partner(name, s0, "x"), plan.partner(name, s1, "y")


def second_sums(chain, plan, name, me, own, came, f0, f1):
    nx, nz, _, rows, cols = own.shape[1:]
    n = 1 + len(came)

    def sums(m):
        at0, at1 = (m.x, ALL, m.other_y), (m.other_x, ALL, m.y)
        return [
            (0, ALL, (nz, rows, cols), both(came, 0, at0) + [(n, (ALL, m.other_y))]),
            (1, ALL, (nz, rows, cols), both(came, 1, at1) + [(n + 1, (m.other_x,))]),
        ]

    outs = [sds((nz, rows, cols), BF16)] * 2
    s0, s1 = add_up(chain, name + "2", me, [own, *came, f0, f1], outs, sums, big=True)
    return plan.partner(name, s0, "y"), plan.partner(name, s1, "x")


def third_sums(chain, plan, name, me, own, came, f0, f1, s0, s1):
    nx, nz, _, rows, cols = own.shape[1:]
    n = 1 + len(came)

    def sums(m):
        out = []
        for k in range(nz):
            z = m.z ^ k
            at = (m.x, z, m.y)
            one = both(came, 0, at) + [(n, (z, m.y)), (n + 2, (z,))]
            two = both(came, 1, at) + [(n + 1, (m.x, z)), (n + 3, (z,))]
            out.append((k, slice(0, rows), (rows, cols), one))
            out.append((k, slice(rows, 2 * rows), (rows, cols), two))
        return out

    outs = [sds((2 * rows, cols), F32 if k == 0 else BF16) for k in range(nz)]
    return add_up(chain, name + "3", me, [own, *came, f0, f1, s0, s1], outs, sums, big=True)


def along_z(chain, plan, name, me, two, came):
    (total,) = add_up(
        chain, name, me, [two, came], [two], lambda m: [(0, ALL, two.shape, [(0, ALL), (1, ALL)])]
    )
    return total


def squared(*values):
    return jnp.broadcast_to(sum(jnp.sum(v * v) for v in values), (1, 128))


def body(
    tokens,
    lengths,
    cotangent,
    qkv_weight,
    out_weight,
    fc_weight,
    proj_weight,
    vectors,
    qkv_first,
    out_first,
    fc_first,
    proj_first,
    vectors_first,
    qkv_second,
    out_second,
    fc_second,
    proj_second,
    vectors_second,
):
    dp, fsdp = lax.axis_size("dp"), lax.axis_size("fsdp")
    model = tokens.shape[1]
    wide, cut = qkv_weight.shape[1], out_weight.shape[1]
    hidden = fc_weight.shape[1] * fsdp
    per = vectors.shape[1]
    plan = Plan(dp, fsdp, model, hidden)
    rows, half, chalf, nz = plan.rows, plan.rows // 2, plan.cols // 2, plan.nz
    a_full = -(-(wide + per) // 128) * 128
    b_full = model + -(-cut // 128) * 128
    chain = Chain()
    at_dp, at_fsdp = lax.axis_index("dp"), lax.axis_index("fsdp")
    me = jnp.stack([at_dp // 2, at_dp % 2, at_fsdp // 2, at_fsdp % 2]).astype(jnp.int32)
    heads = model // HEAD_DIM
    third = [range(i, i + heads // 3) for i in range(0, heads, heads // 3)]

    def turned(value):
        return jnp.transpose(value)

    if plan.direct:
        weights = (qkv_weight, out_weight, fc_weight, turned(proj_weight), turned(vectors))
        a_own, b_own, c_own = pack(chain, plan, weights, a_full, b_full)
        a_came = plan.gather_z("gather_a", a_own)
        c_y, c_x = plan.partner("gather_c", c_own[0], "y"), plan.partner("gather_c", c_own[1], "x")
        chain.wait_for(c_y, c_x)

        def place_a(m):
            return [
                (k, pl.ds(h * half, half), [(h, (m.z ^ k,))]) for k in range(nz) for h in range(2)
            ] + [(nz, ALL, [(2, ALL)])]

        outs = [(nz, half, a_full)] * 2 + [b_own.shape]
        a_z0, a_z1, b_own = move(chain, "place_a1", me, [a_own, *a_came, b_own], outs, place_a)
        a_r0, a_r1 = plan.partner("gather_a", a_z0, "y"), plan.partner("gather_a", a_z1, "x")
        b_came = plan.gather_z("gather_b", b_own)
        a_p0, a_p1, a_p = place_second(chain, "place_a2", plan, me, a_z0, a_r0, a_z1, a_r1)
        a_in = [a_p, plan.partner("gather_a", a_p0, "x"), plan.partner("gather_a", a_p1, "y")]
        a_in = a_in + [plan.partner("gather_a", v, "core") for v in a_in]

        def place_b(m):
            return [
                (k, pl.ds(h * half, half), [(h, (m.z ^ k,))]) for k in range(nz) for h in range(2)
            ] + [
                (nz, (0,), [(2, (m.y,))]),
                (nz + 1, ALL, [(2, (m.other_y,))]),
                (nz, (1,), [(2, (2 + m.x,))]),
                (nz + 2, ALL, [(2, (2 + m.other_x,))]),
            ]

        outs = [(nz, half, b_full), (nz, half, b_full), (4, chalf, plan.deep)]
        arrays = [b_own, *b_came, c_own, c_y, c_x]
        b_z0, b_z1, c_pair = move(chain, "place_b1", me, arrays, outs, place_b)
        b_r0, b_r1 = plan.partner("gather_b", b_z0, "y"), plan.partner("gather_b", b_z1, "x")
        c_came = plan.gather_z("gather_c", c_pair)
    else:

        def whole(shard):
            down = lax.all_gather(shard.astype(BF16), "dp", axis=0, tiled=True)
            return lax.all_gather(down, "fsdp", axis=0, tiled=False)

        def padded(parts, full):
            both = jnp.concatenate(parts, axis=1)
            both = whole(jnp.pad(both, ((0, 0), (0, full - both.shape[1]))))
            return both.reshape(fsdp, *plan.split(), full)

        a_in = [padded([qkv_weight, vectors], a_full)]
        b_in = [padded([fc_weight, out_weight], b_full)]
        c_all = jnp.transpose(whole(proj_weight), (0, 2, 1))
        c_all = c_all.reshape(model, fsdp, 2, hidden // fsdp // 2)
        c_in = [jnp.transpose(c_all, (1, 2, 0, 3))]

    qkv, act_one, a_can, t_can = front(chain, plan, me, tokens, a_in, wide)
    if plan.direct:
        b_p0, b_p1, b_p = place_second(chain, "place_b2", plan, me, b_z0, b_r0, b_z1, b_r1)
        b_q0, b_q1 = plan.partner("gather_b", b_p0, "x"), plan.partner("gather_b", b_p1, "y")
        b_pc = plan.partner("gather_b", b_p, "core")
    parts = []
    for group in third:
        parts.append(attend(chain, qkv, lengths, model, group))
    if plan.direct:
        b_q0, b_q1 = gate(chain, "gate_b", b_q0, b_q1)
        b_in = [b_p, b_q0, b_q1, b_pc] + [plan.partner("gather_b", v, "core") for v in (b_q0, b_q1)]
        def place_c(m):
            return [
                (k, (2 * h + i,), [(h, (i, m.z ^ k)), (2, (h, i, m.z ^ k))])
                for k in range(nz)
                for h in range(2)
                for i in range(2)
            ]

        block = (2, nz, chalf, plan.deep)
        outs = [block, block, (2, *block)]
        chain.wait_for(b_pc)
        c_p0, c_p1, c_p = move(chain, "place_c2", me, [c_pair, *c_came], outs, place_c)
        c_q0, c_q1 = plan.partner("gather_c", c_p0, "x"), plan.partner("gather_c", c_p1, "y")
        c_pc = plan.partner("gather_c", c_p, "core")
    logs = [p[1] for p in parts]
    resid_two, act_two, wout, mixed = join(
        chain, plan, me, cut, tokens, [p[0] for p in parts], b_in, t_can
    )
    gel, slope, b_can, g_b_proj, *g_c = mlp_up(
        chain, plan, me, act_two, cotangent, t_can, b_in, hidden
    )
    if plan.direct:
        c_q0, c_q1, away = gate(chain, "gate_c", c_q0, c_q1, g_c[1], far=1)
        c_in = [c_p, c_q0, c_q1, c_pc] + [plan.partner("gather_c", v, "core") for v in (c_q0, c_q1)]
        c_away = plan.partner("sum_c", away, "core")
    output, gpre, g_b_fc = mlp_down(
        chain, plan, me, cotangent, resid_two, gel, slope, t_can, c_in
    )

    gact, *g_b = mlp_back(chain, plan, me, act_two, gpre, b_can, b_full)
    if plan.direct:
        chain.wait_for(c_away)
    gresid, gmixed, g_two, *g_o = join_back(
        chain, plan, me, gact, cotangent, resid_two, mixed, wout, t_can, g_b
    )
    if plan.direct:
        g_b = g_o
        b_away = plan.partner("sum_b", g_b[1], "core")
        c_f0, c_f1 = first_sums(chain, plan, "sum_c", me, g_c[0], [c_away])
    gparts = [
        attend_back(chain, qkv, gmixed, log, lengths, group) for log, group in zip(logs, third)
    ]
    if plan.direct:

        chain.wait_for(c_f0, c_f1)
        b_f0, b_f1 = first_sums(chain, plan, "sum_b", me, g_b[0], [b_away])

        def sums_cz(m):
            out = []
            for k in range(nz):
                z = m.z ^ k
                at = (0, m.x, z)
                terms = [(0, at), (1, at), (2, (z,))]
                out.append((k, slice(0, 2), (2, chalf, plan.deep), terms))
                at = (1, ALL, z, m.y)
                terms = [(0, at), (1, at), (3, (ALL, z))]
                out.append((k, slice(2, 4), (2, chalf, plan.deep), terms))
            return out

        outs = [sds((4, chalf, plan.deep), F32 if k == 0 else BF16) for k in range(nz)]
        arrays = [g_c[0], c_away, c_f0, c_f1]
        c_u = add_up(chain, "sum_c2", me, arrays, outs, sums_cz, big=True)
        c_far = plan.partner("sum_c", c_u[3], "z", 1)
    input_grad, *g_a = back(
        chain, plan, wide, me, tokens, act_one, gparts, a_can, gresid, t_can, g_two, g_b_fc, g_b_proj
    )

    if plan.direct:
        chain.wait_for(b_f0, b_f1)
        a_away = [plan.partner("sum_a", v, "core") for v in gate(chain, "gate_a", *g_a[1:], far=2)]
        b_s0, b_s1 = second_sums(chain, plan, "sum_b", me, g_b[0], [b_away], b_f0, b_f1)
        a_f0, a_f1 = first_sums(chain, plan, "sum_a", me, g_a[0], a_away)
        c_two = along_z(chain, plan, "sum_c4", me, c_u[2], c_far)
        c_z = [c_u[0], plan.partner("sum_c", c_u[1], "z", 1), plan.partner("sum_c", c_two, "z", 2)]
        b_u = third_sums(chain, plan, "sum_b", me, g_b[0], [b_away], b_f0, b_f1, b_s0, b_s1)
        b_far = plan.partner("sum_b", b_u[3], "z", 1)

        def sums_c3(m):
            block = (chalf, plan.deep)
            one = [(i, (m.other_y,)) for i in range(3)]
            two = [(i, (2 + m.other_x,)) for i in range(3)]
            return [(0, ALL, block, one), (1, ALL, block, two)]

        outs = [sds((chalf, plan.deep), BF16)] * 2
        s0, s1 = add_up(chain, "sum_c3", me, c_z, outs, sums_c3)
        c_l0, c_l1 = plan.partner("sum_c", s0, "y"), plan.partner("sum_c", s1, "x")
        b_two = along_z(chain, plan, "sum_b4", me, b_u[2], b_far)
        b_z = [b_u[0], plan.partner("sum_b", b_u[1], "z", 1), plan.partner("sum_b", b_two, "z", 2)]
        a_s0, a_s1 = second_sums(chain, plan, "sum_a", me, g_a[0], a_away, a_f0, a_f1)

        def sums_c(m):
            block = (chalf, plan.deep)
            one = [(i, (m.y,)) for i in range(3)] + [(3, ALL)]
            two = [(i, (2 + m.x,)) for i in range(3)] + [(4, ALL)]
            return [(0, ALL, block, one), (1, ALL, block, two)]

        def end_c(done, outs):
            outs[0][0:chalf, :] = done[0]
            outs[0][chalf:, :] = done[1]
            outs[1][...] = squared(*done)

        d_proj, s_c = add_up(
            chain,
            "end_c",
            me,
            [*c_z, c_l0, c_l1],
            [sds((plan.cols, plan.deep), F32), sds((1, 128), F32)],
            sums_c,
            end_c,
        )
        a_u = third_sums(chain, plan, "sum_a", me, g_a[0], a_away, a_f0, a_f1, a_s0, a_s1)
        a_z = [a_u[0]] + [plan.partner("sum_a", a_u[k], "z", k) for k in range(1, nz)]

        def last(arrays):
            return lambda m: [(0, ALL, arrays[0].shape, [(i, ALL) for i in range(len(arrays))])]

        def end_b(done, outs):
            total = done[0]
            fc, out = total[:, :model], total[:, model : model + cut]
            outs[0][...] = fc
            outs[1][...] = out
            outs[2][...] = squared(fc, out)

        shapes = [fc_weight.shape, out_weight.shape, (1, 128)]
        d_fc, d_out, s_b = add_up(
            chain, "end_b", me, b_z, [sds(s, F32) for s in shapes], last(b_z), end_b
        )

        def end_a(done, outs):
            total = done[0]
            start = wide // 128 * 128
            vec = jnp.transpose(total[:, start:])[wide - start : wide - start + per]
            qkv = total[:, :wide]
            outs[0][...] = qkv
            outs[1][...] = vec
            outs[2][...] = squared(qkv, vec)

        shapes = [qkv_weight.shape, (per, rows), (1, 128)]
        d_qkv, d_vec, s_a = add_up(
            chain, "end_a", me, a_z, [sds(s, F32) for s in shapes], last(a_z), end_a
        )
        squares = s_a + s_b + s_c
    else:

        def shared(value):
            mine = lax.psum_scatter(value, "fsdp", scatter_dimension=0, tiled=False)
            return lax.psum_scatter(mine, "dp", scatter_dimension=0, tiled=True).astype(F32)

        d_a = shared(g_a[0].reshape(fsdp, model, a_full))
        d_qkv, d_vec = d_a[:, :wide], turned(d_a[:, wide : wide + per])
        d_out = shared(jnp.transpose(g_o[0].reshape(model, fsdp, cut), (1, 0, 2)))
        d_fc = shared(g_b[0].reshape(fsdp, model, model))
        d_c = jnp.transpose(g_c[0], (2, 0, 1, 3)).reshape(fsdp, plan.cols, hidden)
        d_proj = turned(shared(jnp.transpose(d_c, (0, 2, 1))))
        total = sum(jnp.sum(d * d) for d in (d_qkv, d_out, d_fc, d_proj, d_vec))
        squares = jnp.full((1, 128), total)

    sent = jnp.broadcast_to(squares[None], (dp * fsdp, 1, 128))
    with jax.named_scope("norm"):
        norms = lax.all_to_all(sent, ("dp", "fsdp"), 0, 0, tiled=True).reshape(dp * fsdp, 128)
    norm, *new = update(
        chain,
        norms,
        (qkv_weight, out_weight, fc_weight, turned(proj_weight), turned(vectors)),
        (d_qkv, d_out, d_fc, d_proj, d_vec),
        (qkv_first, out_first, fc_first, turned(proj_first), turned(vectors_first)),
        (qkv_second, out_second, fc_second, turned(proj_second), turned(vectors_second)),
    )
    new = [turned(v) if i % 5 in (3, 4) else v for i, v in enumerate(new)]
    return (output, input_grad, norm[0, 0], *new)


def solution(mesh):
    tokens = P(("dp", "fsdp"), None)
    table = P("dp", "fsdp")
    return jax.shard_map(
        body,
        mesh=mesh,
        in_specs=(tokens, P(("dp", "fsdp")), tokens) + (table,) * 15,
        out_specs=(tokens, tokens, P()) + (table,) * 15,
        check_vma=False,
    )
```

```python
import functools

import jax
import jax.numpy as jnp
from jax import lax
from jax.experimental import pallas as pl
from jax.experimental.pallas import tpu as pltpu
from jax.sharding import PartitionSpec as P

HEAD_DIM = 64
STEP = 10

beta_one = 0.9
beta_two = 0.95
clip_limit = 1.0
rate_matrix = 0.1
rate_vector = 1.0
decay_matrix = 0.1
gelu_coeff = 0.7978845608028654
cubic_coeff = 0.044715
neg_large = -1e30
VEC_ROWS = 16

F32 = jnp.float32
BF16 = jnp.bfloat16
VMEM = pl.BlockSpec(memory_space=pltpu.VMEM)
HELD = pl.BlockSpec(memory_space=pltpu.VMEM)
ANY = pl.BlockSpec(memory_space=pl.ANY)
HBM = pl.BlockSpec(memory_space=pltpu.HBM)
SMEM = pl.BlockSpec(memory_space=pltpu.SMEM)
ALL = slice(None)


def dot_nn(a, b):
    return lax.dot_general(a, b, (((1,), (0,)), ((), ())), preferred_element_type=F32)


def dot_nt(a, b):
    return lax.dot_general(a, b, (((1,), (1,)), ((), ())), preferred_element_type=F32)


def dot_tn(a, b):
    return lax.dot_general(a, b, (((0,), (0,)), ((), ())), preferred_element_type=F32)


def sds(shape, dtype):
    return jax.ShapeDtypeStruct(shape, dtype)


class Chain:
    def __init__(self):
        self.waits = []

    def wait_for(self, *arrays):
        self.waits += arrays

    def call(self, name, body, ins, in_specs, outs, out_specs, scratch, limit, aliases=None):
        several = isinstance(outs, (tuple, list))
        if not several:
            outs, out_specs = (outs,), (out_specs,)
        n_in, extra, n_out = len(ins), len(self.waits), len(outs)
        pins = ((HELD, pltpu.VMEM), (HBM, pltpu.HBM))

        def run(*refs):
            given, refs = refs[:n_in], refs[n_in + extra :]
            refs[n_out][...] = jnp.zeros(refs[n_out].shape, F32)
            body(*given, *refs[:n_out], *refs[n_out + 1 :])

        placed, made = [], []
        for v, spec in zip(ins, in_specs):
            for pin, space in pins:
                if spec is pin:
                    v = pltpu.with_memory_space_constraint(v, space)
            placed.append(v)
        for o, spec in zip(outs, out_specs):
            for pin, space in pins:
                if spec is pin:
                    o = space(o.shape, o.dtype)
            made.append(o)
        results = pl.pallas_call(
            run,
            name=name,
            input_output_aliases=aliases or {},
            out_shape=(*made, pltpu.VMEM((8, 128), F32)),
            in_specs=[*in_specs, *[ANY] * extra],
            out_specs=(*out_specs, HELD),
            scratch_shapes=scratch,
            compiler_params=pltpu.CompilerParams(vmem_limit_bytes=limit << 20),
        )(*placed, *self.waits)
        *results, token = results
        self.waits = [pltpu.with_memory_space_constraint(token, pltpu.VMEM)]
        return results if several else results[0]


class Plan:
    def __init__(self, dp, fsdp, model, hidden):
        self.dp, self.fsdp = dp, fsdp
        self.nz, self.nx = dp // 2, fsdp // 2
        self.rows = model // dp
        self.cols = model // fsdp
        self.deep = hidden // dp
        self.direct = (
            dp == 2 * fsdp
            and fsdp % 2 == 0
            and self.rows % 32 == 0
            and self.cols % 32 == 0
            and self.deep % 128 == 0
            and hidden == fsdp * model
            and dp == 8
        )

    def partner(self, name, value, stage, k=1):
        axis, step = {"x": ("fsdp", 2), "y": ("dp", 1), "z": ("dp", 2), "core": ("fsdp", 1)}[stage]
        n = self.dp if axis == "dp" else self.fsdp
        with jax.named_scope(f"{name}_{stage}"):
            return lax.ppermute(value, axis, [(i, i ^ (step * k)) for i in range(n)])

    def opposite(self, name, value):
        n = self.fsdp
        pairs = [(i * n + j, (i ^ 1) * n + (j ^ 2)) for i in range(self.dp) for j in range(n)]
        with jax.named_scope(f"{name}_xy"):
            return lax.ppermute(value, ("dp", "fsdp"), pairs)

    def gather_z(self, name, value):
        near, far = self.partner(name, value, "z", 1), self.partner(name, value, "z", 2)
        return [near, far, self.partner(name, far, "z", 1)]

    def split(self):
        return (self.nz, 2, 2, self.rows // 2) if self.direct else (1, 1, 1, self.rows * self.dp)


class Me:
    def __init__(self, ref):
        self.z, self.y, self.x, self.core = ref[0], ref[1], ref[2], ref[3]
        self.other_y, self.other_x = 1 - self.y, 1 - self.x

    def fsdp(self, x, away):
        return 2 * x + (self.core ^ away)


def move(chain, name, me, arrays, outs, copies):
    n = len(arrays)

    def body(me_ref, *refs):
        for s, si, targets in copies(Me(me_ref)):
            value = refs[s][si]
            for t, ti in targets:
                refs[n + t][ti] = value

    return chain.call(
        name,
        body,
        (me, *arrays),
        [SMEM] + [VMEM] * n,
        tuple(sds(s, BF16) for s in outs),
        (HELD,) * len(outs),
        [],
        6,
    )


def gate(chain, name, *arrays, far=0):
    specs = [ANY] * (len(arrays) - far) + [HBM] * far
    return chain.call(
        name,
        lambda *refs: None,
        arrays,
        specs,
        tuple(sds(v.shape, v.dtype) for v in arrays),
        tuple(specs),
        [],
        1,
        {i: i for i in range(len(arrays))},
    )


def add_up(chain, name, me, arrays, outs, sums, after=None, far=0):
    n, m = len(arrays), len(outs)
    still = sums(Me([0, 0, 0, 0]))
    loaded = [shape for _, _, shape, parts in still for s, _ in parts if s < far]

    def body(me_ref, *refs):
        ins, outs_, refs = refs[:n], refs[n : n + m], refs[n + m :]
        held, sem = refs[: len(loaded)], refs[len(loaded) :]
        todo, i = [], 0
        for t, ti, shape, parts in sums(Me(me_ref)):
            group = []
            for s, si in parts:
                copy = None
                if s < far:
                    copy = pltpu.make_async_copy(ins[s].at[si], held[i], sem[0].at[i])
                    copy.start()
                    i += 1
                group.append((copy, s, si, i - 1))
            todo.append((t, ti, group))
        done = []
        for t, ti, group in todo:
            total = None
            for copy, s, si, k in reversed(group):
                if copy is not None:
                    copy.wait()
                v = (ins[s][si] if copy is None else held[k][...]).astype(F32)
                total = v if total is None else total + v
            if after is None:
                outs_[t][ti] = total.astype(outs_[t].dtype)
            else:
                done.append(total)
        if after is not None:
            after(done, outs_)

    return chain.call(
        name,
        body,
        (me, *arrays),
        [SMEM] + [HBM if i < far else VMEM for i in range(n)],
        tuple(outs),
        (HELD if after is None else VMEM,) * m,
        [pltpu.VMEM(shape, BF16) for shape in loaded]
        + ([pltpu.SemaphoreType.DMA((len(loaded),))] if loaded else []),
        8,
    )


def pack_body(ins, outs, held, sem):
    todo = [pltpu.make_async_copy(i, h, sem.at[k]) for k, (i, h) in enumerate(zip(ins, held))]
    for c in todo:
        c.start()
    for c in todo:
        c.wait()
    qkv, out, fc, proj, vec = (h[...] for h in held)
    a, b, c = outs
    wide, model = qkv.shape[1], fc.shape[1]
    columns = jnp.transpose(vec)
    start = wide // 128 * 128
    a[:, start:] = jnp.zeros((a.shape[0], a.shape[1] - start), BF16)
    a[:, 0:wide] = qkv.astype(BF16)
    a[:, wide : wide + columns.shape[1]] = columns.astype(BF16)
    b[:, model:] = jnp.zeros((b.shape[0], b.shape[1] - model), BF16)
    b[:, 0:model] = fc.astype(BF16)
    b[:, model : model + out.shape[1]] = out.astype(BF16)
    c[...] = proj.astype(BF16).reshape(c.shape)


def pack(chain, plan, weights, a_full, b_full):
    count = len(weights)

    def run(*refs):
        pack_body(refs[:count], refs[count : count + 3], refs[count + 3 : -1], refs[-1])

    return chain.call(
        "pack",
        run,
        weights,
        [HBM] * count,
        (
            sds((plan.rows, a_full), BF16),
            sds((plan.rows, b_full), BF16),
            sds((2, plan.cols // 2, plan.deep), BF16),
        ),
        (VMEM,) * 3,
        [pltpu.VMEM(w.shape, F32) for w in weights] + [pltpu.SemaphoreType.DMA((count,))],
        6,
    )


def normed(values):
    mean = jnp.mean(values, axis=-1, keepdims=True)
    centred = values - mean
    spread = jnp.mean(centred * centred, axis=-1, keepdims=True)
    inverse = lax.rsqrt(spread + 1e-05)
    return centred * inverse, inverse


def norm_back(grad_hidden, n, inverse, gain):
    g = grad_hidden * gain
    mean_plain = jnp.mean(g, axis=-1, keepdims=True)
    mean_cross = jnp.mean(g * n, axis=-1, keepdims=True)
    return inverse * (g - mean_plain - n * mean_cross)


class Table:
    def __init__(self, fsdp):
        self.per = 12 // fsdp

    def row(self, k):
        return (k // self.per) * VEC_ROWS + k % self.per

    def get(self, ref, k):
        r = self.row(k)
        return ref[r : r + 1, :]


def spread_matrix(rows, model, d):
    r = lax.broadcasted_iota(jnp.int32, (128, model), 0)
    c = lax.broadcasted_iota(jnp.int32, (128, model), 1)
    return ((c == r + d * rows) & (r < rows)).astype(BF16)


def table_loads(plan, me, ins):
    for away in range(2):
        p, r0, r1 = ins[3 * away : 3 * away + 3]
        for y in range(2):
            for x, ref in ((me.x, p.at[0]), (me.other_x, r0)):
                yield ref, (y,), me.fsdp(x, away), (ALL, y), 0
        for y, ref in ((me.y, p.at[1]), (me.other_y, r1)):
            for x in range(plan.nx):
                yield ref, (x,), me.fsdp(x, away), (ALL, y), 1


def front_body(plan, n_in, me_ref, tokens, *refs):
    ins = refs[:n_in]
    qkv, act, a_out, t_out = refs[n_in : n_in + 4]
    a_v, bias_v, sem, out_sem = refs[n_in + 4 :]
    fsdp = plan.fsdp
    full = a_v.shape[-1]
    model = tokens.shape[1]
    wide = qkv.shape[2]
    table = Table(fsdp)
    if plan.direct:
        me = Me(me_ref)
        for i, ref in enumerate(ins):
            away, x, y = i // 4, i // 2 % 2, i % 2
            f = me.fsdp(me.x ^ x, away)
            pltpu.make_async_copy(ref, a_v.at[f, :, me.y ^ y], sem.at[f]).start()
    else:
        for f in range(fsdp):
            pltpu.make_async_copy(ins[0].at[f], a_v.at[f], sem.at[f]).start()
    n, _ = normed(tokens[...].astype(F32))
    start = wide // 128 * 128
    for f in range(fsdp):
        pltpu.make_async_copy(a_v.at[f], a_v.at[f], sem.at[f]).wait()
        pltpu.make_async_copy(a_v.at[f], a_out.at[f], out_sem.at[f]).start()
        turned = jnp.transpose(a_v[f].reshape(model, full)[:, start:].astype(F32))
        t_out[f * VEC_ROWS : f * VEC_ROWS + table.per, :] = turned[
            wide - start : wide - start + table.per
        ]
    bias_v[:, 0:model] = jnp.broadcast_to(table.get(t_out, 4), (8, model))
    bias_v[:, model : 2 * model] = jnp.zeros((8, model), F32)
    bias_v[:, 2 * model :] = jnp.broadcast_to(table.get(t_out, 5), (8, model))
    act[...] = (n * table.get(t_out, 0) + table.get(t_out, 1)).astype(BF16)
    for f in range(fsdp):
        r = dot_nn(act[...], a_v[f].reshape(model, full))[:, :wide]
        qkv[f] = (r + bias_v[0:1, f * wide : (f + 1) * wide]).astype(BF16)
    for f in range(fsdp):
        pltpu.make_async_copy(a_v.at[f], a_out.at[f], out_sem.at[f]).wait()


def front(chain, plan, me, tokens, pieces, wide):
    t, model = tokens.shape
    fsdp = plan.fsdp
    full = pieces[0].shape[-1]
    lead = (fsdp, plan.nz, 2, plan.rows, full) if plan.direct else pieces[0].shape
    return chain.call(
        "front",
        functools.partial(front_body, plan, len(pieces)),
        (me, tokens, *pieces),
        [SMEM, VMEM] + [ANY] * len(pieces),
        (
            sds((fsdp, t, wide), BF16),
            sds((t, model), BF16),
            sds(lead, BF16),
            sds((fsdp * VEC_ROWS, model), F32),
        ),
        (HELD, HELD, HBM, HELD),
        [
            pltpu.VMEM(lead, BF16),
            pltpu.VMEM((8, 3 * model), F32),
            pltpu.SemaphoreType.DMA((fsdp,)),
            pltpu.SemaphoreType.DMA((fsdp,)),
        ],
        12,
    )


def head_place(g, wide):
    return g // wide, g % wide


def masks(length, lo, size, keys):
    q = lax.broadcasted_iota(jnp.int32, (size, 1), 0) + lo
    limit = jnp.minimum(q, length - 1)
    k = lax.broadcasted_iota(jnp.int32, (size, keys), 1)
    return k <= limit


QBLOCK = 256


def attend_body(heads, wide, model, length_ref, qkv, mixed, logs):
    t = mixed.shape[0]
    length = length_ref[0]
    scale = HEAD_DIM**-0.5

    def part(h, which):
        f, o = head_place(which * model + h * HEAD_DIM, wide)
        return qkv[f, :, o : o + HEAD_DIM]

    for i, h in enumerate(heads):
        q = part(h, 0) * jnp.asarray(scale, BF16)
        k, v = part(h, 1), part(h, 2)
        for lo in range(0, t, QBLOCK):
            n = lo + QBLOCK
            s = dot_nt(q[lo:n], k[:n])
            s = jnp.where(masks(length, lo, QBLOCK, n), s, neg_large)
            top = jnp.max(s, axis=-1, keepdims=True)
            e = jnp.exp(s - top)
            total = jnp.sum(e, axis=-1, keepdims=True)
            p = (e * (1.0 / total)).astype(BF16)
            o = dot_nn(p, v[:n])
            mixed[lo:n, i * HEAD_DIM : (i + 1) * HEAD_DIM] = o.astype(BF16)
            logs[lo:n, i : i + 1] = top + jnp.log(total)


def attend(chain, qkv, length, model, heads):
    fsdp, t, wide = qkv.shape
    return chain.call(
        "attend",
        functools.partial(attend_body, heads, wide, model),
        (length, qkv),
        [SMEM, HELD],
        (sds((t, len(heads) * HEAD_DIM), BF16), sds((t, 128), F32)),
        (HELD, HELD),
        [],
        6,
    )


def join_body(plan, cut, n_in, n_mixed, me_ref, tokens, t_in, *refs):
    ins, refs = refs[:n_in], refs[n_in:]
    parts, (resid, act, wout, mixed, o_v, sem) = refs[:n_mixed], refs[n_mixed:]
    model = tokens.shape[1]
    fsdp = plan.fsdp
    table = Table(fsdp)
    lanes = pl.ds(model, o_v.shape[-1])
    if plan.direct:
        for ref, si, f, ti, h in table_loads(plan, Me(me_ref), ins):
            src = ref.at[(*si, ALL, ALL, lanes)]
            pltpu.make_async_copy(src, o_v.at[(f, *ti, h)], sem).start()
    else:
        for f in range(fsdp):
            src = ins[0].at[(f, ALL, ALL, ALL, ALL, lanes)]
            pltpu.make_async_copy(src, o_v.at[f], sem).start()
    at = 0
    for p in parts:
        mixed[:, at : at + p.shape[1]] = p[...]
        at += p.shape[1]
    pltpu.make_async_copy(o_v, o_v, sem).wait()
    for f in range(fsdp):
        wout[:, f * cut : (f + 1) * cut] = o_v[f].reshape(model, o_v.shape[-1])[:, :cut]
    r = tokens[...].astype(F32) + dot_nn(mixed[...], wout[...]) + table.get(t_in, 6)
    resid[...] = r
    n, _ = normed(r)
    act[...] = (n * table.get(t_in, 2) + table.get(t_in, 3)).astype(BF16)


def join(chain, plan, me, cut, tokens, parts, pieces, t_can):
    t, model = tokens.shape
    spare = pieces[0].shape[-1] - model
    return chain.call(
        "join",
        functools.partial(join_body, plan, cut, len(pieces), len(parts)),
        (me, tokens, t_can, *pieces, *parts),
        [SMEM, VMEM, HELD] + [ANY] * len(pieces) + [HELD] * len(parts),
        (
            sds((t, model), F32),
            sds((t, model), BF16),
            sds((model, model), BF16),
            sds((t, model), BF16),
        ),
        (HELD,) * 4,
        [pltpu.VMEM((plan.fsdp, *plan.split(), spare), BF16), pltpu.SemaphoreType.DMA],
        10,
    )


def mlp_up_body(plan, n_in, n_out, me_ref, act, cot, t_in, *refs):
    ins, refs = refs[:n_in], refs[n_in:]
    gel_out, slope_out, b_v, g_b_proj = refs[:4]
    gouts, refs = refs[4 : 4 + n_out], refs[4 + n_out :]
    gp_v, sem, gsem = refs
    fsdp, half = plan.fsdp, plan.cols // 2
    model = act.shape[1]
    deep = gp_v.shape[-1]
    table = Table(fsdp)
    me = Me(me_ref)
    if plan.direct:
        for ref, si, f, ti, h in table_loads(plan, me, ins):
            src = ref.at[(*si, ALL, ALL, pl.ds(0, model))]
            pltpu.make_async_copy(src, b_v.at[(f, *ti, h)], sem.at[f]).start()
    else:
        for f in range(fsdp):
            src = ins[0].at[(f, ALL, ALL, ALL, ALL, pl.ds(0, model))]
            pltpu.make_async_copy(src, b_v.at[f], sem.at[f]).start()
    g_b_proj[...] = jnp.sum(cot[...].astype(F32), axis=0, keepdims=True)

    def up(j):
        pltpu.make_async_copy(b_v.at[j], b_v.at[j], sem.at[j]).wait()
        return dot_nn(act[...], b_v[j].reshape(model, model)) + table.get(t_in, 8 + j)

    after = up(0)
    for j in range(fsdp):
        lanes = slice(j * model, (j + 1) * model)
        pre = after
        if j + 1 < fsdp:
            after = up(j + 1)
        sq = pre * pre
        th = jnp.tanh(gelu_coeff * (pre + cubic_coeff * sq * pre))
        plus = 0.5 * (1.0 + th)
        gel = (pre * plus).astype(BF16)
        gel_out[:, lanes] = gel
        slope_out[:, lanes] = plus + 0.5 * pre * (1.0 - th * th) * gelu_coeff * (
            1.0 + 3.0 * cubic_coeff * sq
        )
        grad = dot_tn(cot[...], gel).astype(BF16)
        gp_v[j, 0] = grad[:, :deep]
        gp_v[j, 1] = grad[:, deep:]
        if plan.direct and j % 2 == 1:
            span = pl.ds(j - 1, 2)
            for away in range(2):
                for x in range(plan.nx):
                    f = me.fsdp(x, away)
                    for h in range(2):
                        rows = pl.ds(pl.multiple_of(f * plan.cols + h * half, 16), half)
                        src = gp_v.at[span, :, rows]
                        pltpu.make_async_copy(src, gouts[away].at[h, x, span], gsem).start()
    if not plan.direct:
        pltpu.make_async_copy(gp_v, gouts[0], gsem).start()
    pltpu.make_async_copy(gp_v, gp_v, gsem).wait()


def mlp_up(chain, plan, me, act, cot, t_can, pieces, hidden):
    t, model = act.shape
    fsdp = plan.fsdp
    per = hidden // fsdp // 2
    if plan.direct:
        grads = [sds((2, plan.nx, plan.nz, 2, plan.cols // 2, plan.deep), BF16)] * 2
    else:
        grads = [sds((fsdp, 2, model, per), BF16)]
    lead = (fsdp, *plan.split(), model)
    return chain.call(
        "mlp_up",
        functools.partial(mlp_up_body, plan, len(pieces), len(grads)),
        (me, act, cot, t_can, *pieces),
        [SMEM, HELD, VMEM, HELD] + [ANY] * len(pieces),
        (
            sds((t, hidden), BF16),
            sds((t, hidden), F32),
            sds(lead, BF16),
            sds((1, model), F32),
            *grads,
        ),
        (HELD,) * 4 + (HBM,) * len(grads),
        [
            pltpu.VMEM((fsdp, 2, model, per), BF16),
            pltpu.SemaphoreType.DMA((fsdp,)),
            pltpu.SemaphoreType.DMA,
        ],
        18,
    )


def mlp_down_body(plan, n_in, me_ref, cot, resid, gel, slope, t_in, *refs):
    ins, refs = refs[:n_in], refs[n_in:]
    output, gpre, g_b_fc, c_v, acc = refs
    fsdp, half = plan.fsdp, plan.cols // 2
    model = cot.shape[1]
    table = Table(fsdp)
    if plan.direct:
        for ref, si, f, ti, h in table_loads(plan, Me(me_ref), ins):
            rows = pl.ds(pl.multiple_of(f * plan.cols + h * half, 16), half)
            c_v[(*ti, rows)] = ref[si]
    else:
        c_v[...] = ins[0][...]
    acc[...] = resid[...] + table.get(t_in, 7)
    for j in range(fsdp):
        lanes = slice(j * model, (j + 1) * model)
        down = jnp.concatenate([c_v[j, 0], c_v[j, 1]], axis=1)
        low = (dot_nn(cot[...], down) * slope[:, lanes]).astype(BF16)
        gpre[:, lanes] = low
        g_b_fc[j : j + 1, :] = jnp.sum(low.astype(F32), axis=0, keepdims=True)
        acc[...] += dot_nt(gel[:, lanes], down)
    output[...] = acc[...].astype(BF16)


def mlp_down(chain, plan, me, cot, resid, gel, slope, t_can, pieces):
    t, model = cot.shape
    fsdp, hidden = plan.fsdp, gel.shape[1]
    return chain.call(
        "mlp_down",
        functools.partial(mlp_down_body, plan, len(pieces)),
        (me, cot, resid, gel, slope, t_can, *pieces),
        [SMEM, VMEM, HELD, HELD, HELD, HELD] + [VMEM] * len(pieces),
        (sds((t, model), BF16), sds((t, hidden), BF16), sds((fsdp, model), F32)),
        (VMEM, HELD, HELD),
        [
            pltpu.VMEM((fsdp, 2, model, hidden // fsdp // 2), BF16),
            pltpu.VMEM((t, model), F32),
        ],
        12,
    )


def mlp_back_body(plan, n_out, me_ref, act, gpre, b_in, *refs):
    gact = refs[0]
    gouts = refs[1 : 1 + n_out]
    model = act.shape[1]
    me = Me(me_ref)
    first = True
    order = [
        (x, away, me.fsdp(x, away) if plan.direct else 2 * x + away)
        for away in range(2)
        for x in range(plan.nx)
    ]
    for x, away, f in order:
        part = gpre[:, pl.ds(pl.multiple_of(f * model, model), model)]
        grad = dot_tn(act[...], part).astype(BF16).reshape(b_in.shape[1:])
        if not plan.direct:
            gouts[0][f] = grad
        elif away:
            gouts[1][x], gouts[2][x] = grad[:, :, 0], grad[:, :, 1]
        else:
            gouts[0][0, x], gouts[0][1, x] = grad[:, :, 0], grad[:, :, 1]
        back = dot_nt(part, b_in[f].reshape(model, model))
        if first:
            gact[...] = back
        else:
            gact[...] += back
        first = False


def mlp_back(chain, plan, me, act, gpre, b_can):
    t, model = act.shape
    fsdp = plan.fsdp
    lead = (fsdp, *plan.split(), model)
    if plan.direct:
        one = (plan.nx, plan.nz, 2, plan.rows // 2, model)
        grads = [sds((2, *one), BF16), sds(one, BF16), sds(one, BF16)]
    else:
        grads = [sds(lead, BF16)]
    return chain.call(
        "mlp_back",
        functools.partial(mlp_back_body, plan, len(grads)),
        (me, act, gpre, b_can),
        [SMEM, HELD, HELD, HELD],
        (sds((t, model), F32), *grads),
        (HELD,) + (HELD,) * len(grads),
        [],
        10,
    )


def join_back_body(plan, me_ref, gact, cot, resid, mixed, wout, t_in, *refs):
    gresid, gmixed, inner, g_vec, *gouts = refs[:-1]
    o_v = refs[-1]
    model = cot.shape[1]
    table = Table(plan.fsdp)
    n, inverse = normed(resid[...])
    e = gact[...]
    g_vec[...] = jnp.zeros(g_vec.shape, F32)
    g_vec[0:1, :] = jnp.sum(e * n, axis=0, keepdims=True)
    g_vec[1:2, :] = jnp.sum(e, axis=0, keepdims=True)
    r = cot[...].astype(F32) + norm_back(e, n, inverse, table.get(t_in, 2))
    gresid[...] = r
    branch = r.astype(BF16)
    g_vec[2:3, :] = jnp.sum(branch.astype(F32), axis=0, keepdims=True)
    grad = dot_tn(mixed[...], branch).astype(BF16)
    if plan.direct:
        me = Me(me_ref)
        cut = plan.cols
        for f in range(plan.fsdp):
            o_v[f, :, 0:cut] = grad[:, f * cut : (f + 1) * cut]
            o_v[f, :, cut:] = jnp.zeros((model, o_v.shape[-1] - cut), BF16)
        for away in range(2):
            for x in range(plan.nx):
                part = o_v[me.fsdp(x, away)].reshape(*plan.split(), o_v.shape[-1])
                gouts[away][0, x], gouts[away][1, x] = part[:, :, 0], part[:, :, 1]
    else:
        gouts[0][...] = grad
    low = dot_nt(branch, wout[...]).astype(BF16)
    gmixed[...] = low
    product = low.astype(F32) * mixed[...].astype(F32)
    high = product.astype(BF16)
    rest = (product - high.astype(F32)).astype(BF16)
    head = lax.broadcasted_iota(jnp.int32, (model, 128), 0) // HEAD_DIM
    ones = (head == lax.broadcasted_iota(jnp.int32, (model, 128), 1)).astype(BF16)
    inner[...] = dot_nn(high, ones) + dot_nn(rest, ones)


def join_back(chain, plan, me, gact, cot, resid, mixed, wout, t_can, spare):
    t, model = cot.shape
    ins = [me, gact, cot, resid, mixed, wout, t_can]
    if plan.direct:
        grads = [sds((2, plan.nx, plan.nz, 2, plan.rows // 2, spare), BF16)] * 2
        grad_specs = [HELD] * 2
    else:
        grads, grad_specs = [sds((model, model), BF16)], [VMEM]
    return chain.call(
        "join_back",
        functools.partial(join_back_body, plan),
        ins,
        [SMEM, HELD, VMEM, HELD, HELD, HELD, HELD],
        (
            sds((t, model), F32),
            sds((t, model), BF16),
            sds((t, 128), F32),
            sds((8, model), F32),
            *grads,
        ),
        (HELD, HELD, HELD, HELD, *grad_specs),
        [pltpu.VMEM((plan.fsdp, model, spare), BF16)],
        14,
    )


def attend_back_body(heads, wide, model, length_ref, qkv, gmixed, logs, inner, out):
    t = gmixed.shape[0]
    length = length_ref[0]
    scale = HEAD_DIM**-0.5

    def part(h, which):
        f, o = head_place(which * model + h * HEAD_DIM, wide)
        return qkv[f, :, o : o + HEAD_DIM]

    for i, h in enumerate(heads):
        lanes = slice(i * HEAD_DIM, (i + 1) * HEAD_DIM)
        q = part(h, 0)
        small = q * jnp.asarray(scale, BF16)
        k, v = part(h, 1), part(h, 2)
        go = gmixed[:, h * HEAD_DIM : (h + 1) * HEAD_DIM]
        gk, gv = [], []
        for lo in range(0, t, QBLOCK):
            n = lo + QBLOCK
            s = dot_nt(small[lo:n], k[:n])
            s = jnp.where(masks(length, lo, QBLOCK, n), s, neg_large)
            p = jnp.exp(s - logs[lo:n, i : i + 1])
            gp = dot_nt(go[lo:n], v[:n])
            ds = (p * (gp - inner[lo:n, h : h + 1])).astype(BF16)
            out[0, lo:n, lanes] = (dot_nn(ds, k[:n]) * scale).astype(BF16)
            gv.append(dot_tn(p.astype(BF16), go[lo:n]))
            gk.append(dot_tn(ds, small[lo:n]))
        for b in range(t // QBLOCK):
            rows = slice(b * QBLOCK, (b + 1) * QBLOCK)
            out[1, rows, lanes] = sum(x[rows] for x in gk[b:]).astype(BF16)
            out[2, rows, lanes] = sum(x[rows] for x in gv[b:]).astype(BF16)


def attend_back(chain, qkv, gmixed, logs, inner, length, heads):
    fsdp, t, wide = qkv.shape
    model = gmixed.shape[1]
    return chain.call(
        "attend_back",
        functools.partial(attend_back_body, heads, wide, model),
        (length, qkv, gmixed, logs, inner),
        [SMEM, HELD, HELD, HELD, HELD],
        sds((3, t, len(heads) * HEAD_DIM), BF16),
        HELD,
        [],
        8,
    )


def whole_qkv(parts, gq_v):
    wide = gq_v.shape[2]
    model = gq_v.shape[0] * wide // 3
    at = 0
    for p in parts:
        size = p.shape[2]
        for which in range(3):
            lo = which * model + at
            while lo < which * model + at + size:
                f, first = lo // wide, lo % wide
                n = min(wide - first, which * model + at + size - lo)
                begin = lo - which * model - at
                gq_v[f, :, first : first + n] = p[which, :, begin : begin + n]
                lo += n
        at += size


def back_body(plan, wide, n_parts, n_out, me_ref, tokens, act, a_in, gresid, t_in, g_two, g_b_fc, g_b_proj, *refs):
    parts, refs = refs[:n_parts], refs[n_parts:]
    input_grad, gouts, refs = refs[0], refs[1 : 1 + n_out], refs[1 + n_out :]
    gq_v, sum_v, tab, a_v, in_sem = refs
    late = pltpu.make_async_copy(a_in, a_v, in_sem)
    late.start()
    fsdp = plan.fsdp
    t, model = tokens.shape
    full = a_in.shape[-1]
    table = Table(fsdp)
    spare = full - wide
    whole_qkv(parts, gq_v)
    me = Me(me_ref)

    def each():
        for away in range(2):
            for x in range(plan.nx):
                if plan.direct:
                    ends = [gouts[1 + h].at[x] if away else gouts[0].at[h, x] for h in range(2)]
                    yield me.fsdp(x, away), ends
                else:
                    yield 2 * x + away, [gouts[0].at[2 * x + away, :, :, h] for h in range(1)]

    for f, ends in each():
        grad = dot_tn(act[...], gq_v[f]).astype(BF16).reshape(*plan.split(), wide)
        for h, end in enumerate(ends):
            end[:, :, :, 0:wide] = grad[:, :, h]
    back = jnp.zeros((t, model), F32)
    late.wait()
    for f in range(fsdp):
        back = back + dot_nt(gq_v[f], a_v[f].reshape(model, full)[:, :wide])
    for f in range(fsdp):
        sum_v[0:1, f * wide : (f + 1) * wide] = jnp.sum(gq_v[f].astype(F32), axis=0, keepdims=True)
    n, inverse = normed(tokens[...].astype(F32))
    tab[...] = jnp.zeros(tab.shape, F32)

    def put(k, value):
        r = (k // table.per) * spare + k % table.per
        tab[r : r + 1, :] = value

    put(0, jnp.sum(back * n, axis=0, keepdims=True))
    put(1, jnp.sum(back, axis=0, keepdims=True))
    put(2, g_two[0:1, :])
    put(3, g_two[1:2, :])
    put(4, sum_v[0:1, 0:model])
    put(5, sum_v[0:1, 2 * model :])
    put(6, g_two[2:3, :])
    put(7, g_b_proj[...])
    for j in range(fsdp):
        put(8 + j, g_b_fc[j : j + 1, :])
    for f, ends in each():
        rows = pl.ds(pl.multiple_of(f * spare, 8), spare)
        columns = jnp.transpose(tab[rows, :]).astype(BF16).reshape(*plan.split(), spare)
        for h, end in enumerate(ends):
            end[:, :, :, wide:] = columns[:, :, h]
    r = gresid[...] + norm_back(back, n, inverse, table.get(t_in, 0))
    input_grad[...] = r.astype(BF16)


def back(chain, plan, wide, me, tokens, act, parts, a_can, gresid, t_can, g_two, g_b_fc, g_b_proj):
    t, model = tokens.shape
    fsdp, full = plan.fsdp, a_can.shape[-1]
    lead = (fsdp, *plan.split(), full)
    if plan.direct:
        one = (plan.nx, plan.nz, 2, plan.rows // 2, full)
        grads = [sds((2, *one), BF16), sds(one, BF16), sds(one, BF16)]
    else:
        grads = [sds(lead, BF16)]
    return chain.call(
        "back",
        functools.partial(back_body, plan, wide, len(parts), len(grads)),
        (me, tokens, act, a_can, gresid, t_can, g_two, g_b_fc, g_b_proj, *parts),
        [SMEM, VMEM, HELD, HBM] + [HELD] * (5 + len(parts)),
        (sds((t, model), BF16), *grads),
        (VMEM,) + (HELD,) * len(grads),
        [
            pltpu.VMEM((fsdp, t, wide), BF16),
            pltpu.VMEM((8, 3 * model), F32),
            pltpu.VMEM((fsdp * (full - wide), model), F32),
            pltpu.VMEM(a_can.shape, BF16),
            pltpu.SemaphoreType.DMA,
        ],
        20,
    )


def update_body(count, *refs):
    norms = refs[0]
    n, m = 4 * count, 3 * count
    ins, norm_out, outs = refs[1 : 1 + n], refs[1 + n], refs[2 + n : 2 + n + m]
    held, made = refs[2 + n + m : 2 + 2 * n + m], refs[2 + 2 * n + m : 2 + 2 * n + 2 * m]
    sem, out_sem = refs[-2:]
    todo = [pltpu.make_async_copy(i, h, sem.at[k]) for k, (i, h) in enumerate(zip(ins, held))]
    for c in todo:
        c.start()
    norm = jnp.sqrt(jnp.sum(norms[...], axis=0, keepdims=True))
    norm_out[...] = norm
    factor = jnp.minimum(1.0, clip_limit / (norm[:, 0:1] + 1e-06))
    stores = []
    for i in range(count):
        for c in todo[4 * i : 4 * i + 4]:
            c.wait()
        w, g, one, two = (r[...] for r in held[4 * i : 4 * i + 4])
        last = i == count - 1
        rate, decay = (rate_vector, 0.0) if last else (rate_matrix, decay_matrix)
        clipped = g * factor
        one_new = beta_one * one + (1.0 - beta_one) * clipped
        two_new = beta_two * two + (1.0 - beta_two) * clipped * clipped
        first_hat = one_new / (1.0 - beta_one**STEP)
        second_hat = two_new / (1.0 - beta_two**STEP)
        made[i][...] = w - rate * (first_hat / (jnp.sqrt(second_hat) + 1e-08) + decay * w)
        made[count + i][...] = one_new
        made[2 * count + i][...] = two_new
        for k in (i, count + i, 2 * count + i):
            c = pltpu.make_async_copy(made[k], outs[k], out_sem.at[k])
            c.start()
            stores.append(c)
    for c in stores:
        c.wait()


def update(chain, norms, weights, grads, firsts, seconds):
    count = len(weights)
    ins = []
    for group in zip(weights, grads, firsts, seconds):
        ins += group
    outs = [sds(w.shape, F32) for w in weights] * 3
    return chain.call(
        "update",
        functools.partial(update_body, count),
        [norms, *ins],
        [VMEM] + [HBM if i % 4 != 1 else ANY for i in range(len(ins))],
        (sds((1, 128), F32), *outs),
        (VMEM,) + (HBM,) * len(outs),
        [pltpu.VMEM(v.shape, F32) for v in (*ins, *outs)]
        + [pltpu.SemaphoreType.DMA((len(ins),)), pltpu.SemaphoreType.DMA((len(outs),))],
        12,
    )


def place_second(chain, name, plan, me, z0, r0, z1, r1):
    def copies(m):
        return [
            (0, ALL, [(0, (m.y,)), (2, (0, m.y))]),
            (1, ALL, [(0, (m.other_y,)), (2, (0, m.other_y))]),
            (2, ALL, [(1, (m.x,)), (2, (1, m.x))]),
            (3, ALL, [(1, (m.other_x,)), (2, (1, m.other_x))]),
        ]

    outs = [(2, *z0.shape), (2, *z1.shape), (2, 2, *z0.shape)]
    return move(chain, name, me, [z0, r0, z1, r1], outs, copies)


class Parts:
    def __init__(self, groups, far=0):
        self.count, self.far = len(groups), far
        self.arrays = [own for own, _ in groups] + [v for _, came in groups for v in came]
        self.lanes, self.came, at, place = [], [], 0, self.count
        for own, came in groups:
            self.lanes.append(slice(at, at + own.shape[-1]))
            self.came.append((place, len(came)))
            at += own.shape[-1]
            place += len(came)
        _, self.nx, self.nz, _, self.rows, _ = groups[0][0].shape
        self.cols = at

    def terms(self, g, h, at):
        place, n = self.came[g]
        return [(g, (h, *at)), (place, (h, *at)) if n == 1 else (place + h, at)]

    def sums(self, make):
        return [
            item
            for g, lanes in enumerate(self.lanes)
            for item in make(g, (self.rows, lanes.stop - lanes.start), lanes)
        ]


def first_sums(chain, plan, name, me, parts):
    nx, nz = parts.nx, parts.nz

    def sums(m):
        return parts.sums(
            lambda g, end, lanes: [
                (0, (ALL, ALL, ALL, lanes), (nz, 2, *end), parts.terms(g, 0, (m.other_x,))),
                (1, (ALL, ALL, ALL, lanes), (nx, nz, *end), parts.terms(g, 1, (ALL, ALL, m.other_y))),
            ]
        )

    outs = [sds((nz, 2, parts.rows, parts.cols), BF16), sds((nx, nz, parts.rows, parts.cols), BF16)]
    s0, s1 = add_up(chain, name + "1", me, parts.arrays, outs, sums, far=parts.far)
    return plan.partner(name, s0, "x"), plan.partner(name, s1, "y")


def second_sums(chain, plan, name, me, parts, f0, f1):
    n = len(parts.arrays)

    def sums(m):
        at0, at1 = (m.x, ALL, m.other_y), (m.other_x, ALL, m.y)

        def make(g, end, lanes):
            one = parts.terms(g, 0, at0) + [(n, (ALL, m.other_y, ALL, lanes))]
            two = parts.terms(g, 1, at1) + [(n + 1, (m.other_x, ALL, ALL, lanes))]
            shape = (parts.nz, *end)
            return [(0, (ALL, ALL, lanes), shape, one), (1, (ALL, ALL, lanes), shape, two)]

        return parts.sums(make)

    outs = [sds((parts.nz, parts.rows, parts.cols), BF16)] * 2
    arrays = [*parts.arrays, f0, f1]
    s0, s1 = add_up(chain, name + "2", me, arrays, outs, sums, far=parts.far)
    return plan.partner(name, s0, "y"), plan.partner(name, s1, "x")


def third_sums(chain, plan, name, me, parts, f0, f1, s0, s1, merged):
    n, rows = len(parts.arrays), parts.rows

    def sums(m):
        def make(g, end, lanes):
            out = []
            for k in range(parts.nz):
                z = m.z ^ k
                at = (m.x, z, m.y)
                one = parts.terms(g, 0, at) + [(n, (z, m.y, ALL, lanes)), (n + 2, (z, ALL, lanes))]
                two = parts.terms(g, 1, at) + [(n + 1, (m.x, z, ALL, lanes)), (n + 3, (z, ALL, lanes))]
                t, ti = z_target(k, merged)
                out.append((t, (*ti, slice(0, rows), lanes), end, one))
                out.append((t, (*ti, slice(rows, 2 * rows), lanes), end, two))
            return out

        return parts.sums(make)

    outs = z_outs((2 * rows, parts.cols), merged)
    arrays = [*parts.arrays, f0, f1, s0, s1]
    return add_up(chain, name + "3", me, arrays, outs, sums, far=parts.far)


def z_outs(shape, merged):
    if merged:
        return [sds(shape, F32), sds((2, *shape), BF16), sds(shape, BF16)]
    return [sds(shape, F32)] + [sds(shape, BF16)] * 3


def z_target(k, merged):
    if merged and k in (1, 3):
        return 1, (k // 2,)
    return k, ()


def along_z(chain, plan, name, me, two, came, at):
    (total,) = add_up(
        chain, name, me, [two, came], [two], lambda m: [(0, ALL, two.shape, [(0, ALL), (1, at)])]
    )
    return total


def squared(*values):
    return jnp.broadcast_to(sum(jnp.sum(v * v) for v in values), (1, 128))


def body(
    tokens,
    lengths,
    cotangent,
    qkv_weight,
    out_weight,
    fc_weight,
    proj_weight,
    vectors,
    qkv_first,
    out_first,
    fc_first,
    proj_first,
    vectors_first,
    qkv_second,
    out_second,
    fc_second,
    proj_second,
    vectors_second,
):
    dp, fsdp = lax.axis_size("dp"), lax.axis_size("fsdp")
    model = tokens.shape[1]
    wide, cut = qkv_weight.shape[1], out_weight.shape[1]
    hidden = fc_weight.shape[1] * fsdp
    per = vectors.shape[1]
    plan = Plan(dp, fsdp, model, hidden)
    rows, half, chalf, nz = plan.rows, plan.rows // 2, plan.cols // 2, plan.nz
    a_full = -(-(wide + per) // 128) * 128
    b_full = model + -(-cut // 128) * 128
    chain = Chain()
    at_dp, at_fsdp = lax.axis_index("dp"), lax.axis_index("fsdp")
    me = jnp.stack([at_dp // 2, at_dp % 2, at_fsdp // 2, at_fsdp % 2]).astype(jnp.int32)
    heads = model // HEAD_DIM
    third = [range(i, i + heads // 3) for i in range(0, heads, heads // 3)]

    def turned(value):
        return jnp.transpose(value)

    if plan.direct:
        weights = (qkv_weight, out_weight, fc_weight, turned(proj_weight), turned(vectors))
        a_own, b_own, c_own = pack(chain, plan, weights, a_full, b_full)
        a_came = plan.gather_z("gather_a", a_own)

        def place_a(m):
            return [(k, ALL, [(0, (m.z ^ k,))]) for k in range(nz)] + [
                (nz, ALL, [(1, ALL)])
            ]

        outs = [(nz, rows, a_full), b_own.shape]
        a_z, b_own = move(chain, "place_a1", me, [a_own, *a_came, b_own], outs, place_a)
        a_y, a_x = plan.partner("gather_a", a_z, "y"), plan.partner("gather_a", a_z, "x")
        a_xy = plan.opposite("gather_a", a_z)
        b_came = plan.gather_z("gather_b", b_own)

        def place_b(m):
            return [
                (k, pl.ds(h * half, half), [(h, (m.z ^ k,))]) for k in range(nz) for h in range(2)
            ] + [(nz, ALL, [(2, ALL)])]

        outs = [(nz, half, b_full), (nz, half, b_full), c_own.shape]
        b_z0, b_z1, c_own = move(chain, "place_b1", me, [b_own, *b_came, c_own], outs, place_b)
        b_r0, b_r1 = plan.partner("gather_b", b_z0, "y"), plan.partner("gather_b", b_z1, "x")
        a_zc = plan.partner("gather_a", a_z, "core")
        a_y, a_x, a_xy = gate(chain, "gate_a0", a_y, a_x, a_xy)
        a_in = [a_z, a_y, a_x, a_xy, a_zc]
        a_in = a_in + [plan.partner("gather_a", v, "core") for v in (a_y, a_x, a_xy)]
        c_near, c_far = plan.partner("gather_c", c_own, "z", 1), plan.partner("gather_c", c_own, "z", 2)
    else:

        def whole(shard):
            down = lax.all_gather(shard.astype(BF16), "dp", axis=0, tiled=True)
            return lax.all_gather(down, "fsdp", axis=0, tiled=False)

        def padded(parts, full):
            both = jnp.concatenate(parts, axis=1)
            both = whole(jnp.pad(both, ((0, 0), (0, full - both.shape[1]))))
            return both.reshape(fsdp, *plan.split(), full)

        a_in = [padded([qkv_weight, vectors], a_full)]
        b_in = [padded([fc_weight, out_weight], b_full)]
        c_all = jnp.transpose(whole(proj_weight), (0, 2, 1))
        c_all = c_all.reshape(model, fsdp, 2, hidden // fsdp // 2)
        c_in = [jnp.transpose(c_all, (1, 2, 0, 3))]

    qkv, act_one, a_can, t_can = front(chain, plan, me, tokens, a_in, wide)
    if plan.direct:
        (c_far,) = gate(chain, "gate_c0", c_far)
        c_came = [c_near, c_far, plan.partner("gather_c", c_far, "z", 1)]
        b_p0, b_p1, b_p = place_second(chain, "place_b2", plan, me, b_z0, b_r0, b_z1, b_r1)
        b_q0, b_q1 = plan.partner("gather_b", b_p0, "x"), plan.partner("gather_b", b_p1, "y")
        b_pc = plan.partner("gather_b", b_p, "core")
    parts = [attend(chain, qkv, lengths, model, third[0])]
    if plan.direct:

        def place_c(m):
            return [(k, (h,), [(h, (m.z ^ k,))]) for k in range(nz) for h in range(2)]

        outs = [(nz, chalf, plan.deep)] * 2
        c_z0, c_z1 = move(chain, "place_c1", me, [c_own, *c_came], outs, place_c)
        c_r0, c_r1 = plan.partner("gather_c", c_z0, "y"), plan.partner("gather_c", c_z1, "x")
    for group in third[1:]:
        parts.append(attend(chain, qkv, lengths, model, group))
    if plan.direct:
        chain.wait_for(b_pc)
        c_p0, c_p1, c_p = place_second(chain, "place_c2", plan, me, c_z0, c_r0, c_z1, c_r1)
        c_q0, c_q1 = plan.partner("gather_c", c_p0, "x"), plan.partner("gather_c", c_p1, "y")
        c_pc = plan.partner("gather_c", c_p, "core")
        b_q0, b_q1 = gate(chain, "gate_b", b_q0, b_q1)
        b_in = [b_p, b_q0, b_q1, b_pc] + [plan.partner("gather_b", v, "core") for v in (b_q0, b_q1)]
    logs = [p[1] for p in parts]
    resid_two, act_two, wout, mixed = join(
        chain, plan, me, cut, tokens, [p[0] for p in parts], b_in, t_can
    )
    if plan.direct:
        chain.wait_for(c_pc)
    gel, slope, b_can, g_b_proj, *g_c = mlp_up(
        chain, plan, me, act_two, cotangent, t_can, b_in, hidden
    )
    if plan.direct:
        c_q0, c_q1, away = gate(chain, "gate_c", c_q0, c_q1, g_c[1], far=1)
        c_in = [c_p, c_q0, c_q1, c_pc] + [plan.partner("gather_c", v, "core") for v in (c_q0, c_q1)]
        c_away = plan.partner("sum_c", away, "core")
    if plan.direct:
        c_parts = Parts([(g_c[0], [c_away])], far=1)
        c_f0, c_f1 = first_sums(chain, plan, "sum_c", me, c_parts)
    output, gpre, g_b_fc = mlp_down(
        chain, plan, me, cotangent, resid_two, gel, slope, t_can, c_in
    )

    gact, *g_b = mlp_back(chain, plan, me, act_two, gpre, b_can)
    if plan.direct:
        b_away = [plan.partner("sum_b", v, "core") for v in g_b[1:]]
    gresid, gmixed, inner, g_two, *g_o = join_back(
        chain, plan, me, gact, cotangent, resid_two, mixed, wout, t_can, b_full - model
    )
    if plan.direct:
        chain.wait_for(c_f0, c_f1)
        o_away = [plan.partner("sum_b", *gate(chain, "gate_o", g_o[1]), "core")]
        b_parts = Parts([(g_b[0], b_away), (g_o[0], o_away)])
    gparts = [attend_back(chain, qkv, gmixed, logs[0], inner, lengths, third[0])]
    if plan.direct:
        b_f0, b_f1 = first_sums(chain, plan, "sum_b", me, b_parts)

        def sums_cz(m):
            out = []
            for k in range(nz):
                z = m.z ^ k
                at = (0, m.x, z)
                terms = [(0, at), (1, at), (2, (z,))]
                t, ti = z_target(k, True)
                out.append((t, (*ti, slice(0, 2)), (2, chalf, plan.deep), terms))
                at = (1, ALL, z, m.y)
                terms = [(0, at), (1, at), (3, (ALL, z))]
                out.append((t, (*ti, slice(2, 4)), (2, chalf, plan.deep), terms))
            return out

        outs = z_outs((4, chalf, plan.deep), True)
        arrays = [g_c[0], c_away, c_f0, c_f1]
        c_u = add_up(chain, "sum_c2", me, arrays, outs, sums_cz, far=1)
        c_near = plan.partner("sum_c", c_u[1], "z", 1)
    for log, group in zip(logs[1:], third[1:]):
        gparts.append(attend_back(chain, qkv, gmixed, log, inner, lengths, group))
    input_grad, *g_a = back(
        chain, plan, wide, me, tokens, act_one, gparts, a_can, gresid, t_can, g_two, g_b_fc, g_b_proj
    )

    if plan.direct:
        c_two = along_z(chain, plan, "sum_c4", me, c_u[2], c_near, (1,))
        c_z = [c_u[0], c_near, plan.partner("sum_c", c_two, "z", 2)]
        b_s0, b_s1 = second_sums(chain, plan, "sum_b", me, b_parts, b_f0, b_f1)
        a_away = [plan.partner("sum_a", v, "core") for v in gate(chain, "gate_a", *g_a[1:])]
        a_parts = Parts([(g_a[0], a_away)])
        a_f0, a_f1 = first_sums(chain, plan, "sum_a", me, a_parts)
        chain.wait_for(c_z[2])
        b_u = third_sums(chain, plan, "sum_b", me, b_parts, b_f0, b_f1, b_s0, b_s1, True)
        b_near = plan.partner("sum_b", b_u[1], "z", 1)
        a_s0, a_s1 = second_sums(chain, plan, "sum_a", me, a_parts, a_f0, a_f1)
        z_lead = ((), (0,), ())

        def sums_c3(m):
            block = (chalf, plan.deep)
            one = [(i, (*lead, m.other_y)) for i, lead in enumerate(z_lead)]
            two = [(i, (*lead, 2 + m.other_x)) for i, lead in enumerate(z_lead)]
            return [(0, ALL, block, one), (1, ALL, block, two)]

        outs = [sds((chalf, plan.deep), BF16)] * 2
        s0, s1 = add_up(chain, "sum_c3", me, c_z, outs, sums_c3)
        c_l0, c_l1 = plan.partner("sum_c", s0, "y"), plan.partner("sum_c", s1, "x")
        b_two = along_z(chain, plan, "sum_b4", me, b_u[2], b_near, (1,))
        b_z = [b_u[0], b_near, plan.partner("sum_b", b_two, "z", 2)]
        a_u = third_sums(chain, plan, "sum_a", me, a_parts, a_f0, a_f1, a_s0, a_s1, False)
        a_z = [a_u[0]] + [plan.partner("sum_a", a_u[k], "z", k) for k in range(1, nz)]

        def sums_c(m):
            block = (chalf, plan.deep)
            one = [(i, (*lead, m.y)) for i, lead in enumerate(z_lead)] + [(3, ALL)]
            two = [(i, (*lead, 2 + m.x)) for i, lead in enumerate(z_lead)] + [(4, ALL)]
            return [(0, ALL, block, one), (1, ALL, block, two)]

        def end_c(done, outs):
            outs[0][0:chalf, :] = done[0]
            outs[0][chalf:, :] = done[1]
            outs[1][...] = squared(*done)

        d_proj, s_c = add_up(
            chain,
            "end_c",
            me,
            [*c_z, c_l0, c_l1],
            [sds((plan.cols, plan.deep), F32), sds((1, 128), F32)],
            sums_c,
            end_c,
        )
        def last_b(m):
            shape = b_z[0].shape
            return [(0, ALL, shape, [(i, lead or ALL) for i, lead in enumerate(z_lead)])]

        def last_a(m):
            return [(0, ALL, a_z[0].shape, [(i, ALL) for i in range(nz)])]

        def end_b(done, outs):
            total = done[0]
            fc, out = total[:, :model], total[:, model : model + cut]
            outs[0][...] = fc
            outs[1][...] = out
            outs[2][...] = squared(fc, out)

        shapes = [fc_weight.shape, out_weight.shape, (1, 128)]
        d_fc, d_out, s_b = add_up(
            chain, "end_b", me, b_z, [sds(s, F32) for s in shapes], last_b, end_b
        )

        def end_a(done, outs):
            total = done[0]
            start = wide // 128 * 128
            vec = jnp.transpose(total[:, start:])[wide - start : wide - start + per]
            qkv = total[:, :wide]
            outs[0][...] = qkv
            outs[1][...] = vec
            outs[2][...] = squared(qkv, vec)

        shapes = [qkv_weight.shape, (per, rows), (1, 128)]
        d_qkv, d_vec, s_a = add_up(
            chain, "end_a", me, a_z, [sds(s, F32) for s in shapes], last_a, end_a
        )
        squares = s_a + s_b + s_c
    else:

        def shared(value):
            mine = lax.psum_scatter(value, "fsdp", scatter_dimension=0, tiled=False)
            return lax.psum_scatter(mine, "dp", scatter_dimension=0, tiled=True).astype(F32)

        d_a = shared(g_a[0].reshape(fsdp, model, a_full))
        d_qkv, d_vec = d_a[:, :wide], turned(d_a[:, wide : wide + per])
        d_out = shared(jnp.transpose(g_o[0].reshape(model, fsdp, cut), (1, 0, 2)))
        d_fc = shared(g_b[0].reshape(fsdp, model, model))
        d_c = jnp.transpose(g_c[0], (2, 0, 1, 3)).reshape(fsdp, plan.cols, hidden)
        d_proj = turned(shared(jnp.transpose(d_c, (0, 2, 1))))
        total = sum(jnp.sum(d * d) for d in (d_qkv, d_out, d_fc, d_proj, d_vec))
        squares = jnp.full((1, 128), total)

    sent = jnp.broadcast_to(squares[None], (dp * fsdp, 1, 128))
    with jax.named_scope("norm"):
        norms = lax.all_to_all(sent, ("dp", "fsdp"), 0, 0, tiled=True).reshape(dp * fsdp, 128)
    norm, *new = update(
        chain,
        norms,
        (qkv_weight, out_weight, fc_weight, turned(proj_weight), turned(vectors)),
        (d_qkv, d_out, d_fc, d_proj, d_vec),
        (qkv_first, out_first, fc_first, turned(proj_first), turned(vectors_first)),
        (qkv_second, out_second, fc_second, turned(proj_second), turned(vectors_second)),
    )
    new = [turned(v) if i % 5 in (3, 4) else v for i, v in enumerate(new)]
    return (output, input_grad, norm[0, 0], *new)


def solution(mesh):
    tokens = P(("dp", "fsdp"), None)
    table = P("dp", "fsdp")
    return jax.shard_map(
        body,
        mesh=mesh,
        in_specs=(tokens, P(("dp", "fsdp")), tokens) + (table,) * 15,
        out_specs=(tokens, tokens, P()) + (table,) * 15,
        check_vma=False,
    )
```

```python
import functools

import jax
import jax.numpy as jnp
from jax import lax
from jax.experimental import pallas as pl
from jax.experimental.pallas import tpu as pltpu
from jax.sharding import PartitionSpec as P

HEAD_DIM = 64
STEP = 10

beta_one = 0.9
beta_two = 0.95
clip_limit = 1.0
rate_matrix = 0.1
rate_vector = 1.0
decay_matrix = 0.1
gelu_coeff = 0.7978845608028654
cubic_coeff = 0.044715
neg_large = -1e30
VEC_ROWS = 16

F32 = jnp.float32
BF16 = jnp.bfloat16
VMEM = pl.BlockSpec(memory_space=pltpu.VMEM)
HELD = pl.BlockSpec(memory_space=pltpu.VMEM)
ANY = pl.BlockSpec(memory_space=pl.ANY)
HBM = pl.BlockSpec(memory_space=pltpu.HBM)
SMEM = pl.BlockSpec(memory_space=pltpu.SMEM)
ALL = slice(None)


def dot_nn(a, b):
    return lax.dot_general(a, b, (((1,), (0,)), ((), ())), preferred_element_type=F32)


def dot_nt(a, b):
    return lax.dot_general(a, b, (((1,), (1,)), ((), ())), preferred_element_type=F32)


def dot_tn(a, b):
    return lax.dot_general(a, b, (((0,), (0,)), ((), ())), preferred_element_type=F32)


def sds(shape, dtype):
    return jax.ShapeDtypeStruct(shape, dtype)


class Chain:
    def __init__(self):
        self.waits = []

    def wait_for(self, *arrays):
        self.waits += arrays

    def call(self, name, body, ins, in_specs, outs, out_specs, scratch, limit, aliases=None):
        several = isinstance(outs, (tuple, list))
        if not several:
            outs, out_specs = (outs,), (out_specs,)
        n_in, extra, n_out = len(ins), len(self.waits), len(outs)
        pins = ((HELD, pltpu.VMEM), (HBM, pltpu.HBM))

        def run(*refs):
            given, refs = refs[:n_in], refs[n_in + extra :]
            refs[n_out][...] = jnp.zeros(refs[n_out].shape, F32)
            body(*given, *refs[:n_out], *refs[n_out + 1 :])

        placed, made = [], []
        for v, spec in zip(ins, in_specs):
            for pin, space in pins:
                if spec is pin:
                    v = pltpu.with_memory_space_constraint(v, space)
            placed.append(v)
        for o, spec in zip(outs, out_specs):
            for pin, space in pins:
                if spec is pin:
                    o = space(o.shape, o.dtype)
            made.append(o)
        results = pl.pallas_call(
            run,
            name=name,
            input_output_aliases=aliases or {},
            out_shape=(*made, pltpu.VMEM((8, 128), F32)),
            in_specs=[*in_specs, *[ANY] * extra],
            out_specs=(*out_specs, HELD),
            scratch_shapes=scratch,
            compiler_params=pltpu.CompilerParams(vmem_limit_bytes=limit << 20),
        )(*placed, *self.waits)
        *results, token = results
        self.waits = [pltpu.with_memory_space_constraint(token, pltpu.VMEM)]
        return results if several else results[0]


class Plan:
    def __init__(self, dp, fsdp, model, hidden):
        self.dp, self.fsdp = dp, fsdp
        self.nz, self.nx = dp // 2, fsdp // 2
        self.rows = model // dp
        self.cols = model // fsdp
        self.deep = hidden // dp
        self.direct = (
            dp == 2 * fsdp
            and fsdp % 2 == 0
            and self.rows % 32 == 0
            and self.cols % 32 == 0
            and self.deep % 128 == 0
            and hidden == fsdp * model
            and dp == 8
        )

    def partner(self, name, value, stage, k=1):
        axis, step = {"x": ("fsdp", 2), "y": ("dp", 1), "z": ("dp", 2), "core": ("fsdp", 1)}[stage]
        n = self.dp if axis == "dp" else self.fsdp
        with jax.named_scope(f"{name}_{stage}"):
            return lax.ppermute(value, axis, [(i, i ^ (step * k)) for i in range(n)])

    def opposite(self, name, value):
        n = self.fsdp
        pairs = [(i * n + j, (i ^ 1) * n + (j ^ 2)) for i in range(self.dp) for j in range(n)]
        with jax.named_scope(f"{name}_xy"):
            return lax.ppermute(value, ("dp", "fsdp"), pairs)

    def gather_z(self, name, value):
        near, far = self.partner(name, value, "z", 1), self.partner(name, value, "z", 2)
        return [near, far, self.partner(name, far, "z", 1)]

    def split(self):
        return (self.nz, 2, 2, self.rows // 2) if self.direct else (1, 1, 1, self.rows * self.dp)


class Me:
    def __init__(self, ref):
        self.z, self.y, self.x, self.core = ref[0], ref[1], ref[2], ref[3]
        self.other_y, self.other_x = 1 - self.y, 1 - self.x

    def fsdp(self, x, away):
        return 2 * x + (self.core ^ away)


def move(chain, name, me, arrays, outs, copies):
    n = len(arrays)

    def body(me_ref, *refs):
        for s, si, targets in copies(Me(me_ref)):
            value = refs[s][si]
            for t, ti in targets:
                refs[n + t][ti] = value

    return chain.call(
        name,
        body,
        (me, *arrays),
        [SMEM] + [VMEM] * n,
        tuple(sds(s, BF16) for s in outs),
        (HELD,) * len(outs),
        [],
        6,
    )


def gate(chain, name, *arrays, far=0):
    specs = [ANY] * (len(arrays) - far) + [HBM] * far
    return chain.call(
        name,
        lambda *refs: None,
        arrays,
        specs,
        tuple(sds(v.shape, v.dtype) for v in arrays),
        tuple(specs),
        [],
        1,
        {i: i for i in range(len(arrays))},
    )


def add_up(chain, name, me, arrays, outs, sums, after=None, far=0):
    n, m = len(arrays), len(outs)
    still = sums(Me([0, 0, 0, 0]))
    loaded = [shape for _, _, shape, parts in still for s, _ in parts if s < far]

    def body(me_ref, *refs):
        ins, outs_, refs = refs[:n], refs[n : n + m], refs[n + m :]
        held, sem = refs[: len(loaded)], refs[len(loaded) :]
        todo, i = [], 0
        for t, ti, shape, parts in sums(Me(me_ref)):
            group = []
            for s, si in parts:
                copy = None
                if s < far:
                    copy = pltpu.make_async_copy(ins[s].at[si], held[i], sem[0].at[i])
                    copy.start()
                    i += 1
                group.append((copy, s, si, i - 1))
            todo.append((t, ti, group))
        done = []
        for t, ti, group in todo:
            total = None
            for copy, s, si, k in reversed(group):
                if copy is not None:
                    copy.wait()
                v = (ins[s][si] if copy is None else held[k][...]).astype(F32)
                total = v if total is None else total + v
            if after is None:
                outs_[t][ti] = total.astype(outs_[t].dtype)
            else:
                done.append(total)
        if after is not None:
            after(done, outs_)

    return chain.call(
        name,
        body,
        (me, *arrays),
        [SMEM] + [HBM if i < far else VMEM for i in range(n)],
        tuple(outs),
        (HELD if after is None else VMEM,) * m,
        [pltpu.VMEM(shape, BF16) for shape in loaded]
        + ([pltpu.SemaphoreType.DMA((len(loaded),))] if loaded else []),
        8,
    )


def pack_body(ins, outs, held, sem):
    todo = [pltpu.make_async_copy(i, h, sem.at[k]) for k, (i, h) in enumerate(zip(ins, held))]
    for c in todo:
        c.start()
    for c in todo:
        c.wait()
    qkv, out, fc, proj, vec = (h[...] for h in held)
    a, b, c = outs
    wide, model = qkv.shape[1], fc.shape[1]
    columns = jnp.transpose(vec)
    start = wide // 128 * 128
    a[:, start:] = jnp.zeros((a.shape[0], a.shape[1] - start), BF16)
    a[:, 0:wide] = qkv.astype(BF16)
    a[:, wide : wide + columns.shape[1]] = columns.astype(BF16)
    b[:, model:] = jnp.zeros((b.shape[0], b.shape[1] - model), BF16)
    b[:, 0:model] = fc.astype(BF16)
    b[:, model : model + out.shape[1]] = out.astype(BF16)
    c[...] = proj.astype(BF16).reshape(c.shape)


def pack(chain, plan, weights, a_full, b_full):
    count = len(weights)

    def run(*refs):
        pack_body(refs[:count], refs[count : count + 3], refs[count + 3 : -1], refs[-1])

    return chain.call(
        "pack",
        run,
        weights,
        [HBM] * count,
        (
            sds((plan.rows, a_full), BF16),
            sds((plan.rows, b_full), BF16),
            sds((2, plan.cols // 2, plan.deep), BF16),
        ),
        (VMEM,) * 3,
        [pltpu.VMEM(w.shape, F32) for w in weights] + [pltpu.SemaphoreType.DMA((count,))],
        6,
    )


def normed(values):
    mean = jnp.mean(values, axis=-1, keepdims=True)
    centred = values - mean
    spread = jnp.mean(centred * centred, axis=-1, keepdims=True)
    inverse = lax.rsqrt(spread + 1e-05)
    return centred * inverse, inverse


def norm_back(grad_hidden, n, inverse, gain):
    g = grad_hidden * gain
    mean_plain = jnp.mean(g, axis=-1, keepdims=True)
    mean_cross = jnp.mean(g * n, axis=-1, keepdims=True)
    return inverse * (g - mean_plain - n * mean_cross)


class Table:
    def __init__(self, fsdp):
        self.per = 12 // fsdp

    def row(self, k):
        return (k // self.per) * VEC_ROWS + k % self.per

    def get(self, ref, k):
        r = self.row(k)
        return ref[r : r + 1, :]


def spread_matrix(rows, model, d):
    r = lax.broadcasted_iota(jnp.int32, (128, model), 0)
    c = lax.broadcasted_iota(jnp.int32, (128, model), 1)
    return ((c == r + d * rows) & (r < rows)).astype(BF16)


def halves(ins, away):
    n = len(ins) // 2
    part = ins[n * away : n * away + n]
    own = (part[0].at[0], part[0].at[1]) if n == 3 else part[:2]
    return (*own, *part[-2:])


def table_loads(plan, me, ins):
    for away in range(2):
        p0, p1, r0, r1 = halves(ins, away)
        for y in range(2):
            for x, ref in ((me.x, p0), (me.other_x, r0)):
                yield ref, (y,), me.fsdp(x, away), (ALL, y), 0
        for y, ref in ((me.y, p1), (me.other_y, r1)):
            for x in range(plan.nx):
                yield ref, (x,), me.fsdp(x, away), (ALL, y), 1


def front_body(plan, wide, n_in, me_ref, tokens, *refs):
    ins = refs[:n_in]
    qkv, act, a_out, t_out, n_out, inv_out = refs[n_in : n_in + 6]
    a_v, flat, sem, out_sem = refs[n_in + 6 :]
    fsdp = plan.fsdp
    full = a_v.shape[-1]
    model = tokens.shape[1]
    table = Table(fsdp)
    if plan.direct:
        me = Me(me_ref)
        for i, ref in enumerate(ins):
            away, x, y = i // 4, i // 2 % 2, i % 2
            f = me.fsdp(me.x ^ x, away)
            pltpu.make_async_copy(ref, a_v.at[f, :, me.y ^ y], sem.at[f]).start()
    else:
        for f in range(fsdp):
            pltpu.make_async_copy(ins[0].at[f], a_v.at[f], sem.at[f]).start()
    n, inverse = normed(tokens[...].astype(F32))
    n_out[...] = n
    inv_out[...] = jnp.broadcast_to(inverse, inv_out.shape)
    start = wide // 128 * 128
    for f in range(fsdp):
        pltpu.make_async_copy(a_v.at[f], a_v.at[f], sem.at[f]).wait()
        block = a_v[f].reshape(model, full)
        flat[:, f * wide : (f + 1) * wide] = block[:, :wide]
        turned = jnp.transpose(block[:, start:].astype(F32))
        t_out[f * VEC_ROWS : f * VEC_ROWS + table.per, :] = turned[
            wide - start : wide - start + table.per
        ]
    copy = pltpu.make_async_copy(flat, a_out, out_sem)
    copy.start()
    act[...] = (n * table.get(t_out, 0) + table.get(t_out, 1)).astype(BF16)
    for which in range(3):
        r = dot_nn(act[...], flat[:, which * model : (which + 1) * model])
        if which != 1:
            r = r + table.get(t_out, 4 + which // 2)
        qkv[which] = r.astype(BF16)
    copy.wait()


def front(chain, plan, me, tokens, pieces, wide):
    t, model = tokens.shape
    fsdp = plan.fsdp
    full = pieces[0].shape[-1]
    lead = (fsdp, plan.nz, 2, plan.rows, full) if plan.direct else pieces[0].shape
    return chain.call(
        "front",
        functools.partial(front_body, plan, wide, len(pieces)),
        (me, tokens, *pieces),
        [SMEM, VMEM] + [ANY] * len(pieces),
        (
            sds((3, t, model), BF16),
            sds((t, model), BF16),
            sds((model, 3 * model), BF16),
            sds((fsdp * VEC_ROWS, model), F32),
            sds((t, model), F32),
            sds((t, 128), F32),
        ),
        (HELD, HELD, HBM, HELD, HELD, HELD),
        [
            pltpu.VMEM(lead, BF16),
            pltpu.VMEM((model, 3 * model), BF16),
            pltpu.SemaphoreType.DMA((fsdp,)),
            pltpu.SemaphoreType.DMA,
        ],
        16,
    )


def masks(length, lo, size, keys):
    q = lax.broadcasted_iota(jnp.int32, (size, 1), 0) + lo
    limit = jnp.minimum(q, length - 1)
    k = lax.broadcasted_iota(jnp.int32, (size, keys), 1)
    return k <= limit


QBLOCK = 256


def attend_body(heads, length_ref, qkv, mixed, logs):
    t = mixed.shape[0]
    length = length_ref[0]
    scale = HEAD_DIM**-0.5

    def part(h, which):
        return qkv[which, :, h * HEAD_DIM : (h + 1) * HEAD_DIM]

    for i, h in enumerate(heads):
        q = part(h, 0) * jnp.asarray(scale, BF16)
        k, v = part(h, 1), part(h, 2)
        for lo in range(0, t, QBLOCK):
            n = lo + QBLOCK
            s = dot_nt(q[lo:n], k[:n])
            s = jnp.where(masks(length, lo, QBLOCK, n), s, neg_large)
            top = jnp.max(s, axis=-1, keepdims=True)
            e = jnp.exp(s - top)
            total = jnp.sum(e, axis=-1, keepdims=True)
            p = (e * (1.0 / total)).astype(BF16)
            o = dot_nn(p, v[:n])
            mixed[lo:n, i * HEAD_DIM : (i + 1) * HEAD_DIM] = o.astype(BF16)
            logs[lo:n, i : i + 1] = top + jnp.log(total)


def attend(chain, qkv, length, heads):
    t = qkv.shape[1]
    return chain.call(
        "attend",
        functools.partial(attend_body, heads),
        (length, qkv),
        [SMEM, HELD],
        (sds((t, len(heads) * HEAD_DIM), BF16), sds((t, 128), F32)),
        (HELD, HELD),
        [],
        6,
    )


def join_body(plan, cut, n_in, n_mixed, me_ref, tokens, t_in, *refs):
    ins, refs = refs[:n_in], refs[n_in:]
    parts, (resid, act, wout, mixed, n_out, inv_out, o_v, sem) = refs[:n_mixed], refs[n_mixed:]
    model = tokens.shape[1]
    fsdp = plan.fsdp
    table = Table(fsdp)
    lanes = pl.ds(model, o_v.shape[-1])
    if plan.direct:
        for ref, si, f, ti, h in table_loads(plan, Me(me_ref), ins):
            src = ref.at[(*si, ALL, ALL, lanes)]
            pltpu.make_async_copy(src, o_v.at[(f, *ti, h)], sem).start()
    else:
        for f in range(fsdp):
            src = ins[0].at[(f, ALL, ALL, ALL, ALL, lanes)]
            pltpu.make_async_copy(src, o_v.at[f], sem).start()
    at = 0
    for p in parts:
        mixed[:, at : at + p.shape[1]] = p[...]
        at += p.shape[1]
    pltpu.make_async_copy(o_v, o_v, sem).wait()
    for f in range(fsdp):
        wout[:, f * cut : (f + 1) * cut] = o_v[f].reshape(model, o_v.shape[-1])[:, :cut]
    r = tokens[...].astype(F32) + dot_nn(mixed[...], wout[...]) + table.get(t_in, 6)
    resid[...] = r
    n, inverse = normed(r)
    n_out[...] = n
    inv_out[...] = jnp.broadcast_to(inverse, inv_out.shape)
    act[...] = (n * table.get(t_in, 2) + table.get(t_in, 3)).astype(BF16)


def join(chain, plan, me, cut, tokens, parts, pieces, t_can):
    t, model = tokens.shape
    spare = pieces[0].shape[-1] - model
    return chain.call(
        "join",
        functools.partial(join_body, plan, cut, len(pieces), len(parts)),
        (me, tokens, t_can, *pieces, *parts),
        [SMEM, VMEM, HELD] + [ANY] * len(pieces) + [HELD] * len(parts),
        (
            sds((t, model), F32),
            sds((t, model), BF16),
            sds((model, model), BF16),
            sds((t, model), BF16),
            sds((t, model), F32),
            sds((t, 128), F32),
        ),
        (HELD,) * 6,
        [pltpu.VMEM((plan.fsdp, *plan.split(), spare), BF16), pltpu.SemaphoreType.DMA],
        10,
    )


def gelu_and_slope(pre):
    square = pre * pre
    th = jnp.tanh(pre * (gelu_coeff + (gelu_coeff * cubic_coeff) * square))
    plus = 0.5 * th + 0.5
    bend = 0.5 * gelu_coeff + (1.5 * gelu_coeff * cubic_coeff) * square
    return (pre * plus).astype(BF16), plus + pre * (1.0 - th * th) * bend


def mlp_up_body(plan, n_in, n_out, me_ref, act, cot, t_in, *refs):
    ins, refs = refs[:n_in], refs[n_in:]
    gel_out, slope_out, b_v, g_b_proj = refs[:4]
    gouts, refs = refs[4 : 4 + n_out], refs[4 + n_out :]
    gp_v, sem = refs
    fsdp, half = plan.fsdp, plan.cols // 2
    t, model = act.shape
    deep = gp_v.shape[-1]
    per = Table(fsdp).per
    me = Me(me_ref)
    order = []
    for k in range(fsdp):
        if plan.direct:
            away, x = k // 2, me.x if k % 2 == 0 else me.other_x
            p0, p1, r0, r1 = halves(ins, away)
            f = me.fsdp(x, away)
            own = p0 if k % 2 == 0 else r0
            loads = [(own.at[y], y, 0) for y in range(2)]
            loads += [(p1.at[x], me.y, 1), (r1.at[x], me.other_y, 1)]
            for ref, y, h in loads:
                src = ref.at[:, :, pl.ds(0, model)]
                pltpu.make_async_copy(src, b_v.at[f, :, y, h], sem.at[k]).start()
        else:
            f = k
            src = ins[0].at[(f, ALL, ALL, ALL, ALL, pl.ds(0, model))]
            pltpu.make_async_copy(src, b_v.at[f], sem.at[k]).start()
        order.append(f)
    g_b_proj[...] = jnp.sum(cot[...].astype(F32), axis=0, keepdims=True)

    def up(k, lo, hi):
        row = 8 + order[k]
        bias = t_in[pl.ds(row // per * VEC_ROWS + row % per, 1), :]
        return dot_nn(act[lo:hi], b_v[order[k]].reshape(model, model)) + bias

    step = t // 2
    for k in range(fsdp):
        pltpu.make_async_copy(b_v.at[order[k]], b_v.at[order[k]], sem.at[k]).wait()
        lanes = pl.ds(pl.multiple_of(order[k] * model, model), model)
        for lo in range(0, t, step):
            gel, slope = gelu_and_slope(up(k, lo, lo + step))
            gel_out[lo : lo + step, lanes] = gel
            slope_out[lo : lo + step, lanes] = slope
        grad = dot_tn(cot[...], gel_out[:, lanes]).astype(BF16)
        if not plan.direct:
            gouts[0][k, 0], gouts[0][k, 1] = grad[:, :deep], grad[:, deep:]
            continue
        gp_v[0], gp_v[1] = grad[:, :deep], grad[:, deep:]
        for away in range(2):
            for x in range(plan.nx):
                for h in range(2):
                    row = me.fsdp(x, away) * plan.cols + h * half
                    part = gp_v[:, pl.ds(pl.multiple_of(row, 16), half), :]
                    gouts[away][h, x, pl.ds(order[k], 1)] = part[None]


def mlp_up(chain, plan, me, act, cot, t_can, pieces, hidden):
    t, model = act.shape
    fsdp = plan.fsdp
    per = hidden // fsdp // 2
    if plan.direct:
        grads = [sds((2, plan.nx, plan.nz, 2, plan.cols // 2, plan.deep), BF16)] * 2
    else:
        grads = [sds((fsdp, 2, model, per), BF16)]
    lead = (fsdp, *plan.split(), model)
    return chain.call(
        "mlp_up",
        functools.partial(mlp_up_body, plan, len(pieces), len(grads)),
        (me, act, cot, t_can, *pieces),
        [SMEM, HELD, VMEM, HELD] + [ANY] * len(pieces),
        (
            sds((t, hidden), BF16),
            sds((t, hidden), F32),
            sds(lead, BF16),
            sds((1, model), F32),
            *grads,
        ),
        (HELD,) * (4 + len(grads)),
        [
            pltpu.VMEM((2, model, per), BF16),
            pltpu.SemaphoreType.DMA((fsdp,)),
        ],
        18,
    )


def mlp_down_body(plan, n_in, me_ref, cot, resid, gel, slope, t_in, *refs):
    ins, refs = refs[:n_in], refs[n_in:]
    output, gpre, g_b_fc, c_v, acc = refs
    fsdp, half = plan.fsdp, plan.cols // 2
    model = cot.shape[1]
    table = Table(fsdp)
    if plan.direct:
        for ref, si, f, ti, h in table_loads(plan, Me(me_ref), ins):
            rows = pl.ds(pl.multiple_of(f * plan.cols + h * half, 16), half)
            c_v[(*ti, rows)] = ref[si]
    else:
        c_v[...] = ins[0][...]
    acc[...] = resid[...] + table.get(t_in, 7)
    for j in range(fsdp):
        lanes = slice(j * model, (j + 1) * model)
        down = jnp.concatenate([c_v[j, 0], c_v[j, 1]], axis=1)
        low = (dot_nn(cot[...], down) * slope[:, lanes]).astype(BF16)
        gpre[:, lanes] = low
        g_b_fc[j : j + 1, :] = jnp.sum(low.astype(F32), axis=0, keepdims=True)
        acc[...] += dot_nt(gel[:, lanes], down)
    output[...] = acc[...].astype(BF16)


def mlp_down(chain, plan, me, cot, resid, gel, slope, t_can, pieces):
    t, model = cot.shape
    fsdp, hidden = plan.fsdp, gel.shape[1]
    return chain.call(
        "mlp_down",
        functools.partial(mlp_down_body, plan, len(pieces)),
        (me, cot, resid, gel, slope, t_can, *pieces),
        [SMEM, VMEM, HELD, HELD, HELD, HELD] + [VMEM] * len(pieces),
        (sds((t, model), BF16), sds((t, hidden), BF16), sds((fsdp, model), F32)),
        (VMEM, HELD, HELD),
        [
            pltpu.VMEM((fsdp, 2, model, hidden // fsdp // 2), BF16),
            pltpu.VMEM((t, model), F32),
        ],
        12,
    )


def mlp_back_body(plan, n_out, me_ref, act, gpre, b_in, *refs):
    gact = refs[0]
    gouts = refs[1 : 1 + n_out]
    model = act.shape[1]
    me = Me(me_ref)
    first = True
    order = [
        (x, away, me.fsdp(x, away) if plan.direct else 2 * x + away)
        for away in range(2)
        for x in range(plan.nx)
    ]
    for x, away, f in order:
        part = gpre[:, pl.ds(pl.multiple_of(f * model, model), model)]
        grad = dot_tn(act[...], part).astype(BF16).reshape(b_in.shape[1:])
        if not plan.direct:
            gouts[0][f] = grad
        elif away:
            gouts[1][x], gouts[2][x] = grad[:, :, 0], grad[:, :, 1]
        else:
            gouts[0][0, x], gouts[0][1, x] = grad[:, :, 0], grad[:, :, 1]
        back = dot_nt(part, b_in[f].reshape(model, model))
        if first:
            gact[...] = back
        else:
            gact[...] += back
        first = False


def mlp_back(chain, plan, me, act, gpre, b_can):
    t, model = act.shape
    fsdp = plan.fsdp
    lead = (fsdp, *plan.split(), model)
    if plan.direct:
        one = (plan.nx, plan.nz, 2, plan.rows // 2, model)
        grads = [sds((2, *one), BF16), sds(one, BF16), sds(one, BF16)]
    else:
        grads = [sds(lead, BF16)]
    return chain.call(
        "mlp_back",
        functools.partial(mlp_back_body, plan, len(grads)),
        (me, act, gpre, b_can),
        [SMEM, HELD, HELD, HELD],
        (sds((t, model), F32), *grads),
        (HELD,) + (HELD,) * len(grads),
        [],
        10,
    )


def join_back_body(plan, me_ref, gact, cot, normal, inverse_in, mixed, wout, t_in, *refs):
    gresid, gmixed, inner, g_vec, *gouts = refs[:-1]
    o_v = refs[-1]
    model = cot.shape[1]
    table = Table(plan.fsdp)
    n, inverse = normal[...], inverse_in[:, 0:1]
    e = gact[...]
    g_vec[...] = jnp.zeros(g_vec.shape, F32)
    g_vec[0:1, :] = jnp.sum(e * n, axis=0, keepdims=True)
    g_vec[1:2, :] = jnp.sum(e, axis=0, keepdims=True)
    r = cot[...].astype(F32) + norm_back(e, n, inverse, table.get(t_in, 2))
    gresid[...] = r
    branch = r.astype(BF16)
    g_vec[2:3, :] = jnp.sum(branch.astype(F32), axis=0, keepdims=True)
    grad = dot_tn(mixed[...], branch).astype(BF16)
    if plan.direct:
        me = Me(me_ref)
        cut = plan.cols
        for f in range(plan.fsdp):
            o_v[f, :, 0:cut] = grad[:, f * cut : (f + 1) * cut]
            o_v[f, :, cut:] = jnp.zeros((model, o_v.shape[-1] - cut), BF16)
        for away in range(2):
            for x in range(plan.nx):
                part = o_v[me.fsdp(x, away)].reshape(*plan.split(), o_v.shape[-1])
                gouts[away][0, x], gouts[away][1, x] = part[:, :, 0], part[:, :, 1]
    else:
        gouts[0][...] = grad
    low = dot_nt(branch, wout[...]).astype(BF16)
    gmixed[...] = low
    product = low.astype(F32) * mixed[...].astype(F32)
    high = product.astype(BF16)
    rest = (product - high.astype(F32)).astype(BF16)
    head = lax.broadcasted_iota(jnp.int32, (model, 128), 0) // HEAD_DIM
    ones = (head == lax.broadcasted_iota(jnp.int32, (model, 128), 1)).astype(BF16)
    inner[...] = dot_nn(high, ones) + dot_nn(rest, ones)


def join_back(chain, plan, me, gact, cot, normal, inverse, mixed, wout, t_can, spare):
    t, model = cot.shape
    ins = [me, gact, cot, normal, inverse, mixed, wout, t_can]
    if plan.direct:
        grads = [sds((2, plan.nx, plan.nz, 2, plan.rows // 2, spare), BF16)] * 2
        grad_specs = [HELD] * 2
    else:
        grads, grad_specs = [sds((model, model), BF16)], [VMEM]
    return chain.call(
        "join_back",
        functools.partial(join_back_body, plan),
        ins,
        [SMEM, HELD, VMEM] + [HELD] * 5,
        (
            sds((t, model), F32),
            sds((t, model), BF16),
            sds((t, 128), F32),
            sds((8, model), F32),
            *grads,
        ),
        (HELD, HELD, HELD, HELD, *grad_specs),
        [pltpu.VMEM((plan.fsdp, model, spare), BF16)],
        14,
    )


def attend_back_body(heads, length_ref, qkv, gmixed, logs, inner, out):
    t = gmixed.shape[0]
    length = length_ref[0]
    scale = HEAD_DIM**-0.5

    def part(h, which):
        return qkv[which, :, h * HEAD_DIM : (h + 1) * HEAD_DIM]

    for i, h in enumerate(heads):
        lanes = slice(i * HEAD_DIM, (i + 1) * HEAD_DIM)
        q = part(h, 0)
        small = q * jnp.asarray(scale, BF16)
        k, v = part(h, 1), part(h, 2)
        go = gmixed[:, h * HEAD_DIM : (h + 1) * HEAD_DIM]
        gk, gv = [], []
        for lo in range(0, t, QBLOCK):
            n = lo + QBLOCK
            s = dot_nt(small[lo:n], k[:n])
            s = jnp.where(masks(length, lo, QBLOCK, n), s, neg_large)
            p = jnp.exp(s - logs[lo:n, i : i + 1])
            gp = dot_nt(go[lo:n], v[:n])
            ds = (p * (gp - inner[lo:n, h : h + 1])).astype(BF16)
            out[0, lo:n, lanes] = (dot_nn(ds, k[:n]) * scale).astype(BF16)
            gv.append(dot_tn(p.astype(BF16), go[lo:n]))
            gk.append(dot_tn(ds, small[lo:n]))
        for b in range(t // QBLOCK):
            rows = slice(b * QBLOCK, (b + 1) * QBLOCK)
            out[1, rows, lanes] = sum(x[rows] for x in gk[b:]).astype(BF16)
            out[2, rows, lanes] = sum(x[rows] for x in gv[b:]).astype(BF16)


def attend_back(chain, qkv, gmixed, logs, inner, length, heads):
    t = qkv.shape[1]
    return chain.call(
        "attend_back",
        functools.partial(attend_back_body, heads),
        (length, qkv, gmixed, logs, inner),
        [SMEM, HELD, HELD, HELD, HELD],
        sds((3, t, len(heads) * HEAD_DIM), BF16),
        HELD,
        [],
        8,
    )


def whole_qkv(parts, flat, blocks):
    wide = blocks.shape[2]
    model = flat.shape[1] // 3
    at = 0
    for p in parts:
        size = p.shape[2]
        for which in range(3):
            lo = which * model + at
            flat[:, lo : lo + size] = p[which]
        at += size
    for f in range(blocks.shape[0]):
        blocks[f] = flat[:, f * wide : (f + 1) * wide]


def back_body(plan, wide, n_parts, n_out, me_ref, normal, inverse_in, act, a_in, gresid, t_in, g_two, g_b_fc, g_b_proj, *refs):
    parts, refs = refs[:n_parts], refs[n_parts:]
    input_grad, gouts, refs = refs[0], refs[1 : 1 + n_out], refs[1 + n_out :]
    flat, gq_v, tab, a_v, in_sem = refs
    late = pltpu.make_async_copy(a_in, a_v, in_sem)
    late.start()
    fsdp = plan.fsdp
    t, model = normal.shape
    table = Table(fsdp)
    spare = tab.shape[0] // fsdp
    whole_qkv(parts, flat, gq_v)
    me = Me(me_ref)

    def each():
        for away in range(2):
            for x in range(plan.nx):
                if plan.direct:
                    ends = [gouts[1 + h].at[x] if away else gouts[0].at[h, x] for h in range(2)]
                    yield me.fsdp(x, away), ends
                else:
                    yield 2 * x + away, [gouts[0].at[2 * x + away, :, :, h] for h in range(1)]

    for f, ends in each():
        grad = dot_tn(act[...], gq_v[f]).astype(BF16).reshape(*plan.split(), wide)
        for h, end in enumerate(ends):
            end[:, :, :, 0:wide] = grad[:, :, h]
    late.wait()
    back = dot_nt(flat[...], a_v[...])
    sums = dot_nn(jnp.ones((8, t), BF16), flat[...])
    n, inverse = normal[...], inverse_in[:, 0:1]
    tab[...] = jnp.zeros(tab.shape, F32)

    def put(k, value):
        r = (k // table.per) * spare + k % table.per
        tab[r : r + 1, :] = value

    put(0, jnp.sum(back * n, axis=0, keepdims=True))
    put(1, jnp.sum(back, axis=0, keepdims=True))
    put(2, g_two[0:1, :])
    put(3, g_two[1:2, :])
    put(4, sums[0:1, 0:model])
    put(5, sums[0:1, 2 * model :])
    put(6, g_two[2:3, :])
    put(7, g_b_proj[...])
    for j in range(fsdp):
        put(8 + j, g_b_fc[j : j + 1, :])
    for f, ends in each():
        rows = pl.ds(pl.multiple_of(f * spare, 8), spare)
        columns = jnp.transpose(tab[rows, :]).astype(BF16).reshape(*plan.split(), spare)
        for h, end in enumerate(ends):
            end[:, :, :, wide:] = columns[:, :, h]
    r = gresid[...] + norm_back(back, n, inverse, table.get(t_in, 0))
    input_grad[...] = r.astype(BF16)


def back(
    chain, plan, wide, full, me, normal, inverse, act, parts, a_can, gresid, t_can, g_two, g_b_fc, g_b_proj
):
    t, model = normal.shape
    fsdp = plan.fsdp
    lead = (fsdp, *plan.split(), full)
    if plan.direct:
        one = (plan.nx, plan.nz, 2, plan.rows // 2, full)
        grads = [sds((2, *one), BF16), sds(one, BF16), sds(one, BF16)]
    else:
        grads = [sds(lead, BF16)]
    return chain.call(
        "back",
        functools.partial(back_body, plan, wide, len(parts), len(grads)),
        (me, normal, inverse, act, a_can, gresid, t_can, g_two, g_b_fc, g_b_proj, *parts),
        [SMEM, HELD, HELD, HELD, HBM] + [HELD] * (5 + len(parts)),
        (sds((t, model), BF16), *grads),
        (VMEM,) + (HELD,) * len(grads),
        [
            pltpu.VMEM((t, 3 * model), BF16),
            pltpu.VMEM((fsdp, t, wide), BF16),
            pltpu.VMEM((fsdp * (full - wide), model), F32),
            pltpu.VMEM(a_can.shape, BF16),
            pltpu.SemaphoreType.DMA,
        ],
        20,
    )


def preload(chain, arrays):
    n = len(arrays)

    def body(*refs):
        todo = [
            pltpu.make_async_copy(a, b, refs[-1].at[i])
            for i, (a, b) in enumerate(zip(refs[:n], refs[n:-1]))
        ]
        for c in todo:
            c.start()
        for c in todo:
            c.wait()

    return chain.call(
        "preload",
        body,
        arrays,
        [HBM] * n,
        [sds(a.shape, a.dtype) for a in arrays],
        [HELD] * n,
        [pltpu.SemaphoreType.DMA((n,))],
        1,
    )


def update_body(count, *refs):
    norms = refs[0]
    n, m = 4 * count, 3 * count
    ins, norm_out, outs = refs[1 : 1 + n], refs[1 + n], refs[2 + n : 2 + n + m]
    made, out_sem = refs[2 + n + m : -1], refs[-1]
    norm = jnp.sqrt(jnp.sum(norms[...], axis=0, keepdims=True))
    norm_out[...] = norm
    factor = jnp.minimum(1.0, clip_limit / (norm[:, 0:1] + 1e-06))
    stores = []
    for i in range(count):
        w, g, one, two = (r[...] for r in ins[4 * i : 4 * i + 4])
        last = i == count - 1
        rate, decay = (rate_vector, 0.0) if last else (rate_matrix, decay_matrix)
        clipped = g * factor
        one_new = beta_one * one + (1.0 - beta_one) * clipped
        two_new = beta_two * two + (1.0 - beta_two) * clipped * clipped
        first_hat = one_new / (1.0 - beta_one**STEP)
        second_hat = two_new / (1.0 - beta_two**STEP)
        made[i][...] = w - rate * (first_hat / (jnp.sqrt(second_hat) + 1e-08) + decay * w)
        made[count + i][...] = one_new
        made[2 * count + i][...] = two_new
        for k in (i, count + i, 2 * count + i):
            c = pltpu.make_async_copy(made[k], outs[k], out_sem.at[k])
            c.start()
            stores.append(c)
    for c in stores:
        c.wait()


def update(chain, norms, weights, grads, firsts, seconds):
    count = len(weights)
    ins = []
    for group in zip(weights, grads, firsts, seconds):
        ins += group
    outs = [sds(w.shape, F32) for w in weights] * 3
    return chain.call(
        "update",
        functools.partial(update_body, count),
        [norms, *ins],
        [VMEM] + [HELD if i % 4 != 1 else VMEM for i in range(len(ins))],
        (sds((1, 128), F32), *outs),
        (VMEM,) + (HBM,) * len(outs),
        [pltpu.VMEM(v.shape, F32) for v in outs] + [pltpu.SemaphoreType.DMA((len(outs),))],
        12,
    )


def place_second(chain, name, plan, me, z0, r0, z1, r1):
    def copies(m):
        return [
            (0, ALL, [(0, (m.y,))]),
            (1, ALL, [(0, (m.other_y,))]),
            (2, ALL, [(1, (m.x,))]),
            (3, ALL, [(1, (m.other_x,))]),
        ]

    return move(chain, name, me, [z0, r0, z1, r1], [(2, *z0.shape), (2, *z1.shape)], copies)


class Parts:
    def __init__(self, groups, far=0):
        self.count, self.far = len(groups), far
        self.arrays = [own for own, _ in groups] + [v for _, came in groups for v in came]
        self.lanes, self.came, at, place = [], [], 0, self.count
        for own, came in groups:
            self.lanes.append(slice(at, at + own.shape[-1]))
            self.came.append((place, len(came)))
            at += own.shape[-1]
            place += len(came)
        _, self.nx, self.nz, _, self.rows, _ = groups[0][0].shape
        self.cols = at

    def terms(self, g, h, at):
        place, n = self.came[g]
        return [(g, (h, *at)), (place, (h, *at)) if n == 1 else (place + h, at)]

    def sums(self, make):
        return [
            item
            for g, lanes in enumerate(self.lanes)
            for item in make(g, (self.rows, lanes.stop - lanes.start), lanes)
        ]


def first_sums(chain, plan, name, me, parts):
    nx, nz = parts.nx, parts.nz

    def sums(m):
        return parts.sums(
            lambda g, end, lanes: [
                (0, (ALL, ALL, ALL, lanes), (nz, 2, *end), parts.terms(g, 0, (m.other_x,))),
                (1, (ALL, ALL, ALL, lanes), (nx, nz, *end), parts.terms(g, 1, (ALL, ALL, m.other_y))),
            ]
        )

    outs = [sds((nz, 2, parts.rows, parts.cols), BF16), sds((nx, nz, parts.rows, parts.cols), BF16)]
    s0, s1 = add_up(chain, name + "1", me, parts.arrays, outs, sums, far=parts.far)
    return plan.partner(name, s0, "x"), plan.partner(name, s1, "y")


def second_sums(chain, plan, name, me, parts, f0, f1):
    n = len(parts.arrays)

    def sums(m):
        at0, at1 = (m.x, ALL, m.other_y), (m.other_x, ALL, m.y)

        def make(g, end, lanes):
            one = parts.terms(g, 0, at0) + [(n, (ALL, m.other_y, ALL, lanes))]
            two = parts.terms(g, 1, at1) + [(n + 1, (m.other_x, ALL, ALL, lanes))]
            shape = (parts.nz, *end)
            return [(0, (ALL, ALL, lanes), shape, one), (1, (ALL, ALL, lanes), shape, two)]

        return parts.sums(make)

    outs = [sds((parts.nz, parts.rows, parts.cols), BF16)] * 2
    arrays = [*parts.arrays, f0, f1]
    s0, s1 = add_up(chain, name + "2", me, arrays, outs, sums, far=parts.far)
    return plan.partner(name, s0, "y"), plan.partner(name, s1, "x")


def third_sums(chain, plan, name, me, parts, f0, f1, s0, s1, merged):
    n, rows = len(parts.arrays), parts.rows

    def sums(m):
        def make(g, end, lanes):
            out = []
            for k in range(parts.nz):
                z = m.z ^ k
                at = (m.x, z, m.y)
                one = parts.terms(g, 0, at) + [(n, (z, m.y, ALL, lanes)), (n + 2, (z, ALL, lanes))]
                two = parts.terms(g, 1, at) + [(n + 1, (m.x, z, ALL, lanes)), (n + 3, (z, ALL, lanes))]
                t, ti = z_target(k, merged)
                out.append((t, (*ti, slice(0, rows), lanes), end, one))
                out.append((t, (*ti, slice(rows, 2 * rows), lanes), end, two))
            return out

        return parts.sums(make)

    outs = z_outs((2 * rows, parts.cols), merged)
    arrays = [*parts.arrays, f0, f1, s0, s1]
    return add_up(chain, name + "3", me, arrays, outs, sums, far=parts.far)


def z_outs(shape, merged):
    if merged:
        return [sds(shape, F32), sds((2, *shape), BF16), sds(shape, BF16)]
    return [sds(shape, F32)] + [sds(shape, BF16)] * 3


def z_target(k, merged):
    if merged and k in (1, 3):
        return 1, (k // 2,)
    return k, ()


def along_z(chain, plan, name, me, two, came, at):
    (total,) = add_up(
        chain, name, me, [two, came], [two], lambda m: [(0, ALL, two.shape, [(0, ALL), (1, at)])]
    )
    return total


def squared(*values):
    return jnp.broadcast_to(sum(jnp.sum(v * v) for v in values), (1, 128))


def body(
    tokens,
    lengths,
    cotangent,
    qkv_weight,
    out_weight,
    fc_weight,
    proj_weight,
    vectors,
    qkv_first,
    out_first,
    fc_first,
    proj_first,
    vectors_first,
    qkv_second,
    out_second,
    fc_second,
    proj_second,
    vectors_second,
):
    dp, fsdp = lax.axis_size("dp"), lax.axis_size("fsdp")
    model = tokens.shape[1]
    wide, cut = qkv_weight.shape[1], out_weight.shape[1]
    hidden = fc_weight.shape[1] * fsdp
    per = vectors.shape[1]
    plan = Plan(dp, fsdp, model, hidden)
    rows, half, chalf, nz = plan.rows, plan.rows // 2, plan.cols // 2, plan.nz
    a_full = -(-(wide + per) // 128) * 128
    b_full = model + -(-cut // 128) * 128
    chain = Chain()
    at_dp, at_fsdp = lax.axis_index("dp"), lax.axis_index("fsdp")
    me = jnp.stack([at_dp // 2, at_dp % 2, at_fsdp // 2, at_fsdp % 2]).astype(jnp.int32)
    heads = model // HEAD_DIM
    third = [range(i, i + heads // 3) for i in range(0, heads, heads // 3)]

    def turned(value):
        return jnp.transpose(value)

    state = (
        *(qkv_weight, out_weight, fc_weight, turned(proj_weight), turned(vectors)),
        *(qkv_first, out_first, fc_first, turned(proj_first), turned(vectors_first)),
        *(qkv_second, out_second, fc_second, turned(proj_second), turned(vectors_second)),
    )

    if plan.direct:
        a_own, b_own, c_own = pack(chain, plan, state[:5], a_full, b_full)
        a_came = plan.gather_z("gather_a", a_own)
        c_y, c_x = plan.partner("gather_c", c_own[0], "y"), plan.partner("gather_c", c_own[1], "x")
        chain.wait_for(c_y, c_x)

        def place_a(m):
            return [(k, ALL, [(0, (m.z ^ k,))]) for k in range(nz)] + [
                (nz, ALL, [(1, ALL)])
            ]

        outs = [(nz, rows, a_full), b_own.shape]
        a_z, b_own = move(chain, "place_a1", me, [a_own, *a_came, b_own], outs, place_a)
        a_y, a_x = plan.partner("gather_a", a_z, "y"), plan.partner("gather_a", a_z, "x")
        a_xy = plan.opposite("gather_a", a_z)
        b_came = plan.gather_z("gather_b", b_own)

        def place_b(m):
            return [
                (k, pl.ds(h * half, half), [(h, (m.z ^ k,))]) for k in range(nz) for h in range(2)
            ] + [
                (nz, (0,), [(2, (m.y,))]),
                (nz + 1, ALL, [(2, (m.other_y,))]),
                (nz, (1,), [(2, (2 + m.x,))]),
                (nz + 2, ALL, [(2, (2 + m.other_x,))]),
            ]

        outs = [(nz, half, b_full), (nz, half, b_full), (4, chalf, plan.deep)]
        arrays = [b_own, *b_came, c_own, c_y, c_x]
        b_z0, b_z1, c_pair = move(chain, "place_b1", me, arrays, outs, place_b)
        b_r0, b_r1 = plan.partner("gather_b", b_z0, "y"), plan.partner("gather_b", b_z1, "x")
        a_zc = plan.partner("gather_a", a_z, "core")
        a_y, a_x, a_xy = gate(chain, "gate_a0", a_y, a_x, a_xy)
        a_in = [a_z, a_y, a_x, a_xy, a_zc]
        a_in = a_in + [plan.partner("gather_a", v, "core") for v in (a_y, a_x, a_xy)]
        c_far = plan.partner("gather_c", c_pair, "z", 2)
    else:

        def whole(shard):
            down = lax.all_gather(shard.astype(BF16), "dp", axis=0, tiled=True)
            return lax.all_gather(down, "fsdp", axis=0, tiled=False)

        def padded(parts, full):
            both = jnp.concatenate(parts, axis=1)
            both = whole(jnp.pad(both, ((0, 0), (0, full - both.shape[1]))))
            return both.reshape(fsdp, *plan.split(), full)

        a_in = [padded([qkv_weight, vectors], a_full)]
        b_in = [padded([fc_weight, out_weight], b_full)]
        c_all = jnp.transpose(whole(proj_weight), (0, 2, 1))
        c_all = c_all.reshape(model, fsdp, 2, hidden // fsdp // 2)
        c_in = [jnp.transpose(c_all, (1, 2, 0, 3))]

    qkv, act_one, a_can, t_can, n_one, inv_one = front(chain, plan, me, tokens, a_in, wide)
    if plan.direct:
        b_p0, b_p1 = place_second(chain, "place_b2", plan, me, b_z0, b_r0, b_z1, b_r1)
        b_q0, b_q1 = plan.partner("gather_b", b_p0, "x"), plan.partner("gather_b", b_p1, "y")
        b_pc = [plan.partner("gather_b", v, "core") for v in (b_p0, b_p1)]
    parts = [attend(chain, qkv, lengths, third[0])]
    if plan.direct:

        def place_c1(m):
            return [(0, ALL, [(0, (0,))]), (1, ALL, [(0, (1,))])]

        outs = [(2, *c_pair.shape)]
        (c_both,) = move(chain, "place_c1", me, [c_pair, c_far], outs, place_c1)
        c_near = plan.partner("gather_c", c_both, "z", 1)
    for group in third[1:]:
        parts.append(attend(chain, qkv, lengths, group))
    if plan.direct:
        b_q0, b_q1 = gate(chain, "gate_b", b_q0, b_q1)
        b_qc = [plan.partner("gather_b", v, "core") for v in (b_q0, b_q1)]
        b_in = [b_p0, b_p1, b_q0, b_q1, *b_pc, *b_qc]
        chain.wait_for(*b_pc)

        def place_c2(m):
            found = [(0, (), 0), (2, (0,), 1), (1, (), 2), (2, (1,), 3)]
            return [
                (i, (*lead, 2 * h + p), [(h, (p, m.z ^ k)), (2, (h, p, m.z ^ k))])
                for i, lead, k in found
                for h in range(2)
                for p in range(2)
            ]

        outs = [(2, nz, chalf, plan.deep)] * 2 + [(2, 2, nz, chalf, plan.deep)]
        c_p0, c_p1, c_p = move(chain, "place_c2", me, [c_pair, c_far, c_near], outs, place_c2)
        c_q0, c_q1 = plan.partner("gather_c", c_p0, "x"), plan.partner("gather_c", c_p1, "y")
        c_pc = plan.partner("gather_c", c_p, "core")
    logs = [p[1] for p in parts]
    resid_two, act_two, wout, mixed, n_two, inv_two = join(
        chain, plan, me, cut, tokens, [p[0] for p in parts], b_in, t_can
    )
    if plan.direct:
        chain.wait_for(c_pc)
    gel, slope, b_can, g_b_proj, *g_c = mlp_up(
        chain, plan, me, act_two, cotangent, t_can, b_in, hidden
    )
    if plan.direct:
        c_q0, c_q1, away = gate(chain, "gate_c", c_q0, c_q1, g_c[1])
        c_in = [c_p, c_q0, c_q1, c_pc] + [plan.partner("gather_c", v, "core") for v in (c_q0, c_q1)]
        c_away = plan.partner("sum_c", away, "core")
    if plan.direct:
        c_parts = Parts([(g_c[0], [c_away])])
        c_f0, c_f1 = first_sums(chain, plan, "sum_c", me, c_parts)
    output, gpre, g_b_fc = mlp_down(
        chain, plan, me, cotangent, resid_two, gel, slope, t_can, c_in
    )

    gact, *g_b = mlp_back(chain, plan, me, act_two, gpre, b_can)
    if plan.direct:
        b_away = [plan.partner("sum_b", v, "core") for v in g_b[1:]]
    gresid, gmixed, inner, g_two, *g_o = join_back(
        chain, plan, me, gact, cotangent, n_two, inv_two, mixed, wout, t_can, b_full - model
    )
    if plan.direct:
        chain.wait_for(c_f0, c_f1)
        o_away = [plan.partner("sum_b", *gate(chain, "gate_o", g_o[1]), "core")]
        b_parts = Parts([(g_b[0], b_away), (g_o[0], o_away)])
    gparts = [attend_back(chain, qkv, gmixed, logs[0], inner, lengths, third[0])]
    if plan.direct:
        b_f0, b_f1 = first_sums(chain, plan, "sum_b", me, b_parts)

        def sums_cz(m):
            out = []
            for k in range(nz):
                z = m.z ^ k
                at = (0, m.x, z)
                terms = [(0, at), (1, at), (2, (z,))]
                t, ti = z_target(k, True)
                out.append((t, (*ti, slice(0, 2)), (2, chalf, plan.deep), terms))
                at = (1, ALL, z, m.y)
                terms = [(0, at), (1, at), (3, (ALL, z))]
                out.append((t, (*ti, slice(2, 4)), (2, chalf, plan.deep), terms))
            return out

        outs = z_outs((4, chalf, plan.deep), True)
        arrays = [g_c[0], c_away, c_f0, c_f1]
        c_u = add_up(chain, "sum_c2", me, arrays, outs, sums_cz)
        c_near = plan.partner("sum_c", c_u[1], "z", 1)
    for log, group in zip(logs[1:], third[1:]):
        gparts.append(attend_back(chain, qkv, gmixed, log, inner, lengths, group))
    kept = (n_one, inv_one, act_one, gparts, a_can, gresid, t_can, g_two, g_b_fc, g_b_proj)
    input_grad, *g_a = back(chain, plan, wide, a_full, me, *kept)

    if plan.direct:
        c_two = along_z(chain, plan, "sum_c4", me, c_u[2], c_near, (1,))
        c_z = [c_u[0], c_near, plan.partner("sum_c", c_two, "z", 2)]
        b_s0, b_s1 = second_sums(chain, plan, "sum_b", me, b_parts, b_f0, b_f1)
        a_away = [plan.partner("sum_a", v, "core") for v in gate(chain, "gate_a", *g_a[1:])]
        a_parts = Parts([(g_a[0], a_away)])
        a_f0, a_f1 = first_sums(chain, plan, "sum_a", me, a_parts)
        chain.wait_for(c_z[2])
        b_u = third_sums(chain, plan, "sum_b", me, b_parts, b_f0, b_f1, b_s0, b_s1, True)
        b_near = plan.partner("sum_b", b_u[1], "z", 1)
        a_s0, a_s1 = second_sums(chain, plan, "sum_a", me, a_parts, a_f0, a_f1)
        z_lead = ((), (0,), ())

        def sums_c3(m):
            block = (chalf, plan.deep)
            one = [(i, (*lead, m.other_y)) for i, lead in enumerate(z_lead)]
            two = [(i, (*lead, 2 + m.other_x)) for i, lead in enumerate(z_lead)]
            return [(0, ALL, block, one), (1, ALL, block, two)]

        outs = [sds((chalf, plan.deep), BF16)] * 2
        s0, s1 = add_up(chain, "sum_c3", me, c_z, outs, sums_c3)
        c_l0, c_l1 = plan.partner("sum_c", s0, "y"), plan.partner("sum_c", s1, "x")
        b_two = along_z(chain, plan, "sum_b4", me, b_u[2], b_near, (1,))
        b_z = [b_u[0], b_near, plan.partner("sum_b", b_two, "z", 2)]
        a_u = third_sums(chain, plan, "sum_a", me, a_parts, a_f0, a_f1, a_s0, a_s1, False)
        a_z = [a_u[0]] + [plan.partner("sum_a", a_u[k], "z", k) for k in range(1, nz)]

        def sums_c(m):
            block = (chalf, plan.deep)
            one = [(i, (*lead, m.y)) for i, lead in enumerate(z_lead)] + [(3, ALL)]
            two = [(i, (*lead, 2 + m.x)) for i, lead in enumerate(z_lead)] + [(4, ALL)]
            return [(0, ALL, block, one), (1, ALL, block, two)]

        state = preload(chain, state)

        def end_c(done, outs):
            outs[0][0:chalf, :] = done[0]
            outs[0][chalf:, :] = done[1]
            outs[1][...] = squared(*done)

        d_proj, s_c = add_up(
            chain,
            "end_c",
            me,
            [*c_z, c_l0, c_l1],
            [sds((plan.cols, plan.deep), F32), sds((1, 128), F32)],
            sums_c,
            end_c,
        )
        def last_b(m):
            shape = b_z[0].shape
            return [(0, ALL, shape, [(i, lead or ALL) for i, lead in enumerate(z_lead)])]

        def last_a(m):
            return [(0, ALL, a_z[0].shape, [(i, ALL) for i in range(nz)])]

        def end_b(done, outs):
            total = done[0]
            fc, out = total[:, :model], total[:, model : model + cut]
            outs[0][...] = fc
            outs[1][...] = out
            outs[2][...] = squared(fc, out)

        shapes = [fc_weight.shape, out_weight.shape, (1, 128)]
        d_fc, d_out, s_b = add_up(
            chain, "end_b", me, b_z, [sds(s, F32) for s in shapes], last_b, end_b
        )

        def end_a(done, outs):
            total = done[0]
            start = wide // 128 * 128
            vec = jnp.transpose(total[:, start:])[wide - start : wide - start + per]
            qkv = total[:, :wide]
            outs[0][...] = qkv
            outs[1][...] = vec
            outs[2][...] = squared(qkv, vec)

        shapes = [qkv_weight.shape, (per, rows), (1, 128)]
        d_qkv, d_vec, s_a = add_up(
            chain, "end_a", me, a_z, [sds(s, F32) for s in shapes], last_a, end_a
        )
        squares = s_a + s_b + s_c
    else:

        def shared(value):
            mine = lax.psum_scatter(value, "fsdp", scatter_dimension=0, tiled=False)
            return lax.psum_scatter(mine, "dp", scatter_dimension=0, tiled=True).astype(F32)

        d_a = shared(g_a[0].reshape(fsdp, model, a_full))
        d_qkv, d_vec = d_a[:, :wide], turned(d_a[:, wide : wide + per])
        d_out = shared(jnp.transpose(g_o[0].reshape(model, fsdp, cut), (1, 0, 2)))
        d_fc = shared(g_b[0].reshape(fsdp, model, model))
        d_c = jnp.transpose(g_c[0], (2, 0, 1, 3)).reshape(fsdp, plan.cols, hidden)
        d_proj = turned(shared(jnp.transpose(d_c, (0, 2, 1))))
        total = sum(jnp.sum(d * d) for d in (d_qkv, d_out, d_fc, d_proj, d_vec))
        squares = jnp.full((1, 128), total)

    sent = jnp.broadcast_to(squares[None], (dp * fsdp, 1, 128))
    with jax.named_scope("norm"):
        norms = lax.all_to_all(sent, ("dp", "fsdp"), 0, 0, tiled=True).reshape(dp * fsdp, 128)
    norm, *new = update(
        chain, norms, state[:5], (d_qkv, d_out, d_fc, d_proj, d_vec), state[5:10], state[10:]
    )
    new = [turned(v) if i % 5 in (3, 4) else v for i, v in enumerate(new)]
    return (output, input_grad, norm[0, 0], *new)


def solution(mesh):
    tokens = P(("dp", "fsdp"), None)
    table = P("dp", "fsdp")
    return jax.shard_map(
        body,
        mesh=mesh,
        in_specs=(tokens, P(("dp", "fsdp")), tokens) + (table,) * 15,
        out_specs=(tokens, tokens, P()) + (table,) * 15,
        check_vma=False,
    )
```

```python
import functools

import jax
import jax.numpy as jnp
from jax import lax
from jax.experimental import pallas as pl
from jax.experimental.pallas import tpu as pltpu
from jax.sharding import PartitionSpec as P

HEAD_DIM = 64
STEP = 10

beta_one = 0.9
beta_two = 0.95
clip_limit = 1.0
rate_matrix = 0.1
rate_vector = 1.0
decay_matrix = 0.1
gelu_coeff = 0.7978845608028654
cubic_coeff = 0.044715
neg_large = -1e30
VEC_ROWS = 16

F32 = jnp.float32
BF16 = jnp.bfloat16
VMEM = pl.BlockSpec(memory_space=pltpu.VMEM)
HELD = pl.BlockSpec(memory_space=pltpu.VMEM)
ANY = pl.BlockSpec(memory_space=pl.ANY)
HBM = pl.BlockSpec(memory_space=pltpu.HBM)
SMEM = pl.BlockSpec(memory_space=pltpu.SMEM)
ALL = slice(None)


def dot_nn(a, b):
    return lax.dot_general(a, b, (((1,), (0,)), ((), ())), preferred_element_type=F32)


def dot_nt(a, b):
    return lax.dot_general(a, b, (((1,), (1,)), ((), ())), preferred_element_type=F32)


def dot_tn(a, b):
    return lax.dot_general(a, b, (((0,), (0,)), ((), ())), preferred_element_type=F32)


def sds(shape, dtype):
    return jax.ShapeDtypeStruct(shape, dtype)


class Chain:
    def __init__(self):
        self.waits = []

    def wait_for(self, *arrays):
        self.waits += arrays

    def call(self, name, body, ins, in_specs, outs, out_specs, scratch, limit, aliases=None):
        several = isinstance(outs, (tuple, list))
        if not several:
            outs, out_specs = (outs,), (out_specs,)
        n_in, extra, n_out = len(ins), len(self.waits), len(outs)
        pins = ((HELD, pltpu.VMEM), (HBM, pltpu.HBM))

        def run(*refs):
            given, refs = refs[:n_in], refs[n_in + extra :]
            refs[n_out][...] = jnp.zeros(refs[n_out].shape, F32)
            body(*given, *refs[:n_out], *refs[n_out + 1 :])

        placed, made = [], []
        for v, spec in zip(ins, in_specs):
            for pin, space in pins:
                if spec is pin:
                    v = pltpu.with_memory_space_constraint(v, space)
            placed.append(v)
        for o, spec in zip(outs, out_specs):
            for pin, space in pins:
                if spec is pin:
                    o = space(o.shape, o.dtype)
            made.append(o)
        results = pl.pallas_call(
            run,
            name=name,
            input_output_aliases=aliases or {},
            out_shape=(*made, pltpu.VMEM((8, 128), F32)),
            in_specs=[*in_specs, *[ANY] * extra],
            out_specs=(*out_specs, HELD),
            scratch_shapes=scratch,
            compiler_params=pltpu.CompilerParams(vmem_limit_bytes=limit << 20),
        )(*placed, *self.waits)
        *results, token = results
        self.waits = [pltpu.with_memory_space_constraint(token, pltpu.VMEM)]
        return results if several else results[0]


class Plan:
    def __init__(self, dp, fsdp, model, hidden):
        self.dp, self.fsdp = dp, fsdp
        self.nz, self.nx = dp // 2, fsdp // 2
        self.rows = model // dp
        self.cols = model // fsdp
        self.deep = hidden // dp
        self.direct = (
            dp == 2 * fsdp
            and fsdp % 2 == 0
            and self.rows % 32 == 0
            and self.cols % 32 == 0
            and self.deep % 128 == 0
            and hidden == fsdp * model
            and dp == 8
        )

    def partner(self, name, value, stage, k=1):
        axis, step = {"x": ("fsdp", 2), "y": ("dp", 1), "z": ("dp", 2), "core": ("fsdp", 1)}[stage]
        n = self.dp if axis == "dp" else self.fsdp
        with jax.named_scope(f"{name}_{stage}"):
            return lax.ppermute(value, axis, [(i, i ^ (step * k)) for i in range(n)])

    def opposite(self, name, value):
        n = self.fsdp
        pairs = [(i * n + j, (i ^ 1) * n + (j ^ 2)) for i in range(self.dp) for j in range(n)]
        with jax.named_scope(f"{name}_xy"):
            return lax.ppermute(value, ("dp", "fsdp"), pairs)

    def gather_z(self, name, value):
        near, far = self.partner(name, value, "z", 1), self.partner(name, value, "z", 2)
        return [near, far, self.partner(name, far, "z", 1)]

    def split(self):
        return (self.nz, 2, 2, self.rows // 2) if self.direct else (1, 1, 1, self.rows * self.dp)


class Me:
    def __init__(self, ref):
        self.z, self.y, self.x, self.core = ref[0], ref[1], ref[2], ref[3]
        self.other_y, self.other_x = 1 - self.y, 1 - self.x

    def fsdp(self, x, away):
        return 2 * x + (self.core ^ away)


def move(chain, name, me, arrays, outs, copies):
    n = len(arrays)

    def body(me_ref, *refs):
        for s, si, targets in copies(Me(me_ref)):
            value = refs[s][si]
            for t, ti in targets:
                refs[n + t][ti] = value

    return chain.call(
        name,
        body,
        (me, *arrays),
        [SMEM] + [VMEM] * n,
        tuple(sds(s, BF16) for s in outs),
        (HELD,) * len(outs),
        [],
        6,
    )


def gate(chain, name, *arrays, far=0):
    specs = [ANY] * (len(arrays) - far) + [HBM] * far
    return chain.call(
        name,
        lambda *refs: None,
        arrays,
        specs,
        tuple(sds(v.shape, v.dtype) for v in arrays),
        tuple(specs),
        [],
        1,
        {i: i for i in range(len(arrays))},
    )


def add_up(chain, name, me, arrays, outs, sums, after=None, far=0):
    n, m = len(arrays), len(outs)
    still = sums(Me([0, 0, 0, 0]))
    loaded = [shape for _, _, shape, parts in still for s, _ in parts if s < far]

    def body(me_ref, *refs):
        ins, outs_, refs = refs[:n], refs[n : n + m], refs[n + m :]
        held, sem = refs[: len(loaded)], refs[len(loaded) :]
        todo, i = [], 0
        for t, ti, shape, parts in sums(Me(me_ref)):
            group = []
            for s, si in parts:
                copy = None
                if s < far:
                    copy = pltpu.make_async_copy(ins[s].at[si], held[i], sem[0].at[i])
                    copy.start()
                    i += 1
                group.append((copy, s, si, i - 1))
            todo.append((t, ti, group))
        done = []
        for t, ti, group in todo:
            total = None
            for copy, s, si, k in reversed(group):
                if copy is not None:
                    copy.wait()
                v = (ins[s][si] if copy is None else held[k][...]).astype(F32)
                total = v if total is None else total + v
            if after is None:
                outs_[t][ti] = total.astype(outs_[t].dtype)
            else:
                done.append(total)
        if after is not None:
            after(done, outs_)

    return chain.call(
        name,
        body,
        (me, *arrays),
        [SMEM] + [HBM if i < far else VMEM for i in range(n)],
        tuple(outs),
        (HELD if after is None else VMEM,) * m,
        [pltpu.VMEM(shape, BF16) for shape in loaded]
        + ([pltpu.SemaphoreType.DMA((len(loaded),))] if loaded else []),
        8,
    )


def pack_body(ins, outs, held, sem):
    todo = [pltpu.make_async_copy(i, h, sem.at[k]) for k, (i, h) in enumerate(zip(ins, held))]
    for c in todo:
        c.start()
    for c in todo:
        c.wait()
    qkv, out, fc, proj, vec = (h[...] for h in held)
    a, b, c = outs
    wide, model = qkv.shape[1], fc.shape[1]
    columns = jnp.transpose(vec)
    start = wide // 128 * 128
    a[:, start:] = jnp.zeros((a.shape[0], a.shape[1] - start), BF16)
    a[:, 0:wide] = qkv.astype(BF16)
    a[:, wide : wide + columns.shape[1]] = columns.astype(BF16)
    b[:, model:] = jnp.zeros((b.shape[0], b.shape[1] - model), BF16)
    b[:, 0:model] = fc.astype(BF16)
    b[:, model : model + out.shape[1]] = out.astype(BF16)
    c[...] = proj.astype(BF16).reshape(c.shape)


def pack(chain, plan, weights, a_full, b_full):
    count = len(weights)

    def run(*refs):
        pack_body(refs[:count], refs[count : count + 3], refs[count + 3 : -1], refs[-1])

    return chain.call(
        "pack",
        run,
        weights,
        [HBM] * count,
        (
            sds((plan.rows, a_full), BF16),
            sds((plan.rows, b_full), BF16),
            sds((2, plan.cols // 2, plan.deep), BF16),
        ),
        (VMEM,) * 3,
        [pltpu.VMEM(w.shape, F32) for w in weights] + [pltpu.SemaphoreType.DMA((count,))],
        6,
    )


def normed(values):
    mean = jnp.mean(values, axis=-1, keepdims=True)
    centred = values - mean
    spread = jnp.mean(centred * centred, axis=-1, keepdims=True)
    inverse = lax.rsqrt(spread + 1e-05)
    return centred * inverse, inverse


def norm_back(grad_hidden, n, inverse, gain):
    g = grad_hidden * gain
    mean_plain = jnp.mean(g, axis=-1, keepdims=True)
    mean_cross = jnp.mean(g * n, axis=-1, keepdims=True)
    return inverse * (g - mean_plain - n * mean_cross)


class Table:
    def __init__(self, fsdp):
        self.per = 12 // fsdp

    def row(self, k):
        return (k // self.per) * VEC_ROWS + k % self.per

    def get(self, ref, k):
        r = self.row(k)
        return ref[r : r + 1, :]


def spread_matrix(rows, model, d):
    r = lax.broadcasted_iota(jnp.int32, (128, model), 0)
    c = lax.broadcasted_iota(jnp.int32, (128, model), 1)
    return ((c == r + d * rows) & (r < rows)).astype(BF16)


def halves(ins, away):
    n = len(ins) // 2
    part = ins[n * away : n * away + n]
    own = (part[0].at[0], part[0].at[1]) if n == 3 else part[:2]
    return (*own, *part[-2:])


def table_loads(plan, me, ins):
    for away in range(2):
        p0, p1, r0, r1 = halves(ins, away)
        for y in range(2):
            for x, ref in ((me.x, p0), (me.other_x, r0)):
                yield ref, (y,), me.fsdp(x, away), (ALL, y), 0
        for y, ref in ((me.y, p1), (me.other_y, r1)):
            for x in range(plan.nx):
                yield ref, (x,), me.fsdp(x, away), (ALL, y), 1


def front_body(plan, wide, n_in, me_ref, tokens, *refs):
    ins = refs[:n_in]
    qkv, act, a_out, t_out, n_out, inv_out = refs[n_in : n_in + 6]
    a_v, flat, sem, out_sem = refs[n_in + 6 :]
    fsdp = plan.fsdp
    full = a_v.shape[-1]
    model = tokens.shape[1]
    table = Table(fsdp)
    if plan.direct:
        me = Me(me_ref)
        for i, ref in enumerate(ins):
            away, x, y = i // 4, i // 2 % 2, i % 2
            f = me.fsdp(me.x ^ x, away)
            pltpu.make_async_copy(ref, a_v.at[f, :, me.y ^ y], sem.at[f]).start()
    else:
        for f in range(fsdp):
            pltpu.make_async_copy(ins[0].at[f], a_v.at[f], sem.at[f]).start()
    n, inverse = normed(tokens[...].astype(F32))
    n_out[...] = n
    inv_out[...] = jnp.broadcast_to(inverse, inv_out.shape)
    start = wide // 128 * 128
    for f in range(fsdp):
        pltpu.make_async_copy(a_v.at[f], a_v.at[f], sem.at[f]).wait()
        block = a_v[f].reshape(model, full)
        flat[:, f * wide : (f + 1) * wide] = block[:, :wide]
        turned = jnp.transpose(block[:, start:].astype(F32))
        t_out[f * VEC_ROWS : f * VEC_ROWS + table.per, :] = turned[
            wide - start : wide - start + table.per
        ]
    copy = pltpu.make_async_copy(flat, a_out, out_sem)
    copy.start()
    act[...] = (n * table.get(t_out, 0) + table.get(t_out, 1)).astype(BF16)
    for which in range(3):
        r = dot_nn(act[...], flat[:, which * model : (which + 1) * model])
        if which != 1:
            r = r + table.get(t_out, 4 + which // 2)
        qkv[which] = r.astype(BF16)
    copy.wait()


def front(chain, plan, me, tokens, pieces, wide):
    t, model = tokens.shape
    fsdp = plan.fsdp
    full = pieces[0].shape[-1]
    lead = (fsdp, plan.nz, 2, plan.rows, full) if plan.direct else pieces[0].shape
    return chain.call(
        "front",
        functools.partial(front_body, plan, wide, len(pieces)),
        (me, tokens, *pieces),
        [SMEM, VMEM] + [ANY] * len(pieces),
        (
            sds((3, t, model), BF16),
            sds((t, model), BF16),
            sds((model, 3 * model), BF16),
            sds((fsdp * VEC_ROWS, model), F32),
            sds((t, model), F32),
            sds((t, 128), F32),
        ),
        (HELD, HELD, HBM, HELD, HELD, HELD),
        [
            pltpu.VMEM(lead, BF16),
            pltpu.VMEM((model, 3 * model), BF16),
            pltpu.SemaphoreType.DMA((fsdp,)),
            pltpu.SemaphoreType.DMA,
        ],
        16,
    )


def masks(length, lo, size, keys):
    q = lax.broadcasted_iota(jnp.int32, (size, 1), 0) + lo
    limit = jnp.minimum(q, length - 1)
    k = lax.broadcasted_iota(jnp.int32, (size, keys), 1)
    return k <= limit


QBLOCK = 256


def attend_body(heads, length_ref, qkv, mixed, logs):
    t = mixed.shape[0]
    length = length_ref[0]
    scale = HEAD_DIM**-0.5

    def part(h, which):
        return qkv[which, :, h * HEAD_DIM : (h + 1) * HEAD_DIM]

    for i, h in enumerate(heads):
        q = part(h, 0) * jnp.asarray(scale, BF16)
        k, v = part(h, 1), part(h, 2)
        for lo in range(0, t, QBLOCK):
            n = lo + QBLOCK
            s = dot_nt(q[lo:n], k[:n])
            s = jnp.where(masks(length, lo, QBLOCK, n), s, neg_large)
            top = jnp.max(s, axis=-1, keepdims=True)
            e = jnp.exp(s - top)
            total = jnp.sum(e, axis=-1, keepdims=True)
            p = (e * (1.0 / total)).astype(BF16)
            o = dot_nn(p, v[:n])
            mixed[lo:n, i * HEAD_DIM : (i + 1) * HEAD_DIM] = o.astype(BF16)
            logs[lo:n, i : i + 1] = top + jnp.log(total)


def attend(chain, qkv, length, heads):
    t = qkv.shape[1]
    return chain.call(
        "attend",
        functools.partial(attend_body, heads),
        (length, qkv),
        [SMEM, HELD],
        (sds((t, len(heads) * HEAD_DIM), BF16), sds((t, 128), F32)),
        (HELD, HELD),
        [],
        6,
    )


def join_body(plan, cut, n_in, n_mixed, me_ref, tokens, t_in, *refs):
    ins, refs = refs[:n_in], refs[n_in:]
    parts, (resid, act, wout, mixed, n_out, inv_out, o_v, sem) = refs[:n_mixed], refs[n_mixed:]
    model = tokens.shape[1]
    fsdp = plan.fsdp
    table = Table(fsdp)
    lanes = pl.ds(model, o_v.shape[-1])
    if plan.direct:
        for ref, si, f, ti, h in table_loads(plan, Me(me_ref), ins):
            src = ref.at[(*si, ALL, ALL, lanes)]
            pltpu.make_async_copy(src, o_v.at[(f, *ti, h)], sem).start()
    else:
        for f in range(fsdp):
            src = ins[0].at[(f, ALL, ALL, ALL, ALL, lanes)]
            pltpu.make_async_copy(src, o_v.at[f], sem).start()
    at = 0
    for p in parts:
        mixed[:, at : at + p.shape[1]] = p[...]
        at += p.shape[1]
    pltpu.make_async_copy(o_v, o_v, sem).wait()
    for f in range(fsdp):
        wout[:, f * cut : (f + 1) * cut] = o_v[f].reshape(model, o_v.shape[-1])[:, :cut]
    r = tokens[...].astype(F32) + dot_nn(mixed[...], wout[...]) + table.get(t_in, 6)
    resid[...] = r
    n, inverse = normed(r)
    n_out[...] = n
    inv_out[...] = jnp.broadcast_to(inverse, inv_out.shape)
    act[...] = (n * table.get(t_in, 2) + table.get(t_in, 3)).astype(BF16)


def join(chain, plan, me, cut, tokens, parts, pieces, t_can):
    t, model = tokens.shape
    spare = pieces[0].shape[-1] - model
    return chain.call(
        "join",
        functools.partial(join_body, plan, cut, len(pieces), len(parts)),
        (me, tokens, t_can, *pieces, *parts),
        [SMEM, VMEM, HELD] + [ANY] * len(pieces) + [HELD] * len(parts),
        (
            sds((t, model), F32),
            sds((t, model), BF16),
            sds((model, model), BF16),
            sds((t, model), BF16),
            sds((t, model), F32),
            sds((t, 128), F32),
        ),
        (HELD,) * 6,
        [pltpu.VMEM((plan.fsdp, *plan.split(), spare), BF16), pltpu.SemaphoreType.DMA],
        10,
    )


def gelu_and_slope(pre):
    square = pre * pre
    th = jnp.tanh(pre * (gelu_coeff + (gelu_coeff * cubic_coeff) * square))
    plus = 0.5 * th + 0.5
    bend = 0.5 * gelu_coeff + (1.5 * gelu_coeff * cubic_coeff) * square
    return (pre * plus).astype(BF16), plus + pre * (1.0 - th * th) * bend


def mlp_up_body(plan, n_in, n_out, me_ref, act, cot, t_in, *refs):
    ins, refs = refs[:n_in], refs[n_in:]
    gel_out, slope_out, b_v, g_b_proj = refs[:4]
    gouts, refs = refs[4 : 4 + n_out], refs[4 + n_out :]
    gp_v, sem = refs
    fsdp, half = plan.fsdp, plan.cols // 2
    t, model = act.shape
    deep = gp_v.shape[-1]
    per = Table(fsdp).per
    me = Me(me_ref)
    order = []
    for k in range(fsdp):
        if plan.direct:
            away, x = k // 2, me.x if k % 2 == 0 else me.other_x
            p0, p1, r0, r1 = halves(ins, away)
            f = me.fsdp(x, away)
            own = p0 if k % 2 == 0 else r0
            loads = [(own.at[y], y, 0) for y in range(2)]
            loads += [(p1.at[x], me.y, 1), (r1.at[x], me.other_y, 1)]
            for ref, y, h in loads:
                src = ref.at[:, :, pl.ds(0, model)]
                pltpu.make_async_copy(src, b_v.at[f, :, y, h], sem.at[k]).start()
        else:
            f = k
            src = ins[0].at[(f, ALL, ALL, ALL, ALL, pl.ds(0, model))]
            pltpu.make_async_copy(src, b_v.at[f], sem.at[k]).start()
        order.append(f)
    g_b_proj[...] = jnp.sum(cot[...].astype(F32), axis=0, keepdims=True)

    def up(k, lo, hi):
        row = 8 + order[k]
        bias = t_in[pl.ds(row // per * VEC_ROWS + row % per, 1), :]
        return dot_nn(act[lo:hi], b_v[order[k]].reshape(model, model)) + bias

    step = t // 2
    for k in range(fsdp):
        pltpu.make_async_copy(b_v.at[order[k]], b_v.at[order[k]], sem.at[k]).wait()
        lanes = pl.ds(pl.multiple_of(order[k] * model, model), model)
        for lo in range(0, t, step):
            gel, slope = gelu_and_slope(up(k, lo, lo + step))
            gel_out[lo : lo + step, lanes] = gel
            slope_out[lo : lo + step, lanes] = slope
        grad = dot_tn(cot[...], gel_out[:, lanes]).astype(BF16)
        if not plan.direct:
            gouts[0][k, 0], gouts[0][k, 1] = grad[:, :deep], grad[:, deep:]
            continue
        gp_v[0], gp_v[1] = grad[:, :deep], grad[:, deep:]
        for away in range(2):
            for x in range(plan.nx):
                for h in range(2):
                    row = me.fsdp(x, away) * plan.cols + h * half
                    part = gp_v[:, pl.ds(pl.multiple_of(row, 16), half), :]
                    gouts[away][h, x, pl.ds(order[k], 1)] = part[None]


def mlp_up(chain, plan, me, act, cot, t_can, pieces, hidden):
    t, model = act.shape
    fsdp = plan.fsdp
    per = hidden // fsdp // 2
    if plan.direct:
        grads = [sds((2, plan.nx, plan.nz, 2, plan.cols // 2, plan.deep), BF16)] * 2
    else:
        grads = [sds((fsdp, 2, model, per), BF16)]
    lead = (fsdp, *plan.split(), model)
    return chain.call(
        "mlp_up",
        functools.partial(mlp_up_body, plan, len(pieces), len(grads)),
        (me, act, cot, t_can, *pieces),
        [SMEM, HELD, VMEM, HELD] + [ANY] * len(pieces),
        (
            sds((t, hidden), BF16),
            sds((t, hidden), F32),
            sds(lead, BF16),
            sds((1, model), F32),
            *grads,
        ),
        (HELD,) * (4 + len(grads)),
        [
            pltpu.VMEM((2, model, per), BF16),
            pltpu.SemaphoreType.DMA((fsdp,)),
        ],
        18,
    )


def mlp_down_body(plan, n_in, me_ref, cot, slope, *refs):
    ins, refs = refs[:n_in], refs[n_in:]
    gpre, g_b_fc, c_v = refs
    half = plan.cols // 2
    model = cot.shape[1]
    if plan.direct:
        for ref, si, f, ti, h in table_loads(plan, Me(me_ref), ins):
            rows = pl.ds(pl.multiple_of(f * plan.cols + h * half, 16), half)
            c_v[(*ti, rows)] = ref[si]
    else:
        c_v[...] = ins[0][...]
    for j in range(plan.fsdp):
        lanes = slice(j * model, (j + 1) * model)
        down = jnp.concatenate([c_v[j, 0], c_v[j, 1]], axis=1)
        low = (dot_nn(cot[...], down) * slope[:, lanes]).astype(BF16)
        gpre[:, lanes] = low
        g_b_fc[j : j + 1, :] = jnp.sum(low.astype(F32), axis=0, keepdims=True)


def mlp_down(chain, plan, me, cot, slope, pieces):
    t, model = cot.shape
    fsdp, hidden = plan.fsdp, slope.shape[1]
    return chain.call(
        "mlp_down",
        functools.partial(mlp_down_body, plan, len(pieces)),
        (me, cot, slope, *pieces),
        [SMEM, VMEM, HELD] + [VMEM] * len(pieces),
        (
            sds((t, hidden), BF16),
            sds((fsdp, model), F32),
            sds((fsdp, 2, model, hidden // fsdp // 2), BF16),
        ),
        (HELD,) * 3,
        [],
        10,
    )


def mlp_out_body(table, resid, gel, c_v, t_in, output):
    model = resid.shape[1]
    total = resid[...] + table.get(t_in, 7)
    for j in range(c_v.shape[0]):
        down = jnp.concatenate([c_v[j, 0], c_v[j, 1]], axis=1)
        total = total + dot_nt(gel[:, j * model : (j + 1) * model], down)
    output[...] = total.astype(BF16)


def mlp_out(chain, plan, resid, gel, c_can, t_can):
    return chain.call(
        "mlp_out",
        functools.partial(mlp_out_body, Table(plan.fsdp)),
        (resid, gel, c_can, t_can),
        [HELD] * 4,
        sds(resid.shape, BF16),
        VMEM,
        [],
        10,
    )


def mlp_back_body(plan, n_out, me_ref, act, gpre, b_in, *refs):
    gact = refs[0]
    gouts = refs[1 : 1 + n_out]
    model = act.shape[1]
    me = Me(me_ref)
    first = True
    order = [
        (x, away, me.fsdp(x, away) if plan.direct else 2 * x + away)
        for away in range(2)
        for x in range(plan.nx)
    ]
    for x, away, f in order:
        part = gpre[:, pl.ds(pl.multiple_of(f * model, model), model)]
        grad = dot_tn(act[...], part).astype(BF16).reshape(b_in.shape[1:])
        if not plan.direct:
            gouts[0][f] = grad
        elif away:
            gouts[1][x], gouts[2][x] = grad[:, :, 0], grad[:, :, 1]
        else:
            gouts[0][0, x], gouts[0][1, x] = grad[:, :, 0], grad[:, :, 1]
        back = dot_nt(part, b_in[f].reshape(model, model))
        if first:
            gact[...] = back
        else:
            gact[...] += back
        first = False


def mlp_back(chain, plan, me, act, gpre, b_can):
    t, model = act.shape
    fsdp = plan.fsdp
    lead = (fsdp, *plan.split(), model)
    if plan.direct:
        one = (plan.nx, plan.nz, 2, plan.rows // 2, model)
        grads = [sds((2, *one), BF16), sds(one, BF16), sds(one, BF16)]
    else:
        grads = [sds(lead, BF16)]
    return chain.call(
        "mlp_back",
        functools.partial(mlp_back_body, plan, len(grads)),
        (me, act, gpre, b_can),
        [SMEM, HELD, HELD, HELD],
        (sds((t, model), F32), *grads),
        (HELD,) + (HELD,) * len(grads),
        [],
        10,
    )


def join_back_body(plan, me_ref, gact, cot, normal, inverse_in, mixed, wout, t_in, *refs):
    gresid, gmixed, inner, g_vec, *gouts = refs[:-1]
    o_v = refs[-1]
    model = cot.shape[1]
    table = Table(plan.fsdp)
    n, inverse = normal[...], inverse_in[:, 0:1]
    e = gact[...]
    g_vec[...] = jnp.zeros(g_vec.shape, F32)
    g_vec[0:1, :] = jnp.sum(e * n, axis=0, keepdims=True)
    g_vec[1:2, :] = jnp.sum(e, axis=0, keepdims=True)
    r = cot[...].astype(F32) + norm_back(e, n, inverse, table.get(t_in, 2))
    gresid[...] = r
    branch = r.astype(BF16)
    g_vec[2:3, :] = jnp.sum(branch.astype(F32), axis=0, keepdims=True)
    grad = dot_tn(mixed[...], branch).astype(BF16)
    if plan.direct:
        me = Me(me_ref)
        cut = plan.cols
        for f in range(plan.fsdp):
            o_v[f, :, 0:cut] = grad[:, f * cut : (f + 1) * cut]
            o_v[f, :, cut:] = jnp.zeros((model, o_v.shape[-1] - cut), BF16)
        for away in range(2):
            for x in range(plan.nx):
                part = o_v[me.fsdp(x, away)].reshape(*plan.split(), o_v.shape[-1])
                gouts[away][0, x], gouts[away][1, x] = part[:, :, 0], part[:, :, 1]
    else:
        gouts[0][...] = grad
    low = dot_nt(branch, wout[...]).astype(BF16)
    gmixed[...] = low
    product = low.astype(F32) * mixed[...].astype(F32)
    high = product.astype(BF16)
    rest = (product - high.astype(F32)).astype(BF16)
    head = lax.broadcasted_iota(jnp.int32, (model, 128), 0) // HEAD_DIM
    ones = (head == lax.broadcasted_iota(jnp.int32, (model, 128), 1)).astype(BF16)
    inner[...] = dot_nn(high, ones) + dot_nn(rest, ones)


def join_back(chain, plan, me, gact, cot, normal, inverse, mixed, wout, t_can, spare):
    t, model = cot.shape
    ins = [me, gact, cot, normal, inverse, mixed, wout, t_can]
    if plan.direct:
        grads = [sds((2, plan.nx, plan.nz, 2, plan.rows // 2, spare), BF16)] * 2
        grad_specs = [HELD] * 2
    else:
        grads, grad_specs = [sds((model, model), BF16)], [VMEM]
    return chain.call(
        "join_back",
        functools.partial(join_back_body, plan),
        ins,
        [SMEM, HELD, VMEM] + [HELD] * 5,
        (
            sds((t, model), F32),
            sds((t, model), BF16),
            sds((t, 128), F32),
            sds((8, model), F32),
            *grads,
        ),
        (HELD, HELD, HELD, HELD, *grad_specs),
        [pltpu.VMEM((plan.fsdp, model, spare), BF16)],
        14,
    )


def attend_back_body(heads, length_ref, qkv, gmixed, logs, inner, out):
    t = gmixed.shape[0]
    length = length_ref[0]
    scale = HEAD_DIM**-0.5

    def part(h, which):
        return qkv[which, :, h * HEAD_DIM : (h + 1) * HEAD_DIM]

    for i, h in enumerate(heads):
        lanes = slice(i * HEAD_DIM, (i + 1) * HEAD_DIM)
        q = part(h, 0)
        small = q * jnp.asarray(scale, BF16)
        k, v = part(h, 1), part(h, 2)
        go = gmixed[:, h * HEAD_DIM : (h + 1) * HEAD_DIM]
        gk, gv = [], []
        for lo in range(0, t, QBLOCK):
            n = lo + QBLOCK
            s = dot_nt(small[lo:n], k[:n])
            s = jnp.where(masks(length, lo, QBLOCK, n), s, neg_large)
            p = jnp.exp(s - logs[lo:n, i : i + 1])
            gp = dot_nt(go[lo:n], v[:n])
            ds = (p * (gp - inner[lo:n, h : h + 1])).astype(BF16)
            out[0, lo:n, lanes] = (dot_nn(ds, k[:n]) * scale).astype(BF16)
            gv.append(dot_tn(p.astype(BF16), go[lo:n]))
            gk.append(dot_tn(ds, small[lo:n]))
        for b in range(t // QBLOCK):
            rows = slice(b * QBLOCK, (b + 1) * QBLOCK)
            out[1, rows, lanes] = sum(x[rows] for x in gk[b:]).astype(BF16)
            out[2, rows, lanes] = sum(x[rows] for x in gv[b:]).astype(BF16)


def attend_back(chain, qkv, gmixed, logs, inner, length, heads):
    t = qkv.shape[1]
    return chain.call(
        "attend_back",
        functools.partial(attend_back_body, heads),
        (length, qkv, gmixed, logs, inner),
        [SMEM, HELD, HELD, HELD, HELD],
        sds((3, t, len(heads) * HEAD_DIM), BF16),
        HELD,
        [],
        8,
    )


def whole_qkv(parts, flat, blocks):
    wide = blocks.shape[2]
    model = flat.shape[1] // 3
    at = 0
    for p in parts:
        size = p.shape[2]
        for which in range(3):
            lo = which * model + at
            flat[:, lo : lo + size] = p[which]
        at += size
    for f in range(blocks.shape[0]):
        blocks[f] = flat[:, f * wide : (f + 1) * wide]


def back_body(plan, wide, n_parts, n_out, me_ref, normal, inverse_in, act, a_in, gresid, t_in, g_two, g_b_fc, g_b_proj, *refs):
    parts, refs = refs[:n_parts], refs[n_parts:]
    input_grad, gouts, refs = refs[0], refs[1 : 1 + n_out], refs[1 + n_out :]
    flat, gq_v, tab, a_v, in_sem = refs
    late = pltpu.make_async_copy(a_in, a_v, in_sem)
    late.start()
    fsdp = plan.fsdp
    t, model = normal.shape
    table = Table(fsdp)
    spare = tab.shape[0] // fsdp
    whole_qkv(parts, flat, gq_v)
    me = Me(me_ref)

    def each():
        for away in range(2):
            for x in range(plan.nx):
                if plan.direct:
                    ends = [gouts[1 + h].at[x] if away else gouts[0].at[h, x] for h in range(2)]
                    yield me.fsdp(x, away), ends
                else:
                    yield 2 * x + away, [gouts[0].at[2 * x + away, :, :, h] for h in range(1)]

    for f, ends in each():
        grad = dot_tn(act[...], gq_v[f]).astype(BF16).reshape(*plan.split(), wide)
        for h, end in enumerate(ends):
            end[:, :, :, 0:wide] = grad[:, :, h]
    late.wait()
    back = dot_nt(flat[...], a_v[...])
    sums = dot_nn(jnp.ones((8, t), BF16), flat[...])
    n, inverse = normal[...], inverse_in[:, 0:1]
    tab[...] = jnp.zeros(tab.shape, F32)

    def put(k, value):
        r = (k // table.per) * spare + k % table.per
        tab[r : r + 1, :] = value

    put(0, jnp.sum(back * n, axis=0, keepdims=True))
    put(1, jnp.sum(back, axis=0, keepdims=True))
    put(2, g_two[0:1, :])
    put(3, g_two[1:2, :])
    put(4, sums[0:1, 0:model])
    put(5, sums[0:1, 2 * model :])
    put(6, g_two[2:3, :])
    put(7, g_b_proj[...])
    for j in range(fsdp):
        put(8 + j, g_b_fc[j : j + 1, :])
    for f, ends in each():
        rows = pl.ds(pl.multiple_of(f * spare, 8), spare)
        columns = jnp.transpose(tab[rows, :]).astype(BF16).reshape(*plan.split(), spare)
        for h, end in enumerate(ends):
            end[:, :, :, wide:] = columns[:, :, h]
    r = gresid[...] + norm_back(back, n, inverse, table.get(t_in, 0))
    input_grad[...] = r.astype(BF16)


def back(
    chain, plan, wide, full, me, normal, inverse, act, parts, a_can, gresid, t_can, g_two, g_b_fc, g_b_proj
):
    t, model = normal.shape
    fsdp = plan.fsdp
    lead = (fsdp, *plan.split(), full)
    if plan.direct:
        one = (plan.nx, plan.nz, 2, plan.rows // 2, full)
        grads = [sds((2, *one), BF16), sds(one, BF16), sds(one, BF16)]
    else:
        grads = [sds(lead, BF16)]
    return chain.call(
        "back",
        functools.partial(back_body, plan, wide, len(parts), len(grads)),
        (me, normal, inverse, act, a_can, gresid, t_can, g_two, g_b_fc, g_b_proj, *parts),
        [SMEM, HELD, HELD, HELD, HBM] + [HELD] * (5 + len(parts)),
        (sds((t, model), BF16), *grads),
        (VMEM,) + (HELD,) * len(grads),
        [
            pltpu.VMEM((t, 3 * model), BF16),
            pltpu.VMEM((fsdp, t, wide), BF16),
            pltpu.VMEM((fsdp * (full - wide), model), F32),
            pltpu.VMEM(a_can.shape, BF16),
            pltpu.SemaphoreType.DMA,
        ],
        20,
    )


def preload(chain, arrays):
    n = len(arrays)

    def body(*refs):
        todo = [
            pltpu.make_async_copy(a, b, refs[-1].at[i])
            for i, (a, b) in enumerate(zip(refs[:n], refs[n:-1]))
        ]
        for c in todo:
            c.start()
        for c in todo:
            c.wait()

    return chain.call(
        "preload",
        body,
        arrays,
        [HBM] * n,
        [sds(a.shape, a.dtype) for a in arrays],
        [HELD] * n,
        [pltpu.SemaphoreType.DMA((n,))],
        1,
    )


def update_body(count, *refs):
    norms = refs[0]
    n, m = 4 * count, 3 * count
    ins, norm_out, outs = refs[1 : 1 + n], refs[1 + n], refs[2 + n : 2 + n + m]
    made, out_sem = refs[2 + n + m : -1], refs[-1]
    norm = jnp.sqrt(jnp.sum(norms[...], axis=0, keepdims=True))
    norm_out[...] = norm
    factor = jnp.minimum(1.0, clip_limit / (norm[:, 0:1] + 1e-06))
    stores = []
    for i in range(count):
        w, g, one, two = (r[...] for r in ins[4 * i : 4 * i + 4])
        last = i == count - 1
        rate, decay = (rate_vector, 0.0) if last else (rate_matrix, decay_matrix)
        clipped = g * factor
        one_new = beta_one * one + (1.0 - beta_one) * clipped
        two_new = beta_two * two + (1.0 - beta_two) * clipped * clipped
        first_hat = one_new / (1.0 - beta_one**STEP)
        second_hat = two_new / (1.0 - beta_two**STEP)
        made[i][...] = w - rate * (first_hat / (jnp.sqrt(second_hat) + 1e-08) + decay * w)
        made[count + i][...] = one_new
        made[2 * count + i][...] = two_new
        for k in (i, count + i, 2 * count + i):
            c = pltpu.make_async_copy(made[k], outs[k], out_sem.at[k])
            c.start()
            stores.append(c)
    for c in stores:
        c.wait()


def update(chain, norms, weights, grads, firsts, seconds):
    count = len(weights)
    ins = []
    for group in zip(weights, grads, firsts, seconds):
        ins += group
    outs = [sds(w.shape, F32) for w in weights] * 3
    return chain.call(
        "update",
        functools.partial(update_body, count),
        [norms, *ins],
        [VMEM] + [HELD if i % 4 != 1 else VMEM for i in range(len(ins))],
        (sds((1, 128), F32), *outs),
        (VMEM,) + (HBM,) * len(outs),
        [pltpu.VMEM(v.shape, F32) for v in outs] + [pltpu.SemaphoreType.DMA((len(outs),))],
        12,
    )


def place_second(chain, name, plan, me, z0, r0, z1, r1):
    def copies(m):
        return [
            (0, ALL, [(0, (m.y,))]),
            (1, ALL, [(0, (m.other_y,))]),
            (2, ALL, [(1, (m.x,))]),
            (3, ALL, [(1, (m.other_x,))]),
        ]

    return move(chain, name, me, [z0, r0, z1, r1], [(2, *z0.shape), (2, *z1.shape)], copies)


class Parts:
    def __init__(self, groups, far=0):
        self.count, self.far = len(groups), far
        self.arrays = [own for own, _ in groups] + [v for _, came in groups for v in came]
        self.lanes, self.came, at, place = [], [], 0, self.count
        for own, came in groups:
            self.lanes.append(slice(at, at + own.shape[-1]))
            self.came.append((place, len(came)))
            at += own.shape[-1]
            place += len(came)
        _, self.nx, self.nz, _, self.rows, _ = groups[0][0].shape
        self.cols = at

    def terms(self, g, h, at):
        place, n = self.came[g]
        return [(g, (h, *at)), (place, (h, *at)) if n == 1 else (place + h, at)]

    def sums(self, make):
        return [
            item
            for g, lanes in enumerate(self.lanes)
            for item in make(g, (self.rows, lanes.stop - lanes.start), lanes)
        ]


def first_sums(chain, plan, name, me, parts):
    nx, nz = parts.nx, parts.nz

    def sums(m):
        return parts.sums(
            lambda g, end, lanes: [
                (0, (ALL, ALL, ALL, lanes), (nz, 2, *end), parts.terms(g, 0, (m.other_x,))),
                (1, (ALL, ALL, ALL, lanes), (nx, nz, *end), parts.terms(g, 1, (ALL, ALL, m.other_y))),
            ]
        )

    outs = [sds((nz, 2, parts.rows, parts.cols), BF16), sds((nx, nz, parts.rows, parts.cols), BF16)]
    s0, s1 = add_up(chain, name + "1", me, parts.arrays, outs, sums, far=parts.far)
    return plan.partner(name, s0, "x"), plan.partner(name, s1, "y")


def second_sums(chain, plan, name, me, parts, f0, f1):
    n = len(parts.arrays)

    def sums(m):
        at0, at1 = (m.x, ALL, m.other_y), (m.other_x, ALL, m.y)

        def make(g, end, lanes):
            one = parts.terms(g, 0, at0) + [(n, (ALL, m.other_y, ALL, lanes))]
            two = parts.terms(g, 1, at1) + [(n + 1, (m.other_x, ALL, ALL, lanes))]
            shape = (parts.nz, *end)
            return [(0, (ALL, ALL, lanes), shape, one), (1, (ALL, ALL, lanes), shape, two)]

        return parts.sums(make)

    outs = [sds((parts.nz, parts.rows, parts.cols), BF16)] * 2
    arrays = [*parts.arrays, f0, f1]
    s0, s1 = add_up(chain, name + "2", me, arrays, outs, sums, far=parts.far)
    return plan.partner(name, s0, "y"), plan.partner(name, s1, "x")


def third_sums(chain, plan, name, me, parts, f0, f1, s0, s1, merged):
    n, rows = len(parts.arrays), parts.rows

    def sums(m):
        def make(g, end, lanes):
            out = []
            for k in range(parts.nz):
                z = m.z ^ k
                at = (m.x, z, m.y)
                one = parts.terms(g, 0, at) + [(n, (z, m.y, ALL, lanes)), (n + 2, (z, ALL, lanes))]
                two = parts.terms(g, 1, at) + [(n + 1, (m.x, z, ALL, lanes)), (n + 3, (z, ALL, lanes))]
                t, ti = z_target(k, merged)
                out.append((t, (*ti, slice(0, rows), lanes), end, one))
                out.append((t, (*ti, slice(rows, 2 * rows), lanes), end, two))
            return out

        return parts.sums(make)

    outs = z_outs((2 * rows, parts.cols), merged)
    arrays = [*parts.arrays, f0, f1, s0, s1]
    return add_up(chain, name + "3", me, arrays, outs, sums, far=parts.far)


def z_outs(shape, merged):
    if merged:
        return [sds(shape, F32), sds((2, *shape), BF16), sds(shape, BF16)]
    return [sds(shape, F32)] + [sds(shape, BF16)] * 3


def z_target(k, merged):
    if merged and k in (1, 3):
        return 1, (k // 2,)
    return k, ()


def along_z(chain, plan, name, me, two, came, at):
    (total,) = add_up(
        chain, name, me, [two, came], [two], lambda m: [(0, ALL, two.shape, [(0, ALL), (1, at)])]
    )
    return total


def squared(*values):
    return jnp.broadcast_to(sum(jnp.sum(v * v) for v in values), (1, 128))


def body(
    tokens,
    lengths,
    cotangent,
    qkv_weight,
    out_weight,
    fc_weight,
    proj_weight,
    vectors,
    qkv_first,
    out_first,
    fc_first,
    proj_first,
    vectors_first,
    qkv_second,
    out_second,
    fc_second,
    proj_second,
    vectors_second,
):
    dp, fsdp = lax.axis_size("dp"), lax.axis_size("fsdp")
    model = tokens.shape[1]
    wide, cut = qkv_weight.shape[1], out_weight.shape[1]
    hidden = fc_weight.shape[1] * fsdp
    per = vectors.shape[1]
    plan = Plan(dp, fsdp, model, hidden)
    rows, half, chalf, nz = plan.rows, plan.rows // 2, plan.cols // 2, plan.nz
    a_full = -(-(wide + per) // 128) * 128
    b_full = model + -(-cut // 128) * 128
    chain = Chain()
    at_dp, at_fsdp = lax.axis_index("dp"), lax.axis_index("fsdp")
    me = jnp.stack([at_dp // 2, at_dp % 2, at_fsdp // 2, at_fsdp % 2]).astype(jnp.int32)
    heads = model // HEAD_DIM
    third = [range(i, i + heads // 3) for i in range(0, heads, heads // 3)]

    def turned(value):
        return jnp.transpose(value)

    state = (
        *(qkv_weight, out_weight, fc_weight, turned(proj_weight), turned(vectors)),
        *(qkv_first, out_first, fc_first, turned(proj_first), turned(vectors_first)),
        *(qkv_second, out_second, fc_second, turned(proj_second), turned(vectors_second)),
    )

    if plan.direct:
        a_own, b_own, c_own = pack(chain, plan, state[:5], a_full, b_full)
        a_near, a_far = plan.partner("gather_a", a_own, "z", 1), plan.partner("gather_a", a_own, "z", 2)
        c_y, c_x = plan.partner("gather_c", c_own[0], "y"), plan.partner("gather_c", c_own[1], "x")
        chain.wait_for(c_y, c_x)
        a_far, b_own = gate(chain, "gate_z", a_far, b_own)
        a_came = [a_near, a_far, plan.partner("gather_a", a_far, "z", 1)]
        b_came = plan.gather_z("gather_b", b_own)

        def place_a(m):
            return [(k, ALL, [(0, (m.z ^ k,))]) for k in range(nz)]

        (a_z,) = move(chain, "place_a1", me, [a_own, *a_came], [(nz, rows, a_full)], place_a)
        a_y, a_x = plan.partner("gather_a", a_z, "y"), plan.partner("gather_a", a_z, "x")
        a_xy = plan.opposite("gather_a", a_z)

        def place_b(m):
            return [
                (k, pl.ds(h * half, half), [(h, (m.z ^ k,))]) for k in range(nz) for h in range(2)
            ] + [
                (nz, (0,), [(2, (m.y,))]),
                (nz + 1, ALL, [(2, (m.other_y,))]),
                (nz, (1,), [(2, (2 + m.x,))]),
                (nz + 2, ALL, [(2, (2 + m.other_x,))]),
            ]

        outs = [(nz, half, b_full), (nz, half, b_full), (4, chalf, plan.deep)]
        arrays = [b_own, *b_came, c_own, c_y, c_x]
        chain.wait_for(a_y, a_x, a_xy)
        b_z0, b_z1, c_pair = move(chain, "place_b1", me, arrays, outs, place_b)
        b_r0, b_r1 = plan.partner("gather_b", b_z0, "y"), plan.partner("gather_b", b_z1, "x")
        a_in = gate(chain, "gate_a", a_z, a_y, a_x, a_xy)
        a_in = a_in + [plan.partner("gather_a", v, "core") for v in a_in]
        c_far = plan.partner("gather_c", c_pair, "z", 2)
    else:

        def whole(shard):
            down = lax.all_gather(shard.astype(BF16), "dp", axis=0, tiled=True)
            return lax.all_gather(down, "fsdp", axis=0, tiled=False)

        def padded(parts, full):
            both = jnp.concatenate(parts, axis=1)
            both = whole(jnp.pad(both, ((0, 0), (0, full - both.shape[1]))))
            return both.reshape(fsdp, *plan.split(), full)

        a_in = [padded([qkv_weight, vectors], a_full)]
        b_in = [padded([fc_weight, out_weight], b_full)]
        c_all = jnp.transpose(whole(proj_weight), (0, 2, 1))
        c_all = c_all.reshape(model, fsdp, 2, hidden // fsdp // 2)
        c_in = [jnp.transpose(c_all, (1, 2, 0, 3))]

    qkv, act_one, a_can, t_can, n_one, inv_one = front(chain, plan, me, tokens, a_in, wide)
    if plan.direct:
        b_p0, b_p1 = place_second(chain, "place_b2", plan, me, b_z0, b_r0, b_z1, b_r1)
        b_q0, b_q1 = plan.partner("gather_b", b_p0, "x"), plan.partner("gather_b", b_p1, "y")
        b_pc = [plan.partner("gather_b", v, "core") for v in (b_p0, b_p1)]
    if plan.direct:

        def place_c1(m):
            return [(0, ALL, [(0, (0,))]), (1, ALL, [(0, (1,))])]

        outs = [(2, *c_pair.shape)]
        (c_both,) = move(chain, "place_c1", me, [c_pair, c_far], outs, place_c1)
        c_near = plan.partner("gather_c", c_both, "z", 1)
    parts = [attend(chain, qkv, lengths, group) for group in third]
    if plan.direct:
        b_q0, b_q1 = gate(chain, "gate_b", b_q0, b_q1)
        b_qc = [plan.partner("gather_b", v, "core") for v in (b_q0, b_q1)]
        b_in = [b_p0, b_p1, b_q0, b_q1, *b_pc, *b_qc]
        chain.wait_for(*b_pc)

        def place_c2(m):
            found = [(0, (), 0), (2, (0,), 1), (1, (), 2), (2, (1,), 3)]
            return [
                (i, (*lead, 2 * h + p), [(h, (p, m.z ^ k)), (2, (h, p, m.z ^ k))])
                for i, lead, k in found
                for h in range(2)
                for p in range(2)
            ]

        outs = [(2, nz, chalf, plan.deep)] * 2 + [(2, 2, nz, chalf, plan.deep)]
        c_p0, c_p1, c_p = move(chain, "place_c2", me, [c_pair, c_far, c_near], outs, place_c2)
        c_q0, c_q1 = plan.partner("gather_c", c_p0, "x"), plan.partner("gather_c", c_p1, "y")
        c_pc = plan.partner("gather_c", c_p, "core")
    logs = [p[1] for p in parts]
    resid_two, act_two, wout, mixed, n_two, inv_two = join(
        chain, plan, me, cut, tokens, [p[0] for p in parts], b_in, t_can
    )
    if plan.direct:
        chain.wait_for(c_pc)
    gel, slope, b_can, g_b_proj, *g_c = mlp_up(
        chain, plan, me, act_two, cotangent, t_can, b_in, hidden
    )
    if plan.direct:
        c_q0, c_q1, away = gate(chain, "gate_c", c_q0, c_q1, g_c[1])
        c_in = [c_p, c_q0, c_q1, c_pc] + [plan.partner("gather_c", v, "core") for v in (c_q0, c_q1)]
        c_away = plan.partner("sum_c", away, "core")
    if plan.direct:
        c_parts = Parts([(g_c[0], [c_away])])
        c_f0, c_f1 = first_sums(chain, plan, "sum_c", me, c_parts)
    gpre, g_b_fc, c_can = mlp_down(chain, plan, me, cotangent, slope, c_in)

    gact, *g_b = mlp_back(chain, plan, me, act_two, gpre, b_can)
    if plan.direct:
        b_away = [plan.partner("sum_b", v, "core") for v in g_b[1:]]
    gresid, gmixed, inner, g_two, *g_o = join_back(
        chain, plan, me, gact, cotangent, n_two, inv_two, mixed, wout, t_can, b_full - model
    )
    if plan.direct:
        chain.wait_for(c_f0, c_f1)
        o_away = [plan.partner("sum_b", *gate(chain, "gate_o", g_o[1]), "core")]
        b_parts = Parts([(g_b[0], b_away), (g_o[0], o_away)])
    gparts = [attend_back(chain, qkv, gmixed, logs[0], inner, lengths, third[0])]
    if plan.direct:
        b_f0, b_f1 = first_sums(chain, plan, "sum_b", me, b_parts)

        def sums_cz(m):
            out = []
            for k in range(nz):
                z = m.z ^ k
                at = (0, m.x, z)
                terms = [(0, at), (1, at), (2, (z,))]
                t, ti = z_target(k, True)
                out.append((t, (*ti, slice(0, 2)), (2, chalf, plan.deep), terms))
                at = (1, ALL, z, m.y)
                terms = [(0, at), (1, at), (3, (ALL, z))]
                out.append((t, (*ti, slice(2, 4)), (2, chalf, plan.deep), terms))
            return out

        outs = z_outs((4, chalf, plan.deep), True)
        arrays = [g_c[0], c_away, c_f0, c_f1]
        c_u = add_up(chain, "sum_c2", me, arrays, outs, sums_cz)
        c_near = plan.partner("sum_c", c_u[1], "z", 1)
    for log, group in zip(logs[1:], third[1:]):
        gparts.append(attend_back(chain, qkv, gmixed, log, inner, lengths, group))
    kept = (n_one, inv_one, act_one, gparts, a_can, gresid, t_can, g_two, g_b_fc, g_b_proj)
    input_grad, *g_a = back(chain, plan, wide, a_full, me, *kept)

    if plan.direct:
        c_two = along_z(chain, plan, "sum_c4", me, c_u[2], c_near, (1,))
        c_z = [c_u[0], c_near, plan.partner("sum_c", c_two, "z", 2)]
        b_s0, b_s1 = second_sums(chain, plan, "sum_b", me, b_parts, b_f0, b_f1)
        a_away = [plan.partner("sum_a", v, "core") for v in gate(chain, "gate_s", *g_a[1:])]
        a_parts = Parts([(g_a[0], a_away)])
        a_f0, a_f1 = first_sums(chain, plan, "sum_a", me, a_parts)
        output = mlp_out(chain, plan, resid_two, gel, c_can, t_can)
        b_u = third_sums(chain, plan, "sum_b", me, b_parts, b_f0, b_f1, b_s0, b_s1, True)
        b_near = plan.partner("sum_b", b_u[1], "z", 1)
        a_s0, a_s1 = second_sums(chain, plan, "sum_a", me, a_parts, a_f0, a_f1)
        z_lead = ((), (0,), ())

        def sums_c3(m):
            block = (chalf, plan.deep)
            one = [(i, (*lead, m.other_y)) for i, lead in enumerate(z_lead)]
            two = [(i, (*lead, 2 + m.other_x)) for i, lead in enumerate(z_lead)]
            return [(0, ALL, block, one), (1, ALL, block, two)]

        outs = [sds((chalf, plan.deep), BF16)] * 2
        s0, s1 = add_up(chain, "sum_c3", me, c_z, outs, sums_c3)
        c_l0, c_l1 = plan.partner("sum_c", s0, "y"), plan.partner("sum_c", s1, "x")
        b_two = along_z(chain, plan, "sum_b4", me, b_u[2], b_near, (1,))
        b_z = [b_u[0], b_near, plan.partner("sum_b", b_two, "z", 2)]
        a_u = third_sums(chain, plan, "sum_a", me, a_parts, a_f0, a_f1, a_s0, a_s1, False)
        a_z = [a_u[0]] + [plan.partner("sum_a", a_u[k], "z", k) for k in range(1, nz)]

        def sums_c(m):
            block = (chalf, plan.deep)
            one = [(i, (*lead, m.y)) for i, lead in enumerate(z_lead)] + [(3, ALL)]
            two = [(i, (*lead, 2 + m.x)) for i, lead in enumerate(z_lead)] + [(4, ALL)]
            return [(0, ALL, block, one), (1, ALL, block, two)]

        state = preload(chain, state)

        def end_c(done, outs):
            outs[0][0:chalf, :] = done[0]
            outs[0][chalf:, :] = done[1]
            outs[1][...] = squared(*done)

        d_proj, s_c = add_up(
            chain,
            "end_c",
            me,
            [*c_z, c_l0, c_l1],
            [sds((plan.cols, plan.deep), F32), sds((1, 128), F32)],
            sums_c,
            end_c,
        )
        def last_b(m):
            shape = b_z[0].shape
            return [(0, ALL, shape, [(i, lead or ALL) for i, lead in enumerate(z_lead)])]

        def last_a(m):
            return [(0, ALL, a_z[0].shape, [(i, ALL) for i in range(nz)])]

        def end_b(done, outs):
            total = done[0]
            fc, out = total[:, :model], total[:, model : model + cut]
            outs[0][...] = fc
            outs[1][...] = out
            outs[2][...] = squared(fc, out)

        shapes = [fc_weight.shape, out_weight.shape, (1, 128)]
        d_fc, d_out, s_b = add_up(
            chain, "end_b", me, b_z, [sds(s, F32) for s in shapes], last_b, end_b
        )

        def end_a(done, outs):
            total = done[0]
            start = wide // 128 * 128
            vec = jnp.transpose(total[:, start:])[wide - start : wide - start + per]
            qkv = total[:, :wide]
            outs[0][...] = qkv
            outs[1][...] = vec
            outs[2][...] = squared(qkv, vec)

        shapes = [qkv_weight.shape, (per, rows), (1, 128)]
        d_qkv, d_vec, s_a = add_up(
            chain, "end_a", me, a_z, [sds(s, F32) for s in shapes], last_a, end_a
        )
        squares = s_a + s_b + s_c
    else:
        output = mlp_out(chain, plan, resid_two, gel, c_can, t_can)

        def shared(value):
            mine = lax.psum_scatter(value, "fsdp", scatter_dimension=0, tiled=False)
            return lax.psum_scatter(mine, "dp", scatter_dimension=0, tiled=True).astype(F32)

        d_a = shared(g_a[0].reshape(fsdp, model, a_full))
        d_qkv, d_vec = d_a[:, :wide], turned(d_a[:, wide : wide + per])
        d_out = shared(jnp.transpose(g_o[0].reshape(model, fsdp, cut), (1, 0, 2)))
        d_fc = shared(g_b[0].reshape(fsdp, model, model))
        d_c = jnp.transpose(g_c[0], (2, 0, 1, 3)).reshape(fsdp, plan.cols, hidden)
        d_proj = turned(shared(jnp.transpose(d_c, (0, 2, 1))))
        total = sum(jnp.sum(d * d) for d in (d_qkv, d_out, d_fc, d_proj, d_vec))
        squares = jnp.full((1, 128), total)

    sent = jnp.broadcast_to(squares[None], (dp * fsdp, 1, 128))
    with jax.named_scope("norm"):
        norms = lax.all_to_all(sent, ("dp", "fsdp"), 0, 0, tiled=True).reshape(dp * fsdp, 128)
    norm, *new = update(
        chain, norms, state[:5], (d_qkv, d_out, d_fc, d_proj, d_vec), state[5:10], state[10:]
    )
    new = [turned(v) if i % 5 in (3, 4) else v for i, v in enumerate(new)]
    return (output, input_grad, norm[0, 0], *new)


def solution(mesh):
    tokens = P(("dp", "fsdp"), None)
    table = P("dp", "fsdp")
    return jax.shard_map(
        body,
        mesh=mesh,
        in_specs=(tokens, P(("dp", "fsdp")), tokens) + (table,) * 15,
        out_specs=(tokens, tokens, P()) + (table,) * 15,
        check_vma=False,
    )
```

```python
import functools

import jax
import jax.numpy as jnp
from jax import lax
from jax.experimental import pallas as pl
from jax.experimental.pallas import tpu as pltpu
from jax.sharding import PartitionSpec as P

HEAD_DIM = 64
STEP = 10

beta_one = 0.9
beta_two = 0.95
clip_limit = 1.0
rate_matrix = 0.1
rate_vector = 1.0
decay_matrix = 0.1
gelu_coeff = 0.7978845608028654
cubic_coeff = 0.044715
neg_large = -1e30
VEC_ROWS = 16

F32 = jnp.float32
BF16 = jnp.bfloat16
VMEM = pl.BlockSpec(memory_space=pltpu.VMEM)
HELD = pl.BlockSpec(memory_space=pltpu.VMEM)
ANY = pl.BlockSpec(memory_space=pl.ANY)
HBM = pl.BlockSpec(memory_space=pltpu.HBM)
SMEM = pl.BlockSpec(memory_space=pltpu.SMEM)
ALL = slice(None)


def dot_nn(a, b):
    return lax.dot_general(a, b, (((1,), (0,)), ((), ())), preferred_element_type=F32)


def dot_nt(a, b):
    return lax.dot_general(a, b, (((1,), (1,)), ((), ())), preferred_element_type=F32)


def dot_tn(a, b):
    return lax.dot_general(a, b, (((0,), (0,)), ((), ())), preferred_element_type=F32)


def sds(shape, dtype):
    return jax.ShapeDtypeStruct(shape, dtype)


class Chain:
    def __init__(self):
        self.waits = []

    def wait_for(self, *arrays):
        self.waits += arrays

    def call(self, name, body, ins, in_specs, outs, out_specs, scratch, limit, aliases=None):
        several = isinstance(outs, (tuple, list))
        if not several:
            outs, out_specs = (outs,), (out_specs,)
        n_in, extra, n_out = len(ins), len(self.waits), len(outs)
        pins = ((HELD, pltpu.VMEM), (HBM, pltpu.HBM))

        def run(*refs):
            given, refs = refs[:n_in], refs[n_in + extra :]
            refs[n_out][...] = jnp.zeros(refs[n_out].shape, F32)
            body(*given, *refs[:n_out], *refs[n_out + 1 :])

        placed, made = [], []
        for v, spec in zip(ins, in_specs):
            for pin, space in pins:
                if spec is pin:
                    v = pltpu.with_memory_space_constraint(v, space)
            placed.append(v)
        for o, spec in zip(outs, out_specs):
            for pin, space in pins:
                if spec is pin:
                    o = space(o.shape, o.dtype)
            made.append(o)
        results = pl.pallas_call(
            run,
            name=name,
            input_output_aliases=aliases or {},
            out_shape=(*made, pltpu.VMEM((8, 128), F32)),
            in_specs=[*in_specs, *[ANY] * extra],
            out_specs=(*out_specs, HELD),
            scratch_shapes=scratch,
            compiler_params=pltpu.CompilerParams(vmem_limit_bytes=limit << 20),
        )(*placed, *self.waits)
        *results, token = results
        self.waits = [pltpu.with_memory_space_constraint(token, pltpu.VMEM)]
        return results if several else results[0]


class Plan:
    def __init__(self, dp, fsdp, model, hidden):
        self.dp, self.fsdp = dp, fsdp
        self.nz, self.nx = dp // 2, fsdp // 2
        self.rows = model // dp
        self.cols = model // fsdp
        self.deep = hidden // dp
        self.direct = (
            dp == 2 * fsdp
            and fsdp % 2 == 0
            and self.rows % 32 == 0
            and self.cols % 32 == 0
            and self.deep % 128 == 0
            and hidden == fsdp * model
            and dp == 8
        )

    def partner(self, name, value, stage, k=1):
        axis, step = {"x": ("fsdp", 2), "y": ("dp", 1), "z": ("dp", 2), "core": ("fsdp", 1)}[stage]
        n = self.dp if axis == "dp" else self.fsdp
        with jax.named_scope(f"{name}_{stage}"):
            return lax.ppermute(value, axis, [(i, i ^ (step * k)) for i in range(n)])

    def opposite(self, name, value):
        n = self.fsdp
        pairs = [(i * n + j, (i ^ 1) * n + (j ^ 2)) for i in range(self.dp) for j in range(n)]
        with jax.named_scope(f"{name}_xy"):
            return lax.ppermute(value, ("dp", "fsdp"), pairs)

    def gather_z(self, name, value):
        near, far = self.partner(name, value, "z", 1), self.partner(name, value, "z", 2)
        return [near, far, self.partner(name, far, "z", 1)]

    def split(self):
        return (self.nz, 2, 2, self.rows // 2) if self.direct else (1, 1, 1, self.rows * self.dp)


class Me:
    def __init__(self, ref):
        self.z, self.y, self.x, self.core = ref[0], ref[1], ref[2], ref[3]
        self.other_y, self.other_x = 1 - self.y, 1 - self.x

    def fsdp(self, x, away):
        return 2 * x + (self.core ^ away)


def move(chain, name, me, arrays, outs, copies):
    n = len(arrays)

    def body(me_ref, *refs):
        for s, si, targets in copies(Me(me_ref)):
            value = refs[s][si]
            for t, ti in targets:
                refs[n + t][ti] = value

    return chain.call(
        name,
        body,
        (me, *arrays),
        [SMEM] + [VMEM] * n,
        tuple(sds(s, BF16) for s in outs),
        (HELD,) * len(outs),
        [],
        6,
    )


def gate(chain, name, *arrays, far=0):
    specs = [ANY] * (len(arrays) - far) + [HBM] * far
    return chain.call(
        name,
        lambda *refs: None,
        arrays,
        specs,
        tuple(sds(v.shape, v.dtype) for v in arrays),
        tuple(specs),
        [],
        1,
        {i: i for i in range(len(arrays))},
    )


def add_up(chain, name, me, arrays, outs, sums, after=None, far=0):
    n, m = len(arrays), len(outs)
    still = sums(Me([0, 0, 0, 0]))
    loaded = [shape for _, _, shape, parts in still for s, _ in parts if s < far]

    def body(me_ref, *refs):
        ins, outs_, refs = refs[:n], refs[n : n + m], refs[n + m :]
        held, sem = refs[: len(loaded)], refs[len(loaded) :]
        todo, i = [], 0
        for t, ti, shape, parts in sums(Me(me_ref)):
            group = []
            for s, si in parts:
                copy = None
                if s < far:
                    copy = pltpu.make_async_copy(ins[s].at[si], held[i], sem[0].at[i])
                    copy.start()
                    i += 1
                group.append((copy, s, si, i - 1))
            todo.append((t, ti, group))
        done = []
        for t, ti, group in todo:
            total = None
            for copy, s, si, k in reversed(group):
                if copy is not None:
                    copy.wait()
                v = (ins[s][si] if copy is None else held[k][...]).astype(F32)
                total = v if total is None else total + v
            if after is None:
                outs_[t][ti] = total.astype(outs_[t].dtype)
            else:
                done.append(total)
        if after is not None:
            after(done, outs_)

    return chain.call(
        name,
        body,
        (me, *arrays),
        [SMEM] + [HBM if i < far else VMEM for i in range(n)],
        tuple(outs),
        (HELD if after is None else VMEM,) * m,
        [pltpu.VMEM(shape, BF16) for shape in loaded]
        + ([pltpu.SemaphoreType.DMA((len(loaded),))] if loaded else []),
        8,
    )


def pack_body(ins, outs, held, sem):
    todo = [pltpu.make_async_copy(i, h, sem.at[k]) for k, (i, h) in enumerate(zip(ins, held))]
    for c in todo:
        c.start()
    for c in todo:
        c.wait()
    qkv, out, fc, proj, vec = (h[...] for h in held)
    a, b, c = outs
    wide, model = qkv.shape[1], fc.shape[1]
    columns = jnp.transpose(vec)
    start = wide // 128 * 128
    a[:, start:] = jnp.zeros((a.shape[0], a.shape[1] - start), BF16)
    a[:, 0:wide] = qkv.astype(BF16)
    a[:, wide : wide + columns.shape[1]] = columns.astype(BF16)
    b[:, model:] = jnp.zeros((b.shape[0], b.shape[1] - model), BF16)
    b[:, 0:model] = fc.astype(BF16)
    b[:, model : model + out.shape[1]] = out.astype(BF16)
    c[...] = proj.astype(BF16).reshape(c.shape)


def pack(chain, plan, weights, a_full, b_full):
    count = len(weights)

    def run(*refs):
        pack_body(refs[:count], refs[count : count + 3], refs[count + 3 : -1], refs[-1])

    return chain.call(
        "pack",
        run,
        weights,
        [HBM] * count,
        (
            sds((plan.rows, a_full), BF16),
            sds((plan.rows, b_full), BF16),
            sds((2, plan.cols // 2, plan.deep), BF16),
        ),
        (VMEM,) * 3,
        [pltpu.VMEM(w.shape, F32) for w in weights] + [pltpu.SemaphoreType.DMA((count,))],
        6,
    )


def normed(values):
    mean = jnp.mean(values, axis=-1, keepdims=True)
    centred = values - mean
    spread = jnp.mean(centred * centred, axis=-1, keepdims=True)
    inverse = lax.rsqrt(spread + 1e-05)
    return centred * inverse, inverse


def norm_back(grad_hidden, n, inverse, gain):
    g = grad_hidden * gain
    mean_plain = jnp.mean(g, axis=-1, keepdims=True)
    mean_cross = jnp.mean(g * n, axis=-1, keepdims=True)
    return inverse * (g - mean_plain - n * mean_cross)


class Table:
    def __init__(self, fsdp):
        self.per = 12 // fsdp

    def row(self, k):
        return (k // self.per) * VEC_ROWS + k % self.per

    def get(self, ref, k):
        r = self.row(k)
        return ref[r : r + 1, :]


def spread_matrix(rows, model, d):
    r = lax.broadcasted_iota(jnp.int32, (128, model), 0)
    c = lax.broadcasted_iota(jnp.int32, (128, model), 1)
    return ((c == r + d * rows) & (r < rows)).astype(BF16)


def halves(ins, away):
    n = len(ins) // 2
    part = ins[n * away : n * away + n]
    own = (part[0].at[0], part[0].at[1]) if n == 3 else part[:2]
    return (*own, *part[-2:])


def table_loads(plan, me, ins):
    for away in range(2):
        p0, p1, r0, r1 = halves(ins, away)
        for y in range(2):
            for x, ref in ((me.x, p0), (me.other_x, r0)):
                yield ref, (y,), me.fsdp(x, away), (ALL, y), 0
        for y, ref in ((me.y, p1), (me.other_y, r1)):
            for x in range(plan.nx):
                yield ref, (x,), me.fsdp(x, away), (ALL, y), 1


def front_body(plan, wide, n_in, me_ref, tokens, *refs):
    ins = refs[:n_in]
    qkv, act, a_out, t_out, n_out, inv_out = refs[n_in : n_in + 6]
    a_v, flat, sem, out_sem = refs[n_in + 6 :]
    fsdp = plan.fsdp
    full = a_v.shape[-1]
    model = tokens.shape[1]
    table = Table(fsdp)
    if plan.direct:
        me = Me(me_ref)
        for i, ref in enumerate(ins):
            away, x, y = i // 4, i // 2 % 2, i % 2
            f = me.fsdp(me.x ^ x, away)
            pltpu.make_async_copy(ref, a_v.at[f, :, me.y ^ y], sem.at[f]).start()
    else:
        for f in range(fsdp):
            pltpu.make_async_copy(ins[0].at[f], a_v.at[f], sem.at[f]).start()
    n, inverse = normed(tokens[...].astype(F32))
    n_out[...] = n
    inv_out[...] = jnp.broadcast_to(inverse, inv_out.shape)
    start = wide // 128 * 128
    for f in range(fsdp):
        pltpu.make_async_copy(a_v.at[f], a_v.at[f], sem.at[f]).wait()
        block = a_v[f].reshape(model, full)
        flat[:, f * wide : (f + 1) * wide] = block[:, :wide]
        turned = jnp.transpose(block[:, start:].astype(F32))
        t_out[f * VEC_ROWS : f * VEC_ROWS + table.per, :] = turned[
            wide - start : wide - start + table.per
        ]
    copy = pltpu.make_async_copy(flat, a_out, out_sem)
    copy.start()
    act[...] = (n * table.get(t_out, 0) + table.get(t_out, 1)).astype(BF16)
    for which in range(3):
        r = dot_nn(act[...], flat[:, which * model : (which + 1) * model])
        if which != 1:
            r = r + table.get(t_out, 4 + which // 2)
        qkv[which] = r.astype(BF16)
    copy.wait()


def front(chain, plan, me, tokens, pieces, wide):
    t, model = tokens.shape
    fsdp = plan.fsdp
    full = pieces[0].shape[-1]
    lead = (fsdp, plan.nz, 2, plan.rows, full) if plan.direct else pieces[0].shape
    return chain.call(
        "front",
        functools.partial(front_body, plan, wide, len(pieces)),
        (me, tokens, *pieces),
        [SMEM, VMEM] + [ANY] * len(pieces),
        (
            sds((3, t, model), BF16),
            sds((t, model), BF16),
            sds((model, 3 * model), BF16),
            sds((fsdp * VEC_ROWS, model), F32),
            sds((t, model), F32),
            sds((t, 128), F32),
        ),
        (HELD, HELD, HBM, HELD, HELD, HELD),
        [
            pltpu.VMEM(lead, BF16),
            pltpu.VMEM((model, 3 * model), BF16),
            pltpu.SemaphoreType.DMA((fsdp,)),
            pltpu.SemaphoreType.DMA,
        ],
        16,
    )


def masks(length, lo, size, keys):
    q = lax.broadcasted_iota(jnp.int32, (size, 1), 0) + lo
    limit = jnp.minimum(q, length - 1)
    k = lax.broadcasted_iota(jnp.int32, (size, keys), 1)
    return k <= limit


QBLOCK = 256


def attend_body(heads, length_ref, qkv, mixed, logs):
    t = mixed.shape[0]
    length = length_ref[0]
    scale = HEAD_DIM**-0.5

    def part(h, which):
        return qkv[which, :, h * HEAD_DIM : (h + 1) * HEAD_DIM]

    for i, h in enumerate(heads):
        q = part(h, 0) * jnp.asarray(scale, BF16)
        k, v = part(h, 1), part(h, 2)
        for lo in range(0, t, QBLOCK):
            n = lo + QBLOCK
            s = dot_nt(q[lo:n], k[:n])
            s = jnp.where(masks(length, lo, QBLOCK, n), s, neg_large)
            top = jnp.max(s, axis=-1, keepdims=True)
            e = jnp.exp(s - top)
            total = jnp.sum(e, axis=-1, keepdims=True)
            p = (e * (1.0 / total)).astype(BF16)
            o = dot_nn(p, v[:n])
            mixed[lo:n, i * HEAD_DIM : (i + 1) * HEAD_DIM] = o.astype(BF16)
            logs[lo:n, i : i + 1] = top + jnp.log(total)


def attend(chain, qkv, length, heads):
    t = qkv.shape[1]
    return chain.call(
        "attend",
        functools.partial(attend_body, heads),
        (length, qkv),
        [SMEM, HELD],
        (sds((t, len(heads) * HEAD_DIM), BF16), sds((t, 128), F32)),
        (HELD, HELD),
        [],
        6,
    )


def join_body(plan, cut, n_in, n_mixed, me_ref, tokens, t_in, *refs):
    ins, refs = refs[:n_in], refs[n_in:]
    parts, (resid, act, wout, mixed, n_out, inv_out, o_v, sem) = refs[:n_mixed], refs[n_mixed:]
    model = tokens.shape[1]
    fsdp = plan.fsdp
    table = Table(fsdp)
    lanes = pl.ds(model, o_v.shape[-1])
    if plan.direct:
        for ref, si, f, ti, h in table_loads(plan, Me(me_ref), ins):
            src = ref.at[(*si, ALL, ALL, lanes)]
            pltpu.make_async_copy(src, o_v.at[(f, *ti, h)], sem).start()
    else:
        for f in range(fsdp):
            src = ins[0].at[(f, ALL, ALL, ALL, ALL, lanes)]
            pltpu.make_async_copy(src, o_v.at[f], sem).start()
    at = 0
    for p in parts:
        mixed[:, at : at + p.shape[1]] = p[...]
        at += p.shape[1]
    pltpu.make_async_copy(o_v, o_v, sem).wait()
    for f in range(fsdp):
        wout[:, f * cut : (f + 1) * cut] = o_v[f].reshape(model, o_v.shape[-1])[:, :cut]
    r = tokens[...].astype(F32) + dot_nn(mixed[...], wout[...]) + table.get(t_in, 6)
    resid[...] = r
    n, inverse = normed(r)
    n_out[...] = n
    inv_out[...] = jnp.broadcast_to(inverse, inv_out.shape)
    act[...] = (n * table.get(t_in, 2) + table.get(t_in, 3)).astype(BF16)


def join(chain, plan, me, cut, tokens, parts, pieces, t_can):
    t, model = tokens.shape
    spare = pieces[0].shape[-1] - model
    return chain.call(
        "join",
        functools.partial(join_body, plan, cut, len(pieces), len(parts)),
        (me, tokens, t_can, *pieces, *parts),
        [SMEM, VMEM, HELD] + [ANY] * len(pieces) + [HELD] * len(parts),
        (
            sds((t, model), F32),
            sds((t, model), BF16),
            sds((model, model), BF16),
            sds((t, model), BF16),
            sds((t, model), F32),
            sds((t, 128), F32),
        ),
        (HELD,) * 6,
        [pltpu.VMEM((plan.fsdp, *plan.split(), spare), BF16), pltpu.SemaphoreType.DMA],
        10,
    )


def gelu_and_slope(pre):
    square = pre * pre
    th = jnp.tanh(pre * (gelu_coeff + (gelu_coeff * cubic_coeff) * square))
    plus = 0.5 * th + 0.5
    bend = 0.5 * gelu_coeff + (1.5 * gelu_coeff * cubic_coeff) * square
    return (pre * plus).astype(BF16), plus + pre * (1.0 - th * th) * bend


def mlp_up_body(plan, n_in, n_out, me_ref, act, cot, t_in, *refs):
    ins, refs = refs[:n_in], refs[n_in:]
    gel_out, slope_out, b_v, g_b_proj = refs[:4]
    gouts, refs = refs[4 : 4 + n_out], refs[4 + n_out :]
    gp_v, sem = refs
    fsdp, half = plan.fsdp, plan.cols // 2
    t, model = act.shape
    deep = gp_v.shape[-1]
    per = Table(fsdp).per
    me = Me(me_ref)
    order = []
    for k in range(fsdp):
        if plan.direct:
            away, x = k // 2, me.x if k % 2 == 0 else me.other_x
            p0, p1, r0, r1 = halves(ins, away)
            f = me.fsdp(x, away)
            own = p0 if k % 2 == 0 else r0
            loads = [(own.at[y], y, 0) for y in range(2)]
            loads += [(p1.at[x], me.y, 1), (r1.at[x], me.other_y, 1)]
            for ref, y, h in loads:
                src = ref.at[:, :, pl.ds(0, model)]
                pltpu.make_async_copy(src, b_v.at[f, :, y, h], sem.at[k]).start()
        else:
            f = k
            src = ins[0].at[(f, ALL, ALL, ALL, ALL, pl.ds(0, model))]
            pltpu.make_async_copy(src, b_v.at[f], sem.at[k]).start()
        order.append(f)
    g_b_proj[...] = jnp.sum(cot[...].astype(F32), axis=0, keepdims=True)

    def up(k, lo, hi):
        row = 8 + order[k]
        bias = t_in[pl.ds(row // per * VEC_ROWS + row % per, 1), :]
        return dot_nn(act[lo:hi], b_v[order[k]].reshape(model, model)) + bias

    step = t // 2
    for k in range(fsdp):
        pltpu.make_async_copy(b_v.at[order[k]], b_v.at[order[k]], sem.at[k]).wait()
        lanes = pl.ds(pl.multiple_of(order[k] * model, model), model)
        for lo in range(0, t, step):
            gel, slope = gelu_and_slope(up(k, lo, lo + step))
            gel_out[lo : lo + step, lanes] = gel
            slope_out[lo : lo + step, lanes] = slope
        grad = dot_tn(cot[...], gel_out[:, lanes]).astype(BF16)
        if not plan.direct:
            gouts[0][k, 0], gouts[0][k, 1] = grad[:, :deep], grad[:, deep:]
            continue
        gp_v[0], gp_v[1] = grad[:, :deep], grad[:, deep:]
        for away in range(2):
            for x in range(plan.nx):
                for h in range(2):
                    row = me.fsdp(x, away) * plan.cols + h * half
                    part = gp_v[:, pl.ds(pl.multiple_of(row, 16), half), :]
                    gouts[away][h, x, pl.ds(order[k], 1)] = part[None]


def mlp_up(chain, plan, me, act, cot, t_can, pieces, hidden):
    t, model = act.shape
    fsdp = plan.fsdp
    per = hidden // fsdp // 2
    if plan.direct:
        grads = [sds((2, plan.nx, plan.nz, 2, plan.cols // 2, plan.deep), BF16)] * 2
    else:
        grads = [sds((fsdp, 2, model, per), BF16)]
    lead = (fsdp, *plan.split(), model)
    return chain.call(
        "mlp_up",
        functools.partial(mlp_up_body, plan, len(pieces), len(grads)),
        (me, act, cot, t_can, *pieces),
        [SMEM, HELD, VMEM, HELD] + [ANY] * len(pieces),
        (
            sds((t, hidden), BF16),
            sds((t, hidden), F32),
            sds(lead, BF16),
            sds((1, model), F32),
            *grads,
        ),
        (HELD,) * (4 + len(grads)),
        [
            pltpu.VMEM((2, model, per), BF16),
            pltpu.SemaphoreType.DMA((fsdp,)),
        ],
        18,
    )


def mlp_down_body(plan, n_in, me_ref, cot, slope, *refs):
    ins, refs = refs[:n_in], refs[n_in:]
    gpre, g_b_fc, c_v = refs
    half = plan.cols // 2
    model = cot.shape[1]
    if plan.direct:
        for ref, si, f, ti, h in table_loads(plan, Me(me_ref), ins):
            rows = pl.ds(pl.multiple_of(f * plan.cols + h * half, 16), half)
            c_v[(*ti, rows)] = ref[si]
    else:
        c_v[...] = ins[0][...]
    for j in range(plan.fsdp):
        lanes = slice(j * model, (j + 1) * model)
        down = jnp.concatenate([c_v[j, 0], c_v[j, 1]], axis=1)
        low = (dot_nn(cot[...], down) * slope[:, lanes]).astype(BF16)
        gpre[:, lanes] = low
        g_b_fc[j : j + 1, :] = jnp.sum(low.astype(F32), axis=0, keepdims=True)


def mlp_down(chain, plan, me, cot, slope, pieces):
    t, model = cot.shape
    fsdp, hidden = plan.fsdp, slope.shape[1]
    return chain.call(
        "mlp_down",
        functools.partial(mlp_down_body, plan, len(pieces)),
        (me, cot, slope, *pieces),
        [SMEM, VMEM, HELD] + [VMEM] * len(pieces),
        (
            sds((t, hidden), BF16),
            sds((fsdp, model), F32),
            sds((fsdp, 2, model, hidden // fsdp // 2), BF16),
        ),
        (HELD,) * 3,
        [],
        10,
    )


def mlp_out_body(table, resid, gel, c_v, t_in, output):
    model = resid.shape[1]
    total = resid[...] + table.get(t_in, 7)
    for j in range(c_v.shape[0]):
        down = jnp.concatenate([c_v[j, 0], c_v[j, 1]], axis=1)
        total = total + dot_nt(gel[:, j * model : (j + 1) * model], down)
    output[...] = total.astype(BF16)


def mlp_out(chain, plan, resid, gel, c_can, t_can):
    return chain.call(
        "mlp_out",
        functools.partial(mlp_out_body, Table(plan.fsdp)),
        (resid, gel, c_can, t_can),
        [HELD] * 4,
        sds(resid.shape, BF16),
        VMEM,
        [],
        10,
    )


def mlp_back_body(plan, n_out, me_ref, act, gpre, b_in, *refs):
    gact = refs[0]
    gouts = refs[1 : 1 + n_out]
    model = act.shape[1]
    me = Me(me_ref)
    first = True
    order = [
        (x, away, me.fsdp(x, away) if plan.direct else 2 * x + away)
        for away in range(2)
        for x in range(plan.nx)
    ]
    for x, away, f in order:
        part = gpre[:, pl.ds(pl.multiple_of(f * model, model), model)]
        grad = dot_tn(act[...], part).astype(BF16).reshape(b_in.shape[1:])
        if not plan.direct:
            gouts[0][f] = grad
        elif away:
            gouts[1][x], gouts[2][x] = grad[:, :, 0], grad[:, :, 1]
        else:
            gouts[0][0, x], gouts[0][1, x] = grad[:, :, 0], grad[:, :, 1]
        back = dot_nt(part, b_in[f].reshape(model, model))
        if first:
            gact[...] = back
        else:
            gact[...] += back
        first = False


def mlp_back(chain, plan, me, act, gpre, b_can):
    t, model = act.shape
    fsdp = plan.fsdp
    lead = (fsdp, *plan.split(), model)
    if plan.direct:
        one = (plan.nx, plan.nz, 2, plan.rows // 2, model)
        grads = [sds((2, *one), BF16), sds(one, BF16), sds(one, BF16)]
    else:
        grads = [sds(lead, BF16)]
    return chain.call(
        "mlp_back",
        functools.partial(mlp_back_body, plan, len(grads)),
        (me, act, gpre, b_can),
        [SMEM, HELD, HELD, HELD],
        (sds((t, model), F32), *grads),
        (HELD,) + (HELD,) * len(grads),
        [],
        10,
    )


def join_back_body(plan, me_ref, gact, cot, normal, inverse_in, mixed, wout, t_in, *refs):
    gresid, gmixed, inner, g_vec, *gouts = refs[:-1]
    o_v = refs[-1]
    model = cot.shape[1]
    table = Table(plan.fsdp)
    n, inverse = normal[...], inverse_in[:, 0:1]
    e = gact[...]
    g_vec[...] = jnp.zeros(g_vec.shape, F32)
    g_vec[0:1, :] = jnp.sum(e * n, axis=0, keepdims=True)
    g_vec[1:2, :] = jnp.sum(e, axis=0, keepdims=True)
    r = cot[...].astype(F32) + norm_back(e, n, inverse, table.get(t_in, 2))
    gresid[...] = r
    branch = r.astype(BF16)
    g_vec[2:3, :] = jnp.sum(branch.astype(F32), axis=0, keepdims=True)
    grad = dot_tn(mixed[...], branch).astype(BF16)
    if plan.direct:
        me = Me(me_ref)
        cut = plan.cols
        for f in range(plan.fsdp):
            o_v[f, :, 0:cut] = grad[:, f * cut : (f + 1) * cut]
            o_v[f, :, cut:] = jnp.zeros((model, o_v.shape[-1] - cut), BF16)
        for away in range(2):
            for x in range(plan.nx):
                part = o_v[me.fsdp(x, away)].reshape(*plan.split(), o_v.shape[-1])
                gouts[away][0, x], gouts[away][1, x] = part[:, :, 0], part[:, :, 1]
    else:
        gouts[0][...] = grad
    low = dot_nt(branch, wout[...]).astype(BF16)
    gmixed[...] = low
    product = low.astype(F32) * mixed[...].astype(F32)
    high = product.astype(BF16)
    rest = (product - high.astype(F32)).astype(BF16)
    head = lax.broadcasted_iota(jnp.int32, (model, 128), 0) // HEAD_DIM
    ones = (head == lax.broadcasted_iota(jnp.int32, (model, 128), 1)).astype(BF16)
    inner[...] = dot_nn(high, ones) + dot_nn(rest, ones)


def join_back(chain, plan, me, gact, cot, normal, inverse, mixed, wout, t_can, spare):
    t, model = cot.shape
    ins = [me, gact, cot, normal, inverse, mixed, wout, t_can]
    if plan.direct:
        grads = [sds((2, plan.nx, plan.nz, 2, plan.rows // 2, spare), BF16)] * 2
        grad_specs = [HELD] * 2
    else:
        grads, grad_specs = [sds((model, model), BF16)], [VMEM]
    return chain.call(
        "join_back",
        functools.partial(join_back_body, plan),
        ins,
        [SMEM, HELD, VMEM] + [HELD] * 5,
        (
            sds((t, model), F32),
            sds((t, model), BF16),
            sds((t, 128), F32),
            sds((8, model), F32),
            *grads,
        ),
        (HELD, HELD, HELD, HELD, *grad_specs),
        [pltpu.VMEM((plan.fsdp, model, spare), BF16)],
        14,
    )


def attend_back_body(heads, length_ref, qkv, gmixed, logs, inner, out):
    t = gmixed.shape[0]
    length = length_ref[0]
    scale = HEAD_DIM**-0.5

    def part(h, which):
        return qkv[which, :, h * HEAD_DIM : (h + 1) * HEAD_DIM]

    for i, h in enumerate(heads):
        lanes = slice(i * HEAD_DIM, (i + 1) * HEAD_DIM)
        q = part(h, 0)
        small = q * jnp.asarray(scale, BF16)
        k, v = part(h, 1), part(h, 2)
        go = gmixed[:, h * HEAD_DIM : (h + 1) * HEAD_DIM]
        gk, gv = [], []
        for lo in range(0, t, QBLOCK):
            n = lo + QBLOCK
            s = dot_nt(small[lo:n], k[:n])
            s = jnp.where(masks(length, lo, QBLOCK, n), s, neg_large)
            p = jnp.exp(s - logs[lo:n, i : i + 1])
            gp = dot_nt(go[lo:n], v[:n])
            ds = (p * (gp - inner[lo:n, h : h + 1])).astype(BF16)
            out[0, lo:n, lanes] = (dot_nn(ds, k[:n]) * scale).astype(BF16)
            gv.append(dot_tn(p.astype(BF16), go[lo:n]))
            gk.append(dot_tn(ds, small[lo:n]))
        for b in range(t // QBLOCK):
            rows = slice(b * QBLOCK, (b + 1) * QBLOCK)
            out[1, rows, lanes] = sum(x[rows] for x in gk[b:]).astype(BF16)
            out[2, rows, lanes] = sum(x[rows] for x in gv[b:]).astype(BF16)


def attend_back(chain, qkv, gmixed, logs, inner, length, heads):
    t = qkv.shape[1]
    return chain.call(
        "attend_back",
        functools.partial(attend_back_body, heads),
        (length, qkv, gmixed, logs, inner),
        [SMEM, HELD, HELD, HELD, HELD],
        sds((3, t, len(heads) * HEAD_DIM), BF16),
        HELD,
        [],
        8,
    )


def whole_qkv(parts, flat, blocks):
    wide = blocks.shape[2]
    model = flat.shape[1] // 3
    at = 0
    for p in parts:
        size = p.shape[2]
        for which in range(3):
            lo = which * model + at
            flat[:, lo : lo + size] = p[which]
        at += size
    for f in range(blocks.shape[0]):
        blocks[f] = flat[:, f * wide : (f + 1) * wide]


def back_body(plan, wide, n_parts, n_out, me_ref, normal, inverse_in, act, a_in, gresid, t_in, g_two, g_b_fc, g_b_proj, *refs):
    parts, refs = refs[:n_parts], refs[n_parts:]
    input_grad, gouts, refs = refs[0], refs[1 : 1 + n_out], refs[1 + n_out :]
    flat, gq_v, tab, a_v, in_sem = refs
    late = pltpu.make_async_copy(a_in, a_v, in_sem)
    late.start()
    fsdp = plan.fsdp
    t, model = normal.shape
    table = Table(fsdp)
    spare = tab.shape[0] // fsdp
    whole_qkv(parts, flat, gq_v)
    me = Me(me_ref)

    def each():
        for away in range(2):
            for x in range(plan.nx):
                if plan.direct:
                    ends = [gouts[1 + h].at[x] if away else gouts[0].at[h, x] for h in range(2)]
                    yield me.fsdp(x, away), ends
                else:
                    yield 2 * x + away, [gouts[0].at[2 * x + away, :, :, h] for h in range(1)]

    for f, ends in each():
        grad = dot_tn(act[...], gq_v[f]).astype(BF16).reshape(*plan.split(), wide)
        for h, end in enumerate(ends):
            end[:, :, :, 0:wide] = grad[:, :, h]
    late.wait()
    back = dot_nt(flat[...], a_v[...])
    sums = dot_nn(jnp.ones((8, t), BF16), flat[...])
    n, inverse = normal[...], inverse_in[:, 0:1]
    tab[...] = jnp.zeros(tab.shape, F32)

    def put(k, value):
        r = (k // table.per) * spare + k % table.per
        tab[r : r + 1, :] = value

    put(0, jnp.sum(back * n, axis=0, keepdims=True))
    put(1, jnp.sum(back, axis=0, keepdims=True))
    put(2, g_two[0:1, :])
    put(3, g_two[1:2, :])
    put(4, sums[0:1, 0:model])
    put(5, sums[0:1, 2 * model :])
    put(6, g_two[2:3, :])
    put(7, g_b_proj[...])
    for j in range(fsdp):
        put(8 + j, g_b_fc[j : j + 1, :])
    for f, ends in each():
        rows = pl.ds(pl.multiple_of(f * spare, 8), spare)
        columns = jnp.transpose(tab[rows, :]).astype(BF16).reshape(*plan.split(), spare)
        for h, end in enumerate(ends):
            end[:, :, :, wide:] = columns[:, :, h]
    r = gresid[...] + norm_back(back, n, inverse, table.get(t_in, 0))
    input_grad[...] = r.astype(BF16)


def back(
    chain, plan, wide, full, me, normal, inverse, act, parts, a_can, gresid, t_can, g_two, g_b_fc, g_b_proj
):
    t, model = normal.shape
    fsdp = plan.fsdp
    lead = (fsdp, *plan.split(), full)
    if plan.direct:
        one = (plan.nx, plan.nz, 2, plan.rows // 2, full)
        grads = [sds((2, *one), BF16), sds(one, BF16), sds(one, BF16)]
    else:
        grads = [sds(lead, BF16)]
    return chain.call(
        "back",
        functools.partial(back_body, plan, wide, len(parts), len(grads)),
        (me, normal, inverse, act, a_can, gresid, t_can, g_two, g_b_fc, g_b_proj, *parts),
        [SMEM, HELD, HELD, HELD, HBM] + [HELD] * (5 + len(parts)),
        (sds((t, model), BF16), *grads),
        (VMEM,) + (HELD,) * len(grads),
        [
            pltpu.VMEM((t, 3 * model), BF16),
            pltpu.VMEM((fsdp, t, wide), BF16),
            pltpu.VMEM((fsdp * (full - wide), model), F32),
            pltpu.VMEM(a_can.shape, BF16),
            pltpu.SemaphoreType.DMA,
        ],
        20,
    )


def preload(chain, arrays):
    n = len(arrays)

    def body(*refs):
        todo = [
            pltpu.make_async_copy(a, b, refs[-1].at[i])
            for i, (a, b) in enumerate(zip(refs[:n], refs[n:-1]))
        ]
        for c in todo:
            c.start()
        for c in todo:
            c.wait()

    return chain.call(
        "preload",
        body,
        arrays,
        [HBM] * n,
        [sds(a.shape, a.dtype) for a in arrays],
        [HELD] * n,
        [pltpu.SemaphoreType.DMA((n,))],
        1,
    )


def update_body(count, *refs):
    norms = refs[0]
    n, m = 4 * count, 3 * count
    ins, norm_out, outs = refs[1 : 1 + n], refs[1 + n], refs[2 + n : 2 + n + m]
    made, out_sem = refs[2 + n + m : -1], refs[-1]
    norm = jnp.sqrt(jnp.sum(norms[...], axis=0, keepdims=True))
    norm_out[...] = norm
    factor = jnp.minimum(1.0, clip_limit / (norm[:, 0:1] + 1e-06))
    stores = []
    for i in range(count):
        w, g, one, two = (r[...] for r in ins[4 * i : 4 * i + 4])
        last = i == count - 1
        rate, decay = (rate_vector, 0.0) if last else (rate_matrix, decay_matrix)
        clipped = g * factor
        one_new = beta_one * one + (1.0 - beta_one) * clipped
        two_new = beta_two * two + (1.0 - beta_two) * clipped * clipped
        first_hat = one_new / (1.0 - beta_one**STEP)
        second_hat = two_new / (1.0 - beta_two**STEP)
        made[i][...] = w - rate * (first_hat / (jnp.sqrt(second_hat) + 1e-08) + decay * w)
        made[count + i][...] = one_new
        made[2 * count + i][...] = two_new
        for k in (i, count + i, 2 * count + i):
            c = pltpu.make_async_copy(made[k], outs[k], out_sem.at[k])
            c.start()
            stores.append(c)
    for c in stores:
        c.wait()


def update(chain, norms, weights, grads, firsts, seconds):
    count = len(weights)
    ins = []
    for group in zip(weights, grads, firsts, seconds):
        ins += group
    outs = [sds(w.shape, F32) for w in weights] * 3
    return chain.call(
        "update",
        functools.partial(update_body, count),
        [norms, *ins],
        [VMEM] + [HELD if i % 4 != 1 else VMEM for i in range(len(ins))],
        (sds((1, 128), F32), *outs),
        (VMEM,) + (HBM,) * len(outs),
        [pltpu.VMEM(v.shape, F32) for v in outs] + [pltpu.SemaphoreType.DMA((len(outs),))],
        12,
    )


def place_second(chain, name, plan, me, z0, r0, z1, r1):
    def copies(m):
        return [
            (0, ALL, [(0, (m.y,)), (2, (m.y,))]),
            (1, ALL, [(0, (m.other_y,)), (2, (m.other_y,))]),
            (2, ALL, [(1, (m.x,)), (3, (m.x,))]),
            (3, ALL, [(1, (m.other_x,)), (3, (m.other_x,))]),
        ]

    return move(chain, name, me, [z0, r0, z1, r1], [(2, *z0.shape), (2, *z1.shape)] * 2, copies)


class Parts:
    def __init__(self, groups, far=0):
        self.count, self.far = len(groups), far
        self.arrays = [own for own, _ in groups] + [v for _, came in groups for v in came]
        self.lanes, self.came, at, place = [], [], 0, self.count
        for own, came in groups:
            self.lanes.append(slice(at, at + own.shape[-1]))
            self.came.append((place, len(came)))
            at += own.shape[-1]
            place += len(came)
        _, self.nx, self.nz, _, self.rows, _ = groups[0][0].shape
        self.cols = at

    def terms(self, g, h, at):
        place, n = self.came[g]
        return [(g, (h, *at)), (place, (h, *at)) if n == 1 else (place + h, at)]

    def sums(self, make):
        return [
            item
            for g, lanes in enumerate(self.lanes)
            for item in make(g, (self.rows, lanes.stop - lanes.start), lanes)
        ]


def first_sums(chain, plan, name, me, parts):
    nx, nz = parts.nx, parts.nz

    def sums(m):
        return parts.sums(
            lambda g, end, lanes: [
                (0, (ALL, ALL, ALL, lanes), (nz, 2, *end), parts.terms(g, 0, (m.other_x,))),
                (1, (ALL, ALL, ALL, lanes), (nx, nz, *end), parts.terms(g, 1, (ALL, ALL, m.other_y))),
            ]
        )

    outs = [sds((nz, 2, parts.rows, parts.cols), BF16), sds((nx, nz, parts.rows, parts.cols), BF16)]
    s0, s1 = add_up(chain, name + "1", me, parts.arrays, outs, sums, far=parts.far)
    return plan.partner(name, s0, "x"), plan.partner(name, s1, "y")


def second_sums(chain, plan, name, me, parts, f0, f1):
    n = len(parts.arrays)

    def sums(m):
        at0, at1 = (m.x, ALL, m.other_y), (m.other_x, ALL, m.y)

        def make(g, end, lanes):
            one = parts.terms(g, 0, at0) + [(n, (ALL, m.other_y, ALL, lanes))]
            two = parts.terms(g, 1, at1) + [(n + 1, (m.other_x, ALL, ALL, lanes))]
            shape = (parts.nz, *end)
            return [(0, (ALL, ALL, lanes), shape, one), (1, (ALL, ALL, lanes), shape, two)]

        return parts.sums(make)

    outs = [sds((parts.nz, parts.rows, parts.cols), BF16)] * 2
    arrays = [*parts.arrays, f0, f1]
    s0, s1 = add_up(chain, name + "2", me, arrays, outs, sums, far=parts.far)
    return plan.partner(name, s0, "y"), plan.partner(name, s1, "x")


def third_sums(chain, plan, name, me, parts, f0, f1, s0, s1, merged):
    n, rows = len(parts.arrays), parts.rows

    def sums(m):
        def make(g, end, lanes):
            out = []
            for k in range(parts.nz):
                z = m.z ^ k
                at = (m.x, z, m.y)
                one = parts.terms(g, 0, at) + [(n, (z, m.y, ALL, lanes)), (n + 2, (z, ALL, lanes))]
                two = parts.terms(g, 1, at) + [(n + 1, (m.x, z, ALL, lanes)), (n + 3, (z, ALL, lanes))]
                t, ti = z_target(k, merged)
                out.append((t, (*ti, slice(0, rows), lanes), end, one))
                out.append((t, (*ti, slice(rows, 2 * rows), lanes), end, two))
            return out

        return parts.sums(make)

    outs = z_outs((2 * rows, parts.cols), merged)
    arrays = [*parts.arrays, f0, f1, s0, s1]
    return add_up(chain, name + "3", me, arrays, outs, sums, far=parts.far)


def z_outs(shape, merged):
    if merged:
        return [sds(shape, F32), sds((2, *shape), BF16), sds(shape, BF16)]
    return [sds(shape, F32)] + [sds(shape, BF16)] * 3


def z_target(k, merged):
    if merged and k in (1, 3):
        return 1, (k // 2,)
    return k, ()


def along_z(chain, plan, name, me, two, came, at):
    (total,) = add_up(
        chain, name, me, [two, came], [two], lambda m: [(0, ALL, two.shape, [(0, ALL), (1, at)])]
    )
    return total


def squared(*values):
    return jnp.broadcast_to(sum(jnp.sum(v * v) for v in values), (1, 128))


def body(
    tokens,
    lengths,
    cotangent,
    qkv_weight,
    out_weight,
    fc_weight,
    proj_weight,
    vectors,
    qkv_first,
    out_first,
    fc_first,
    proj_first,
    vectors_first,
    qkv_second,
    out_second,
    fc_second,
    proj_second,
    vectors_second,
):
    dp, fsdp = lax.axis_size("dp"), lax.axis_size("fsdp")
    model = tokens.shape[1]
    wide, cut = qkv_weight.shape[1], out_weight.shape[1]
    hidden = fc_weight.shape[1] * fsdp
    per = vectors.shape[1]
    plan = Plan(dp, fsdp, model, hidden)
    rows, half, chalf, nz = plan.rows, plan.rows // 2, plan.cols // 2, plan.nz
    a_full = -(-(wide + per) // 128) * 128
    b_full = model + -(-cut // 128) * 128
    chain = Chain()
    at_dp, at_fsdp = lax.axis_index("dp"), lax.axis_index("fsdp")
    me = jnp.stack([at_dp // 2, at_dp % 2, at_fsdp // 2, at_fsdp % 2]).astype(jnp.int32)
    heads = model // HEAD_DIM
    third = [range(i, i + heads // 3) for i in range(0, heads, heads // 3)]

    def turned(value):
        return jnp.transpose(value)

    state = (
        *(qkv_weight, out_weight, fc_weight, turned(proj_weight), turned(vectors)),
        *(qkv_first, out_first, fc_first, turned(proj_first), turned(vectors_first)),
        *(qkv_second, out_second, fc_second, turned(proj_second), turned(vectors_second)),
    )

    if plan.direct:
        a_own, b_own, c_own = pack(chain, plan, state[:5], a_full, b_full)
        a_near, a_far = plan.partner("gather_a", a_own, "z", 1), plan.partner("gather_a", a_own, "z", 2)
        c_y, c_x = plan.partner("gather_c", c_own[0], "y"), plan.partner("gather_c", c_own[1], "x")
        chain.wait_for(c_y, c_x)
        a_far, b_own = gate(chain, "gate_z", a_far, b_own)
        a_came = [a_near, a_far, plan.partner("gather_a", a_far, "z", 1)]
        b_came = plan.gather_z("gather_b", b_own)

        def place_a(m):
            return [(k, ALL, [(0, (m.z ^ k,))]) for k in range(nz)]

        (a_z,) = move(chain, "place_a1", me, [a_own, *a_came], [(nz, rows, a_full)], place_a)
        a_y, a_x = plan.partner("gather_a", a_z, "y"), plan.partner("gather_a", a_z, "x")
        a_xy = plan.opposite("gather_a", a_z)

        def place_b(m):
            return [
                (k, pl.ds(h * half, half), [(h, (m.z ^ k,))]) for k in range(nz) for h in range(2)
            ] + [
                (nz, (0,), [(2, (m.y,))]),
                (nz + 1, ALL, [(2, (m.other_y,))]),
                (nz, (1,), [(2, (2 + m.x,))]),
                (nz + 2, ALL, [(2, (2 + m.other_x,))]),
            ]

        outs = [(nz, half, b_full), (nz, half, b_full), (4, chalf, plan.deep)]
        arrays = [b_own, *b_came, c_own, c_y, c_x]
        chain.wait_for(a_y, a_x, a_xy)
        b_z0, b_z1, c_pair = move(chain, "place_b1", me, arrays, outs, place_b)
        b_r0, b_r1 = plan.partner("gather_b", b_z0, "y"), plan.partner("gather_b", b_z1, "x")
        a_in = gate(chain, "gate_a", a_z, a_y, a_x, a_xy)
        a_in = a_in + [plan.partner("gather_a", v, "core") for v in a_in]
        c_near, c_far = plan.partner("gather_c", c_pair, "z", 1), plan.partner("gather_c", c_pair, "z", 2)
    else:

        def whole(shard):
            down = lax.all_gather(shard.astype(BF16), "dp", axis=0, tiled=True)
            return lax.all_gather(down, "fsdp", axis=0, tiled=False)

        def padded(parts, full):
            both = jnp.concatenate(parts, axis=1)
            both = whole(jnp.pad(both, ((0, 0), (0, full - both.shape[1]))))
            return both.reshape(fsdp, *plan.split(), full)

        a_in = [padded([qkv_weight, vectors], a_full)]
        b_in = [padded([fc_weight, out_weight], b_full)]
        c_all = jnp.transpose(whole(proj_weight), (0, 2, 1))
        c_all = c_all.reshape(model, fsdp, 2, hidden // fsdp // 2)
        c_in = [jnp.transpose(c_all, (1, 2, 0, 3))]

    qkv, act_one, a_can, t_can, n_one, inv_one = front(chain, plan, me, tokens, a_in, wide)
    if plan.direct:
        b_p0, b_p1, *b_pc = place_second(chain, "place_b2", plan, me, b_z0, b_r0, b_z1, b_r1)
        b_q0, b_q1 = plan.partner("gather_b", b_p0, "x"), plan.partner("gather_b", b_p1, "y")
    if plan.direct:
        c_near, c_far, *b_pc = gate(chain, "gate_c1", c_near, c_far, *b_pc)
        c_last = plan.partner("gather_c", c_far, "z", 1)
        b_pc = [plan.partner("gather_b", v, "core") for v in b_pc]
    parts = [attend(chain, qkv, lengths, group) for group in third]
    if plan.direct:
        b_q0, b_q1 = gate(chain, "gate_b", b_q0, b_q1)
        b_qc = [plan.partner("gather_b", v, "core") for v in (b_q0, b_q1)]
        b_in = [b_p0, b_p1, b_q0, b_q1, *b_pc, *b_qc]
        chain.wait_for(*b_pc)

        def place_c2(m):
            return [
                (k, (2 * h + p,), [(h, (p, m.z ^ k)), (2, (h, p, m.z ^ k))])
                for k in range(nz)
                for h in range(2)
                for p in range(2)
            ]

        outs = [(2, nz, chalf, plan.deep)] * 2 + [(2, 2, nz, chalf, plan.deep)]
        c_p0, c_p1, c_p = move(chain, "place_c2", me, [c_pair, c_near, c_far, c_last], outs, place_c2)
        c_q0, c_q1 = plan.partner("gather_c", c_p0, "x"), plan.partner("gather_c", c_p1, "y")
        c_pc = plan.partner("gather_c", c_p, "core")
    logs = [p[1] for p in parts]
    resid_two, act_two, wout, mixed, n_two, inv_two = join(
        chain, plan, me, cut, tokens, [p[0] for p in parts], b_in, t_can
    )
    if plan.direct:
        chain.wait_for(c_pc)
    gel, slope, b_can, g_b_proj, *g_c = mlp_up(
        chain, plan, me, act_two, cotangent, t_can, b_in, hidden
    )
    if plan.direct:
        c_q0, c_q1, away = gate(chain, "gate_c", c_q0, c_q1, g_c[1])
        c_in = [c_p, c_q0, c_q1, c_pc] + [plan.partner("gather_c", v, "core") for v in (c_q0, c_q1)]
        c_away = plan.partner("sum_c", away, "core")
    if plan.direct:
        c_parts = Parts([(g_c[0], [c_away])])
        c_f0, c_f1 = first_sums(chain, plan, "sum_c", me, c_parts)
    gpre, g_b_fc, c_can = mlp_down(chain, plan, me, cotangent, slope, c_in)

    gact, *g_b = mlp_back(chain, plan, me, act_two, gpre, b_can)
    if plan.direct:
        b_away = [plan.partner("sum_b", v, "core") for v in g_b[1:]]
    gresid, gmixed, inner, g_two, *g_o = join_back(
        chain, plan, me, gact, cotangent, n_two, inv_two, mixed, wout, t_can, b_full - model
    )
    if plan.direct:
        chain.wait_for(c_f0, c_f1)
        o_away = [plan.partner("sum_b", *gate(chain, "gate_o", g_o[1]), "core")]
        b_parts = Parts([(g_b[0], b_away), (g_o[0], o_away)])
    gparts = [attend_back(chain, qkv, gmixed, logs[0], inner, lengths, third[0])]
    if plan.direct:
        b_f0, b_f1 = first_sums(chain, plan, "sum_b", me, b_parts)

        def sums_cz(m):
            out = []
            for k in range(nz):
                z = m.z ^ k
                at = (0, m.x, z)
                terms = [(0, at), (1, at), (2, (z,))]
                t, ti = z_target(k, True)
                out.append((t, (*ti, slice(0, 2)), (2, chalf, plan.deep), terms))
                at = (1, ALL, z, m.y)
                terms = [(0, at), (1, at), (3, (ALL, z))]
                out.append((t, (*ti, slice(2, 4)), (2, chalf, plan.deep), terms))
            return out

        outs = z_outs((4, chalf, plan.deep), True)
        arrays = [g_c[0], c_away, c_f0, c_f1]
        c_u = add_up(chain, "sum_c2", me, arrays, outs, sums_cz)
        c_near = plan.partner("sum_c", c_u[1], "z", 1)
    for log, group in zip(logs[1:], third[1:]):
        gparts.append(attend_back(chain, qkv, gmixed, log, inner, lengths, group))
    kept = (n_one, inv_one, act_one, gparts, a_can, gresid, t_can, g_two, g_b_fc, g_b_proj)
    input_grad, *g_a = back(chain, plan, wide, a_full, me, *kept)

    if plan.direct:
        c_two = along_z(chain, plan, "sum_c4", me, c_u[2], c_near, (1,))
        c_z = [c_u[0], c_near, plan.partner("sum_c", c_two, "z", 2)]
        b_s0, b_s1 = second_sums(chain, plan, "sum_b", me, b_parts, b_f0, b_f1)
        a_away = [plan.partner("sum_a", v, "core") for v in gate(chain, "gate_s", *g_a[1:])]
        a_parts = Parts([(g_a[0], a_away)])
        a_f0, a_f1 = first_sums(chain, plan, "sum_a", me, a_parts)
        output = mlp_out(chain, plan, resid_two, gel, c_can, t_can)
        b_u = third_sums(chain, plan, "sum_b", me, b_parts, b_f0, b_f1, b_s0, b_s1, True)
        b_near = plan.partner("sum_b", b_u[1], "z", 1)
        a_s0, a_s1 = second_sums(chain, plan, "sum_a", me, a_parts, a_f0, a_f1)
        z_lead = ((), (0,), ())

        def sums_c3(m):
            block = (chalf, plan.deep)
            one = [(i, (*lead, m.other_y)) for i, lead in enumerate(z_lead)]
            two = [(i, (*lead, 2 + m.other_x)) for i, lead in enumerate(z_lead)]
            return [(0, ALL, block, one), (1, ALL, block, two)]

        outs = [sds((chalf, plan.deep), BF16)] * 2
        s0, s1 = add_up(chain, "sum_c3", me, c_z, outs, sums_c3)
        c_l0, c_l1 = plan.partner("sum_c", s0, "y"), plan.partner("sum_c", s1, "x")
        b_two = along_z(chain, plan, "sum_b4", me, b_u[2], b_near, (1,))
        b_z = [b_u[0], b_near, plan.partner("sum_b", b_two, "z", 2)]
        a_u = third_sums(chain, plan, "sum_a", me, a_parts, a_f0, a_f1, a_s0, a_s1, False)
        a_z = [a_u[0]] + [plan.partner("sum_a", a_u[k], "z", k) for k in range(1, nz)]

        def sums_c(m):
            block = (chalf, plan.deep)
            one = [(i, (*lead, m.y)) for i, lead in enumerate(z_lead)] + [(3, ALL)]
            two = [(i, (*lead, 2 + m.x)) for i, lead in enumerate(z_lead)] + [(4, ALL)]
            return [(0, ALL, block, one), (1, ALL, block, two)]

        state = preload(chain, state)

        def end_c(done, outs):
            outs[0][0:chalf, :] = done[0]
            outs[0][chalf:, :] = done[1]
            outs[1][...] = squared(*done)

        d_proj, s_c = add_up(
            chain,
            "end_c",
            me,
            [*c_z, c_l0, c_l1],
            [sds((plan.cols, plan.deep), F32), sds((1, 128), F32)],
            sums_c,
            end_c,
        )
        def last_b(m):
            shape = b_z[0].shape
            return [(0, ALL, shape, [(i, lead or ALL) for i, lead in enumerate(z_lead)])]

        def last_a(m):
            return [(0, ALL, a_z[0].shape, [(i, ALL) for i in range(nz)])]

        def end_b(done, outs):
            total = done[0]
            fc, out = total[:, :model], total[:, model : model + cut]
            outs[0][...] = fc
            outs[1][...] = out
            outs[2][...] = squared(fc, out)

        shapes = [fc_weight.shape, out_weight.shape, (1, 128)]
        d_fc, d_out, s_b = add_up(
            chain, "end_b", me, b_z, [sds(s, F32) for s in shapes], last_b, end_b
        )

        def end_a(done, outs):
            total = done[0]
            start = wide // 128 * 128
            vec = jnp.transpose(total[:, start:])[wide - start : wide - start + per]
            qkv = total[:, :wide]
            outs[0][...] = qkv
            outs[1][...] = vec
            outs[2][...] = squared(qkv, vec)

        shapes = [qkv_weight.shape, (per, rows), (1, 128)]
        d_qkv, d_vec, s_a = add_up(
            chain, "end_a", me, a_z, [sds(s, F32) for s in shapes], last_a, end_a
        )
        squares = s_a + s_b + s_c
    else:
        output = mlp_out(chain, plan, resid_two, gel, c_can, t_can)

        def shared(value):
            mine = lax.psum_scatter(value, "fsdp", scatter_dimension=0, tiled=False)
            return lax.psum_scatter(mine, "dp", scatter_dimension=0, tiled=True).astype(F32)

        d_a = shared(g_a[0].reshape(fsdp, model, a_full))
        d_qkv, d_vec = d_a[:, :wide], turned(d_a[:, wide : wide + per])
        d_out = shared(jnp.transpose(g_o[0].reshape(model, fsdp, cut), (1, 0, 2)))
        d_fc = shared(g_b[0].reshape(fsdp, model, model))
        d_c = jnp.transpose(g_c[0], (2, 0, 1, 3)).reshape(fsdp, plan.cols, hidden)
        d_proj = turned(shared(jnp.transpose(d_c, (0, 2, 1))))
        total = sum(jnp.sum(d * d) for d in (d_qkv, d_out, d_fc, d_proj, d_vec))
        squares = jnp.full((1, 128), total)

    sent = jnp.broadcast_to(squares[None], (dp * fsdp, 1, 128))
    with jax.named_scope("norm"):
        norms = lax.all_to_all(sent, ("dp", "fsdp"), 0, 0, tiled=True).reshape(dp * fsdp, 128)
    norm, *new = update(
        chain, norms, state[:5], (d_qkv, d_out, d_fc, d_proj, d_vec), state[5:10], state[10:]
    )
    new = [turned(v) if i % 5 in (3, 4) else v for i, v in enumerate(new)]
    return (output, input_grad, norm[0, 0], *new)


def solution(mesh):
    tokens = P(("dp", "fsdp"), None)
    table = P("dp", "fsdp")
    return jax.shard_map(
        body,
        mesh=mesh,
        in_specs=(tokens, P(("dp", "fsdp")), tokens) + (table,) * 15,
        out_specs=(tokens, tokens, P()) + (table,) * 15,
        check_vma=False,
    )
```

```python
import functools

import jax
import jax.numpy as jnp
from jax import lax
from jax.experimental import pallas as pl
from jax.experimental.pallas import tpu as pltpu
from jax.sharding import PartitionSpec as P

HEAD_DIM = 64
STEP = 10

beta_one = 0.9
beta_two = 0.95
clip_limit = 1.0
rate_matrix = 0.1
rate_vector = 1.0
decay_matrix = 0.1
gelu_coeff = 0.7978845608028654
cubic_coeff = 0.044715
neg_large = -1e30
VEC_ROWS = 16

F32 = jnp.float32
BF16 = jnp.bfloat16
VMEM = pl.BlockSpec(memory_space=pltpu.VMEM)
HELD = pl.BlockSpec(memory_space=pltpu.VMEM)
ANY = pl.BlockSpec(memory_space=pl.ANY)
HBM = pl.BlockSpec(memory_space=pltpu.HBM)
SMEM = pl.BlockSpec(memory_space=pltpu.SMEM)
ALL = slice(None)


def dot_nn(a, b):
    return lax.dot_general(a, b, (((1,), (0,)), ((), ())), preferred_element_type=F32)


def dot_nt(a, b):
    return lax.dot_general(a, b, (((1,), (1,)), ((), ())), preferred_element_type=F32)


def dot_tn(a, b):
    return lax.dot_general(a, b, (((0,), (0,)), ((), ())), preferred_element_type=F32)


def sds(shape, dtype):
    return jax.ShapeDtypeStruct(shape, dtype)


class Chain:
    def __init__(self):
        self.waits = []

    def wait_for(self, *arrays):
        self.waits += arrays

    def call(self, name, body, ins, in_specs, outs, out_specs, scratch, limit, aliases=None):
        several = isinstance(outs, (tuple, list))
        if not several:
            outs, out_specs = (outs,), (out_specs,)
        n_in, extra, n_out = len(ins), len(self.waits), len(outs)
        pins = ((HELD, pltpu.VMEM), (HBM, pltpu.HBM))

        def run(*refs):
            given, refs = refs[:n_in], refs[n_in + extra :]
            refs[n_out][...] = jnp.zeros(refs[n_out].shape, F32)
            body(*given, *refs[:n_out], *refs[n_out + 1 :])

        placed, made = [], []
        for v, spec in zip(ins, in_specs):
            for pin, space in pins:
                if spec is pin:
                    v = pltpu.with_memory_space_constraint(v, space)
            placed.append(v)
        for o, spec in zip(outs, out_specs):
            for pin, space in pins:
                if spec is pin:
                    o = space(o.shape, o.dtype)
            made.append(o)
        results = pl.pallas_call(
            run,
            name=name,
            input_output_aliases=aliases or {},
            out_shape=(*made, pltpu.VMEM((8, 128), F32)),
            in_specs=[*in_specs, *[ANY] * extra],
            out_specs=(*out_specs, HELD),
            scratch_shapes=scratch,
            compiler_params=pltpu.CompilerParams(vmem_limit_bytes=limit << 20),
        )(*placed, *self.waits)
        *results, token = results
        self.waits = [pltpu.with_memory_space_constraint(token, pltpu.VMEM)]
        return results if several else results[0]


class Plan:
    def __init__(self, dp, fsdp, model, hidden):
        self.dp, self.fsdp = dp, fsdp
        self.nz, self.nx = dp // 2, fsdp // 2
        self.rows = model // dp
        self.cols = model // fsdp
        self.deep = hidden // dp
        self.direct = (
            dp == 2 * fsdp
            and fsdp % 2 == 0
            and self.rows % 32 == 0
            and self.cols % 32 == 0
            and self.deep % 128 == 0
            and hidden == fsdp * model
            and dp == 8
        )

    def partner(self, name, value, stage, k=1):
        axis, step = {"x": ("fsdp", 2), "y": ("dp", 1), "z": ("dp", 2), "core": ("fsdp", 1)}[stage]
        n = self.dp if axis == "dp" else self.fsdp
        with jax.named_scope(f"{name}_{stage}"):
            return lax.ppermute(value, axis, [(i, i ^ (step * k)) for i in range(n)])

    def opposite(self, name, value):
        n = self.fsdp
        pairs = [(i * n + j, (i ^ 1) * n + (j ^ 2)) for i in range(self.dp) for j in range(n)]
        with jax.named_scope(f"{name}_xy"):
            return lax.ppermute(value, ("dp", "fsdp"), pairs)

    def gather_z(self, name, value):
        near, far = self.partner(name, value, "z", 1), self.partner(name, value, "z", 2)
        return [near, far, self.partner(name, far, "z", 1)]

    def split(self):
        return (self.nz, 2, 2, self.rows // 2) if self.direct else (1, 1, 1, self.rows * self.dp)


class Me:
    def __init__(self, ref):
        self.z, self.y, self.x, self.core = ref[0], ref[1], ref[2], ref[3]
        self.other_y, self.other_x = 1 - self.y, 1 - self.x

    def fsdp(self, x, away):
        return 2 * x + (self.core ^ away)


def move(chain, name, me, arrays, outs, copies):
    n = len(arrays)

    def body(me_ref, *refs):
        for s, si, targets in copies(Me(me_ref)):
            value = refs[s][si]
            for t, ti in targets:
                refs[n + t][ti] = value

    return chain.call(
        name,
        body,
        (me, *arrays),
        [SMEM] + [VMEM] * n,
        tuple(sds(s, BF16) for s in outs),
        (HELD,) * len(outs),
        [],
        6,
    )


def gate(chain, name, *arrays, far=0):
    specs = [ANY] * (len(arrays) - far) + [HBM] * far
    return chain.call(
        name,
        lambda *refs: None,
        arrays,
        specs,
        tuple(sds(v.shape, v.dtype) for v in arrays),
        tuple(specs),
        [],
        1,
        {i: i for i in range(len(arrays))},
    )


def add_up(chain, name, me, arrays, outs, sums, after=None, far=0):
    n, m = len(arrays), len(outs)
    still = sums(Me([0, 0, 0, 0]))
    loaded = [shape for _, _, shape, parts in still for s, _ in parts if s < far]

    def body(me_ref, *refs):
        ins, outs_, refs = refs[:n], refs[n : n + m], refs[n + m :]
        held, sem = refs[: len(loaded)], refs[len(loaded) :]
        todo, i = [], 0
        for t, ti, shape, parts in sums(Me(me_ref)):
            group = []
            for s, si in parts:
                copy = None
                if s < far:
                    copy = pltpu.make_async_copy(ins[s].at[si], held[i], sem[0].at[i])
                    copy.start()
                    i += 1
                group.append((copy, s, si, i - 1))
            todo.append((t, ti, group))
        done = []
        for t, ti, group in todo:
            total = None
            for copy, s, si, k in reversed(group):
                if copy is not None:
                    copy.wait()
                v = (ins[s][si] if copy is None else held[k][...]).astype(F32)
                total = v if total is None else total + v
            if after is None:
                outs_[t][ti] = total.astype(outs_[t].dtype)
            else:
                done.append(total)
        if after is not None:
            after(done, outs_)

    return chain.call(
        name,
        body,
        (me, *arrays),
        [SMEM] + [HBM if i < far else VMEM for i in range(n)],
        tuple(outs),
        (HELD if after is None else VMEM,) * m,
        [pltpu.VMEM(shape, BF16) for shape in loaded]
        + ([pltpu.SemaphoreType.DMA((len(loaded),))] if loaded else []),
        8,
    )


def pack_body(ins, outs, held, sem):
    todo = [pltpu.make_async_copy(i, h, sem.at[k]) for k, (i, h) in enumerate(zip(ins, held))]
    for c in todo:
        c.start()
    for c in todo:
        c.wait()
    qkv, out, fc, proj, vec = (h[...] for h in held)
    a, b, c = outs
    wide, model = qkv.shape[1], fc.shape[1]
    columns = jnp.transpose(vec)
    start = wide // 128 * 128
    a[:, start:] = jnp.zeros((a.shape[0], a.shape[1] - start), BF16)
    a[:, 0:wide] = qkv.astype(BF16)
    a[:, wide : wide + columns.shape[1]] = columns.astype(BF16)
    b[:, model:] = jnp.zeros((b.shape[0], b.shape[1] - model), BF16)
    b[:, 0:model] = fc.astype(BF16)
    b[:, model : model + out.shape[1]] = out.astype(BF16)
    c[...] = proj.astype(BF16).reshape(c.shape)


def pack(chain, plan, weights, a_full, b_full):
    count = len(weights)

    def run(*refs):
        pack_body(refs[:count], refs[count : count + 3], refs[count + 3 : -1], refs[-1])

    return chain.call(
        "pack",
        run,
        weights,
        [HBM] * count,
        (
            sds((plan.rows, a_full), BF16),
            sds((plan.rows, b_full), BF16),
            sds((2, plan.cols // 2, plan.deep), BF16),
        ),
        (VMEM,) * 3,
        [pltpu.VMEM(w.shape, F32) for w in weights] + [pltpu.SemaphoreType.DMA((count,))],
        6,
    )


def normed(values):
    mean = jnp.mean(values, axis=-1, keepdims=True)
    centred = values - mean
    spread = jnp.mean(centred * centred, axis=-1, keepdims=True)
    inverse = lax.rsqrt(spread + 1e-05)
    return centred * inverse, inverse


def norm_back(grad_hidden, n, inverse, gain):
    g = grad_hidden * gain
    mean_plain = jnp.mean(g, axis=-1, keepdims=True)
    mean_cross = jnp.mean(g * n, axis=-1, keepdims=True)
    return inverse * (g - mean_plain - n * mean_cross)


class Table:
    def __init__(self, fsdp):
        self.per = 12 // fsdp

    def row(self, k):
        return (k // self.per) * VEC_ROWS + k % self.per

    def get(self, ref, k):
        r = self.row(k)
        return ref[r : r + 1, :]


def spread_matrix(rows, model, d):
    r = lax.broadcasted_iota(jnp.int32, (128, model), 0)
    c = lax.broadcasted_iota(jnp.int32, (128, model), 1)
    return ((c == r + d * rows) & (r < rows)).astype(BF16)


def halves(ins, away):
    n = len(ins) // 2
    part = ins[n * away : n * away + n]
    own = (part[0].at[0], part[0].at[1]) if n == 3 else part[:2]
    return (*own, *part[-2:])


def table_loads(plan, me, ins):
    for away in range(2):
        p0, p1, r0, r1 = halves(ins, away)
        for y in range(2):
            for x, ref in ((me.x, p0), (me.other_x, r0)):
                yield ref, (y,), me.fsdp(x, away), (ALL, y), 0
        for y, ref in ((me.y, p1), (me.other_y, r1)):
            for x in range(plan.nx):
                yield ref, (x,), me.fsdp(x, away), (ALL, y), 1


def front_body(plan, wide, n_in, me_ref, tokens, *refs):
    ins = refs[:n_in]
    qkv, act, a_out, t_out, n_out, inv_out = refs[n_in : n_in + 6]
    a_v, flat, sem, out_sem = refs[n_in + 6 :]
    fsdp = plan.fsdp
    full = a_v.shape[-1]
    model = tokens.shape[1]
    table = Table(fsdp)
    if plan.direct:
        me = Me(me_ref)
        for i, ref in enumerate(ins):
            away, x, y = i // 4, i // 2 % 2, i % 2
            f = me.fsdp(me.x ^ x, away)
            pltpu.make_async_copy(ref, a_v.at[f, :, me.y ^ y], sem.at[f]).start()
    else:
        for f in range(fsdp):
            pltpu.make_async_copy(ins[0].at[f], a_v.at[f], sem.at[f]).start()
    n, inverse = normed(tokens[...].astype(F32))
    n_out[...] = n
    inv_out[...] = jnp.broadcast_to(inverse, inv_out.shape)
    start = wide // 128 * 128
    for f in range(fsdp):
        pltpu.make_async_copy(a_v.at[f], a_v.at[f], sem.at[f]).wait()
        block = a_v[f].reshape(model, full)
        flat[:, f * wide : (f + 1) * wide] = block[:, :wide]
        turned = jnp.transpose(block[:, start:].astype(F32))
        t_out[f * VEC_ROWS : f * VEC_ROWS + table.per, :] = turned[
            wide - start : wide - start + table.per
        ]
    copy = pltpu.make_async_copy(flat, a_out, out_sem)
    copy.start()
    act[...] = (n * table.get(t_out, 0) + table.get(t_out, 1)).astype(BF16)
    for which in range(3):
        r = dot_nn(act[...], flat[:, which * model : (which + 1) * model])
        if which != 1:
            r = r + table.get(t_out, 4 + which // 2)
        qkv[which] = r.astype(BF16)
    copy.wait()


def front(chain, plan, me, tokens, pieces, wide):
    t, model = tokens.shape
    fsdp = plan.fsdp
    full = pieces[0].shape[-1]
    lead = (fsdp, plan.nz, 2, plan.rows, full) if plan.direct else pieces[0].shape
    return chain.call(
        "front",
        functools.partial(front_body, plan, wide, len(pieces)),
        (me, tokens, *pieces),
        [SMEM, VMEM] + [ANY] * len(pieces),
        (
            sds((3, t, model), BF16),
            sds((t, model), BF16),
            sds((model, 3 * model), BF16),
            sds((fsdp * VEC_ROWS, model), F32),
            sds((t, model), F32),
            sds((t, 128), F32),
        ),
        (HELD, HELD, HBM, HELD, HELD, HELD),
        [
            pltpu.VMEM(lead, BF16),
            pltpu.VMEM((model, 3 * model), BF16),
            pltpu.SemaphoreType.DMA((fsdp,)),
            pltpu.SemaphoreType.DMA,
        ],
        16,
    )


def masks(length, lo, size, keys):
    q = lax.broadcasted_iota(jnp.int32, (size, 1), 0) + lo
    limit = jnp.minimum(q, length - 1)
    k = lax.broadcasted_iota(jnp.int32, (size, keys), 1)
    return k <= limit


QBLOCK = 256


def attend_body(heads, length_ref, qkv, mixed, logs):
    t = mixed.shape[0]
    length = length_ref[0]
    scale = HEAD_DIM**-0.5

    def part(h, which):
        return qkv[which, :, h * HEAD_DIM : (h + 1) * HEAD_DIM]

    for i, h in enumerate(heads):
        q = part(h, 0) * jnp.asarray(scale, BF16)
        k, v = part(h, 1), part(h, 2)
        for lo in range(0, t, QBLOCK):
            n = lo + QBLOCK
            s = dot_nt(q[lo:n], k[:n])
            s = jnp.where(masks(length, lo, QBLOCK, n), s, neg_large)
            top = jnp.max(s, axis=-1, keepdims=True)
            e = jnp.exp(s - top)
            total = jnp.sum(e, axis=-1, keepdims=True)
            p = (e * (1.0 / total)).astype(BF16)
            o = dot_nn(p, v[:n])
            mixed[lo:n, i * HEAD_DIM : (i + 1) * HEAD_DIM] = o.astype(BF16)
            logs[lo:n, i : i + 1] = top + jnp.log(total)


def attend(chain, qkv, length, heads):
    t = qkv.shape[1]
    return chain.call(
        "attend",
        functools.partial(attend_body, heads),
        (length, qkv),
        [SMEM, HELD],
        (sds((t, len(heads) * HEAD_DIM), BF16), sds((t, 128), F32)),
        (HELD, HELD),
        [],
        6,
    )


def join_body(plan, cut, n_in, n_mixed, me_ref, tokens, t_in, *refs):
    ins, refs = refs[:n_in], refs[n_in:]
    parts, (resid, act, wout, mixed, n_out, inv_out, o_v, sem) = refs[:n_mixed], refs[n_mixed:]
    model = tokens.shape[1]
    fsdp = plan.fsdp
    table = Table(fsdp)
    lanes = pl.ds(model, o_v.shape[-1])
    if plan.direct:
        for ref, si, f, ti, h in table_loads(plan, Me(me_ref), ins):
            src = ref.at[(*si, ALL, ALL, lanes)]
            pltpu.make_async_copy(src, o_v.at[(f, *ti, h)], sem).start()
    else:
        for f in range(fsdp):
            src = ins[0].at[(f, ALL, ALL, ALL, ALL, lanes)]
            pltpu.make_async_copy(src, o_v.at[f], sem).start()
    at = 0
    for p in parts:
        mixed[:, at : at + p.shape[1]] = p[...]
        at += p.shape[1]
    pltpu.make_async_copy(o_v, o_v, sem).wait()
    for f in range(fsdp):
        wout[:, f * cut : (f + 1) * cut] = o_v[f].reshape(model, o_v.shape[-1])[:, :cut]
    r = tokens[...].astype(F32) + dot_nn(mixed[...], wout[...]) + table.get(t_in, 6)
    resid[...] = r
    n, inverse = normed(r)
    n_out[...] = n
    inv_out[...] = jnp.broadcast_to(inverse, inv_out.shape)
    act[...] = (n * table.get(t_in, 2) + table.get(t_in, 3)).astype(BF16)


def join(chain, plan, me, cut, tokens, parts, pieces, t_can):
    t, model = tokens.shape
    spare = pieces[0].shape[-1] - model
    return chain.call(
        "join",
        functools.partial(join_body, plan, cut, len(pieces), len(parts)),
        (me, tokens, t_can, *pieces, *parts),
        [SMEM, VMEM, HELD] + [ANY] * len(pieces) + [HELD] * len(parts),
        (
            sds((t, model), F32),
            sds((t, model), BF16),
            sds((model, model), BF16),
            sds((t, model), BF16),
            sds((t, model), F32),
            sds((t, 128), F32),
        ),
        (HELD,) * 6,
        [pltpu.VMEM((plan.fsdp, *plan.split(), spare), BF16), pltpu.SemaphoreType.DMA],
        10,
    )


def gelu_and_slope(pre):
    square = pre * pre
    th = jnp.tanh(pre * (gelu_coeff + (gelu_coeff * cubic_coeff) * square))
    plus = 0.5 * th + 0.5
    bend = 0.5 * gelu_coeff + (1.5 * gelu_coeff * cubic_coeff) * square
    return (pre * plus).astype(BF16), plus + pre * (1.0 - th * th) * bend


def mlp_up_body(plan, n_in, n_out, me_ref, act, cot, t_in, *refs):
    ins, refs = refs[:n_in], refs[n_in:]
    gel_out, slope_out, b_v, g_b_proj = refs[:4]
    gouts, refs = refs[4 : 4 + n_out], refs[4 + n_out :]
    gp_v, sem = refs
    fsdp, half = plan.fsdp, plan.cols // 2
    t, model = act.shape
    deep = gp_v.shape[-1]
    per = Table(fsdp).per
    me = Me(me_ref)
    order = []
    for k in range(fsdp):
        if plan.direct:
            away, x = k // 2, me.x if k % 2 == 0 else me.other_x
            p0, p1, r0, r1 = halves(ins, away)
            f = me.fsdp(x, away)
            own = p0 if k % 2 == 0 else r0
            loads = [(own.at[y], y, 0) for y in range(2)]
            loads += [(p1.at[x], me.y, 1), (r1.at[x], me.other_y, 1)]
            for ref, y, h in loads:
                src = ref.at[:, :, pl.ds(0, model)]
                pltpu.make_async_copy(src, b_v.at[f, :, y, h], sem.at[k]).start()
        else:
            f = k
            src = ins[0].at[(f, ALL, ALL, ALL, ALL, pl.ds(0, model))]
            pltpu.make_async_copy(src, b_v.at[f], sem.at[k]).start()
        order.append(f)
    g_b_proj[...] = jnp.sum(cot[...].astype(F32), axis=0, keepdims=True)

    def up(k, lo, hi):
        row = 8 + order[k]
        bias = t_in[pl.ds(row // per * VEC_ROWS + row % per, 1), :]
        return dot_nn(act[lo:hi], b_v[order[k]].reshape(model, model)) + bias

    step = t // 2
    for k in range(fsdp):
        pltpu.make_async_copy(b_v.at[order[k]], b_v.at[order[k]], sem.at[k]).wait()
        lanes = pl.ds(pl.multiple_of(order[k] * model, model), model)
        for lo in range(0, t, step):
            gel, slope = gelu_and_slope(up(k, lo, lo + step))
            gel_out[lo : lo + step, lanes] = gel
            slope_out[lo : lo + step, lanes] = slope
        grad = dot_tn(cot[...], gel_out[:, lanes]).astype(BF16)
        if not plan.direct:
            gouts[0][k, 0], gouts[0][k, 1] = grad[:, :deep], grad[:, deep:]
            continue
        gp_v[0], gp_v[1] = grad[:, :deep], grad[:, deep:]
        for away in range(2):
            for x in range(plan.nx):
                for h in range(2):
                    row = me.fsdp(x, away) * plan.cols + h * half
                    part = gp_v[:, pl.ds(pl.multiple_of(row, 16), half), :]
                    gouts[away][h, x, pl.ds(order[k], 1)] = part[None]


def mlp_up(chain, plan, me, act, cot, t_can, pieces, hidden):
    t, model = act.shape
    fsdp = plan.fsdp
    per = hidden // fsdp // 2
    if plan.direct:
        grads = [sds((2, plan.nx, plan.nz, 2, plan.cols // 2, plan.deep), BF16)] * 2
    else:
        grads = [sds((fsdp, 2, model, per), BF16)]
    lead = (fsdp, *plan.split(), model)
    return chain.call(
        "mlp_up",
        functools.partial(mlp_up_body, plan, len(pieces), len(grads)),
        (me, act, cot, t_can, *pieces),
        [SMEM, HELD, VMEM, HELD] + [ANY] * len(pieces),
        (
            sds((t, hidden), BF16),
            sds((t, hidden), F32),
            sds(lead, BF16),
            sds((1, model), F32),
            *grads,
        ),
        (HELD,) * (4 + len(grads)),
        [
            pltpu.VMEM((2, model, per), BF16),
            pltpu.SemaphoreType.DMA((fsdp,)),
        ],
        18,
    )


def mlp_down_body(plan, n_in, me_ref, cot, slope, *refs):
    ins, refs = refs[:n_in], refs[n_in:]
    gpre, g_b_fc, c_v = refs
    half = plan.cols // 2
    model = cot.shape[1]
    if plan.direct:
        for ref, si, f, ti, h in table_loads(plan, Me(me_ref), ins):
            rows = pl.ds(pl.multiple_of(f * plan.cols + h * half, 16), half)
            c_v[(*ti, rows)] = ref[si]
    else:
        c_v[...] = ins[0][...]
    for j in range(plan.fsdp):
        lanes = slice(j * model, (j + 1) * model)
        down = jnp.concatenate([c_v[j, 0], c_v[j, 1]], axis=1)
        low = (dot_nn(cot[...], down) * slope[:, lanes]).astype(BF16)
        gpre[:, lanes] = low
        g_b_fc[j : j + 1, :] = jnp.sum(low.astype(F32), axis=0, keepdims=True)


def mlp_down(chain, plan, me, cot, slope, pieces):
    t, model = cot.shape
    fsdp, hidden = plan.fsdp, slope.shape[1]
    return chain.call(
        "mlp_down",
        functools.partial(mlp_down_body, plan, len(pieces)),
        (me, cot, slope, *pieces),
        [SMEM, VMEM, HELD] + [VMEM] * len(pieces),
        (
            sds((t, hidden), BF16),
            sds((fsdp, model), F32),
            sds((fsdp, 2, model, hidden // fsdp // 2), BF16),
        ),
        (HELD,) * 3,
        [],
        10,
    )


def mlp_out_body(table, resid, gel, c_v, t_in, output):
    model = resid.shape[1]
    total = resid[...] + table.get(t_in, 7)
    for j in range(c_v.shape[0]):
        down = jnp.concatenate([c_v[j, 0], c_v[j, 1]], axis=1)
        total = total + dot_nt(gel[:, j * model : (j + 1) * model], down)
    output[...] = total.astype(BF16)


def mlp_out(chain, plan, resid, gel, c_can, t_can):
    return chain.call(
        "mlp_out",
        functools.partial(mlp_out_body, Table(plan.fsdp)),
        (resid, gel, c_can, t_can),
        [HELD] * 4,
        sds(resid.shape, BF16),
        VMEM,
        [],
        10,
    )


def mlp_back_body(plan, n_out, me_ref, act, gpre, b_in, *refs):
    gact = refs[0]
    gouts = refs[1 : 1 + n_out]
    model = act.shape[1]
    me = Me(me_ref)
    first = True
    order = [
        (x, away, me.fsdp(x, away) if plan.direct else 2 * x + away)
        for away in range(2)
        for x in range(plan.nx)
    ]
    for x, away, f in order:
        part = gpre[:, pl.ds(pl.multiple_of(f * model, model), model)]
        grad = dot_tn(act[...], part).astype(BF16).reshape(b_in.shape[1:])
        if not plan.direct:
            gouts[0][f] = grad
        elif away:
            gouts[1][x], gouts[2][x] = grad[:, :, 0], grad[:, :, 1]
        else:
            gouts[0][0, x], gouts[0][1, x] = grad[:, :, 0], grad[:, :, 1]
        back = dot_nt(part, b_in[f].reshape(model, model))
        if first:
            gact[...] = back
        else:
            gact[...] += back
        first = False


def mlp_back(chain, plan, me, act, gpre, b_can):
    t, model = act.shape
    fsdp = plan.fsdp
    lead = (fsdp, *plan.split(), model)
    if plan.direct:
        one = (plan.nx, plan.nz, 2, plan.rows // 2, model)
        grads = [sds((2, *one), BF16), sds(one, BF16), sds(one, BF16)]
    else:
        grads = [sds(lead, BF16)]
    return chain.call(
        "mlp_back",
        functools.partial(mlp_back_body, plan, len(grads)),
        (me, act, gpre, b_can),
        [SMEM, HELD, HELD, HELD],
        (sds((t, model), F32), *grads),
        (HELD,) + (HELD,) * len(grads),
        [],
        10,
    )


def join_back_body(plan, me_ref, gact, cot, normal, inverse_in, mixed, wout, t_in, *refs):
    gresid, gmixed, inner, g_vec, *gouts = refs[:-1]
    o_v = refs[-1]
    model = cot.shape[1]
    table = Table(plan.fsdp)
    n, inverse = normal[...], inverse_in[:, 0:1]
    e = gact[...]
    g_vec[...] = jnp.zeros(g_vec.shape, F32)
    g_vec[0:1, :] = jnp.sum(e * n, axis=0, keepdims=True)
    g_vec[1:2, :] = jnp.sum(e, axis=0, keepdims=True)
    r = cot[...].astype(F32) + norm_back(e, n, inverse, table.get(t_in, 2))
    gresid[...] = r
    branch = r.astype(BF16)
    g_vec[2:3, :] = jnp.sum(branch.astype(F32), axis=0, keepdims=True)
    grad = dot_tn(mixed[...], branch).astype(BF16)
    if plan.direct:
        me = Me(me_ref)
        cut = plan.cols
        for f in range(plan.fsdp):
            o_v[f, :, 0:cut] = grad[:, f * cut : (f + 1) * cut]
            o_v[f, :, cut:] = jnp.zeros((model, o_v.shape[-1] - cut), BF16)
        for away in range(2):
            for x in range(plan.nx):
                part = o_v[me.fsdp(x, away)].reshape(*plan.split(), o_v.shape[-1])
                gouts[away][0, x], gouts[away][1, x] = part[:, :, 0], part[:, :, 1]
    else:
        gouts[0][...] = grad
    low = dot_nt(branch, wout[...]).astype(BF16)
    gmixed[...] = low
    product = low.astype(F32) * mixed[...].astype(F32)
    high = product.astype(BF16)
    rest = (product - high.astype(F32)).astype(BF16)
    head = lax.broadcasted_iota(jnp.int32, (model, 128), 0) // HEAD_DIM
    ones = (head == lax.broadcasted_iota(jnp.int32, (model, 128), 1)).astype(BF16)
    inner[...] = dot_nn(high, ones) + dot_nn(rest, ones)


def join_back(chain, plan, me, gact, cot, normal, inverse, mixed, wout, t_can, spare):
    t, model = cot.shape
    ins = [me, gact, cot, normal, inverse, mixed, wout, t_can]
    if plan.direct:
        grads = [sds((2, plan.nx, plan.nz, 2, plan.rows // 2, spare), BF16)] * 2
        grad_specs = [HELD] * 2
    else:
        grads, grad_specs = [sds((model, model), BF16)], [VMEM]
    return chain.call(
        "join_back",
        functools.partial(join_back_body, plan),
        ins,
        [SMEM, HELD, VMEM] + [HELD] * 5,
        (
            sds((t, model), F32),
            sds((t, model), BF16),
            sds((t, 128), F32),
            sds((8, model), F32),
            *grads,
        ),
        (HELD, HELD, HELD, HELD, *grad_specs),
        [pltpu.VMEM((plan.fsdp, model, spare), BF16)],
        14,
    )


def attend_back_body(heads, length_ref, qkv, gmixed, logs, inner, out):
    t = gmixed.shape[0]
    length = length_ref[0]
    scale = HEAD_DIM**-0.5

    def part(h, which):
        return qkv[which, :, h * HEAD_DIM : (h + 1) * HEAD_DIM]

    for i, h in enumerate(heads):
        lanes = slice(i * HEAD_DIM, (i + 1) * HEAD_DIM)
        q = part(h, 0)
        small = q * jnp.asarray(scale, BF16)
        k, v = part(h, 1), part(h, 2)
        go = gmixed[:, h * HEAD_DIM : (h + 1) * HEAD_DIM]
        gk, gv = [], []
        for lo in range(0, t, QBLOCK):
            n = lo + QBLOCK
            s = dot_nt(small[lo:n], k[:n])
            s = jnp.where(masks(length, lo, QBLOCK, n), s, neg_large)
            p = jnp.exp(s - logs[lo:n, i : i + 1])
            gp = dot_nt(go[lo:n], v[:n])
            ds = (p * (gp - inner[lo:n, h : h + 1])).astype(BF16)
            out[0, lo:n, lanes] = (dot_nn(ds, k[:n]) * scale).astype(BF16)
            gv.append(dot_tn(p.astype(BF16), go[lo:n]))
            gk.append(dot_tn(ds, small[lo:n]))
        for b in range(t // QBLOCK):
            rows = slice(b * QBLOCK, (b + 1) * QBLOCK)
            out[1, rows, lanes] = sum(x[rows] for x in gk[b:]).astype(BF16)
            out[2, rows, lanes] = sum(x[rows] for x in gv[b:]).astype(BF16)


def attend_back(chain, qkv, gmixed, logs, inner, length, heads):
    t = qkv.shape[1]
    return chain.call(
        "attend_back",
        functools.partial(attend_back_body, heads),
        (length, qkv, gmixed, logs, inner),
        [SMEM, HELD, HELD, HELD, HELD],
        sds((3, t, len(heads) * HEAD_DIM), BF16),
        HELD,
        [],
        8,
    )


def whole_qkv(parts, flat, blocks):
    wide = blocks.shape[2]
    model = flat.shape[1] // 3
    at = 0
    for p in parts:
        size = p.shape[2]
        for which in range(3):
            lo = which * model + at
            flat[:, lo : lo + size] = p[which]
        at += size
    for f in range(blocks.shape[0]):
        blocks[f] = flat[:, f * wide : (f + 1) * wide]


def back_body(plan, wide, n_parts, n_out, me_ref, normal, inverse_in, act, a_in, gresid, t_in, g_two, g_b_fc, g_b_proj, *refs):
    parts, refs = refs[:n_parts], refs[n_parts:]
    input_grad, gouts, refs = refs[0], refs[1 : 1 + n_out], refs[1 + n_out :]
    flat, gq_v, tab, a_v, in_sem = refs
    late = pltpu.make_async_copy(a_in, a_v, in_sem)
    late.start()
    fsdp = plan.fsdp
    t, model = normal.shape
    table = Table(fsdp)
    spare = tab.shape[0] // fsdp
    whole_qkv(parts, flat, gq_v)
    me = Me(me_ref)

    def each():
        for away in range(2):
            for x in range(plan.nx):
                if plan.direct:
                    ends = [gouts[1 + h].at[x] if away else gouts[0].at[h, x] for h in range(2)]
                    yield me.fsdp(x, away), ends
                else:
                    yield 2 * x + away, [gouts[0].at[2 * x + away, :, :, h] for h in range(1)]

    for f, ends in each():
        grad = dot_tn(act[...], gq_v[f]).astype(BF16).reshape(*plan.split(), wide)
        for h, end in enumerate(ends):
            end[:, :, :, 0:wide] = grad[:, :, h]
    late.wait()
    back = dot_nt(flat[...], a_v[...])
    sums = dot_nn(jnp.ones((8, t), BF16), flat[...])
    n, inverse = normal[...], inverse_in[:, 0:1]
    tab[...] = jnp.zeros(tab.shape, F32)

    def put(k, value):
        r = (k // table.per) * spare + k % table.per
        tab[r : r + 1, :] = value

    put(0, jnp.sum(back * n, axis=0, keepdims=True))
    put(1, jnp.sum(back, axis=0, keepdims=True))
    put(2, g_two[0:1, :])
    put(3, g_two[1:2, :])
    put(4, sums[0:1, 0:model])
    put(5, sums[0:1, 2 * model :])
    put(6, g_two[2:3, :])
    put(7, g_b_proj[...])
    for j in range(fsdp):
        put(8 + j, g_b_fc[j : j + 1, :])
    for f, ends in each():
        rows = pl.ds(pl.multiple_of(f * spare, 8), spare)
        columns = jnp.transpose(tab[rows, :]).astype(BF16).reshape(*plan.split(), spare)
        for h, end in enumerate(ends):
            end[:, :, :, wide:] = columns[:, :, h]
    r = gresid[...] + norm_back(back, n, inverse, table.get(t_in, 0))
    input_grad[...] = r.astype(BF16)


def back(
    chain, plan, wide, full, me, normal, inverse, act, parts, a_can, gresid, t_can, g_two, g_b_fc, g_b_proj
):
    t, model = normal.shape
    fsdp = plan.fsdp
    lead = (fsdp, *plan.split(), full)
    if plan.direct:
        one = (plan.nx, plan.nz, 2, plan.rows // 2, full)
        grads = [sds((2, *one), BF16), sds(one, BF16), sds(one, BF16)]
    else:
        grads = [sds(lead, BF16)]
    return chain.call(
        "back",
        functools.partial(back_body, plan, wide, len(parts), len(grads)),
        (me, normal, inverse, act, a_can, gresid, t_can, g_two, g_b_fc, g_b_proj, *parts),
        [SMEM, HELD, HELD, HELD, HBM] + [HELD] * (5 + len(parts)),
        (sds((t, model), BF16), *grads),
        (VMEM,) + (HELD,) * len(grads),
        [
            pltpu.VMEM((t, 3 * model), BF16),
            pltpu.VMEM((fsdp, t, wide), BF16),
            pltpu.VMEM((fsdp * (full - wide), model), F32),
            pltpu.VMEM(a_can.shape, BF16),
            pltpu.SemaphoreType.DMA,
        ],
        20,
    )


def preload(chain, arrays):
    n = len(arrays)

    def body(*refs):
        todo = [
            pltpu.make_async_copy(a, b, refs[-1].at[i])
            for i, (a, b) in enumerate(zip(refs[:n], refs[n:-1]))
        ]
        for c in todo:
            c.start()
        for c in todo:
            c.wait()

    return chain.call(
        "preload",
        body,
        arrays,
        [HBM] * n,
        [sds(a.shape, a.dtype) for a in arrays],
        [HELD] * n,
        [pltpu.SemaphoreType.DMA((n,))],
        1,
    )


def update_body(count, *refs):
    norms = refs[0]
    n, m = 4 * count, 3 * count
    ins, norm_out, outs = refs[1 : 1 + n], refs[1 + n], refs[2 + n : 2 + n + m]
    made, out_sem = refs[2 + n + m : -1], refs[-1]
    norm = jnp.sqrt(jnp.sum(norms[...], axis=0, keepdims=True))
    norm_out[...] = norm
    factor = jnp.minimum(1.0, clip_limit / (norm[:, 0:1] + 1e-06))
    stores = []
    for i in range(count):
        w, g, one, two = (r[...] for r in ins[4 * i : 4 * i + 4])
        last = i == count - 1
        rate, decay = (rate_vector, 0.0) if last else (rate_matrix, decay_matrix)
        clipped = g * factor
        one_new = beta_one * one + (1.0 - beta_one) * clipped
        two_new = beta_two * two + (1.0 - beta_two) * clipped * clipped
        first_hat = one_new / (1.0 - beta_one**STEP)
        second_hat = two_new / (1.0 - beta_two**STEP)
        made[i][...] = w - rate * (first_hat / (jnp.sqrt(second_hat) + 1e-08) + decay * w)
        made[count + i][...] = one_new
        made[2 * count + i][...] = two_new
        for k in (i, count + i, 2 * count + i):
            c = pltpu.make_async_copy(made[k], outs[k], out_sem.at[k])
            c.start()
            stores.append(c)
    for c in stores:
        c.wait()


def update(chain, norms, weights, grads, firsts, seconds):
    count = len(weights)
    ins = []
    for group in zip(weights, grads, firsts, seconds):
        ins += group
    outs = [sds(w.shape, F32) for w in weights] * 3
    return chain.call(
        "update",
        functools.partial(update_body, count),
        [norms, *ins],
        [VMEM] + [HELD if i % 4 != 1 else VMEM for i in range(len(ins))],
        (sds((1, 128), F32), *outs),
        (VMEM,) + (HBM,) * len(outs),
        [pltpu.VMEM(v.shape, F32) for v in outs] + [pltpu.SemaphoreType.DMA((len(outs),))],
        12,
    )


def place_second(chain, name, plan, me, z0, r0, z1, r1):
    def copies(m):
        return [
            (0, ALL, [(0, (m.y,)), (2, (m.y,))]),
            (1, ALL, [(0, (m.other_y,)), (2, (m.other_y,))]),
            (2, ALL, [(1, (m.x,)), (3, (m.x,))]),
            (3, ALL, [(1, (m.other_x,)), (3, (m.other_x,))]),
        ]

    return move(chain, name, me, [z0, r0, z1, r1], [(2, *z0.shape), (2, *z1.shape)] * 2, copies)


class Parts:
    def __init__(self, groups, far=0):
        self.count, self.far = len(groups), far
        self.arrays = [own for own, _ in groups] + [v for _, came in groups for v in came]
        self.lanes, self.came, at, place = [], [], 0, self.count
        for own, came in groups:
            self.lanes.append(slice(at, at + own.shape[-1]))
            self.came.append((place, len(came)))
            at += own.shape[-1]
            place += len(came)
        _, self.nx, self.nz, _, self.rows, _ = groups[0][0].shape
        self.cols = at

    def terms(self, g, h, at):
        place, n = self.came[g]
        return [(g, (h, *at)), (place, (h, *at)) if n == 1 else (place + h, at)]

    def sums(self, make):
        return [
            item
            for g, lanes in enumerate(self.lanes)
            for item in make(g, (self.rows, lanes.stop - lanes.start), lanes)
        ]


def first_sums(chain, plan, name, me, parts):
    nx, nz = parts.nx, parts.nz

    def sums(m):
        return parts.sums(
            lambda g, end, lanes: [
                (0, (ALL, ALL, ALL, lanes), (nz, 2, *end), parts.terms(g, 0, (m.other_x,))),
                (1, (ALL, ALL, ALL, lanes), (nx, nz, *end), parts.terms(g, 1, (ALL, ALL, m.other_y))),
            ]
        )

    outs = [sds((nz, 2, parts.rows, parts.cols), BF16), sds((nx, nz, parts.rows, parts.cols), BF16)]
    s0, s1 = add_up(chain, name + "1", me, parts.arrays, outs, sums, far=parts.far)
    return plan.partner(name, s0, "x"), plan.partner(name, s1, "y")


def second_sums(chain, plan, name, me, parts, f0, f1):
    n = len(parts.arrays)

    def sums(m):
        at0, at1 = (m.x, ALL, m.other_y), (m.other_x, ALL, m.y)

        def make(g, end, lanes):
            one = parts.terms(g, 0, at0) + [(n, (ALL, m.other_y, ALL, lanes))]
            two = parts.terms(g, 1, at1) + [(n + 1, (m.other_x, ALL, ALL, lanes))]
            shape = (parts.nz, *end)
            return [(0, (ALL, ALL, lanes), shape, one), (1, (ALL, ALL, lanes), shape, two)]

        return parts.sums(make)

    outs = [sds((parts.nz, parts.rows, parts.cols), BF16)] * 2
    arrays = [*parts.arrays, f0, f1]
    s0, s1 = add_up(chain, name + "2", me, arrays, outs, sums, far=parts.far)
    return plan.partner(name, s0, "y"), plan.partner(name, s1, "x")


def third_sums(chain, plan, name, me, parts, f0, f1, s0, s1, merged):
    n, rows = len(parts.arrays), parts.rows

    def sums(m):
        def make(g, end, lanes):
            out = []
            for k in range(parts.nz):
                z = m.z ^ k
                at = (m.x, z, m.y)
                one = parts.terms(g, 0, at) + [(n, (z, m.y, ALL, lanes)), (n + 2, (z, ALL, lanes))]
                two = parts.terms(g, 1, at) + [(n + 1, (m.x, z, ALL, lanes)), (n + 3, (z, ALL, lanes))]
                t, ti = z_target(k, merged)
                out.append((t, (*ti, slice(0, rows), lanes), end, one))
                out.append((t, (*ti, slice(rows, 2 * rows), lanes), end, two))
            return out

        return parts.sums(make)

    outs = z_outs((2 * rows, parts.cols), merged)
    arrays = [*parts.arrays, f0, f1, s0, s1]
    return add_up(chain, name + "3", me, arrays, outs, sums, far=parts.far)


def z_outs(shape, merged):
    if merged:
        return [sds(shape, F32), sds((2, *shape), BF16), sds(shape, BF16)]
    return [sds(shape, F32)] + [sds(shape, BF16)] * 3


def z_target(k, merged):
    if merged and k in (1, 3):
        return 1, (k // 2,)
    return k, ()


def along_z(chain, plan, name, me, two, came, at):
    (total,) = add_up(
        chain, name, me, [two, came], [two], lambda m: [(0, ALL, two.shape, [(0, ALL), (1, at)])]
    )
    return total


def squared(*values):
    return jnp.broadcast_to(sum(jnp.sum(v * v) for v in values), (1, 128))


def body(
    tokens,
    lengths,
    cotangent,
    qkv_weight,
    out_weight,
    fc_weight,
    proj_weight,
    vectors,
    qkv_first,
    out_first,
    fc_first,
    proj_first,
    vectors_first,
    qkv_second,
    out_second,
    fc_second,
    proj_second,
    vectors_second,
):
    dp, fsdp = lax.axis_size("dp"), lax.axis_size("fsdp")
    model = tokens.shape[1]
    wide, cut = qkv_weight.shape[1], out_weight.shape[1]
    hidden = fc_weight.shape[1] * fsdp
    per = vectors.shape[1]
    plan = Plan(dp, fsdp, model, hidden)
    rows, half, chalf, nz = plan.rows, plan.rows // 2, plan.cols // 2, plan.nz
    a_full = -(-(wide + per) // 128) * 128
    b_full = model + -(-cut // 128) * 128
    chain = Chain()
    at_dp, at_fsdp = lax.axis_index("dp"), lax.axis_index("fsdp")
    me = jnp.stack([at_dp // 2, at_dp % 2, at_fsdp // 2, at_fsdp % 2]).astype(jnp.int32)
    heads = model // HEAD_DIM
    third = [range(i, i + heads // 3) for i in range(0, heads, heads // 3)]

    def turned(value):
        return jnp.transpose(value)

    state = (
        *(qkv_weight, out_weight, fc_weight, turned(proj_weight), turned(vectors)),
        *(qkv_first, out_first, fc_first, turned(proj_first), turned(vectors_first)),
        *(qkv_second, out_second, fc_second, turned(proj_second), turned(vectors_second)),
    )

    if plan.direct:
        a_own, b_own, c_own = pack(chain, plan, state[:5], a_full, b_full)
        a_near, a_far = plan.partner("gather_a", a_own, "z", 1), plan.partner("gather_a", a_own, "z", 2)
        c_y, c_x = plan.partner("gather_c", c_own[0], "y"), plan.partner("gather_c", c_own[1], "x")
        chain.wait_for(c_y, c_x)
        a_far, b_own = gate(chain, "gate_z", a_far, b_own)
        a_came = [a_near, a_far, plan.partner("gather_a", a_far, "z", 1)]
        b_came = plan.gather_z("gather_b", b_own)

        def place_a(m):
            return [(k, ALL, [(0, (m.z ^ k,))]) for k in range(nz)]

        (a_z,) = move(chain, "place_a1", me, [a_own, *a_came], [(nz, rows, a_full)], place_a)
        a_y, a_x = plan.partner("gather_a", a_z, "y"), plan.partner("gather_a", a_z, "x")
        a_xy = plan.opposite("gather_a", a_z)

        def place_b(m):
            return [
                (k, pl.ds(h * half, half), [(h, (m.z ^ k,))]) for k in range(nz) for h in range(2)
            ] + [
                (nz, (0,), [(2, (m.y,))]),
                (nz + 1, ALL, [(2, (m.other_y,))]),
                (nz, (1,), [(2, (2 + m.x,))]),
                (nz + 2, ALL, [(2, (2 + m.other_x,))]),
            ]

        outs = [(nz, half, b_full), (nz, half, b_full), (4, chalf, plan.deep)]
        arrays = [b_own, *b_came, c_own, c_y, c_x]
        chain.wait_for(a_y, a_x, a_xy)
        b_z0, b_z1, c_pair = move(chain, "place_b1", me, arrays, outs, place_b)
        b_r0, b_r1 = plan.partner("gather_b", b_z0, "y"), plan.partner("gather_b", b_z1, "x")
        a_in = gate(chain, "gate_a", a_z, a_y, a_x, a_xy)
        a_in = a_in + [plan.partner("gather_a", v, "core") for v in a_in]
        c_near, c_far = plan.partner("gather_c", c_pair, "z", 1), plan.partner("gather_c", c_pair, "z", 2)
    else:

        def whole(shard):
            down = lax.all_gather(shard.astype(BF16), "dp", axis=0, tiled=True)
            return lax.all_gather(down, "fsdp", axis=0, tiled=False)

        def padded(parts, full):
            both = jnp.concatenate(parts, axis=1)
            both = whole(jnp.pad(both, ((0, 0), (0, full - both.shape[1]))))
            return both.reshape(fsdp, *plan.split(), full)

        a_in = [padded([qkv_weight, vectors], a_full)]
        b_in = [padded([fc_weight, out_weight], b_full)]
        c_all = jnp.transpose(whole(proj_weight), (0, 2, 1))
        c_all = c_all.reshape(model, fsdp, 2, hidden // fsdp // 2)
        c_in = [jnp.transpose(c_all, (1, 2, 0, 3))]

    qkv, act_one, a_can, t_can, n_one, inv_one = front(chain, plan, me, tokens, a_in, wide)
    if plan.direct:
        b_p0, b_p1, *b_pc = place_second(chain, "place_b2", plan, me, b_z0, b_r0, b_z1, b_r1)
        b_q0, b_q1 = plan.partner("gather_b", b_p0, "x"), plan.partner("gather_b", b_p1, "y")
    if plan.direct:
        c_near, c_far, *b_pc = gate(chain, "gate_c1", c_near, c_far, *b_pc)
        c_last = plan.partner("gather_c", c_far, "z", 1)
        b_pc = [plan.partner("gather_b", v, "core") for v in b_pc]
    parts = [attend(chain, qkv, lengths, group) for group in third]
    if plan.direct:
        b_q0, b_q1 = gate(chain, "gate_b", b_q0, b_q1)
        b_qc = [plan.partner("gather_b", v, "core") for v in (b_q0, b_q1)]
        b_in = [b_p0, b_p1, b_q0, b_q1, *b_pc, *b_qc]
        chain.wait_for(*b_pc)

        def place_c2(m):
            return [
                (k, (2 * h + p,), [(h, (p, m.z ^ k)), (2, (h, p, m.z ^ k))])
                for k in range(nz)
                for h in range(2)
                for p in range(2)
            ]

        outs = [(2, nz, chalf, plan.deep)] * 2 + [(2, 2, nz, chalf, plan.deep)]
        c_p0, c_p1, c_p = move(chain, "place_c2", me, [c_pair, c_near, c_far, c_last], outs, place_c2)
        c_q0, c_q1 = plan.partner("gather_c", c_p0, "x"), plan.partner("gather_c", c_p1, "y")
        c_pc = plan.partner("gather_c", c_p, "core")
    logs = [p[1] for p in parts]
    resid_two, act_two, wout, mixed, n_two, inv_two = join(
        chain, plan, me, cut, tokens, [p[0] for p in parts], b_in, t_can
    )
    if plan.direct:
        chain.wait_for(c_pc)
    gel, slope, b_can, g_b_proj, *g_c = mlp_up(
        chain, plan, me, act_two, cotangent, t_can, b_in, hidden
    )
    if plan.direct:
        c_q0, c_q1, away = gate(chain, "gate_c", c_q0, c_q1, g_c[1])
        c_in = [c_p, c_q0, c_q1, c_pc] + [plan.partner("gather_c", v, "core") for v in (c_q0, c_q1)]
        c_away = plan.partner("sum_c", away, "core")
    if plan.direct:
        c_parts = Parts([(g_c[0], [c_away])])
        c_f0, c_f1 = first_sums(chain, plan, "sum_c", me, c_parts)
    gpre, g_b_fc, c_can = mlp_down(chain, plan, me, cotangent, slope, c_in)

    gact, *g_b = mlp_back(chain, plan, me, act_two, gpre, b_can)
    if plan.direct:
        b_away = [plan.partner("sum_b", v, "core") for v in g_b[1:]]
    gresid, gmixed, inner, g_two, *g_o = join_back(
        chain, plan, me, gact, cotangent, n_two, inv_two, mixed, wout, t_can, b_full - model
    )
    if plan.direct:
        chain.wait_for(c_f0, c_f1)
        o_away = [plan.partner("sum_b", *gate(chain, "gate_o", g_o[1]), "core")]
        b_parts = Parts([(g_b[0], b_away), (g_o[0], o_away)])
    gparts = [attend_back(chain, qkv, gmixed, logs[0], inner, lengths, third[0])]
    if plan.direct:
        b_f0, b_f1 = first_sums(chain, plan, "sum_b", me, b_parts)

        def sums_cz(m):
            out = []
            for k in range(nz):
                z = m.z ^ k
                at = (0, m.x, z)
                terms = [(0, at), (1, at), (2, (z,))]
                t, ti = z_target(k, True)
                out.append((t, (*ti, slice(0, 2)), (2, chalf, plan.deep), terms))
                at = (1, ALL, z, m.y)
                terms = [(0, at), (1, at), (3, (ALL, z))]
                out.append((t, (*ti, slice(2, 4)), (2, chalf, plan.deep), terms))
            return out

        outs = z_outs((4, chalf, plan.deep), True)
        arrays = [g_c[0], c_away, c_f0, c_f1]
        c_u = add_up(chain, "sum_c2", me, arrays, outs, sums_cz)
        c_near = plan.partner("sum_c", c_u[1], "z", 1)
    for log, group in zip(logs[1:], third[1:]):
        gparts.append(attend_back(chain, qkv, gmixed, log, inner, lengths, group))
    kept = (n_one, inv_one, act_one, gparts, a_can, gresid, t_can, g_two, g_b_fc, g_b_proj)
    input_grad, *g_a = back(chain, plan, wide, a_full, me, *kept)

    if plan.direct:
        c_two = along_z(chain, plan, "sum_c4", me, c_u[2], c_near, (1,))
        c_z = [c_u[0], c_near, plan.partner("sum_c", c_two, "z", 2)]
        b_s0, b_s1 = second_sums(chain, plan, "sum_b", me, b_parts, b_f0, b_f1)
        a_away = [plan.partner("sum_a", v, "core") for v in gate(chain, "gate_s", *g_a[1:])]
        a_parts = Parts([(g_a[0], a_away)])
        a_f0, a_f1 = first_sums(chain, plan, "sum_a", me, a_parts)
        output = mlp_out(chain, plan, resid_two, gel, c_can, t_can)
        b_u = third_sums(chain, plan, "sum_b", me, b_parts, b_f0, b_f1, b_s0, b_s1, True)
        b_near = plan.partner("sum_b", b_u[1], "z", 1)
        a_s0, a_s1 = second_sums(chain, plan, "sum_a", me, a_parts, a_f0, a_f1)
        z_lead = ((), (0,), ())

        def sums_c3(m):
            block = (chalf, plan.deep)
            one = [(i, (*lead, m.other_y)) for i, lead in enumerate(z_lead)]
            two = [(i, (*lead, 2 + m.other_x)) for i, lead in enumerate(z_lead)]
            return [(0, ALL, block, one), (1, ALL, block, two)]

        outs = [sds((chalf, plan.deep), BF16)] * 2
        s0, s1 = add_up(chain, "sum_c3", me, c_z, outs, sums_c3)
        c_l0, c_l1 = plan.partner("sum_c", s0, "y"), plan.partner("sum_c", s1, "x")
        b_two = along_z(chain, plan, "sum_b4", me, b_u[2], b_near, (1,))
        b_z = [b_u[0], b_near, plan.partner("sum_b", b_two, "z", 2)]
        a_u = third_sums(chain, plan, "sum_a", me, a_parts, a_f0, a_f1, a_s0, a_s1, False)
        a_via, a_near = plan.partner("sum_a", a_u[3], "z", 1), plan.partner("sum_a", a_u[1], "z", 1)

        def sums_c(m):
            block = (chalf, plan.deep)
            one = [(i, (*lead, m.y)) for i, lead in enumerate(z_lead)] + [(3, ALL)]
            two = [(i, (*lead, 2 + m.x)) for i, lead in enumerate(z_lead)] + [(4, ALL)]
            return [(0, ALL, block, one), (1, ALL, block, two)]

        state = preload(chain, state)
        a_two = along_z(chain, plan, "sum_a4", me, a_u[2], a_via, ALL)
        a_z = [a_u[0], a_near, plan.partner("sum_a", a_two, "z", 2)]

        def end_c(done, outs):
            outs[0][0:chalf, :] = done[0]
            outs[0][chalf:, :] = done[1]
            outs[1][...] = squared(*done)

        d_proj, s_c = add_up(
            chain,
            "end_c",
            me,
            [*c_z, c_l0, c_l1],
            [sds((plan.cols, plan.deep), F32), sds((1, 128), F32)],
            sums_c,
            end_c,
        )
        def last_b(m):
            shape = b_z[0].shape
            return [(0, ALL, shape, [(i, lead or ALL) for i, lead in enumerate(z_lead)])]

        def last_a(m):
            return [(0, ALL, a_z[0].shape, [(i, ALL) for i in range(len(a_z))])]

        def end_b(done, outs):
            total = done[0]
            fc, out = total[:, :model], total[:, model : model + cut]
            outs[0][...] = fc
            outs[1][...] = out
            outs[2][...] = squared(fc, out)

        shapes = [fc_weight.shape, out_weight.shape, (1, 128)]
        d_fc, d_out, s_b = add_up(
            chain, "end_b", me, b_z, [sds(s, F32) for s in shapes], last_b, end_b
        )

        def end_a(done, outs):
            total = done[0]
            start = wide // 128 * 128
            vec = jnp.transpose(total[:, start:])[wide - start : wide - start + per]
            qkv = total[:, :wide]
            outs[0][...] = qkv
            outs[1][...] = vec
            outs[2][...] = squared(qkv, vec)

        shapes = [qkv_weight.shape, (per, rows), (1, 128)]
        d_qkv, d_vec, s_a = add_up(
            chain, "end_a", me, a_z, [sds(s, F32) for s in shapes], last_a, end_a
        )
        squares = s_a + s_b + s_c
    else:
        output = mlp_out(chain, plan, resid_two, gel, c_can, t_can)

        def shared(value):
            mine = lax.psum_scatter(value, "fsdp", scatter_dimension=0, tiled=False)
            return lax.psum_scatter(mine, "dp", scatter_dimension=0, tiled=True).astype(F32)

        d_a = shared(g_a[0].reshape(fsdp, model, a_full))
        d_qkv, d_vec = d_a[:, :wide], turned(d_a[:, wide : wide + per])
        d_out = shared(jnp.transpose(g_o[0].reshape(model, fsdp, cut), (1, 0, 2)))
        d_fc = shared(g_b[0].reshape(fsdp, model, model))
        d_c = jnp.transpose(g_c[0], (2, 0, 1, 3)).reshape(fsdp, plan.cols, hidden)
        d_proj = turned(shared(jnp.transpose(d_c, (0, 2, 1))))
        total = sum(jnp.sum(d * d) for d in (d_qkv, d_out, d_fc, d_proj, d_vec))
        squares = jnp.full((1, 128), total)

    sent = jnp.broadcast_to(squares[None], (dp * fsdp, 1, 128))
    with jax.named_scope("norm"):
        norms = lax.all_to_all(sent, ("dp", "fsdp"), 0, 0, tiled=True).reshape(dp * fsdp, 128)
    norm, *new = update(
        chain, norms, state[:5], (d_qkv, d_out, d_fc, d_proj, d_vec), state[5:10], state[10:]
    )
    new = [turned(v) if i % 5 in (3, 4) else v for i, v in enumerate(new)]
    return (output, input_grad, norm[0, 0], *new)


def solution(mesh):
    tokens = P(("dp", "fsdp"), None)
    table = P("dp", "fsdp")
    return jax.shard_map(
        body,
        mesh=mesh,
        in_specs=(tokens, P(("dp", "fsdp")), tokens) + (table,) * 15,
        out_specs=(tokens, tokens, P()) + (table,) * 15,
        check_vma=False,
    )
```

```python
import functools

import jax
import jax.numpy as jnp
from jax import lax
from jax.experimental import pallas as pl
from jax.experimental.pallas import tpu as pltpu
from jax.sharding import PartitionSpec as P

HEAD_DIM = 64
STEP = 10

beta_one = 0.9
beta_two = 0.95
clip_limit = 1.0
rate_matrix = 0.1
rate_vector = 1.0
decay_matrix = 0.1
gelu_coeff = 0.7978845608028654
cubic_coeff = 0.044715
neg_large = -1e30
VEC_ROWS = 16

F32 = jnp.float32
BF16 = jnp.bfloat16
VMEM = pl.BlockSpec(memory_space=pltpu.VMEM)
HELD = pl.BlockSpec(memory_space=pltpu.VMEM)
ANY = pl.BlockSpec(memory_space=pl.ANY)
HBM = pl.BlockSpec(memory_space=pltpu.HBM)
SMEM = pl.BlockSpec(memory_space=pltpu.SMEM)
ALL = slice(None)


def dot_nn(a, b):
    return lax.dot_general(a, b, (((1,), (0,)), ((), ())), preferred_element_type=F32)


def dot_nt(a, b):
    return lax.dot_general(a, b, (((1,), (1,)), ((), ())), preferred_element_type=F32)


def dot_tn(a, b):
    return lax.dot_general(a, b, (((0,), (0,)), ((), ())), preferred_element_type=F32)


def sds(shape, dtype):
    return jax.ShapeDtypeStruct(shape, dtype)


class Chain:
    def __init__(self):
        self.waits = []

    def wait_for(self, *arrays):
        self.waits += arrays

    def call(self, name, body, ins, in_specs, outs, out_specs, scratch, limit, aliases=None):
        several = isinstance(outs, (tuple, list))
        if not several:
            outs, out_specs = (outs,), (out_specs,)
        n_in, extra, n_out = len(ins), len(self.waits), len(outs)
        pins = ((HELD, pltpu.VMEM), (HBM, pltpu.HBM))

        def run(*refs):
            given, refs = refs[:n_in], refs[n_in + extra :]
            refs[n_out][...] = jnp.zeros(refs[n_out].shape, F32)
            body(*given, *refs[:n_out], *refs[n_out + 1 :])

        placed, made = [], []
        for v, spec in zip(ins, in_specs):
            for pin, space in pins:
                if spec is pin:
                    v = pltpu.with_memory_space_constraint(v, space)
            placed.append(v)
        for o, spec in zip(outs, out_specs):
            for pin, space in pins:
                if spec is pin:
                    o = space(o.shape, o.dtype)
            made.append(o)
        results = pl.pallas_call(
            run,
            name=name,
            input_output_aliases=aliases or {},
            out_shape=(*made, pltpu.VMEM((8, 128), F32)),
            in_specs=[*in_specs, *[ANY] * extra],
            out_specs=(*out_specs, HELD),
            scratch_shapes=scratch,
            compiler_params=pltpu.CompilerParams(vmem_limit_bytes=limit << 20),
        )(*placed, *self.waits)
        *results, token = results
        self.waits = [pltpu.with_memory_space_constraint(token, pltpu.VMEM)]
        return results if several else results[0]


class Plan:
    def __init__(self, dp, fsdp, model, hidden):
        self.dp, self.fsdp = dp, fsdp
        self.nz, self.nx = dp // 2, fsdp // 2
        self.rows = model // dp
        self.cols = model // fsdp
        self.deep = hidden // dp
        self.direct = (
            dp == 2 * fsdp
            and fsdp % 2 == 0
            and self.rows % 32 == 0
            and self.cols % 32 == 0
            and self.deep % 128 == 0
            and hidden == fsdp * model
            and dp == 8
        )

    def partner(self, name, value, stage, k=1):
        axis, step = {"x": ("fsdp", 2), "y": ("dp", 1), "z": ("dp", 2), "core": ("fsdp", 1)}[stage]
        n = self.dp if axis == "dp" else self.fsdp
        with jax.named_scope(f"{name}_{stage}"):
            return lax.ppermute(value, axis, [(i, i ^ (step * k)) for i in range(n)])

    def opposite(self, name, value):
        n = self.fsdp
        pairs = [(i * n + j, (i ^ 1) * n + (j ^ 2)) for i in range(self.dp) for j in range(n)]
        with jax.named_scope(f"{name}_xy"):
            return lax.ppermute(value, ("dp", "fsdp"), pairs)

    def gather_z(self, name, value):
        near, far = self.partner(name, value, "z", 1), self.partner(name, value, "z", 2)
        return [near, far, self.partner(name, far, "z", 1)]

    def split(self):
        return (self.nz, 2, 2, self.rows // 2) if self.direct else (1, 1, 1, self.rows * self.dp)


class Me:
    def __init__(self, ref):
        self.z, self.y, self.x, self.core = ref[0], ref[1], ref[2], ref[3]
        self.other_y, self.other_x = 1 - self.y, 1 - self.x

    def fsdp(self, x, away):
        return 2 * x + (self.core ^ away)


def move(chain, name, me, arrays, outs, copies):
    n = len(arrays)

    def body(me_ref, *refs):
        for s, si, targets in copies(Me(me_ref)):
            value = refs[s][si]
            for t, ti in targets:
                refs[n + t][ti] = value

    return chain.call(
        name,
        body,
        (me, *arrays),
        [SMEM] + [VMEM] * n,
        tuple(sds(s, BF16) for s in outs),
        (HELD,) * len(outs),
        [],
        6,
    )


def gate(chain, name, *arrays, far=0):
    specs = [ANY] * (len(arrays) - far) + [HBM] * far
    return chain.call(
        name,
        lambda *refs: None,
        arrays,
        specs,
        tuple(sds(v.shape, v.dtype) for v in arrays),
        tuple(specs),
        [],
        1,
        {i: i for i in range(len(arrays))},
    )


def add_up(chain, name, me, arrays, outs, sums, after=None, far=0):
    n, m = len(arrays), len(outs)
    still = sums(Me([0, 0, 0, 0]))
    loaded = [shape for _, _, shape, parts in still for s, _ in parts if s < far]

    def body(me_ref, *refs):
        ins, outs_, refs = refs[:n], refs[n : n + m], refs[n + m :]
        held, sem = refs[: len(loaded)], refs[len(loaded) :]
        todo, i = [], 0
        for t, ti, shape, parts in sums(Me(me_ref)):
            group = []
            for s, si in parts:
                copy = None
                if s < far:
                    copy = pltpu.make_async_copy(ins[s].at[si], held[i], sem[0].at[i])
                    copy.start()
                    i += 1
                group.append((copy, s, si, i - 1))
            todo.append((t, ti, group))
        done = []
        for t, ti, group in todo:
            total = None
            for copy, s, si, k in reversed(group):
                if copy is not None:
                    copy.wait()
                v = (ins[s][si] if copy is None else held[k][...]).astype(F32)
                total = v if total is None else total + v
            if after is None:
                outs_[t][ti] = total.astype(outs_[t].dtype)
            else:
                done.append(total)
        if after is not None:
            after(done, outs_)

    return chain.call(
        name,
        body,
        (me, *arrays),
        [SMEM] + [HBM if i < far else VMEM for i in range(n)],
        tuple(outs),
        (HELD if after is None else VMEM,) * m,
        [pltpu.VMEM(shape, BF16) for shape in loaded]
        + ([pltpu.SemaphoreType.DMA((len(loaded),))] if loaded else []),
        8,
    )


def pack_body(ins, outs, held, sem):
    todo = [pltpu.make_async_copy(i, h, sem.at[k]) for k, (i, h) in enumerate(zip(ins, held))]
    for c in todo:
        c.start()
    for c in todo:
        c.wait()
    qkv, out, fc, proj, vec = (h[...] for h in held)
    a, b, c = outs
    wide, model = qkv.shape[1], fc.shape[1]
    columns = jnp.transpose(vec)
    start = wide // 128 * 128
    a[:, start:] = jnp.zeros((a.shape[0], a.shape[1] - start), BF16)
    a[:, 0:wide] = qkv.astype(BF16)
    a[:, wide : wide + columns.shape[1]] = columns.astype(BF16)
    b[:, model:] = jnp.zeros((b.shape[0], b.shape[1] - model), BF16)
    b[:, 0:model] = fc.astype(BF16)
    b[:, model : model + out.shape[1]] = out.astype(BF16)
    c[...] = proj.astype(BF16).reshape(c.shape)


def pack(chain, plan, weights, a_full, b_full):
    count = len(weights)

    def run(*refs):
        pack_body(refs[:count], refs[count : count + 3], refs[count + 3 : -1], refs[-1])

    return chain.call(
        "pack",
        run,
        weights,
        [HBM] * count,
        (
            sds((plan.rows, a_full), BF16),
            sds((plan.rows, b_full), BF16),
            sds((2, plan.cols // 2, plan.deep), BF16),
        ),
        (VMEM,) * 3,
        [pltpu.VMEM(w.shape, F32) for w in weights] + [pltpu.SemaphoreType.DMA((count,))],
        6,
    )


def normed(values):
    mean = jnp.mean(values, axis=-1, keepdims=True)
    centred = values - mean
    spread = jnp.mean(centred * centred, axis=-1, keepdims=True)
    inverse = lax.rsqrt(spread + 1e-05)
    return centred * inverse, inverse


def norm_back(grad_hidden, n, inverse, gain):
    g = grad_hidden * gain
    mean_plain = jnp.mean(g, axis=-1, keepdims=True)
    mean_cross = jnp.mean(g * n, axis=-1, keepdims=True)
    return inverse * (g - mean_plain - n * mean_cross)


class Table:
    def __init__(self, fsdp):
        self.per = 12 // fsdp

    def row(self, k):
        return (k // self.per) * VEC_ROWS + k % self.per

    def get(self, ref, k):
        r = self.row(k)
        return ref[r : r + 1, :]


def spread_matrix(rows, model, d):
    r = lax.broadcasted_iota(jnp.int32, (128, model), 0)
    c = lax.broadcasted_iota(jnp.int32, (128, model), 1)
    return ((c == r + d * rows) & (r < rows)).astype(BF16)


def halves(ins, away):
    n = len(ins) // 2
    part = ins[n * away : n * away + n]
    own = (part[0].at[0], part[0].at[1]) if n == 3 else part[:2]
    return (*own, *part[-2:])


def table_loads(plan, me, ins):
    for away in range(2):
        p0, p1, r0, r1 = halves(ins, away)
        for y in range(2):
            for x, ref in ((me.x, p0), (me.other_x, r0)):
                yield ref, (y,), me.fsdp(x, away), (ALL, y), 0
        for y, ref in ((me.y, p1), (me.other_y, r1)):
            for x in range(plan.nx):
                yield ref, (x,), me.fsdp(x, away), (ALL, y), 1


def front_body(plan, wide, n_in, me_ref, tokens, *refs):
    ins = refs[:n_in]
    qkv, act, a_out, t_out, n_out, inv_out = refs[n_in : n_in + 6]
    a_v, flat, sem, out_sem = refs[n_in + 6 :]
    fsdp = plan.fsdp
    full = a_v.shape[-1]
    model = tokens.shape[1]
    table = Table(fsdp)
    if plan.direct:
        me = Me(me_ref)
        for i, ref in enumerate(ins):
            away, x, y = i // 4, i // 2 % 2, i % 2
            f = me.fsdp(me.x ^ x, away)
            pltpu.make_async_copy(ref, a_v.at[f, :, me.y ^ y], sem.at[f]).start()
    else:
        for f in range(fsdp):
            pltpu.make_async_copy(ins[0].at[f], a_v.at[f], sem.at[f]).start()
    n, inverse = normed(tokens[...].astype(F32))
    n_out[...] = n
    inv_out[...] = jnp.broadcast_to(inverse, inv_out.shape)
    start = wide // 128 * 128
    for f in range(fsdp):
        pltpu.make_async_copy(a_v.at[f], a_v.at[f], sem.at[f]).wait()
        block = a_v[f].reshape(model, full)
        flat[:, f * wide : (f + 1) * wide] = block[:, :wide]
        turned = jnp.transpose(block[:, start:].astype(F32))
        t_out[f * VEC_ROWS : f * VEC_ROWS + table.per, :] = turned[
            wide - start : wide - start + table.per
        ]
    copy = pltpu.make_async_copy(flat, a_out, out_sem)
    copy.start()
    act[...] = (n * table.get(t_out, 0) + table.get(t_out, 1)).astype(BF16)
    for which in range(3):
        r = dot_nn(act[...], flat[:, which * model : (which + 1) * model])
        if which != 1:
            r = r + table.get(t_out, 4 + which // 2)
        qkv[which] = r.astype(BF16)
    copy.wait()


def front(chain, plan, me, tokens, pieces, wide):
    t, model = tokens.shape
    fsdp = plan.fsdp
    full = pieces[0].shape[-1]
    lead = (fsdp, plan.nz, 2, plan.rows, full) if plan.direct else pieces[0].shape
    return chain.call(
        "front",
        functools.partial(front_body, plan, wide, len(pieces)),
        (me, tokens, *pieces),
        [SMEM, VMEM] + [ANY] * len(pieces),
        (
            sds((3, t, model), BF16),
            sds((t, model), BF16),
            sds((model, 3 * model), BF16),
            sds((fsdp * VEC_ROWS, model), F32),
            sds((t, model), F32),
            sds((t, 128), F32),
        ),
        (HELD, HELD, HBM, HELD, HELD, HELD),
        [
            pltpu.VMEM(lead, BF16),
            pltpu.VMEM((model, 3 * model), BF16),
            pltpu.SemaphoreType.DMA((fsdp,)),
            pltpu.SemaphoreType.DMA,
        ],
        16,
    )


def masks(length, lo, size, keys):
    q = lax.broadcasted_iota(jnp.int32, (size, 1), 0) + lo
    limit = jnp.minimum(q, length - 1)
    k = lax.broadcasted_iota(jnp.int32, (size, keys), 1)
    return k <= limit


QBLOCK = 256


def attend_body(heads, length_ref, qkv, mixed, logs):
    t = mixed.shape[0]
    length = length_ref[0]
    scale = HEAD_DIM**-0.5

    def part(h, which):
        return qkv[which, :, h * HEAD_DIM : (h + 1) * HEAD_DIM]

    for i, h in enumerate(heads):
        q = part(h, 0) * jnp.asarray(scale, BF16)
        k, v = part(h, 1), part(h, 2)
        for lo in range(0, t, QBLOCK):
            n = lo + QBLOCK
            s = dot_nt(q[lo:n], k[:n])
            s = jnp.where(masks(length, lo, QBLOCK, n), s, neg_large)
            top = jnp.max(s, axis=-1, keepdims=True)
            e = jnp.exp(s - top)
            total = jnp.sum(e, axis=-1, keepdims=True)
            p = (e * (1.0 / total)).astype(BF16)
            o = dot_nn(p, v[:n])
            mixed[lo:n, i * HEAD_DIM : (i + 1) * HEAD_DIM] = o.astype(BF16)
            logs[lo:n, i : i + 1] = top + jnp.log(total)


def attend(chain, qkv, length, heads):
    t = qkv.shape[1]
    return chain.call(
        "attend",
        functools.partial(attend_body, heads),
        (length, qkv),
        [SMEM, HELD],
        (sds((t, len(heads) * HEAD_DIM), BF16), sds((t, 128), F32)),
        (HELD, HELD),
        [],
        6,
    )


def join_body(plan, cut, n_in, n_mixed, me_ref, tokens, t_in, *refs):
    ins, refs = refs[:n_in], refs[n_in:]
    parts, (resid, act, wout, mixed, n_out, inv_out, o_v, sem) = refs[:n_mixed], refs[n_mixed:]
    model = tokens.shape[1]
    fsdp = plan.fsdp
    table = Table(fsdp)
    lanes = pl.ds(model, o_v.shape[-1])
    if plan.direct:
        for ref, si, f, ti, h in table_loads(plan, Me(me_ref), ins):
            src = ref.at[(*si, ALL, ALL, lanes)]
            pltpu.make_async_copy(src, o_v.at[(f, *ti, h)], sem).start()
    else:
        for f in range(fsdp):
            src = ins[0].at[(f, ALL, ALL, ALL, ALL, lanes)]
            pltpu.make_async_copy(src, o_v.at[f], sem).start()
    at = 0
    for p in parts:
        mixed[:, at : at + p.shape[1]] = p[...]
        at += p.shape[1]
    pltpu.make_async_copy(o_v, o_v, sem).wait()
    for f in range(fsdp):
        wout[:, f * cut : (f + 1) * cut] = o_v[f].reshape(model, o_v.shape[-1])[:, :cut]
    r = tokens[...].astype(F32) + dot_nn(mixed[...], wout[...]) + table.get(t_in, 6)
    resid[...] = r
    n, inverse = normed(r)
    n_out[...] = n
    inv_out[...] = jnp.broadcast_to(inverse, inv_out.shape)
    act[...] = (n * table.get(t_in, 2) + table.get(t_in, 3)).astype(BF16)


def join(chain, plan, me, cut, tokens, parts, pieces, t_can):
    t, model = tokens.shape
    spare = pieces[0].shape[-1] - model
    return chain.call(
        "join",
        functools.partial(join_body, plan, cut, len(pieces), len(parts)),
        (me, tokens, t_can, *pieces, *parts),
        [SMEM, VMEM, HELD] + [ANY] * len(pieces) + [HELD] * len(parts),
        (
            sds((t, model), F32),
            sds((t, model), BF16),
            sds((model, model), BF16),
            sds((t, model), BF16),
            sds((t, model), F32),
            sds((t, 128), F32),
        ),
        (HELD,) * 6,
        [pltpu.VMEM((plan.fsdp, *plan.split(), spare), BF16), pltpu.SemaphoreType.DMA],
        10,
    )


def gelu_and_slope(pre):
    square = pre * pre
    th = jnp.tanh(pre * (gelu_coeff + (gelu_coeff * cubic_coeff) * square))
    plus = 0.5 * th + 0.5
    bend = 0.5 * gelu_coeff + (1.5 * gelu_coeff * cubic_coeff) * square
    return (pre * plus).astype(BF16), plus + pre * (1.0 - th * th) * bend


def mlp_up_body(plan, n_in, n_out, me_ref, act, cot, t_in, *refs):
    ins, refs = refs[:n_in], refs[n_in:]
    gel_out, slope_out, b_v, g_b_proj = refs[:4]
    gouts, refs = refs[4 : 4 + n_out], refs[4 + n_out :]
    gp_v, sem = refs
    fsdp, half = plan.fsdp, plan.cols // 2
    t, model = act.shape
    deep = gp_v.shape[-1]
    per = Table(fsdp).per
    me = Me(me_ref)
    order = []
    for k in range(fsdp):
        if plan.direct:
            away, x = k // 2, me.x if k % 2 == 0 else me.other_x
            p0, p1, r0, r1 = halves(ins, away)
            f = me.fsdp(x, away)
            own = p0 if k % 2 == 0 else r0
            loads = [(own.at[y], y, 0) for y in range(2)]
            loads += [(p1.at[x], me.y, 1), (r1.at[x], me.other_y, 1)]
            for ref, y, h in loads:
                src = ref.at[:, :, pl.ds(0, model)]
                pltpu.make_async_copy(src, b_v.at[f, :, y, h], sem.at[k]).start()
        else:
            f = k
            src = ins[0].at[(f, ALL, ALL, ALL, ALL, pl.ds(0, model))]
            pltpu.make_async_copy(src, b_v.at[f], sem.at[k]).start()
        order.append(f)
    g_b_proj[...] = jnp.sum(cot[...].astype(F32), axis=0, keepdims=True)

    def up(k, lo, hi):
        row = 8 + order[k]
        bias = t_in[pl.ds(row // per * VEC_ROWS + row % per, 1), :]
        return dot_nn(act[lo:hi], b_v[order[k]].reshape(model, model)) + bias

    step = t // 2
    for k in range(fsdp):
        pltpu.make_async_copy(b_v.at[order[k]], b_v.at[order[k]], sem.at[k]).wait()
        lanes = pl.ds(pl.multiple_of(order[k] * model, model), model)
        for lo in range(0, t, step):
            gel, slope = gelu_and_slope(up(k, lo, lo + step))
            gel_out[lo : lo + step, lanes] = gel
            slope_out[lo : lo + step, lanes] = slope
        grad = dot_tn(cot[...], gel_out[:, lanes]).astype(BF16)
        if not plan.direct:
            gouts[0][k, 0], gouts[0][k, 1] = grad[:, :deep], grad[:, deep:]
            continue
        gp_v[0], gp_v[1] = grad[:, :deep], grad[:, deep:]
        for away in range(2):
            for x in range(plan.nx):
                for h in range(2):
                    row = me.fsdp(x, away) * plan.cols + h * half
                    part = gp_v[:, pl.ds(pl.multiple_of(row, 16), half), :]
                    gouts[away][h, x, pl.ds(order[k], 1)] = part[None]


def mlp_up(chain, plan, me, act, cot, t_can, pieces, hidden):
    t, model = act.shape
    fsdp = plan.fsdp
    per = hidden // fsdp // 2
    if plan.direct:
        grads = [sds((2, plan.nx, plan.nz, 2, plan.cols // 2, plan.deep), BF16)] * 2
    else:
        grads = [sds((fsdp, 2, model, per), BF16)]
    lead = (fsdp, *plan.split(), model)
    return chain.call(
        "mlp_up",
        functools.partial(mlp_up_body, plan, len(pieces), len(grads)),
        (me, act, cot, t_can, *pieces),
        [SMEM, HELD, VMEM, HELD] + [ANY] * len(pieces),
        (
            sds((t, hidden), BF16),
            sds((t, hidden), F32),
            sds(lead, BF16),
            sds((1, model), F32),
            *grads,
        ),
        (HELD,) * (4 + len(grads)),
        [
            pltpu.VMEM((2, model, per), BF16),
            pltpu.SemaphoreType.DMA((fsdp,)),
        ],
        18,
    )


def mlp_down_body(plan, n_in, me_ref, cot, slope, *refs):
    ins, refs = refs[:n_in], refs[n_in:]
    gpre, g_b_fc, c_v = refs
    half = plan.cols // 2
    model = cot.shape[1]
    if plan.direct:
        for ref, si, f, ti, h in table_loads(plan, Me(me_ref), ins):
            rows = pl.ds(pl.multiple_of(f * plan.cols + h * half, 16), half)
            c_v[(*ti, rows)] = ref[si]
    else:
        c_v[...] = ins[0][...]
    for j in range(plan.fsdp):
        lanes = slice(j * model, (j + 1) * model)
        down = jnp.concatenate([c_v[j, 0], c_v[j, 1]], axis=1)
        low = (dot_nn(cot[...], down) * slope[:, lanes]).astype(BF16)
        gpre[:, lanes] = low
        g_b_fc[j : j + 1, :] = jnp.sum(low.astype(F32), axis=0, keepdims=True)


def mlp_down(chain, plan, me, cot, slope, pieces):
    t, model = cot.shape
    fsdp, hidden = plan.fsdp, slope.shape[1]
    return chain.call(
        "mlp_down",
        functools.partial(mlp_down_body, plan, len(pieces)),
        (me, cot, slope, *pieces),
        [SMEM, VMEM, HELD] + [VMEM] * len(pieces),
        (
            sds((t, hidden), BF16),
            sds((fsdp, model), F32),
            sds((fsdp, 2, model, hidden // fsdp // 2), BF16),
        ),
        (HELD,) * 3,
        [],
        10,
    )


def mlp_out_body(table, resid, gel, c_v, t_in, output):
    model = resid.shape[1]
    total = resid[...] + table.get(t_in, 7)
    for j in range(c_v.shape[0]):
        down = jnp.concatenate([c_v[j, 0], c_v[j, 1]], axis=1)
        total = total + dot_nt(gel[:, j * model : (j + 1) * model], down)
    output[...] = total.astype(BF16)


def mlp_out(chain, plan, resid, gel, c_can, t_can):
    return chain.call(
        "mlp_out",
        functools.partial(mlp_out_body, Table(plan.fsdp)),
        (resid, gel, c_can, t_can),
        [HELD] * 4,
        sds(resid.shape, BF16),
        VMEM,
        [],
        10,
    )


def mlp_back_body(plan, n_out, me_ref, act, gpre, b_in, *refs):
    gact = refs[0]
    gouts = refs[1 : 1 + n_out]
    model = act.shape[1]
    me = Me(me_ref)
    first = True
    order = [
        (x, away, me.fsdp(x, away) if plan.direct else 2 * x + away)
        for away in range(2)
        for x in range(plan.nx)
    ]
    for x, away, f in order:
        part = gpre[:, pl.ds(pl.multiple_of(f * model, model), model)]
        grad = dot_tn(act[...], part).astype(BF16).reshape(b_in.shape[1:])
        if not plan.direct:
            gouts[0][f] = grad
        elif away:
            gouts[1][x], gouts[2][x] = grad[:, :, 0], grad[:, :, 1]
        else:
            gouts[0][0, x], gouts[0][1, x] = grad[:, :, 0], grad[:, :, 1]
        back = dot_nt(part, b_in[f].reshape(model, model))
        if first:
            gact[...] = back
        else:
            gact[...] += back
        first = False


def mlp_back(chain, plan, me, act, gpre, b_can):
    t, model = act.shape
    fsdp = plan.fsdp
    lead = (fsdp, *plan.split(), model)
    if plan.direct:
        one = (plan.nx, plan.nz, 2, plan.rows // 2, model)
        grads = [sds((2, *one), BF16), sds(one, BF16), sds(one, BF16)]
    else:
        grads = [sds(lead, BF16)]
    return chain.call(
        "mlp_back",
        functools.partial(mlp_back_body, plan, len(grads)),
        (me, act, gpre, b_can),
        [SMEM, HELD, HELD, HELD],
        (sds((t, model), F32), *grads),
        (HELD,) + (HELD,) * len(grads),
        [],
        10,
    )


def join_back_body(plan, me_ref, gact, cot, normal, inverse_in, mixed, wout, t_in, *refs):
    gresid, gmixed, inner, g_vec, *gouts = refs[:-1]
    o_v = refs[-1]
    model = cot.shape[1]
    table = Table(plan.fsdp)
    n, inverse = normal[...], inverse_in[:, 0:1]
    e = gact[...]
    g_vec[...] = jnp.zeros(g_vec.shape, F32)
    g_vec[0:1, :] = jnp.sum(e * n, axis=0, keepdims=True)
    g_vec[1:2, :] = jnp.sum(e, axis=0, keepdims=True)
    r = cot[...].astype(F32) + norm_back(e, n, inverse, table.get(t_in, 2))
    gresid[...] = r
    branch = r.astype(BF16)
    g_vec[2:3, :] = jnp.sum(branch.astype(F32), axis=0, keepdims=True)
    grad = dot_tn(mixed[...], branch).astype(BF16)
    if plan.direct:
        me = Me(me_ref)
        cut = plan.cols
        for f in range(plan.fsdp):
            o_v[f, :, 0:cut] = grad[:, f * cut : (f + 1) * cut]
            o_v[f, :, cut:] = jnp.zeros((model, o_v.shape[-1] - cut), BF16)
        for away in range(2):
            for x in range(plan.nx):
                part = o_v[me.fsdp(x, away)].reshape(*plan.split(), o_v.shape[-1])
                gouts[away][0, x], gouts[away][1, x] = part[:, :, 0], part[:, :, 1]
    else:
        gouts[0][...] = grad
    low = dot_nt(branch, wout[...]).astype(BF16)
    gmixed[...] = low
    product = low.astype(F32) * mixed[...].astype(F32)
    high = product.astype(BF16)
    rest = (product - high.astype(F32)).astype(BF16)
    head = lax.broadcasted_iota(jnp.int32, (model, 128), 0) // HEAD_DIM
    ones = (head == lax.broadcasted_iota(jnp.int32, (model, 128), 1)).astype(BF16)
    inner[...] = dot_nn(high, ones) + dot_nn(rest, ones)


def join_back(chain, plan, me, gact, cot, normal, inverse, mixed, wout, t_can, spare):
    t, model = cot.shape
    ins = [me, gact, cot, normal, inverse, mixed, wout, t_can]
    if plan.direct:
        grads = [sds((2, plan.nx, plan.nz, 2, plan.rows // 2, spare), BF16)] * 2
        grad_specs = [HELD] * 2
    else:
        grads, grad_specs = [sds((model, model), BF16)], [VMEM]
    return chain.call(
        "join_back",
        functools.partial(join_back_body, plan),
        ins,
        [SMEM, HELD, VMEM] + [HELD] * 5,
        (
            sds((t, model), F32),
            sds((t, model), BF16),
            sds((t, 128), F32),
            sds((8, model), F32),
            *grads,
        ),
        (HELD, HELD, HELD, HELD, *grad_specs),
        [pltpu.VMEM((plan.fsdp, model, spare), BF16)],
        14,
    )


def attend_back_body(heads, length_ref, qkv, gmixed, logs, inner, out):
    t = gmixed.shape[0]
    length = length_ref[0]
    scale = HEAD_DIM**-0.5

    def part(h, which):
        return qkv[which, :, h * HEAD_DIM : (h + 1) * HEAD_DIM]

    for i, h in enumerate(heads):
        lanes = slice(i * HEAD_DIM, (i + 1) * HEAD_DIM)
        q = part(h, 0)
        small = q * jnp.asarray(scale, BF16)
        k, v = part(h, 1), part(h, 2)
        go = gmixed[:, h * HEAD_DIM : (h + 1) * HEAD_DIM]
        gk, gv = [], []
        for lo in range(0, t, QBLOCK):
            n = lo + QBLOCK
            s = dot_nt(small[lo:n], k[:n])
            s = jnp.where(masks(length, lo, QBLOCK, n), s, neg_large)
            p = jnp.exp(s - logs[lo:n, i : i + 1])
            gp = dot_nt(go[lo:n], v[:n])
            ds = (p * (gp - inner[lo:n, h : h + 1])).astype(BF16)
            out[0, lo:n, lanes] = (dot_nn(ds, k[:n]) * scale).astype(BF16)
            gv.append(dot_tn(p.astype(BF16), go[lo:n]))
            gk.append(dot_tn(ds, small[lo:n]))
        for b in range(t // QBLOCK):
            rows = slice(b * QBLOCK, (b + 1) * QBLOCK)
            out[1, rows, lanes] = sum(x[rows] for x in gk[b:]).astype(BF16)
            out[2, rows, lanes] = sum(x[rows] for x in gv[b:]).astype(BF16)


def attend_back(chain, qkv, gmixed, logs, inner, length, heads):
    t = qkv.shape[1]
    return chain.call(
        "attend_back",
        functools.partial(attend_back_body, heads),
        (length, qkv, gmixed, logs, inner),
        [SMEM, HELD, HELD, HELD, HELD],
        sds((3, t, len(heads) * HEAD_DIM), BF16),
        HELD,
        [],
        8,
    )


def whole_qkv(parts, flat, blocks):
    wide = blocks.shape[2]
    model = flat.shape[1] // 3
    at = 0
    for p in parts:
        size = p.shape[2]
        for which in range(3):
            lo = which * model + at
            flat[:, lo : lo + size] = p[which]
        at += size
    for f in range(blocks.shape[0]):
        blocks[f] = flat[:, f * wide : (f + 1) * wide]


def back_body(plan, wide, n_parts, n_out, me_ref, normal, inverse_in, act, a_in, gresid, t_in, g_two, g_b_fc, g_b_proj, *refs):
    parts, refs = refs[:n_parts], refs[n_parts:]
    input_grad, gouts, refs = refs[0], refs[1 : 1 + n_out], refs[1 + n_out :]
    flat, gq_v, tab, a_v, in_sem = refs
    late = pltpu.make_async_copy(a_in, a_v, in_sem)
    late.start()
    fsdp = plan.fsdp
    t, model = normal.shape
    table = Table(fsdp)
    spare = tab.shape[0] // fsdp
    whole_qkv(parts, flat, gq_v)
    me = Me(me_ref)

    def each():
        for away in range(2):
            for x in range(plan.nx):
                if plan.direct:
                    ends = [gouts[1 + h].at[x] if away else gouts[0].at[h, x] for h in range(2)]
                    yield me.fsdp(x, away), ends
                else:
                    yield 2 * x + away, [gouts[0].at[2 * x + away, :, :, h] for h in range(1)]

    for f, ends in each():
        grad = dot_tn(act[...], gq_v[f]).astype(BF16).reshape(*plan.split(), wide)
        for h, end in enumerate(ends):
            end[:, :, :, 0:wide] = grad[:, :, h]
    late.wait()
    back = dot_nt(flat[...], a_v[...])
    sums = dot_nn(jnp.ones((8, t), BF16), flat[...])
    n, inverse = normal[...], inverse_in[:, 0:1]
    tab[...] = jnp.zeros(tab.shape, F32)

    def put(k, value):
        r = (k // table.per) * spare + k % table.per
        tab[r : r + 1, :] = value

    put(0, jnp.sum(back * n, axis=0, keepdims=True))
    put(1, jnp.sum(back, axis=0, keepdims=True))
    put(2, g_two[0:1, :])
    put(3, g_two[1:2, :])
    put(4, sums[0:1, 0:model])
    put(5, sums[0:1, 2 * model :])
    put(6, g_two[2:3, :])
    put(7, g_b_proj[...])
    for j in range(fsdp):
        put(8 + j, g_b_fc[j : j + 1, :])
    for f, ends in each():
        rows = pl.ds(pl.multiple_of(f * spare, 8), spare)
        columns = jnp.transpose(tab[rows, :]).astype(BF16).reshape(*plan.split(), spare)
        for h, end in enumerate(ends):
            end[:, :, :, wide:] = columns[:, :, h]
    r = gresid[...] + norm_back(back, n, inverse, table.get(t_in, 0))
    input_grad[...] = r.astype(BF16)


def back(
    chain, plan, wide, full, me, normal, inverse, act, parts, a_can, gresid, t_can, g_two, g_b_fc, g_b_proj
):
    t, model = normal.shape
    fsdp = plan.fsdp
    lead = (fsdp, *plan.split(), full)
    if plan.direct:
        one = (plan.nx, plan.nz, 2, plan.rows // 2, full)
        grads = [sds((2, *one), BF16), sds(one, BF16), sds(one, BF16)]
    else:
        grads = [sds(lead, BF16)]
    return chain.call(
        "back",
        functools.partial(back_body, plan, wide, len(parts), len(grads)),
        (me, normal, inverse, act, a_can, gresid, t_can, g_two, g_b_fc, g_b_proj, *parts),
        [SMEM, HELD, HELD, HELD, HBM] + [HELD] * (5 + len(parts)),
        (sds((t, model), BF16), *grads),
        (VMEM,) + (HELD,) * len(grads),
        [
            pltpu.VMEM((t, 3 * model), BF16),
            pltpu.VMEM((fsdp, t, wide), BF16),
            pltpu.VMEM((fsdp * (full - wide), model), F32),
            pltpu.VMEM(a_can.shape, BF16),
            pltpu.SemaphoreType.DMA,
        ],
        20,
    )


def preload(chain, arrays):
    n = len(arrays)

    def body(*refs):
        todo = [
            pltpu.make_async_copy(a, b, refs[-1].at[i])
            for i, (a, b) in enumerate(zip(refs[:n], refs[n:-1]))
        ]
        for c in todo:
            c.start()
        for c in todo:
            c.wait()

    return chain.call(
        "preload",
        body,
        arrays,
        [HBM] * n,
        [sds(a.shape, a.dtype) for a in arrays],
        [HELD] * n,
        [pltpu.SemaphoreType.DMA((n,))],
        1,
    )


def update_body(count, *refs):
    norms = refs[0]
    n, m = 4 * count, 3 * count
    ins, norm_out, outs = refs[1 : 1 + n], refs[1 + n], refs[2 + n : 2 + n + m]
    made, out_sem = refs[2 + n + m : -1], refs[-1]
    norm = jnp.sqrt(jnp.sum(norms[...], axis=0, keepdims=True))
    norm_out[...] = norm
    factor = jnp.minimum(1.0, clip_limit / (norm[:, 0:1] + 1e-06))
    stores = []
    for i in range(count):
        w, g, one, two = (r[...] for r in ins[4 * i : 4 * i + 4])
        last = i == count - 1
        rate, decay = (rate_vector, 0.0) if last else (rate_matrix, decay_matrix)
        clipped = g * factor
        one_new = beta_one * one + (1.0 - beta_one) * clipped
        two_new = beta_two * two + (1.0 - beta_two) * clipped * clipped
        first_hat = one_new / (1.0 - beta_one**STEP)
        second_hat = two_new / (1.0 - beta_two**STEP)
        made[i][...] = w - rate * (first_hat / (jnp.sqrt(second_hat) + 1e-08) + decay * w)
        made[count + i][...] = one_new
        made[2 * count + i][...] = two_new
        for k in (i, count + i, 2 * count + i):
            c = pltpu.make_async_copy(made[k], outs[k], out_sem.at[k])
            c.start()
            stores.append(c)
    for c in stores:
        c.wait()


def update(chain, norms, weights, grads, firsts, seconds):
    count = len(weights)
    ins = []
    for group in zip(weights, grads, firsts, seconds):
        ins += group
    outs = [sds(w.shape, F32) for w in weights] * 3
    return chain.call(
        "update",
        functools.partial(update_body, count),
        [norms, *ins],
        [VMEM] + [HELD if i % 4 != 1 else VMEM for i in range(len(ins))],
        (sds((1, 128), F32), *outs),
        (VMEM,) + (HBM,) * len(outs),
        [pltpu.VMEM(v.shape, F32) for v in outs] + [pltpu.SemaphoreType.DMA((len(outs),))],
        12,
    )


def place_second(chain, name, plan, me, z0, r0, z1, r1):
    def copies(m):
        return [
            (0, ALL, [(0, (m.y,)), (2, (m.y,))]),
            (1, ALL, [(0, (m.other_y,)), (2, (m.other_y,))]),
            (2, ALL, [(1, (m.x,)), (3, (m.x,))]),
            (3, ALL, [(1, (m.other_x,)), (3, (m.other_x,))]),
        ]

    return move(chain, name, me, [z0, r0, z1, r1], [(2, *z0.shape), (2, *z1.shape)] * 2, copies)


class Parts:
    def __init__(self, groups, far=0):
        self.count, self.far = len(groups), far
        self.arrays = [own for own, _ in groups] + [v for _, came in groups for v in came]
        self.lanes, self.came, at, place = [], [], 0, self.count
        for own, came in groups:
            self.lanes.append(slice(at, at + own.shape[-1]))
            self.came.append((place, len(came)))
            at += own.shape[-1]
            place += len(came)
        _, self.nx, self.nz, _, self.rows, _ = groups[0][0].shape
        self.cols = at

    def terms(self, g, h, at):
        place, n = self.came[g]
        return [(g, (h, *at)), (place, (h, *at)) if n == 1 else (place + h, at)]

    def sums(self, make):
        return [
            item
            for g, lanes in enumerate(self.lanes)
            for item in make(g, (self.rows, lanes.stop - lanes.start), lanes)
        ]


def first_sums(chain, plan, name, me, parts):
    nx, nz = parts.nx, parts.nz

    def sums(m):
        return parts.sums(
            lambda g, end, lanes: [
                (0, (ALL, ALL, ALL, lanes), (nz, 2, *end), parts.terms(g, 0, (m.other_x,))),
                (1, (ALL, ALL, ALL, lanes), (nx, nz, *end), parts.terms(g, 1, (ALL, ALL, m.other_y))),
            ]
        )

    outs = [sds((nz, 2, parts.rows, parts.cols), BF16), sds((nx, nz, parts.rows, parts.cols), BF16)]
    s0, s1 = add_up(chain, name + "1", me, parts.arrays, outs, sums, far=parts.far)
    return plan.partner(name, s0, "x"), plan.partner(name, s1, "y")


def second_sums(chain, plan, name, me, parts, f0, f1):
    n = len(parts.arrays)

    def sums(m):
        at0, at1 = (m.x, ALL, m.other_y), (m.other_x, ALL, m.y)

        def make(g, end, lanes):
            one = parts.terms(g, 0, at0) + [(n, (ALL, m.other_y, ALL, lanes))]
            two = parts.terms(g, 1, at1) + [(n + 1, (m.other_x, ALL, ALL, lanes))]
            shape = (parts.nz, *end)
            return [(0, (ALL, ALL, lanes), shape, one), (1, (ALL, ALL, lanes), shape, two)]

        return parts.sums(make)

    outs = [sds((parts.nz, parts.rows, parts.cols), BF16)] * 2
    arrays = [*parts.arrays, f0, f1]
    s0, s1 = add_up(chain, name + "2", me, arrays, outs, sums, far=parts.far)
    return plan.partner(name, s0, "y"), plan.partner(name, s1, "x")


def third_sums(chain, plan, name, me, parts, f0, f1, s0, s1, merged):
    n, rows = len(parts.arrays), parts.rows

    def sums(m):
        def make(g, end, lanes):
            out = []
            for k in range(parts.nz):
                z = m.z ^ k
                at = (m.x, z, m.y)
                one = parts.terms(g, 0, at) + [(n, (z, m.y, ALL, lanes)), (n + 2, (z, ALL, lanes))]
                two = parts.terms(g, 1, at) + [(n + 1, (m.x, z, ALL, lanes)), (n + 3, (z, ALL, lanes))]
                t, ti = z_target(k, merged)
                out.append((t, (*ti, slice(0, rows), lanes), end, one))
                out.append((t, (*ti, slice(rows, 2 * rows), lanes), end, two))
            return out

        return parts.sums(make)

    outs = z_outs((2 * rows, parts.cols), merged)
    arrays = [*parts.arrays, f0, f1, s0, s1]
    return add_up(chain, name + "3", me, arrays, outs, sums, far=parts.far)


def z_outs(shape, merged):
    if merged:
        return [sds(shape, F32), sds((2, *shape), BF16), sds(shape, BF16)]
    return [sds(shape, F32)] + [sds(shape, BF16)] * 3


def z_target(k, merged):
    if merged and k in (1, 3):
        return 1, (k // 2,)
    return k, ()


def along_z(chain, plan, name, me, two, came, at):
    (total,) = add_up(
        chain, name, me, [two, came], [two], lambda m: [(0, ALL, two.shape, [(0, ALL), (1, at)])]
    )
    return total


def squared(*values):
    return jnp.broadcast_to(sum(jnp.sum(v * v) for v in values), (1, 128))


def body(
    tokens,
    lengths,
    cotangent,
    qkv_weight,
    out_weight,
    fc_weight,
    proj_weight,
    vectors,
    qkv_first,
    out_first,
    fc_first,
    proj_first,
    vectors_first,
    qkv_second,
    out_second,
    fc_second,
    proj_second,
    vectors_second,
):
    dp, fsdp = lax.axis_size("dp"), lax.axis_size("fsdp")
    model = tokens.shape[1]
    wide, cut = qkv_weight.shape[1], out_weight.shape[1]
    hidden = fc_weight.shape[1] * fsdp
    per = vectors.shape[1]
    plan = Plan(dp, fsdp, model, hidden)
    rows, half, chalf, nz = plan.rows, plan.rows // 2, plan.cols // 2, plan.nz
    a_full = -(-(wide + per) // 128) * 128
    b_full = model + -(-cut // 128) * 128
    chain = Chain()
    at_dp, at_fsdp = lax.axis_index("dp"), lax.axis_index("fsdp")
    me = jnp.stack([at_dp // 2, at_dp % 2, at_fsdp // 2, at_fsdp % 2]).astype(jnp.int32)
    heads = model // HEAD_DIM
    third = [range(i, i + heads // 3) for i in range(0, heads, heads // 3)]

    def turned(value):
        return jnp.transpose(value)

    state = (
        *(qkv_weight, out_weight, fc_weight, turned(proj_weight), turned(vectors)),
        *(qkv_first, out_first, fc_first, turned(proj_first), turned(vectors_first)),
        *(qkv_second, out_second, fc_second, turned(proj_second), turned(vectors_second)),
    )

    if plan.direct:
        a_own, b_own, c_own = pack(chain, plan, state[:5], a_full, b_full)
        a_near, a_far = plan.partner("gather_a", a_own, "z", 1), plan.partner("gather_a", a_own, "z", 2)
        c_y, c_x = plan.partner("gather_c", c_own[0], "y"), plan.partner("gather_c", c_own[1], "x")
        chain.wait_for(c_y, c_x)
        a_far, b_own = gate(chain, "gate_z", a_far, b_own)
        a_came = [a_near, a_far, plan.partner("gather_a", a_far, "z", 1)]
        b_came = plan.gather_z("gather_b", b_own)

        def place_a(m):
            return [(k, ALL, [(0, (m.z ^ k,))]) for k in range(nz)]

        (a_z,) = move(chain, "place_a1", me, [a_own, *a_came], [(nz, rows, a_full)], place_a)
        a_y, a_x = plan.partner("gather_a", a_z, "y"), plan.partner("gather_a", a_z, "x")
        a_xy = plan.opposite("gather_a", a_z)

        def place_b(m):
            return [
                (k, pl.ds(h * half, half), [(h, (m.z ^ k,))]) for k in range(nz) for h in range(2)
            ] + [
                (nz, (0,), [(2, (m.y,))]),
                (nz + 1, ALL, [(2, (m.other_y,))]),
                (nz, (1,), [(2, (2 + m.x,))]),
                (nz + 2, ALL, [(2, (2 + m.other_x,))]),
            ]

        outs = [(nz, half, b_full), (nz, half, b_full), (4, chalf, plan.deep)]
        arrays = [b_own, *b_came, c_own, c_y, c_x]
        chain.wait_for(a_y, a_x, a_xy)
        b_z0, b_z1, c_pair = move(chain, "place_b1", me, arrays, outs, place_b)
        b_r0, b_r1 = plan.partner("gather_b", b_z0, "y"), plan.partner("gather_b", b_z1, "x")
        a_in = gate(chain, "gate_a", a_z, a_y, a_x, a_xy)
        a_in = a_in + [plan.partner("gather_a", v, "core") for v in a_in]
        c_near, c_far = plan.partner("gather_c", c_pair, "z", 1), plan.partner("gather_c", c_pair, "z", 2)
    else:

        def whole(shard):
            down = lax.all_gather(shard.astype(BF16), "dp", axis=0, tiled=True)
            return lax.all_gather(down, "fsdp", axis=0, tiled=False)

        def padded(parts, full):
            both = jnp.concatenate(parts, axis=1)
            both = whole(jnp.pad(both, ((0, 0), (0, full - both.shape[1]))))
            return both.reshape(fsdp, *plan.split(), full)

        a_in = [padded([qkv_weight, vectors], a_full)]
        b_in = [padded([fc_weight, out_weight], b_full)]
        c_all = jnp.transpose(whole(proj_weight), (0, 2, 1))
        c_all = c_all.reshape(model, fsdp, 2, hidden // fsdp // 2)
        c_in = [jnp.transpose(c_all, (1, 2, 0, 3))]

    qkv, act_one, a_can, t_can, n_one, inv_one = front(chain, plan, me, tokens, a_in, wide)
    if plan.direct:
        b_p0, b_p1, *b_pc = place_second(chain, "place_b2", plan, me, b_z0, b_r0, b_z1, b_r1)
        b_q0, b_q1 = plan.partner("gather_b", b_p0, "x"), plan.partner("gather_b", b_p1, "y")
    if plan.direct:
        c_near, c_far, *b_pc = gate(chain, "gate_c1", c_near, c_far, *b_pc)
        c_last = plan.partner("gather_c", c_far, "z", 1)
        b_pc = [plan.partner("gather_b", v, "core") for v in b_pc]
    parts = [attend(chain, qkv, lengths, group) for group in third]
    if plan.direct:
        b_q0, b_q1 = gate(chain, "gate_b", b_q0, b_q1)
        b_qc = [plan.partner("gather_b", v, "core") for v in (b_q0, b_q1)]
        b_in = [b_p0, b_p1, b_q0, b_q1, *b_pc, *b_qc]
        chain.wait_for(*b_pc)

        def place_c2(m):
            return [
                (k, (2 * h + p,), [(h, (p, m.z ^ k)), (2, (h, p, m.z ^ k))])
                for k in range(nz)
                for h in range(2)
                for p in range(2)
            ]

        outs = [(2, nz, chalf, plan.deep)] * 2 + [(2, 2, nz, chalf, plan.deep)]
        c_p0, c_p1, c_p = move(chain, "place_c2", me, [c_pair, c_near, c_far, c_last], outs, place_c2)
        c_q0, c_q1 = plan.partner("gather_c", c_p0, "x"), plan.partner("gather_c", c_p1, "y")
        c_pc = plan.partner("gather_c", c_p, "core")
    logs = [p[1] for p in parts]
    resid_two, act_two, wout, mixed, n_two, inv_two = join(
        chain, plan, me, cut, tokens, [p[0] for p in parts], b_in, t_can
    )
    if plan.direct:
        chain.wait_for(c_pc)
    gel, slope, b_can, g_b_proj, *g_c = mlp_up(
        chain, plan, me, act_two, cotangent, t_can, b_in, hidden
    )
    if plan.direct:
        c_q0, c_q1, away = gate(chain, "gate_c", c_q0, c_q1, g_c[1])
        c_in = [c_p, c_q0, c_q1, c_pc] + [plan.partner("gather_c", v, "core") for v in (c_q0, c_q1)]
        c_away = plan.partner("sum_c", away, "core")
    if plan.direct:
        c_parts = Parts([(g_c[0], [c_away])])
        c_f0, c_f1 = first_sums(chain, plan, "sum_c", me, c_parts)
    gpre, g_b_fc, c_can = mlp_down(chain, plan, me, cotangent, slope, c_in)

    gact, *g_b = mlp_back(chain, plan, me, act_two, gpre, b_can)
    if plan.direct:
        b_away = [plan.partner("sum_b", v, "core") for v in g_b[1:]]
    gresid, gmixed, inner, g_two, *g_o = join_back(
        chain, plan, me, gact, cotangent, n_two, inv_two, mixed, wout, t_can, b_full - model
    )
    if plan.direct:
        chain.wait_for(c_f0, c_f1)
        o_away = [plan.partner("sum_b", *gate(chain, "gate_o", g_o[1]), "core")]
        b_parts = Parts([(g_b[0], b_away), (g_o[0], o_away)])
    gparts = [attend_back(chain, qkv, gmixed, logs[0], inner, lengths, third[0])]
    if plan.direct:
        b_f0, b_f1 = first_sums(chain, plan, "sum_b", me, b_parts)

        def sums_cz(m):
            out = []
            for k in range(nz):
                z = m.z ^ k
                at = (0, m.x, z)
                terms = [(0, at), (1, at), (2, (z,))]
                t, ti = z_target(k, True)
                out.append((t, (*ti, slice(0, 2)), (2, chalf, plan.deep), terms))
                at = (1, ALL, z, m.y)
                terms = [(0, at), (1, at), (3, (ALL, z))]
                out.append((t, (*ti, slice(2, 4)), (2, chalf, plan.deep), terms))
            return out

        outs = z_outs((4, chalf, plan.deep), True)
        arrays = [g_c[0], c_away, c_f0, c_f1]
        c_u = add_up(chain, "sum_c2", me, arrays, outs, sums_cz)
        c_near = plan.partner("sum_c", c_u[1], "z", 1)
    for log, group in zip(logs[1:], third[1:]):
        gparts.append(attend_back(chain, qkv, gmixed, log, inner, lengths, group))
    kept = (n_one, inv_one, act_one, gparts, a_can, gresid, t_can, g_two, g_b_fc, g_b_proj)
    input_grad, *g_a = back(chain, plan, wide, a_full, me, *kept)

    if plan.direct:
        c_two = along_z(chain, plan, "sum_c4", me, c_u[2], c_near, (1,))
        c_z = [c_u[0], c_near, plan.partner("sum_c", c_two, "z", 2)]
        b_s0, b_s1 = second_sums(chain, plan, "sum_b", me, b_parts, b_f0, b_f1)
        a_away = [plan.partner("sum_a", v, "core") for v in gate(chain, "gate_s", *g_a[1:])]
        a_parts = Parts([(g_a[0], a_away)])
        a_f0, a_f1 = first_sums(chain, plan, "sum_a", me, a_parts)
        output = mlp_out(chain, plan, resid_two, gel, c_can, t_can)
        b_u = third_sums(chain, plan, "sum_b", me, b_parts, b_f0, b_f1, b_s0, b_s1, True)
        b_near = plan.partner("sum_b", b_u[1], "z", 1)
        a_s0, a_s1 = second_sums(chain, plan, "sum_a", me, a_parts, a_f0, a_f1)
        z_lead = ((), (0,), ())

        def sums_c3(m):
            block = (chalf, plan.deep)
            one = [(i, (*lead, m.other_y)) for i, lead in enumerate(z_lead)]
            two = [(i, (*lead, 2 + m.other_x)) for i, lead in enumerate(z_lead)]
            return [(0, ALL, block, one), (1, ALL, block, two)]

        outs = [sds((chalf, plan.deep), BF16)] * 2
        s0, s1 = add_up(chain, "sum_c3", me, c_z, outs, sums_c3)
        c_l0, c_l1 = plan.partner("sum_c", s0, "y"), plan.partner("sum_c", s1, "x")
        b_two = along_z(chain, plan, "sum_b4", me, b_u[2], b_near, (1,))
        b_z = [b_u[0], b_near, plan.partner("sum_b", b_two, "z", 2)]
        a_u = third_sums(chain, plan, "sum_a", me, a_parts, a_f0, a_f1, a_s0, a_s1, False)
        a_via = plan.partner("sum_a", a_u[3], "z", 1)

        def sums_c(m):
            block = (chalf, plan.deep)
            one = [(i, (*lead, m.y)) for i, lead in enumerate(z_lead)] + [(3, ALL)]
            two = [(i, (*lead, 2 + m.x)) for i, lead in enumerate(z_lead)] + [(4, ALL)]
            return [(0, ALL, block, one), (1, ALL, block, two)]

        a_two = along_z(chain, plan, "sum_a4", me, a_u[2], a_via, ALL)
        a_far = plan.partner("sum_a", a_two, "z", 2)
        a_near = plan.partner("sum_a", *gate(chain, "gate_z", a_u[1]), "z", 1)
        a_z = [a_u[0], a_far, a_near]
        state = preload(chain, state)


        def end_c(done, outs):
            outs[0][0:chalf, :] = done[0]
            outs[0][chalf:, :] = done[1]
            outs[1][...] = squared(*done)

        d_proj, s_c = add_up(
            chain,
            "end_c",
            me,
            [*c_z, c_l0, c_l1],
            [sds((plan.cols, plan.deep), F32), sds((1, 128), F32)],
            sums_c,
            end_c,
        )
        def last_b(m):
            shape = b_z[0].shape
            return [(0, ALL, shape, [(i, lead or ALL) for i, lead in enumerate(z_lead)])]

        def last_a(m):
            return [(0, ALL, a_z[0].shape, [(i, ALL) for i in range(len(a_z))])]

        def end_b(done, outs):
            total = done[0]
            fc, out = total[:, :model], total[:, model : model + cut]
            outs[0][...] = fc
            outs[1][...] = out
            outs[2][...] = squared(fc, out)

        shapes = [fc_weight.shape, out_weight.shape, (1, 128)]
        d_fc, d_out, s_b = add_up(
            chain, "end_b", me, b_z, [sds(s, F32) for s in shapes], last_b, end_b
        )

        def end_a(done, outs):
            total = done[0]
            start = wide // 128 * 128
            vec = jnp.transpose(total[:, start:])[wide - start : wide - start + per]
            qkv = total[:, :wide]
            outs[0][...] = qkv
            outs[1][...] = vec
            outs[2][...] = squared(qkv, vec)

        shapes = [qkv_weight.shape, (per, rows), (1, 128)]
        d_qkv, d_vec, s_a = add_up(
            chain, "end_a", me, a_z, [sds(s, F32) for s in shapes], last_a, end_a
        )
        squares = s_a + s_b + s_c
    else:
        output = mlp_out(chain, plan, resid_two, gel, c_can, t_can)

        def shared(value):
            mine = lax.psum_scatter(value, "fsdp", scatter_dimension=0, tiled=False)
            return lax.psum_scatter(mine, "dp", scatter_dimension=0, tiled=True).astype(F32)

        d_a = shared(g_a[0].reshape(fsdp, model, a_full))
        d_qkv, d_vec = d_a[:, :wide], turned(d_a[:, wide : wide + per])
        d_out = shared(jnp.transpose(g_o[0].reshape(model, fsdp, cut), (1, 0, 2)))
        d_fc = shared(g_b[0].reshape(fsdp, model, model))
        d_c = jnp.transpose(g_c[0], (2, 0, 1, 3)).reshape(fsdp, plan.cols, hidden)
        d_proj = turned(shared(jnp.transpose(d_c, (0, 2, 1))))
        total = sum(jnp.sum(d * d) for d in (d_qkv, d_out, d_fc, d_proj, d_vec))
        squares = jnp.full((1, 128), total)

    sent = jnp.broadcast_to(squares[None], (dp * fsdp, 1, 128))
    with jax.named_scope("norm"):
        norms = lax.all_to_all(sent, ("dp", "fsdp"), 0, 0, tiled=True).reshape(dp * fsdp, 128)
    norm, *new = update(
        chain, norms, state[:5], (d_qkv, d_out, d_fc, d_proj, d_vec), state[5:10], state[10:]
    )
    new = [turned(v) if i % 5 in (3, 4) else v for i, v in enumerate(new)]
    return (output, input_grad, norm[0, 0], *new)


def solution(mesh):
    tokens = P(("dp", "fsdp"), None)
    table = P("dp", "fsdp")
    return jax.shard_map(
        body,
        mesh=mesh,
        in_specs=(tokens, P(("dp", "fsdp")), tokens) + (table,) * 15,
        out_specs=(tokens, tokens, P()) + (table,) * 15,
        check_vma=False,
    )
```
